128 devices in a mesh: dp: 8 (over y, z_lo), sp: 16 (over x, z_hi, core).
Axes of the slice: x: 4, y: 4, z: 4 (z_hi: 2, z_lo: 2; z = z_hi * 2 + z_lo), core: 2. Of those that a mesh axis runs over, the one named last changes fastest.
Arguments:
- inputs: bfloat16 [16384, 2048], P(('dp', 'sp')), may hold values from -6 to 6
- cotangent: bfloat16 [16384, 2048], P(('dp', 'sp')), may hold values from -6 to 6
- mix_weights: bfloat16 [4, 2048, 2048], P(None, None, 'sp'), may hold values from -0.125 to 0.125
- out_weight: bfloat16 [2048, 2048], P('sp'), may hold values from -0.25 to 0.25
- key_weight: bfloat16 [2048, 7168], P(None, 'sp'), may hold values from -0.125 to 0.125
- value_weight: bfloat16 [7168, 2048], P('sp'), may hold values from -0.0625 to 0.0625
- recept_weight: bfloat16 [2048, 2048], P(None, 'sp'), may hold values from -0.125 to 0.125
- vectors: float32 [14, 2048], replicated, may hold values from -12 to 2, as said below
- segment_ids: int32 [16384], P('dp'), may hold values from 0 to 2, as said below
Outputs:
- mixed: bfloat16 [16384, 2048], P(('dp', 'sp'))
- input_grad: float32 [16384, 2048], P(('dp', 'sp'))
- mix_weights_grad: float32 [4, 2048, 2048], P(None, 'dp', 'sp')
- out_weight_grad: float32 [2048, 2048], P('sp', 'dp')
- key_weight_grad: float32 [2048, 7168], P('dp', 'sp')
- value_weight_grad: float32 [7168, 2048], P('sp', 'dp')
- recept_weight_grad: float32 [2048, 2048], P('dp', 'sp')
- vectors_grad: float32 [14, 2048], P(None, ('dp', 'sp'))
The draws below stay inside these ranges and needn't reach their ends.
Inputs may be any that keep to these rules, and one draw needn't show every extreme that they name: `vectors`: rows in order: w1, b1, mu_r, mu_k, mu_v, mu_g, dec, u, gw, gb, w2, b2, nu_k, nu_r; the recurrence multiplies its state by exp(-exp(dec)) per token. `segment_ids`: within each group of 2048 tokens the numbers start at 0, never fall and rise by one where a new sequence starts; a group holds two or three sequences.
All inputs are finite; a program needn't handle non-finite values.
Results may differ from the reference program's by a relative error of at most 0.02.
Values may be sent and summed in bfloat16 or wider, within the bound.
A program may use at most 448 MiB of HBM per device.

```python
import math
import jax
import jax.numpy as jnp
from jax import lax

EMBED_SIZE = 2048
HEADS = 32
FF = 7168
ATTENTION_WIDTH = 64
TOK_DEV = 128
SPAN = 64
GROUP = 2048
TOKENS = 16384


def draw_vectors(key, part):
    key = jax.random.fold_in(key, 7)
    lookup_arrays = jax.random.split(key, 7)
    gain_low, gain_high, slow_share = (0.5, 1.5, 0.5)
    scaling_coefficients = jax.random.uniform(lookup_arrays[0], (3, EMBED_SIZE), jnp.float32, gain_low, gain_high)
    shift_offsets = 0.5 * jax.random.uniform(lookup_arrays[1], (3, EMBED_SIZE), jnp.float32, -1.0, 1.0)
    blend_coefficients = jax.random.uniform(lookup_arrays[2], (6, EMBED_SIZE), jnp.float32, 0.1, 0.9)
    slow_heads = jax.random.uniform(lookup_arrays[3], (HEADS,), jnp.float32) < slow_share
    fast_log = jax.random.uniform(lookup_arrays[4], (HEADS, EMBED_SIZE // HEADS), jnp.float32, math.log(1.0 / 20.0), math.log(1.0 / 8.0))
    slow_log = jax.random.uniform(lookup_arrays[5], (HEADS, EMBED_SIZE // HEADS), jnp.float32, math.log(0.2 / GROUP), math.log(2.0 / GROUP))
    forgetting_multiplier = jnp.where(slow_heads[:, None], slow_log, fast_log).reshape(EMBED_SIZE)
    present_reward = jax.random.uniform(lookup_arrays[6], (EMBED_SIZE,), jnp.float32, -1.0, 1.0)
    return jnp.stack([scaling_coefficients[0], shift_offsets[0], blend_coefficients[0], blend_coefficients[1], blend_coefficients[2], blend_coefficients[3], forgetting_multiplier, present_reward, scaling_coefficients[1], shift_offsets[1], scaling_coefficients[2], shift_offsets[2], blend_coefficients[4], blend_coefficients[5]]).astype(jnp.float32)


def draw_segment_ids(key, part):
    key = jax.random.fold_in(key, 11)
    groups = TOKENS // GROUP
    position = jnp.arange(GROUP)

    def one_group(group_key):
        lookup_arrays = jax.random.split(group_key, 3)
        layout = jax.random.randint(lookup_arrays[0], (), 0, 3)
        early = jax.random.randint(lookup_arrays[1], (), 1, TOK_DEV)
        late = jax.random.randint(lookup_arrays[2], (), GROUP - TOK_DEV + 1, GROUP)
        first_long = (position >= late).astype(jnp.int32)
        middle_long = (position >= early).astype(jnp.int32) + (position >= late).astype(jnp.int32)
        last_long = (position >= early).astype(jnp.int32)
        return jnp.where(layout == 0, first_long, jnp.where(layout == 1, middle_long, last_long))
    return jax.vmap(one_group)(jax.random.split(key, groups)).reshape(-1).astype(jnp.int32)


def block_levels(key, shape, cuts, least, high):
    factor_of = 1.0
    for dim, blocks in cuts:
        steps = jax.random.uniform(jax.random.fold_in(jax.random.fold_in(key, 6), dim), (blocks,), jnp.float32, least / len(cuts), high / len(cuts))
        factor_of = factor_of * jnp.repeat(jnp.exp(steps), shape[dim] // blocks).reshape((-1,) + (1,) * (len(shape) - 1 - dim))
    return factor_of


def noise(own_key, dims, scale, reach, cuts=(), dtype=jnp.bfloat16):
    entries = jax.random.normal(own_key, dims, jnp.float32) * scale
    if len(cuts) > 0:
        entries = block_levels(own_key, dims, cuts, -0.22, 0.18) * entries
    return jnp.clip(entries, min=-reach, max=reach).astype(dtype)


def setup_inputs(seed: int = 0) -> dict:
    key_of = jax.random.split(jax.random.key(seed), 10)
    return {
        "inputs": noise(key_of[0], (TOKENS, EMBED_SIZE), 1.0, 6.0, ((0, 128),)),
        "cotangent": noise(key_of[1], (TOKENS, EMBED_SIZE), 1.0, 6.0, ((0, 128),)),
        "mix_weights": noise(key_of[2], (4, EMBED_SIZE, EMBED_SIZE), EMBED_SIZE ** -0.5, 0.125, ((2, 16),)),
        "out_weight": noise(key_of[3], (EMBED_SIZE, EMBED_SIZE), (EMBED_SIZE // 4) ** -0.5, 0.25, ((0, 16),)),
        "key_weight": noise(key_of[4], (EMBED_SIZE, FF), EMBED_SIZE ** -0.5, 0.125, ((1, 16),)),
        "value_weight": noise(key_of[5], (FF, EMBED_SIZE), FF ** -0.5, 0.0625, ((0, 16),)),
        "recept_weight": noise(key_of[6], (EMBED_SIZE, EMBED_SIZE), EMBED_SIZE ** -0.5, 0.125, ((1, 16),)),
        "vectors": draw_vectors(jax.random.fold_in(key_of[9], 71), 0),
        "segment_ids": draw_segment_ids(jax.random.fold_in(key_of[9], 71), 0),
    }


highest = lax.Precision.HIGHEST

@jax.custom_vjp
def low(v):
    return lax.optimization_barrier(v.astype(jnp.bfloat16)).astype(jnp.float32)

@jax.custom_vjp
def low_back(v):
    return v

def low_keep(v):
    return (low(v), None)

def low_pass(kept, grad):
    return (grad,)

def back_keep(v):
    return (v, None)

def back_low(kept, grad):
    return (low(grad),)
low.defvjp(low_keep, low_pass)
low_back.defvjp(back_keep, back_low)

def layer_norm(tensor, gain_row, bias_row):
    center = tensor - lax.optimization_barrier(jnp.mean(tensor, axis=-1, keepdims=True))
    spread = lax.optimization_barrier(jnp.mean(center * center, axis=-1, keepdims=True))
    return center * lax.rsqrt(spread + 1e-05) * gain_row + bias_row

def head_norm(tensor, gain_row, bias_row):
    tokens = tensor.shape[0]
    grouped = tensor.reshape(tokens, -1, ATTENTION_WIDTH)
    center = grouped - lax.optimization_barrier(jnp.mean(grouped, axis=-1, keepdims=True))
    spread = lax.optimization_barrier(jnp.mean(center * center, axis=-1, keepdims=True))
    return (center * lax.rsqrt(spread + 0.00064)).reshape(tokens, -1) * gain_row + bias_row

def previous(tensor, same_seg):
    moved = jnp.concatenate([jnp.zeros_like(tensor[:1]), tensor[:-1]], axis=0)
    return moved * same_seg[:, None]

def memory_per_tile(memory_collection, prior_sequence, acceptance_records, lookup_records, payload_records, sequence_records, natural_log_speed, present_reward):
    length = acceptance_records.shape[0]
    position = jnp.arange(length)
    offsets = position.astype(jnp.float32)[:, None, None]
    rising = jnp.exp(natural_log_speed[None] * offsets)
    falling = jnp.exp(-natural_log_speed[None] * (offsets + 1.0))
    r_scaled = acceptance_records * rising
    k_scaled = lookup_records * falling
    scores = jnp.einsum('ihc,jhc->hij', r_scaled, k_scaled, precision=highest)
    block_mask = ((position[None, :] < position[:, None]) & (sequence_records[None, :] == sequence_records[:, None])).astype(jnp.float32)
    scores = scores * block_mask[None]
    reward_extra = lax.optimization_barrier(jnp.sum(acceptance_records * lookup_records * present_reward[None], axis=-1))
    kept_rows = (sequence_records == prior_sequence).astype(jnp.float32)
    level_result = jnp.einsum('hij,jhe->ihe', scores, payload_records, precision=highest)
    level_result = level_result + reward_extra[:, :, None] * payload_records
    level_result = level_result + kept_rows[:, None, None] * jnp.einsum('ihc,hce->ihe', r_scaled, memory_collection, precision=highest)
    last_seg = sequence_records[length - 1]
    tail_rows = (sequence_records == last_seg).astype(jnp.float32)
    carried = (last_seg == prior_sequence).astype(jnp.float32)
    whole_decay = jnp.exp(natural_log_speed * length)
    k_end = lookup_records * jnp.exp(natural_log_speed[None] * (length - 1.0 - offsets)) * tail_rows[:, None, None]
    revised_memory = carried * whole_decay[:, :, None] * memory_collection + jnp.einsum('jhc,jhe->hce', k_end, payload_records, precision=highest)
    return (revised_memory, level_result)

def temporal_blend(acceptance_entries, lookup_entries, payload_entries, sequence_identifiers, forgetting_multiplier, present_reward):
    tokens = acceptance_entries.shape[0]
    blocks = tokens // SPAN
    attention_total = acceptance_entries.shape[1] // ATTENTION_WIDTH
    shape_blk = (blocks, SPAN, attention_total, ATTENTION_WIDTH)
    natural_log_speed = -jnp.exp(forgetting_multiplier).reshape(attention_total, ATTENTION_WIDTH)
    reward_each_group = present_reward.reshape(attention_total, ATTENTION_WIDTH)

    def one_block(carried, pieces):
        memory_collection, prior_sequence = carried
        acceptance_slice, lookup_slice, payload_slice, sequence_slice = pieces
        revised_memory, level_result = memory_per_tile(memory_collection, prior_sequence, acceptance_slice, lookup_slice, payload_slice, sequence_slice, natural_log_speed, reward_each_group)
        return ((revised_memory, sequence_slice[SPAN - 1]), level_result)
    init_state = (jnp.zeros((attention_total, ATTENTION_WIDTH, ATTENTION_WIDTH), jnp.float32), jnp.array(-1, jnp.int32))
    unused_item, results = lax.scan(jax.checkpoint(one_block), init_state, (acceptance_entries.reshape(shape_blk), lookup_entries.reshape(shape_blk), payload_entries.reshape(shape_blk), sequence_identifiers.reshape(blocks, SPAN).astype(jnp.int32)))
    return results.reshape(tokens, -1)

def layer_group(inputs_f, sequence_identifiers, mix_weights, out_weight, key_weight, value_weight, recept_weight, vectors):
    same_seg = jnp.concatenate([jnp.zeros((1,), jnp.float32), (sequence_identifiers[1:] == sequence_identifiers[:-1]).astype(jnp.float32)])
    normed = low(layer_norm(inputs_f, vectors[0], vectors[1]))
    shift_one = previous(normed, same_seg) - normed
    projected = []
    for slot_idx in range(4):
        mixed = low(normed + shift_one * vectors[2 + slot_idx])
        projected.append(low_back(jnp.dot(mixed, mix_weights[slot_idx], precision=highest)))
    mixed_time = temporal_blend(projected[0], projected[1], projected[2], sequence_identifiers, vectors[6], vectors[7])
    gated = low(head_norm(mixed_time, vectors[8], vectors[9]) * jax.nn.silu(projected[3]))
    hidden = inputs_f + low_back(jnp.dot(gated, out_weight, precision=highest))
    normed_two = low(layer_norm(hidden, vectors[10], vectors[11]))
    shift_two = previous(normed_two, same_seg) - normed_two
    key_in = low(normed_two + shift_two * vectors[12])
    recept_in = low(normed_two + shift_two * vectors[13])
    key_pre = low_back(jnp.dot(key_in, key_weight, precision=highest))
    squared = low(jnp.square(jax.nn.relu(key_pre)))
    value_rows = low_back(jnp.dot(squared, value_weight, precision=highest))
    gate_val = jax.nn.sigmoid(low_back(jnp.dot(recept_in, recept_weight, precision=highest)))
    return hidden + low_back(low(gate_val * value_rows))

def whole_layer(inputs_f, sequence_identifiers, mix_weights, out_weight, key_weight, value_weight, recept_weight, vectors):
    groups = inputs_f.shape[0] // GROUP

    def one_group(carried, pieces):
        return (carried, layer_group(pieces[0], pieces[1], mix_weights, out_weight, key_weight, value_weight, recept_weight, vectors))
    unused_item, outputs = lax.scan(jax.checkpoint(one_group), jnp.zeros((), jnp.float32), (inputs_f.reshape(groups, GROUP, -1), sequence_identifiers.reshape(groups, GROUP)))
    return outputs.reshape(inputs_f.shape)

def reference(inputs, cotangent, mix_weights, out_weight, key_weight, value_weight, recept_weight, vectors, segment_ids):
    sequence_identifiers = segment_ids.astype(jnp.int32)

    def layer_fn(x_in, w_mix, w_out, w_key, w_value, w_recept, vec_in):
        return whole_layer(x_in, sequence_identifiers, w_mix, w_out, w_key, w_value, w_recept, vec_in)
    level_result, pull_back = jax.vjp(layer_fn, inputs.astype(jnp.float32), mix_weights.astype(jnp.float32), out_weight.astype(jnp.float32), key_weight.astype(jnp.float32), value_weight.astype(jnp.float32), recept_weight.astype(jnp.float32), vectors.astype(jnp.float32))
    grads = pull_back(cotangent.astype(jnp.float32))
    return (level_result.astype(jnp.bfloat16), grads[0], grads[1], grads[2], grads[3], grads[4], grads[5], grads[6])
```

```python
import functools

import jax
import jax.numpy as jnp
from jax import lax
from jax.experimental import pallas as pl
from jax.experimental.pallas import tpu as pltpu
from jax.sharding import PartitionSpec as P

MESH = pl.DeviceIdType.MESH
VMEM = pltpu.VMEM
DMA = pltpu.SemaphoreType.DMA

ATTENTION_WIDTH = 64
SPAN = 64


class Place:
    def __init__(self):
        self.dp = lax.axis_index("dp")
        s = lax.axis_index("sp")
        self.s = s
        self.x, self.z, self.c = s // 4, (s // 2) % 2, s % 2

    def at(self, dx=0, dz=0, dc=0):
        x = (self.x + dx) % 4
        z = (self.z + dz) % 2
        c = (self.c + dc) % 2
        return x * 4 + z * 2 + c

    def dev(self, s):
        return (self.dp, s)


def greet(place, peers):
    barrier = pltpu.get_barrier_semaphore()
    for peer in peers:
        pl.semaphore_signal(barrier, inc=1, device_id=place.dev(peer), device_id_type=MESH)
    pl.semaphore_wait(barrier, len(peers))


def ag_kernel(a_ref, o_ref, ss, rs, ls):
    p = Place()
    R = a_ref.shape[0]
    H = R // 2
    here, core = p.at(), p.at(dc=1)
    xp, xm, zz = p.at(dx=1), p.at(dx=-1), p.at(dz=1)
    greet(p, [core, xp, xm, zz])

    def rows(s, off=0, n=R):
        return o_ref.at[pl.ds(pl.multiple_of(s * R + off, 16), n)]

    def send(k, src, dst, to):
        cp = pltpu.make_async_remote_copy(src_ref=src, dst_ref=dst, send_sem=ss.at[k], recv_sem=rs.at[k], device_id=p.dev(to), device_id_type=MESH)
        cp.start()
        sent.append(cp)

    def landed(k, ref):
        pltpu.make_async_remote_copy(src_ref=ref, dst_ref=ref, send_sem=ss.at[k], recv_sem=rs.at[k], device_id=p.dev(here), device_id_type=MESH).wait_recv()

    sent = []
    own = pltpu.make_async_copy(a_ref, rows(here), ls.at[0])
    own.start()
    send(0, a_ref, rows(here), xp)
    send(1, a_ref, rows(here), xm)
    send(2, a_ref, rows(here), zz)
    send(3, a_ref, rows(here), core)
    b_xm, b_xp, b_z = p.at(dx=-1), p.at(dx=1), p.at(dz=1)
    b_d2 = p.at(dx=2)
    landed(0, rows(b_xm))
    send(4, rows(b_xm, 0, H), rows(b_xm, 0, H), xp)
    landed(1, rows(b_xp))
    send(5, rows(b_xp, H, H), rows(b_xp, H, H), xm)
    send(6, rows(b_xm), rows(b_xm), core)
    send(7, rows(b_xp), rows(b_xp), core)
    landed(2, rows(b_z))
    send(8, rows(b_z), rows(b_z), xp)
    send(9, rows(b_z), rows(b_z), xm)
    send(10, rows(b_z), rows(b_z), core)
    landed(4, rows(b_d2, 0, H))
    send(11, rows(b_d2, 0, H), rows(b_d2, 0, H), zz)
    landed(5, rows(b_d2, H, H))
    send(12, rows(b_d2, H, H), rows(b_d2, H, H), zz)
    send(13, rows(b_d2), rows(b_d2), core)
    b_zxm, b_zxp, b_zd2 = p.at(dx=-1, dz=1), p.at(dx=1, dz=1), p.at(dx=2, dz=1)
    landed(8, rows(b_zxm))
    send(14, rows(b_zxm), rows(b_zxm), core)
    landed(9, rows(b_zxp))
    send(15, rows(b_zxp), rows(b_zxp), core)
    landed(11, rows(b_zd2, 0, H))
    send(16, rows(b_zd2, 0, H), rows(b_zd2, 0, H), core)
    landed(12, rows(b_zd2, H, H))
    send(17, rows(b_zd2, H, H), rows(b_zd2, H, H), core)
    o = lambda **k: p.at(dc=1, **k)
    landed(3, rows(core))
    landed(6, rows(o(dx=-1)))
    landed(7, rows(o(dx=1)))
    landed(10, rows(o(dz=1)))
    landed(13, rows(o(dx=2)))
    landed(14, rows(o(dx=-1, dz=1)))
    landed(15, rows(o(dx=1, dz=1)))
    landed(16, rows(o(dx=2, dz=1), 0, H))
    landed(17, rows(o(dx=2, dz=1), H, H))
    own.wait()
    for cp in sent:
        cp.wait_send()


def all_gather(a, cid):
    R, C = a.shape
    return pl.pallas_call(
        ag_kernel,
        out_shape=jax.ShapeDtypeStruct((16 * R, C), a.dtype),
        in_specs=[pl.BlockSpec(memory_space=pl.ANY)],
        out_specs=pl.BlockSpec(memory_space=pl.ANY),
        scratch_shapes=[DMA((18,)), DMA((18,)), DMA((1,))],
        compiler_params=pltpu.CompilerParams(collective_id=cid, has_side_effects=True),
        name="gather_tokens",
    )(a)


def rs_kernel(a_hbm, o_ref, pa, cb, zt, xs, zf, hv, xf, ss, rs, ls):
    p = Place()
    R = o_ref.shape[0]
    H = R // 2
    here, core = p.at(), p.at(dc=1)
    xp, xm, zz = p.at(dx=1), p.at(dx=-1), p.at(dz=1)
    f32, bf = jnp.float32, jnp.bfloat16
    order = [(2, 1), (-1, 1), (1, 1), (2, 0), (0, 1), (1, 0), (-1, 0), (0, 0)]
    loads = []
    for i, (dx, dz) in enumerate(order):
        for j, dc in enumerate((1, 0)):
            b = p.at(dx, dz, dc)
            cp = pltpu.make_async_copy(a_hbm.at[pl.ds(pl.multiple_of(b * R, 16), R)], pa.at[i, j], ls.at[2 * i + j])
            cp.start()
            loads.append(cp)
    greet(p, [core, xp, xm, zz])
    sent = []

    def send(k, src, dst, to):
        cp = pltpu.make_async_remote_copy(src_ref=src, dst_ref=dst, send_sem=ss.at[k], recv_sem=rs.at[k], device_id=p.dev(to), device_id_type=MESH)
        cp.start()
        sent.append(cp)

    def landed(k, ref):
        pltpu.make_async_remote_copy(src_ref=ref, dst_ref=ref, send_sem=ss.at[k], recv_sem=rs.at[k], device_id=p.dev(here), device_id_type=MESH).wait_recv()

    for i in range(8):
        loads[2 * i].wait()
        send(i, pa.at[i, 0], cb.at[i], core)

    def pair(i):
        loads[2 * i + 1].wait()
        landed(i, cb.at[i])
        pa[i, 1] = (pa[i, 1].astype(f32) + cb[i].astype(f32)).astype(bf)

    upper, lower = pl.ds(0, H), pl.ds(H, H)
    pair(0)
    send(8, pa.at[0, 1], zt, zz)
    pair(1)
    send(9, pa.at[1, 1], xs.at[1], xm)
    pair(2)
    send(10, pa.at[2, 1], xs.at[0], xp)
    pair(3)
    pair(4)
    pair(5)
    send(11, pa.at[5, 1, lower], xf.at[0, lower], xp)
    pair(6)
    send(12, pa.at[6, 1, upper], xf.at[1, upper], xm)
    pair(7)
    landed(8, zt)
    pa[3, 1] = (pa[3, 1].astype(f32) + zt[...].astype(f32)).astype(bf)
    send(13, pa.at[3, 1, upper], hv.at[0], xp)
    send(14, pa.at[3, 1, lower], hv.at[1], xm)
    landed(9, xs.at[1])
    landed(10, xs.at[0])
    pa[4, 1] = (pa[4, 1].astype(f32) + xs[0].astype(f32) + xs[1].astype(f32)).astype(bf)
    send(15, pa.at[4, 1], zf, zz)
    landed(13, hv.at[0])
    pa[5, 1, upper] = (pa[5, 1, upper].astype(f32) + hv[0].astype(f32)).astype(bf)
    send(16, pa.at[5, 1, upper], xf.at[0, upper], xp)
    landed(14, hv.at[1])
    pa[6, 1, lower] = (pa[6, 1, lower].astype(f32) + hv[1].astype(f32)).astype(bf)
    send(17, pa.at[6, 1, lower], xf.at[1, lower], xm)
    landed(15, zf)
    landed(11, xf.at[0, lower])
    landed(12, xf.at[1, upper])
    landed(16, xf.at[0, upper])
    landed(17, xf.at[1, lower])
    o_ref[...] = pa[7, 1].astype(f32) + zf[...].astype(f32) + xf[0].astype(f32) + xf[1].astype(f32)
    for cp in sent:
        cp.wait_send()


def reduce_scatter(a, cid):
    R, C = a.shape[0] // 16, a.shape[1]
    bf = jnp.bfloat16
    return pl.pallas_call(
        rs_kernel,
        out_shape=jax.ShapeDtypeStruct((R, C), jnp.float32),
        in_specs=[pl.BlockSpec(memory_space=pl.ANY)],
        out_specs=pl.BlockSpec(memory_space=VMEM),
        scratch_shapes=[
            VMEM((8, 2, R, C), bf), VMEM((8, R, C), bf), VMEM((R, C), bf), VMEM((2, R, C), bf), VMEM((R, C), bf),
            VMEM((2, R // 2, C), bf), VMEM((2, R, C), bf), DMA((18,)), DMA((18,)), DMA((16,)),
        ],
        compiler_params=pltpu.CompilerParams(collective_id=cid, has_side_effects=True, vmem_limit_bytes=40 * 2**20),
        name="sum_tokens",
    )(a)


def swap_kernel(a_ref, o_ref, ss, rs, ls):
    p = Place()
    n = 16
    greet(p, [(p.s + k) % n for k in range(1, n)])
    cps = []
    for k in range(1, n):
        to = (p.s + k) % n
        cp = pltpu.make_async_remote_copy(src_ref=a_ref.at[to], dst_ref=o_ref.at[p.s], send_sem=ss.at[k], recv_sem=rs.at[k], device_id=p.dev(to), device_id_type=MESH)
        cp.start()
        cps.append(cp)
    own = pltpu.make_async_copy(a_ref.at[p.s], o_ref.at[p.s], ls.at[0])
    own.start()
    own.wait()
    for cp in cps:
        cp.wait()


def swap(a, cid, space=VMEM):
    n = a.shape[0]
    return pl.pallas_call(
        swap_kernel,
        out_shape=jax.ShapeDtypeStruct(a.shape, a.dtype),
        in_specs=[pl.BlockSpec(memory_space=space)],
        out_specs=pl.BlockSpec(memory_space=space),
        scratch_shapes=[DMA((n,)), DMA((n,)), DMA((1,))],
        compiler_params=pltpu.CompilerParams(collective_id=cid, has_side_effects=True),
        name="swap_blocks",
    )(a)


def vec_kernel(nd, a_ref, o_ref, b1, t1, b2, ss, rs, ss2, rs2):
    p = Place()
    n = 16
    d = p.dp
    barrier = pltpu.get_barrier_semaphore()
    for k in range(1, n):
        pl.semaphore_signal(barrier, inc=1, device_id=(d, (p.s + k) % n), device_id_type=MESH)
    for k in range(1, nd):
        pl.semaphore_signal(barrier, inc=1, device_id=((d + k) % nd, p.s), device_id_type=MESH)
    pl.semaphore_wait(barrier, n + nd - 2)
    cps = []
    for k in range(1, n):
        to = (p.s + k) % n
        cp = pltpu.make_async_remote_copy(src_ref=a_ref.at[to], dst_ref=b1.at[k - 1], send_sem=ss.at[k], recv_sem=rs.at[k], device_id=(d, to), device_id_type=MESH)
        cp.start()
        cps.append(cp)
    total = a_ref[p.s]
    for k in range(1, n):
        cps[k - 1].wait_recv()
        total = total + b1[k - 1]
    t1[...] = total
    cps2 = []
    for k in range(1, nd):
        to = (d + k) % nd
        cp = pltpu.make_async_remote_copy(src_ref=t1.at[to], dst_ref=b2.at[k - 1], send_sem=ss2.at[k], recv_sem=rs2.at[k], device_id=(to, p.s), device_id_type=MESH)
        cp.start()
        cps2.append(cp)
    acc = t1[d]
    for k in range(1, nd):
        cps2[k - 1].wait_recv()
        acc = acc + b2[k - 1]
    o_ref[...] = acc
    for cp in cps + cps2:
        cp.wait_send()


def vec_sum(a, cid):
    n, nd = a.shape[:2]
    piece = a.shape[2:]
    return pl.pallas_call(
        functools.partial(vec_kernel, nd),
        out_shape=jax.ShapeDtypeStruct(piece, a.dtype),
        in_specs=[pl.BlockSpec(memory_space=VMEM)],
        out_specs=pl.BlockSpec(memory_space=VMEM),
        scratch_shapes=[VMEM((n - 1, nd) + piece, a.dtype), VMEM((nd,) + piece, a.dtype), VMEM((max(nd - 1, 1),) + piece, a.dtype), DMA((n,)), DMA((n,)), DMA((nd,)), DMA((nd,))],
        compiler_params=pltpu.CompilerParams(collective_id=cid, has_side_effects=True),
        name="sum_vectors",
    )(a)


highest = lax.Precision.HIGHEST
BF = jnp.bfloat16
F32 = jnp.float32


def layer_norm(tensor, gain_row, bias_row):
    center = tensor - jnp.mean(tensor, axis=-1, keepdims=True)
    spread = jnp.mean(center * center, axis=-1, keepdims=True)
    return center * lax.rsqrt(spread + 1e-05) * gain_row + bias_row


def head_norm(tensor, gain_row, bias_row):
    tokens = tensor.shape[0]
    grouped = tensor.reshape(tokens, -1, ATTENTION_WIDTH)
    center = grouped - jnp.mean(grouped, axis=-1, keepdims=True)
    spread = jnp.mean(center * center, axis=-1, keepdims=True)
    return (center * lax.rsqrt(spread + 0.00064)).reshape(tokens, -1) * gain_row + bias_row


def gate_out(mixed_time, projected, gain_row, bias_row):
    return head_norm(mixed_time, gain_row, bias_row) * jax.nn.silu(projected)


def later(tensor):
    return jnp.concatenate([jnp.zeros_like(tensor[:1]), tensor[:-1]], axis=0)


def earlier(tensor):
    return jnp.concatenate([tensor[1:], jnp.zeros_like(tensor[:1])], axis=0)


def contract(left, right, left_dim, right_dim):
    return lax.dot_general(left, right, (((left_dim,), (right_dim,)), ((), ())), preferred_element_type=F32)


def scan_kernel(reverse, keep_ref, decay_ref, add_ref, out_ref):
    blocks = add_ref.shape[0]

    def step(i, state):
        at = blocks - 1 - i if reverse else i
        out_ref[at] = state
        return add_ref[at] + keep_ref[at] * decay_ref[...] * state

    lax.fori_loop(0, blocks, step, jnp.zeros(add_ref.shape[1:], F32))


def state_scan(keep, decay, add, reverse):
    return pl.pallas_call(
        functools.partial(scan_kernel, reverse),
        out_shape=jax.ShapeDtypeStruct(add.shape, F32),
        in_specs=[pl.BlockSpec(memory_space=pltpu.SMEM), pl.BlockSpec(memory_space=VMEM), pl.BlockSpec(memory_space=VMEM)],
        out_specs=pl.BlockSpec(memory_space=VMEM),
        name="scan_states",
    )(keep, decay, add)


def block_output(memory, prior, r, k, v, seq, lam, bonus):
    length = r.shape[0]
    position = jnp.arange(length)
    offsets = position.astype(F32)[:, None, None]
    r_scaled = r * jnp.exp(lam[None] * offsets)
    k_scaled = k * jnp.exp(-lam[None] * (offsets + 1.0))
    scores = jnp.einsum("ihc,jhc->hij", r_scaled, k_scaled, precision=highest)
    block_mask = ((position[None, :] < position[:, None]) & (seq[None, :] == seq[:, None])).astype(F32)
    scores = scores * block_mask[None]
    reward = jnp.sum(r * k * bonus[None], axis=-1)
    kept = (seq == prior).astype(F32)
    out = jnp.einsum("hij,jhe->ihe", scores, v, precision=highest)
    out = out + reward[:, :, None] * v
    return out + kept[:, None, None] * jnp.einsum("ihc,hce->ihe", r_scaled, memory, precision=highest)


def block_carry(prior, k, v, seq, lam):
    length = k.shape[0]
    offsets = jnp.arange(length).astype(F32)[:, None, None]
    last = seq[length - 1]
    tail = (seq == last).astype(F32)
    carried = (last == prior).astype(F32)
    k_end = k * jnp.exp(lam[None] * (length - 1.0 - offsets)) * tail[:, None, None]
    return (carried, jnp.einsum("jhc,jhe->hce", k_end, v, precision=highest))


def block_whole(memory, prior, r, k, v, seq, lam, bonus):
    out = block_output(memory, prior, r, k, v, seq, lam, bonus)
    carried, kv_end = block_carry(prior, k, v, seq, lam)
    decay = jnp.exp(lam * r.shape[0])
    return (carried * decay[:, :, None] * memory + kv_end, out)


def body(nd, inputs, cotangent, mix_weights, out_weight, key_weight, value_weight, recept_weight, vectors, segment_ids):
    tokens, width = inputs.shape
    group = segment_ids.shape[0]
    cols = mix_weights.shape[2]
    heads = cols // ATTENTION_WIDTH
    s = lax.axis_index("sp")
    ring = group // tokens
    own = lax.dynamic_slice_in_dim(vectors, s * cols, cols, 1)
    same = jnp.concatenate([jnp.zeros((1,), F32), (segment_ids[1:] == segment_ids[:-1]).astype(F32)])
    same_next = earlier(same)
    here = s * tokens
    same_here = lax.dynamic_slice_in_dim(same, here, tokens, 0)[:, None]
    mu = vectors[2:6]
    nu_k, nu_r = vectors[12], vectors[13]

    out_full = lax.all_gather(out_weight, "sp", axis=0, tiled=True)
    recept_full = lax.all_gather(recept_weight, "sp", axis=0)
    recept_full = recept_full.transpose(1, 0, 2).reshape(width, width)

    mix_f = mix_weights.astype(F32)
    folded = jnp.concatenate(
        [((1.0 - mu)[:, :, None] * mix_f).astype(BF), (mu[:, :, None] * mix_f).astype(BF)], axis=0
    )
    folded = folded.transpose(1, 0, 2).reshape(width, 8 * cols)
    x = inputs.astype(F32)
    n1 = layer_norm(x, vectors[0], vectors[1]).astype(BF)
    n1_all = all_gather(n1, 0)
    half = 4 * cols
    n1_f = n1_all.astype(F32)
    shift_one = later(n1_f) * same[:, None] - n1_f
    r, k, v, p = (
        jnp.dot((n1_f + shift_one * mu[q]).astype(BF), mix_weights[q], preferred_element_type=F32) for q in range(4)
    )

    blocks = group // SPAN
    shape_blk = (blocks, SPAN, heads, ATTENTION_WIDTH)
    lam = -jnp.exp(own[6]).reshape(heads, ATTENTION_WIDTH)
    bonus = own[7].reshape(heads, ATTENTION_WIDTH)
    seg_blk = segment_ids.reshape(blocks, SPAN)
    prior = jnp.concatenate([jnp.full((1,), -1, jnp.int32), seg_blk[:-1, SPAN - 1]])
    r_blk, k_blk, v_blk = r.reshape(shape_blk), k.reshape(shape_blk), v.reshape(shape_blk)
    decay = jnp.exp(lam * SPAN)[:, :, None] * jnp.ones((1, 1, ATTENTION_WIDTH), F32)
    carried, kv_end = jax.vmap(block_carry, in_axes=(0, 0, 0, 0, None))(prior, k_blk, v_blk, seg_blk, lam)
    states = state_scan(carried, decay, kv_end, False)
    out_blk = jax.vmap(block_output, in_axes=(0, 0, 0, 0, 0, 0, None, None))(
        states, prior, r_blk, k_blk, v_blk, seg_blk, lam, bonus
    )
    mixed_time = out_blk.reshape(group, cols)
    z = gate_out(mixed_time, p, own[8], own[9]).astype(BF)

    z_here = swap(z.reshape(ring, tokens, cols), 1).transpose(1, 0, 2).reshape(tokens, width)
    hidden = x + jnp.dot(z_here, out_full, preferred_element_type=F32)
    n2 = layer_norm(hidden, vectors[10], vectors[11]).astype(BF)

    n2_all = all_gather(n2, 2)
    shift_all = later(n2_all).astype(F32) * same[:, None] - n2_all.astype(F32)
    key_in = (n2_all.astype(F32) + shift_all * nu_k).astype(BF)
    before = lax.dynamic_slice_in_dim(n2_all, jnp.maximum(here - 1, 0), 1, 0)
    n2_f = n2.astype(F32)
    shift_here = jnp.concatenate([before, n2[:-1]], axis=0).astype(F32) * same_here - n2_f
    recept_in = (n2_f + shift_here * nu_r).astype(BF)
    key_pre = jnp.dot(key_in, key_weight, preferred_element_type=F32)
    lifted = jax.nn.relu(key_pre)
    squared = jnp.square(lifted).astype(BF)
    value_part = jnp.dot(squared, value_weight, preferred_element_type=F32).astype(BF)
    value_here = reduce_scatter(value_part, 3)
    gate = jax.nn.sigmoid(jnp.dot(recept_in, recept_full, preferred_element_type=F32))
    channel = (gate * value_here).astype(BF)
    result = (hidden + channel.astype(F32)).astype(BF)

    g = cotangent.astype(F32)
    grad_value = (g * gate).astype(BF)
    grad_recept = (g * value_here * (gate * (1.0 - gate))).astype(BF)
    grad_value_all = all_gather(grad_value, 4)
    grad_sq = contract(grad_value_all, value_weight, 1, 1)
    grad_key = (grad_sq * 2.0 * lifted).astype(BF)
    key_back = reduce_scatter(contract(grad_key, key_weight, 1, 1).astype(BF), 5)
    value_grad = contract(squared, grad_value_all, 0, 0)
    key_grad = contract(key_in, grad_key, 0, 0)
    recept_cols = swap(grad_recept.reshape(tokens, ring, cols).transpose(1, 0, 2), 6).reshape(group, cols)
    recept_two = jnp.concatenate([recept_cols, earlier(recept_cols) * same_next[:, None].astype(BF)], axis=1)
    recept_np = contract(n2_all, recept_two, 0, 0)
    recept_grad = (1.0 - nu_r)[:, None] * recept_np[:, :cols] + nu_r[:, None] * recept_np[:, cols:]
    recept_back = contract(grad_recept, recept_full, 1, 1)
    nu_k_grad = jnp.sum(key_back * shift_here, axis=0)
    nu_r_grad = jnp.sum(recept_back * shift_here, axis=0)
    moved = (key_back * nu_k + recept_back * nu_r) * same_here
    after = lax.ppermute(moved[:1], "sp", [(i, i - 1) for i in range(1, ring)])
    grad_n2 = key_back * (1.0 - nu_k) + recept_back * (1.0 - nu_r) + jnp.concatenate([moved[1:], after], axis=0)
    unused, pull_two = jax.vjp(layer_norm, hidden, vectors[10], vectors[11])
    grad_hidden, gain_two, bias_two = pull_two(grad_n2)
    grad_hidden = g + grad_hidden

    grad_hidden_b = grad_hidden.astype(BF)
    gz_here = contract(grad_hidden_b, out_full, 1, 1).astype(BF)
    gz = swap(gz_here.reshape(tokens, ring, cols).transpose(1, 0, 2), 7).reshape(group, cols).astype(F32)
    grad_hidden_all = lax.all_gather(grad_hidden_b, "sp", axis=0, tiled=True)
    unused, gate_pull = jax.vjp(gate_out, mixed_time, p, own[8], own[9])
    grad_time, grad_gate, gain_head, bias_head = gate_pull(gz)
    go_blk = grad_time.reshape(shape_blk)
    offsets = jnp.arange(SPAN).astype(F32)[:, None, None]
    kept_all = (seg_blk == prior[:, None]).astype(F32)
    read = r_blk * jnp.exp(lam[None] * offsets)[None] * kept_all[:, :, None, None]
    local = jnp.einsum("bihc,bihe->bhce", read, go_blk, precision=highest)
    state_grads = state_scan(carried, decay, local, True)

    def every_block(memory, r_in, k_in, v_in, lam_in, bonus_in):
        return jax.vmap(block_whole, in_axes=(0, 0, 0, 0, 0, 0, None, None))(
            memory, prior, r_in, k_in, v_in, seg_blk, lam_in, bonus_in
        )

    unused, block_pull = jax.vjp(every_block, states, r_blk, k_blk, v_blk, lam, bonus)
    unused, gr, gk, gv, lam_grad, bonus_grad = block_pull((state_grads, go_blk))
    decay_grad = (lam_grad * lam).reshape(cols)
    grads = jnp.concatenate([t.reshape(group, cols).astype(BF) for t in (gr, gk, gv, grad_gate)], axis=1)
    grads_two = jnp.concatenate([grads, earlier(grads) * same_next[:, None].astype(BF)], axis=1)
    n1_part = contract(grads_two, folded, 1, 1).astype(BF)
    mix_np = contract(n1_all, grads_two, 0, 0)
    mix_n = mix_np[:, :half].reshape(width, 4, cols).transpose(1, 0, 2)
    mix_p = mix_np[:, half:].reshape(width, 4, cols).transpose(1, 0, 2)
    mix_d = mix_p - mix_n
    mix_grad = mix_n + mu[:, :, None] * mix_d
    mu_grads = jnp.sum(mix_f * mix_d, axis=2)
    n1_back = reduce_scatter(n1_part, 8)
    out_grad = contract(z, grad_hidden_all, 0, 0)
    unused, pull_one = jax.vjp(layer_norm, x, vectors[0], vectors[1])
    grad_x, gain_one, bias_one = pull_one(n1_back)
    input_grad = grad_hidden + grad_x

    def place(part):
        return lax.dynamic_update_slice_in_dim(jnp.zeros((width,), F32), part, s * cols, 0)

    terms = jnp.stack(
        [gain_one, bias_one, mu_grads[0], mu_grads[1], mu_grads[2], mu_grads[3]]
        + [place(t) for t in (decay_grad, bonus_grad.reshape(cols), gain_head, bias_head)]
        + [gain_two, bias_two, nu_k_grad, nu_r_grad]
    )
    rows, piece = terms.shape[0], width // (nd * ring)
    terms = terms.reshape(rows, nd, ring, piece).transpose(2, 1, 0, 3).reshape(ring, nd, rows * piece)
    packed = -(-rows * piece // 1024) * 1024
    terms = jnp.pad(terms, ((0, 0), (0, 0), (0, packed - rows * piece))).reshape(ring, nd, packed // 128, 128)
    vectors_grad = vec_sum(terms, 9).reshape(packed)[: rows * piece].reshape(rows, piece)

    def over_dp(grad, dim):
        return lax.psum_scatter(grad.astype(BF), "dp", scatter_dimension=dim, tiled=True).astype(F32)

    return (
        result,
        input_grad,
        over_dp(mix_grad, 1),
        over_dp(out_grad, 1),
        over_dp(key_grad, 0),
        over_dp(value_grad, 1),
        over_dp(recept_grad, 0),
        vectors_grad,
    )


def solution(mesh):
    placed = (
        P(("dp", "sp"), None),
        P(("dp", "sp"), None),
        P(None, None, "sp"),
        P("sp", None),
        P(None, "sp"),
        P("sp", None),
        P(None, "sp"),
        P(),
        P("dp"),
    )
    return jax.shard_map(
        functools.partial(body, mesh.shape["dp"]),
        mesh=mesh,
        in_specs=placed,
        out_specs=(
            P(("dp", "sp"), None),
            P(("dp", "sp"), None),
            P(None, "dp", "sp"),
            P("sp", "dp"),
            P("dp", "sp"),
            P("sp", "dp"),
            P("dp", "sp"),
            P(None, ("dp", "sp")),
        ),
        check_vma=False,
    )
```

```python
import functools

import jax
import jax.numpy as jnp
from jax import lax
from jax.experimental import pallas as pl
from jax.experimental.pallas import tpu as pltpu
from jax.sharding import PartitionSpec as P

MESH = pl.DeviceIdType.MESH
VMEM = pltpu.VMEM
DMA = pltpu.SemaphoreType.DMA
BF = jnp.bfloat16
F32 = jnp.float32

ATTENTION_WIDTH = 64


class Place:
    def __init__(self):
        self.dp = lax.axis_index("dp")
        s = lax.axis_index("sp")
        self.s = s
        self.x, self.z, self.c = s // 4, (s // 2) % 2, s % 2

    def at(self, dx=0, dz=0, dc=0):
        x = (self.x + dx) % 4
        z = (self.z + dz) % 2
        c = (self.c + dc) % 2
        return x * 4 + z * 2 + c

    def dev(self, s):
        return (self.dp, s)


def greet(place, peers):
    barrier = pltpu.get_barrier_semaphore()
    for peer in peers:
        pl.semaphore_signal(barrier, inc=1, device_id=place.dev(peer), device_id_type=MESH)
    pl.semaphore_wait(barrier, len(peers))


class Traffic:
    def __init__(self, place, ss, rs):
        self.place, self.ss, self.rs, self.sent = place, ss, rs, []

    def copy(self, k, src, dst, to):
        return pltpu.make_async_remote_copy(
            src_ref=src, dst_ref=dst, send_sem=self.ss.at[k], recv_sem=self.rs.at[k],
            device_id=self.place.dev(to), device_id_type=MESH,
        )

    def send(self, k, src, dst, to):
        cp = self.copy(k, src, dst, to)
        cp.start()
        self.sent.append(cp)

    def landed(self, k, ref):
        self.copy(k, ref, ref, self.place.s).wait_recv()

    def finish(self):
        for cp in self.sent:
            cp.wait_send()


def gather_steps(p, t, a_ref, land):
    H = a_ref.shape[0] // 2
    upper, lower = pl.ds(0, H), pl.ds(H, H)
    core, xp, xm, zz = p.at(dc=1), p.at(dx=1), p.at(dx=-1), p.at(dz=1)
    here = p.s
    t.send(0, a_ref, land.at[here], xp)
    t.send(1, a_ref, land.at[here], xm)
    t.send(2, a_ref, land.at[here], zz)
    t.send(3, a_ref, land.at[here], core)
    yield []
    t.landed(3, land.at[core])
    yield [core]
    d2, zxm, zxp, zd2 = p.at(dx=2), p.at(dx=-1, dz=1), p.at(dx=1, dz=1), p.at(dx=2, dz=1)

    def other(**k):
        return p.at(dc=1, **k)

    t.landed(0, land.at[xm])
    t.send(4, land.at[xm, upper], land.at[xm, upper], xp)
    t.landed(1, land.at[xp])
    t.send(5, land.at[xp, lower], land.at[xp, lower], xm)
    t.send(6, land.at[xm], land.at[xm], core)
    t.send(7, land.at[xp], land.at[xp], core)
    t.landed(2, land.at[zz])
    t.send(8, land.at[zz], land.at[zz], xp)
    t.send(9, land.at[zz], land.at[zz], xm)
    t.send(10, land.at[zz], land.at[zz], core)
    yield [xm, xp, zz]
    t.landed(6, land.at[other(dx=-1)])
    yield [other(dx=-1)]
    t.landed(4, land.at[d2, upper])
    t.send(11, land.at[d2, upper], land.at[d2, upper], zz)
    t.landed(5, land.at[d2, lower])
    t.send(12, land.at[d2, lower], land.at[d2, lower], zz)
    t.send(13, land.at[d2], land.at[d2], core)
    yield [d2]
    t.landed(7, land.at[other(dx=1)])
    t.landed(10, land.at[other(dz=1)])
    yield [other(dx=1), other(dz=1)]
    t.landed(13, land.at[other(dx=2)])
    yield [other(dx=2)]
    t.landed(8, land.at[zxm])
    t.send(14, land.at[zxm], land.at[zxm], core)
    t.landed(9, land.at[zxp])
    t.send(15, land.at[zxp], land.at[zxp], core)
    yield [zxm, zxp]
    t.landed(11, land.at[zd2, upper])
    t.send(16, land.at[zd2, upper], land.at[zd2, upper], core)
    t.landed(12, land.at[zd2, lower])
    t.send(17, land.at[zd2, lower], land.at[zd2, lower], core)
    t.landed(14, land.at[other(dx=-1, dz=1)])
    t.landed(15, land.at[other(dx=1, dz=1)])
    yield [other(dx=-1, dz=1), other(dx=1, dz=1), zd2]
    t.landed(16, land.at[other(dx=2, dz=1), upper])
    t.landed(17, land.at[other(dx=2, dz=1), lower])
    yield [other(dx=2, dz=1)]


def run_gather(a_ref, land, ss, rs, work):
    p = Place()
    t = Traffic(p, ss, rs)
    greet(p, [p.at(dc=1), p.at(dx=1), p.at(dx=-1), p.at(dz=1)])
    steps = gather_steps(p, t, a_ref, land)
    next(steps)
    land[p.s] = a_ref[...]
    ready = [p.s]
    for arrived in steps:
        ready += arrived
        for unused in range(min(2, len(ready))):
            work(ready.pop(0))
    for b in ready:
        work(b)
    return t


def save_blocks(land, all_ref, sem):
    R = land.shape[1]

    def start(b):
        pltpu.make_async_copy(land.at[b], all_ref.at[pl.ds(pl.multiple_of(b * R, 16), R)], sem.at[b]).start()

    def wait():
        for b in range(16):
            pltpu.make_async_copy(land.at[b], all_ref.at[pl.ds(b * R, R)], sem.at[b]).wait()

    return start, wait


def heads_of_blocks(land):
    R = land.shape[1]
    first = [land[b, 0:16, :].astype(F32)[0:1] for b in range(16)]
    before = [jnp.zeros_like(first[0])] + [land[b, R - 16 : R, :].astype(F32)[15:16] for b in range(15)]
    return jnp.concatenate(first, axis=0), jnp.concatenate(before, axis=0)


def shifted(n, same):
    rows = lax.broadcasted_iota(jnp.int32, n.shape, 0)
    before = jnp.where(rows == 0, 0.0, pltpu.roll(n, 1, 0))
    return before * same - n


def project_kernel(a_ref, w_ref, mu_ref, same_ref, all_ref, o_ref, land, ss, rs, ls):
    R = a_ref.shape[0]
    Q, cols = w_ref.shape[0], w_ref.shape[2]
    start, wait = save_blocks(land, all_ref, ls)

    def work(b):
        start(b)
        rows = pl.ds(pl.multiple_of(b * R, 16), R)
        n = land[b].astype(F32)
        shift = shifted(n, same_ref[rows, :])
        for q in range(Q):
            m = (n + shift * mu_ref[q : q + 1, :]).astype(BF)
            o_ref[rows, q * cols : (q + 1) * cols] = jnp.dot(m, w_ref[q], preferred_element_type=F32)

    t = run_gather(a_ref, land, ss, rs, work)
    first, before = heads_of_blocks(land)
    same = jnp.concatenate([same_ref[b * R : b * R + 1, :] for b in range(16)], axis=0)
    shift = before * same - first
    for q in range(Q):
        m = (first + shift * mu_ref[q : q + 1, :]).astype(BF)
        out = jnp.dot(m, w_ref[q], preferred_element_type=F32)
        for b in range(16):
            o_ref[b * R : b * R + 1, q * cols : (q + 1) * cols] = out[b : b + 1]
    wait()
    t.finish()


def project(a, w, mu, same, cid):
    R, C = a.shape
    Q, cols = w.shape[0], w.shape[2]
    return pl.pallas_call(
        project_kernel,
        out_shape=(jax.ShapeDtypeStruct((16 * R, C), BF), jax.ShapeDtypeStruct((16 * R, Q * cols), F32)),
        in_specs=[pl.BlockSpec(memory_space=VMEM)] * 4,
        out_specs=(pl.BlockSpec(memory_space=pl.ANY), pl.BlockSpec(memory_space=VMEM)),
        scratch_shapes=[VMEM((16, R, C), BF), DMA((18,)), DMA((18,)), DMA((16,))],
        compiler_params=pltpu.CompilerParams(collective_id=cid, has_side_effects=True, vmem_limit_bytes=48 * 2**20),
        name="gather_project",
    )(a, w, mu, same)


def key_kernel(a_ref, w_ref, nu_ref, same_ref, all_ref, in_ref, lift_ref, sq_ref, land, mixed, ss, rs, ls, ms):
    R = a_ref.shape[0]
    start, wait = save_blocks(land, all_ref, ls)

    def put(b, rows, m):
        e = jnp.maximum(jnp.dot(m, w_ref[...], preferred_element_type=F32), 0.0)
        lift_ref[rows, :] = e
        sq_ref[rows, :] = (e * e).astype(BF)

    def work(b):
        start(b)
        n = land[b].astype(F32)
        rows = pl.ds(pl.multiple_of(b * R, 16), R)
        m = (n + shifted(n, same_ref[rows, :]) * nu_ref[...]).astype(BF)
        mixed[b] = m
        put(b, rows, m)

    t = run_gather(a_ref, land, ss, rs, work)
    first, before = heads_of_blocks(land)
    same = jnp.concatenate([same_ref[b * R : b * R + 1, :] for b in range(16)], axis=0)
    head = first + (before * same - first) * nu_ref[...]
    e = jnp.maximum(jnp.dot(head.astype(BF), w_ref[...], preferred_element_type=F32), 0.0)
    sq = e * e
    copies = []
    for b in range(16):
        rows = slice(b * R, b * R + 16)
        top = lax.broadcasted_iota(jnp.int32, (16, 1), 0) == 0
        mixed[b, 0:16, :] = jnp.where(top, head[b : b + 1], mixed[b, 0:16, :].astype(F32)).astype(BF)
        lift_ref[b * R : b * R + 1, :] = e[b : b + 1]
        sq_ref[rows, :] = jnp.where(top, sq[b : b + 1], sq_ref[rows, :].astype(F32)).astype(BF)
        cp = pltpu.make_async_copy(mixed.at[b], in_ref.at[pl.ds(b * R, R)], ms.at[b])
        cp.start()
        copies.append(cp)
    for cp in copies:
        cp.wait()
    wait()
    t.finish()


def key_side(a, w, nu, same, cid):
    R, C = a.shape
    units = w.shape[1]
    return pl.pallas_call(
        key_kernel,
        out_shape=(
            jax.ShapeDtypeStruct((16 * R, C), BF),
            jax.ShapeDtypeStruct((16 * R, C), BF),
            jax.ShapeDtypeStruct((16 * R, units), F32),
            jax.ShapeDtypeStruct((16 * R, units), BF),
        ),
        in_specs=[pl.BlockSpec(memory_space=VMEM)] * 4,
        out_specs=(pl.BlockSpec(memory_space=pl.ANY), pl.BlockSpec(memory_space=pl.ANY), pl.BlockSpec(memory_space=VMEM), pl.BlockSpec(memory_space=VMEM)),
        scratch_shapes=[VMEM((16, R, C), BF), VMEM((16, R, C), BF), DMA((18,)), DMA((18,)), DMA((16,)), DMA((16,))],
        compiler_params=pltpu.CompilerParams(collective_id=cid, has_side_effects=True, vmem_limit_bytes=56 * 2**20),
        name="gather_key",
    )(a, w, nu, same)


def back_kernel(a_ref, w_ref, lift_ref, all_ref, o_ref, land, ss, rs, ls):
    R = a_ref.shape[0]
    start, wait = save_blocks(land, all_ref, ls)

    def work(b):
        start(b)
        rows = pl.ds(pl.multiple_of(b * R, 16), R)
        gs = jnp.dot(land[b], w_ref[...], preferred_element_type=F32)
        o_ref[rows, :] = (gs * 2.0 * lift_ref[rows, :]).astype(BF)

    t = run_gather(a_ref, land, ss, rs, work)
    wait()
    t.finish()


def value_back(a, w, lift, cid):
    R, C = a.shape
    units = w.shape[1]
    return pl.pallas_call(
        back_kernel,
        out_shape=(jax.ShapeDtypeStruct((16 * R, C), BF), jax.ShapeDtypeStruct((16 * R, units), BF)),
        in_specs=[pl.BlockSpec(memory_space=VMEM)] * 3,
        out_specs=(pl.BlockSpec(memory_space=pl.ANY), pl.BlockSpec(memory_space=VMEM)),
        scratch_shapes=[VMEM((16, R, C), BF), DMA((18,)), DMA((18,)), DMA((16,))],
        compiler_params=pltpu.CompilerParams(collective_id=cid, has_side_effects=True, vmem_limit_bytes=48 * 2**20),
        name="gather_value_back",
    )(a, w, lift)


def sum_kernel(l_ref, w_ref, o_ref, pa, cb, zt, xs, zf, hv, xf, ss, rs):
    p = Place()
    t = Traffic(p, ss, rs)
    R = o_ref.shape[0]
    H = R // 2
    core, xp, xm, zz = p.at(dc=1), p.at(dx=1), p.at(dx=-1), p.at(dz=1)
    order = [(2, 1), (-1, 1), (1, 1), (2, 0), (0, 1), (1, 0), (-1, 0), (0, 0)]
    greet(p, [core, xp, xm, zz])

    def term(i, dc):
        b = p.at(order[i][0], order[i][1], dc)
        rows = l_ref[pl.ds(pl.multiple_of(b * R, 16), R), :]
        return jnp.dot(rows, w_ref[...], preferred_element_type=F32)

    def give(i):
        pa[i, 0] = term(i, 1).astype(BF)
        t.send(i, pa.at[i, 0], cb.at[i], core)

    def pair(i):
        pa[i, 1] = term(i, 0).astype(BF)
        t.landed(i, cb.at[i])
        pa[i, 1] = (pa[i, 1].astype(F32) + cb[i].astype(F32)).astype(BF)

    upper, lower = pl.ds(0, H), pl.ds(H, H)
    give(0)
    give(1)
    pair(0)
    t.send(8, pa.at[0, 1], zt, zz)
    give(2)
    pair(1)
    t.send(9, pa.at[1, 1], xs.at[1], xm)
    give(3)
    pair(2)
    t.send(10, pa.at[2, 1], xs.at[0], xp)
    give(4)
    give(5)
    pair(3)
    give(6)
    pair(4)
    pair(5)
    t.send(11, pa.at[5, 1, lower], xf.at[0, lower], xp)
    give(7)
    pair(6)
    t.send(12, pa.at[6, 1, upper], xf.at[1, upper], xm)
    pair(7)
    t.landed(8, zt)
    pa[3, 1] = (pa[3, 1].astype(F32) + zt[...].astype(F32)).astype(BF)
    t.send(13, pa.at[3, 1, upper], hv.at[0], xp)
    t.send(14, pa.at[3, 1, lower], hv.at[1], xm)
    t.landed(9, xs.at[1])
    t.landed(10, xs.at[0])
    pa[4, 1] = (pa[4, 1].astype(F32) + xs[0].astype(F32) + xs[1].astype(F32)).astype(BF)
    t.send(15, pa.at[4, 1], zf, zz)
    t.landed(13, hv.at[0])
    pa[5, 1, upper] = (pa[5, 1, upper].astype(F32) + hv[0].astype(F32)).astype(BF)
    t.send(16, pa.at[5, 1, upper], xf.at[0, upper], xp)
    t.landed(14, hv.at[1])
    pa[6, 1, lower] = (pa[6, 1, lower].astype(F32) + hv[1].astype(F32)).astype(BF)
    t.send(17, pa.at[6, 1, lower], xf.at[1, lower], xm)
    t.landed(11, xf.at[0, lower])
    t.landed(12, xf.at[1, upper])
    t.landed(15, zf)
    o_ref[...] = pa[7, 1].astype(F32) + zf[...].astype(F32)
    t.landed(16, xf.at[0, upper])
    t.landed(17, xf.at[1, lower])
    o_ref[...] = o_ref[...] + xf[0].astype(F32) + xf[1].astype(F32)
    t.finish()


def matmul_sum(l, w, cid):
    R, C = l.shape[0] // 16, w.shape[1]
    return pl.pallas_call(
        sum_kernel,
        out_shape=jax.ShapeDtypeStruct((R, C), F32),
        in_specs=[pl.BlockSpec(memory_space=VMEM)] * 2,
        out_specs=pl.BlockSpec(memory_space=VMEM),
        scratch_shapes=[
            VMEM((8, 2, R, C), BF), VMEM((8, R, C), BF), VMEM((R, C), BF), VMEM((2, R, C), BF), VMEM((R, C), BF),
            VMEM((2, R // 2, C), BF), VMEM((2, R, C), BF), DMA((18,)), DMA((18,)),
        ],
        compiler_params=pltpu.CompilerParams(collective_id=cid, has_side_effects=True, vmem_limit_bytes=48 * 2**20),
        name="matmul_sum",
    )(l, w)


def swap_kernel(a_ref, o_ref, ss, rs, ls):
    p = Place()
    n = 16
    greet(p, [(p.s + k) % n for k in range(1, n)])
    cps = []
    for k in range(1, n):
        to = (p.s + k) % n
        cp = pltpu.make_async_remote_copy(src_ref=a_ref.at[to], dst_ref=o_ref.at[p.s], send_sem=ss.at[k], recv_sem=rs.at[k], device_id=p.dev(to), device_id_type=MESH)
        cp.start()
        cps.append(cp)
    own = pltpu.make_async_copy(a_ref.at[p.s], o_ref.at[p.s], ls.at[0])
    own.start()
    own.wait()
    for cp in cps:
        cp.wait()


def swap(a, cid, space=VMEM):
    n = a.shape[0]
    return pl.pallas_call(
        swap_kernel,
        out_shape=jax.ShapeDtypeStruct(a.shape, a.dtype),
        in_specs=[pl.BlockSpec(memory_space=space)],
        out_specs=pl.BlockSpec(memory_space=space),
        scratch_shapes=[DMA((n,)), DMA((n,)), DMA((1,))],
        compiler_params=pltpu.CompilerParams(collective_id=cid, has_side_effects=True),
        name="swap_blocks",
    )(a)


def vec_kernel(nd, a_ref, o_ref, b1, t1, b2, ss, rs, ss2, rs2):
    p = Place()
    n = 16
    d = p.dp
    barrier = pltpu.get_barrier_semaphore()
    for k in range(1, n):
        pl.semaphore_signal(barrier, inc=1, device_id=(d, (p.s + k) % n), device_id_type=MESH)
    for k in range(1, nd):
        pl.semaphore_signal(barrier, inc=1, device_id=((d + k) % nd, p.s), device_id_type=MESH)
    pl.semaphore_wait(barrier, n + nd - 2)
    cps = []
    for k in range(1, n):
        to = (p.s + k) % n
        cp = pltpu.make_async_remote_copy(src_ref=a_ref.at[to], dst_ref=b1.at[k - 1], send_sem=ss.at[k], recv_sem=rs.at[k], device_id=(d, to), device_id_type=MESH)
        cp.start()
        cps.append(cp)
    total = a_ref[p.s]
    for k in range(1, n):
        cps[k - 1].wait_recv()
        total = total + b1[k - 1]
    t1[...] = total
    cps2 = []
    for k in range(1, nd):
        to = (d + k) % nd
        cp = pltpu.make_async_remote_copy(src_ref=t1.at[to], dst_ref=b2.at[k - 1], send_sem=ss2.at[k], recv_sem=rs2.at[k], device_id=(to, p.s), device_id_type=MESH)
        cp.start()
        cps2.append(cp)
    acc = t1[d]
    for k in range(1, nd):
        cps2[k - 1].wait_recv()
        acc = acc + b2[k - 1]
    o_ref[...] = acc
    for cp in cps + cps2:
        cp.wait_send()


def vec_sum(a, cid):
    n, nd = a.shape[:2]
    piece = a.shape[2:]
    return pl.pallas_call(
        functools.partial(vec_kernel, nd),
        out_shape=jax.ShapeDtypeStruct(piece, a.dtype),
        in_specs=[pl.BlockSpec(memory_space=VMEM)],
        out_specs=pl.BlockSpec(memory_space=VMEM),
        scratch_shapes=[VMEM((n - 1, nd) + piece, a.dtype), VMEM((nd,) + piece, a.dtype), VMEM((max(nd - 1, 1),) + piece, a.dtype), DMA((n,)), DMA((n,)), DMA((nd,)), DMA((nd,))],
        compiler_params=pltpu.CompilerParams(collective_id=cid, has_side_effects=True),
        name="sum_vectors",
    )(a)


CHUNK = 128


def halves(a):
    high = a.astype(BF)
    return high, (a - high.astype(F32)).astype(BF)


def dot3(a, b, dims):
    def one(x, y):
        return lax.dot_general(x, y, (dims, ((), ())), preferred_element_type=F32)

    return one(a[0], b[0]) + (one(a[0], b[1]) + one(a[1], b[0]))


NN, NT, TN = ((1,), (0,)), ((1,), (1,)), ((0,), (0,))


def head_sums(a, ones):
    high, rest = a.astype(BF), a - a.astype(BF).astype(F32)
    mid = rest.astype(BF)
    low = (rest - mid.astype(F32)).astype(BF)

    def one(x):
        return lax.dot_general(x, ones, (NN, ((), ())), preferred_element_type=F32)

    return one(high) + (one(mid) + one(low))


def iota(shape, dim):
    return lax.broadcasted_iota(jnp.int32, shape, dim)


def head_ones(width, dtype):
    return (iota((width, width), 0) // ATTENTION_WIDTH == iota((width, width), 1) // ATTENTION_WIDTH).astype(dtype)


def by_head(pair):
    lane = iota(pair[0].shape, 1) // ATTENTION_WIDTH
    heads = pair[0].shape[1] // ATTENTION_WIDTH
    zero = jnp.zeros_like(pair[0])
    return tuple(jnp.concatenate([jnp.where(lane == h, a, zero) for h in range(heads)], axis=0) for a in pair)


def pick_heads(a, rows):
    lane = iota((rows, a.shape[1]), 1) // ATTENTION_WIDTH
    out = a[:rows]
    for h in range(1, a.shape[1] // ATTENTION_WIDTH):
        out = jnp.where(lane == h, a[h * rows : (h + 1) * rows], out)
    return out


def powers(lam, tab):
    L = tab.shape[1]
    at = iota((L, 1), 0).astype(F32)
    mid = L // 2
    tab[0] = jnp.exp(lam * (at - mid))
    tab[1] = jnp.exp(-lam * (at + (1.0 - mid)))
    tab[2] = jnp.exp(lam * at)
    tab[3] = jnp.exp(lam * (L - 1.0 - at))


def chunk_mask(col, row):
    L = col.shape[0]
    return (iota((L, L), 1) < iota((L, L), 0)) & (col == row)


def forward_kernel(x_ref, col_ref, row_ref, keep_ref, vec_ref, z_ref, o_ref, s_ref, tab, state):
    chunks, L = row_ref.shape[0], row_ref.shape[2]
    W = vec_ref.shape[1]
    heads = W // ATTENTION_WIDTH
    lam, bonus, gain, bias = (vec_ref[q : q + 1, :] for q in range(4))
    powers(lam, tab)
    ones = head_ones(W, BF)
    diag = head_ones(W, F32)
    decay = vec_ref[8 : 8 + W, :]
    state[...] = jnp.zeros_like(state)

    def step(i, unused):
        rows = pl.ds(pl.multiple_of(i * L, L), L)
        r, k, v, p = (x_ref[rows, q * W : (q + 1) * W] for q in range(4))
        col = col_ref[rows, :]
        seg, kept, tail = col[:, 0:1], col[:, 1:2], col[:, 2:3]
        mask = chunk_mask(seg, row_ref[i])
        mask = jnp.concatenate([mask] * heads, axis=1)
        rs, ks = halves(r * tab[0]), halves(k * tab[1])
        scores = jnp.where(mask, dot3(rs, by_head(ks), NT), 0.0)
        vh = halves(v)
        out = dot3(halves(scores), by_head(vh), NN) + head_sums(r * k * bonus, ones) * v
        memory = state[...]
        s_ref[i] = memory
        out = out + kept * dot3(halves(r * tab[2]), halves(memory), NN)
        state[...] = keep_ref[i] * decay * memory + diag * dot3(halves(k * tab[3] * tail), vh, TN)
        o_ref[rows, :] = out
        center = out - head_sums(out, ones) * (1.0 / ATTENTION_WIDTH)
        spread = head_sums(center * center, ones) * (1.0 / ATTENTION_WIDTH)
        normed = center * lax.rsqrt(spread + 0.00064) * gain + bias
        z_ref[rows, :] = (normed * (p * (1.0 / (1.0 + jnp.exp(-p))))).astype(BF)
        return 0

    lax.fori_loop(0, chunks, step, 0, unroll=2)


def recurrence(x, cols, rows, keep, vec):
    T, W = x.shape[0], vec.shape[1]
    chunks, L = rows.shape[0], rows.shape[2]
    return pl.pallas_call(
        forward_kernel,
        out_shape=(jax.ShapeDtypeStruct((T, W), BF), jax.ShapeDtypeStruct((T, W), F32), jax.ShapeDtypeStruct((chunks, W, W), F32)),
        in_specs=[pl.BlockSpec(memory_space=VMEM)] * 3 + [pl.BlockSpec(memory_space=pltpu.SMEM), pl.BlockSpec(memory_space=VMEM)],
        out_specs=(pl.BlockSpec(memory_space=VMEM),) * 3,
        scratch_shapes=[VMEM((4, L, W), F32), VMEM((W, W), F32)],
        compiler_params=pltpu.CompilerParams(vmem_limit_bytes=40 * 2**20),
        name="recurrence",
    )(x, cols, rows, keep, vec)


def backward_kernel(x_ref, o_ref, s_ref, gz_ref, col_ref, row_ref, keep_ref, vec_ref, g_ref, sums_ref, tab, grad_state, acc, carry):
    chunks, L = row_ref.shape[0], row_ref.shape[2]
    W = vec_ref.shape[1]
    heads = W // ATTENTION_WIDTH
    lam, bonus, gain, bias = (vec_ref[q : q + 1, :] for q in range(4))
    powers(lam, tab)
    ones = head_ones(W, BF)
    diag = head_ones(W, F32)
    decay = vec_ref[8 : 8 + W, :]
    at = iota((L, 1), 0).astype(F32)
    mid = float(L // 2)
    grad_state[...] = jnp.zeros_like(grad_state)
    acc[...] = jnp.zeros_like(acc)
    carry[...] = jnp.zeros_like(carry)
    sums_ref[...] = jnp.zeros_like(sums_ref)

    def add(q, term):
        sums_ref[q : q + 1, :] += jnp.sum(term, axis=0, keepdims=True)

    def step(n, unused):
        i = chunks - 1 - n
        rows = pl.ds(pl.multiple_of(i * L, L), L)
        r, k, v, p = (x_ref[rows, q * W : (q + 1) * W] for q in range(4))
        col = col_ref[rows, :]
        seg, kept, tail, same_next = col[:, 0:1], col[:, 1:2], col[:, 2:3], col[:, 3:4]
        o = o_ref[rows, :]
        gz = gz_ref[rows, :].astype(F32)
        center = o - head_sums(o, ones) * (1.0 / ATTENTION_WIDTH)
        spread = head_sums(center * center, ones) * (1.0 / ATTENTION_WIDTH)
        scale = lax.rsqrt(spread + 0.00064)
        normed = center * scale
        gate = 1.0 / (1.0 + jnp.exp(-p))
        silu = p * gate
        gy = gz * silu
        gp = gz * (normed * gain + bias) * (gate * (1.0 + p * (1.0 - gate)))
        add(2, gy * normed)
        add(3, gy)
        gn = gy * gain
        go = scale * (
            gn
            - head_sums(gn, ones) * (1.0 / ATTENTION_WIDTH)
            - normed * (head_sums(gn * normed, ones) * (1.0 / ATTENTION_WIDTH))
        )
        mask = chunk_mask(seg, row_ref[i])
        mask = jnp.concatenate([mask] * heads, axis=1)
        rs_f, ks_f = r * tab[0], k * tab[1]
        r0_f, ke_f = r * tab[2] * kept, k * tab[3] * tail
        rs, ks, vh, goh = halves(rs_f), halves(ks_f), halves(v), halves(go)
        ks_by, v_by = by_head(ks), by_head(vh)
        scores = halves(jnp.where(mask, dot3(rs, ks_by, NT), 0.0))
        grad_scores = halves(jnp.where(mask, dot3(goh, v_by, NT), 0.0))
        memory = s_ref[i]
        gs = grad_state[...]
        mh, gsh = halves(memory), halves(gs)
        reward = head_sums(r * k * bonus, ones)
        grad_reward = head_sums(go * v, ones)
        g_rs = dot3(grad_scores, ks_by, NN)
        g_r0 = dot3(goh, mh, NT)
        g_ks = pick_heads(dot3(grad_scores, rs, TN), L)
        g_ke = dot3(vh, gsh, NT)
        gv = pick_heads(dot3(scores, goh, TN), L) + reward * go + dot3(halves(ke_f), gsh, NN)
        keep = keep_ref[i]
        acc[...] += keep * memory * gs
        grad_state[...] = keep * decay * gs + diag * dot3(halves(r0_f), goh, TN)
        gr = g_rs * tab[0] + g_r0 * (tab[2] * kept) + grad_reward * bonus * k
        gk = g_ks * tab[1] + g_ke * (tab[3] * tail) + grad_reward * bonus * r
        add(1, grad_reward * r * k)
        add(0, (at - mid) * (g_rs * rs_f) - (at + (1.0 - mid)) * (g_ks * ks_f) + at * (g_r0 * r0_f) + (L - 1.0 - at) * (g_ke * ke_f))
        grads = jnp.concatenate([gr, gk, gv, gp], axis=1).astype(BF).astype(F32)
        last = iota((L, 1), 0) == L - 1
        after = jnp.where(last, carry[0:1, :], pltpu.roll(grads, L - 1, 0)) * same_next
        carry[0:1, :] = grads[0:1, :]
        g_ref[rows, : 4 * W] = grads.astype(BF)
        g_ref[rows, 4 * W :] = after.astype(BF)
        return 0

    lax.fori_loop(0, chunks, step, 0)
    whole = dot3(halves(jnp.ones((8, W), F32)), halves(acc[...] * decay), NT)
    sums_ref[0:1, :] = (sums_ref[0:1, :] + L * whole[0:1, :]) * lam


def recurrence_back(x, o, states, gz, cols, rows, keep, vec):
    T, W = x.shape[0], vec.shape[1]
    chunks, L = rows.shape[0], rows.shape[2]
    return pl.pallas_call(
        backward_kernel,
        out_shape=(jax.ShapeDtypeStruct((T, 8 * W), BF), jax.ShapeDtypeStruct((8, W), F32)),
        in_specs=[pl.BlockSpec(memory_space=VMEM)] * 6 + [pl.BlockSpec(memory_space=pltpu.SMEM), pl.BlockSpec(memory_space=VMEM)],
        out_specs=(pl.BlockSpec(memory_space=VMEM),) * 2,
        scratch_shapes=[VMEM((4, L, W), F32), VMEM((W, W), F32), VMEM((W, W), F32), VMEM((8, 4 * W), F32)],
        compiler_params=pltpu.CompilerParams(vmem_limit_bytes=48 * 2**20),
        name="recurrence_back",
    )(x, o, states, gz, cols, rows, keep, vec)


def layer_norm(tensor, gain_row, bias_row):
    center = tensor - jnp.mean(tensor, axis=-1, keepdims=True)
    spread = jnp.mean(center * center, axis=-1, keepdims=True)
    return center * lax.rsqrt(spread + 1e-05) * gain_row + bias_row


def earlier(tensor):
    return jnp.concatenate([tensor[1:], jnp.zeros_like(tensor[:1])], axis=0)


def contract(left, right, left_dim, right_dim):
    return lax.dot_general(left, right, (((left_dim,), (right_dim,)), ((), ())), preferred_element_type=F32)


def body(nd, inputs, cotangent, mix_weights, out_weight, key_weight, value_weight, recept_weight, vectors, segment_ids):
    tokens, width = inputs.shape
    group = segment_ids.shape[0]
    cols = mix_weights.shape[2]
    s = lax.axis_index("sp")
    ring = group // tokens
    own = lax.dynamic_slice_in_dim(vectors, s * cols, cols, 1)
    same = jnp.concatenate([jnp.zeros((1,), F32), (segment_ids[1:] == segment_ids[:-1]).astype(F32)])
    same_next = earlier(same)
    here = s * tokens
    same_here = lax.dynamic_slice_in_dim(same, here, tokens, 0)[:, None]
    mu = vectors[2:6]
    nu_k, nu_r = vectors[12], vectors[13]

    out_full = lax.all_gather(out_weight, "sp", axis=0, tiled=True)
    recept_full = lax.all_gather(recept_weight.T, "sp", axis=0, tiled=True)

    mix_f = mix_weights.astype(F32)
    folded = jnp.concatenate(
        [((1.0 - mu)[:, :, None] * mix_f).astype(BF), (mu[:, :, None] * mix_f).astype(BF)], axis=0
    )
    folded = folded.transpose(0, 2, 1).reshape(8 * cols, width)
    x = inputs.astype(F32)
    n1 = layer_norm(x, vectors[0], vectors[1]).astype(BF)
    half = 4 * cols
    n1_all, projected = project(n1, mix_weights, mu, same[:, None], 0)

    chunks = group // CHUNK
    seg = segment_ids.reshape(chunks, CHUNK)
    last = seg[:, CHUNK - 1 :]
    prior = jnp.concatenate([jnp.full((1, 1), -1, jnp.int32), last[:-1]], axis=0)
    tok_cols = jnp.stack(
        [t.astype(F32).reshape(group) for t in (seg, seg == prior, seg == last, same_next.reshape(seg.shape))], axis=1
    )
    tok_rows = seg.astype(F32)[:, None, :]
    keep = (last == prior).astype(F32).reshape(chunks)
    lam = -jnp.exp(own[6])
    decay = jnp.broadcast_to(jnp.exp(lam * CHUNK)[:, None], (cols, cols))
    vec = jnp.concatenate([lam[None], own[7:10], jnp.zeros((4, cols), F32), decay], axis=0)
    z, mixed_time, states = recurrence(projected, tok_cols, tok_rows, keep, vec)

    z_here = swap(z.reshape(ring, tokens, cols), 1).transpose(1, 0, 2).reshape(tokens, width)
    hidden = x + jnp.dot(z_here, out_full, preferred_element_type=F32)
    n2 = layer_norm(hidden, vectors[10], vectors[11]).astype(BF)

    n2_all, key_in, lifted, squared = key_side(n2, key_weight, nu_k[None], same[:, None], 2)
    before = lax.dynamic_slice_in_dim(n2_all, jnp.maximum(here - 1, 0), 1, 0)
    n2_f = n2.astype(F32)
    shift_here = jnp.concatenate([before, n2[:-1]], axis=0).astype(F32) * same_here - n2_f
    recept_in = (n2_f + shift_here * nu_r).astype(BF)
    value_here = matmul_sum(squared, value_weight, 3)
    gate = jax.nn.sigmoid(contract(recept_in, recept_full, 1, 1))
    channel = (gate * value_here).astype(BF)
    result = (hidden + channel.astype(F32)).astype(BF)

    g = cotangent.astype(F32)
    grad_value = (g * gate).astype(BF)
    grad_recept = (g * value_here * (gate * (1.0 - gate))).astype(BF)
    grad_value_all, grad_key = value_back(grad_value, value_weight.T, lifted, 4)
    key_back = matmul_sum(grad_key, key_weight.T, 5)
    value_grad = contract(squared, grad_value_all, 0, 0)
    key_grad = contract(key_in, grad_key, 0, 0)
    recept_cols = swap(grad_recept.reshape(tokens, ring, cols).transpose(1, 0, 2), 6).reshape(group, cols)
    recept_two = jnp.concatenate([recept_cols, earlier(recept_cols) * same_next[:, None].astype(BF)], axis=1)
    recept_np = contract(n2_all, recept_two, 0, 0)
    recept_grad = (1.0 - nu_r)[:, None] * recept_np[:, :cols] + nu_r[:, None] * recept_np[:, cols:]
    recept_back = contract(grad_recept, recept_full, 1, 0)
    nu_k_grad = jnp.sum(key_back * shift_here, axis=0)
    nu_r_grad = jnp.sum(recept_back * shift_here, axis=0)
    moved = (key_back * nu_k + recept_back * nu_r) * same_here
    after = lax.ppermute(moved[:1], "sp", [(i, i - 1) for i in range(1, ring)])
    grad_n2 = key_back * (1.0 - nu_k) + recept_back * (1.0 - nu_r) + jnp.concatenate([moved[1:], after], axis=0)
    unused, pull_two = jax.vjp(layer_norm, hidden, vectors[10], vectors[11])
    grad_hidden, gain_two, bias_two = pull_two(grad_n2)
    grad_hidden = g + grad_hidden

    grad_hidden_b = grad_hidden.astype(BF)
    gz_here = contract(grad_hidden_b, out_full, 1, 1).astype(BF)
    gz = swap(gz_here.reshape(tokens, ring, cols).transpose(1, 0, 2), 7).reshape(group, cols)
    grad_hidden_all = lax.all_gather(grad_hidden_b, "sp", axis=0, tiled=True)
    grads_two, head_sums_grad = recurrence_back(projected, mixed_time, states, gz, tok_cols, tok_rows, keep, vec)
    mix_np = contract(n1_all, grads_two, 0, 0)
    mix_n = mix_np[:, :half].reshape(width, 4, cols).transpose(1, 0, 2)
    mix_p = mix_np[:, half:].reshape(width, 4, cols).transpose(1, 0, 2)
    mix_d = mix_p - mix_n
    mix_grad = mix_n + mu[:, :, None] * mix_d
    mu_grads = jnp.sum(mix_f * mix_d, axis=2)
    n1_back = matmul_sum(grads_two, folded, 8)
    out_grad = contract(z, grad_hidden_all, 0, 0)
    unused, pull_one = jax.vjp(layer_norm, x, vectors[0], vectors[1])
    grad_x, gain_one, bias_one = pull_one(n1_back)
    input_grad = grad_hidden + grad_x

    def place(part):
        return lax.dynamic_update_slice_in_dim(jnp.zeros((width,), F32), part, s * cols, 0)

    terms = jnp.stack(
        [gain_one, bias_one, mu_grads[0], mu_grads[1], mu_grads[2], mu_grads[3]]
        + [place(head_sums_grad[q]) for q in range(4)]
        + [gain_two, bias_two, nu_k_grad, nu_r_grad]
    )
    rows, piece = terms.shape[0], width // (nd * ring)
    terms = terms.reshape(rows, nd, ring, piece).transpose(2, 1, 0, 3).reshape(ring, nd, rows * piece)
    packed = -(-rows * piece // 1024) * 1024
    terms = jnp.pad(terms, ((0, 0), (0, 0), (0, packed - rows * piece))).reshape(ring, nd, packed // 128, 128)
    vectors_grad = vec_sum(terms, 9).reshape(packed)[: rows * piece].reshape(rows, piece)

    def over_dp(grad, dim):
        return lax.psum_scatter(grad.astype(BF), "dp", scatter_dimension=dim, tiled=True).astype(F32)

    return (
        result,
        input_grad,
        over_dp(mix_grad, 1),
        over_dp(out_grad, 1),
        over_dp(key_grad, 0),
        over_dp(value_grad, 1),
        over_dp(recept_grad, 0),
        vectors_grad,
    )


def solution(mesh):
    placed = (
        P(("dp", "sp"), None),
        P(("dp", "sp"), None),
        P(None, None, "sp"),
        P("sp", None),
        P(None, "sp"),
        P("sp", None),
        P(None, "sp"),
        P(),
        P("dp"),
    )
    return jax.shard_map(
        functools.partial(body, mesh.shape["dp"]),
        mesh=mesh,
        in_specs=placed,
        out_specs=(
            P(("dp", "sp"), None),
            P(("dp", "sp"), None),
            P(None, "dp", "sp"),
            P("sp", "dp"),
            P("dp", "sp"),
            P("sp", "dp"),
            P("dp", "sp"),
            P(None, ("dp", "sp")),
        ),
        check_vma=False,
    )
```

```python
import functools

import jax
import jax.numpy as jnp
from jax import lax
from jax.experimental import pallas as pl
from jax.experimental.pallas import tpu as pltpu
from jax.sharding import PartitionSpec as P

MESH = pl.DeviceIdType.MESH
VMEM = pltpu.VMEM
DMA = pltpu.SemaphoreType.DMA
BF = jnp.bfloat16
F32 = jnp.float32

ATTENTION_WIDTH = 64


class Place:
    def __init__(self):
        self.dp = lax.axis_index("dp")
        s = lax.axis_index("sp")
        self.s = s
        self.x, self.z, self.c = s // 4, (s // 2) % 2, s % 2

    def at(self, dx=0, dz=0, dc=0):
        x = (self.x + dx) % 4
        z = (self.z + dz) % 2
        c = (self.c + dc) % 2
        return x * 4 + z * 2 + c

    def dev(self, s):
        return (self.dp, s)


def greet(place, peers):
    barrier = pltpu.get_barrier_semaphore()
    for peer in peers:
        pl.semaphore_signal(barrier, inc=1, device_id=place.dev(peer), device_id_type=MESH)
    pl.semaphore_wait(barrier, len(peers))


class Traffic:
    def __init__(self, place, ss, rs):
        self.place, self.ss, self.rs, self.sent = place, ss, rs, []

    def copy(self, k, src, dst, to):
        return pltpu.make_async_remote_copy(
            src_ref=src, dst_ref=dst, send_sem=self.ss.at[k], recv_sem=self.rs.at[k],
            device_id=self.place.dev(to), device_id_type=MESH,
        )

    def send(self, k, src, dst, to):
        cp = self.copy(k, src, dst, to)
        cp.start()
        self.sent.append(cp)

    def landed(self, k, ref):
        self.copy(k, ref, ref, self.place.s).wait_recv()

    def finish(self):
        for cp in self.sent:
            cp.wait_send()


def gather_steps(p, t, a_ref, land):
    H = a_ref.shape[0] // 2
    upper, lower = pl.ds(0, H), pl.ds(H, H)
    core, xp, xm, zz = p.at(dc=1), p.at(dx=1), p.at(dx=-1), p.at(dz=1)
    here = p.s
    t.send(0, a_ref, land.at[here], xp)
    t.send(1, a_ref, land.at[here], xm)
    t.send(2, a_ref, land.at[here], zz)
    t.send(3, a_ref, land.at[here], core)
    yield []
    t.landed(3, land.at[core])
    yield [core]
    d2, zxm, zxp, zd2 = p.at(dx=2), p.at(dx=-1, dz=1), p.at(dx=1, dz=1), p.at(dx=2, dz=1)

    def other(**k):
        return p.at(dc=1, **k)

    t.landed(0, land.at[xm])
    t.send(4, land.at[xm, upper], land.at[xm, upper], xp)
    t.landed(1, land.at[xp])
    t.send(5, land.at[xp, lower], land.at[xp, lower], xm)
    t.send(6, land.at[xm], land.at[xm], core)
    t.send(7, land.at[xp], land.at[xp], core)
    t.landed(2, land.at[zz])
    t.send(8, land.at[zz], land.at[zz], xp)
    t.send(9, land.at[zz], land.at[zz], xm)
    t.send(10, land.at[zz], land.at[zz], core)
    yield [xm, xp, zz]
    t.landed(6, land.at[other(dx=-1)])
    yield [other(dx=-1)]
    t.landed(4, land.at[d2, upper])
    t.send(11, land.at[d2, upper], land.at[d2, upper], zz)
    t.landed(5, land.at[d2, lower])
    t.send(12, land.at[d2, lower], land.at[d2, lower], zz)
    t.send(13, land.at[d2], land.at[d2], core)
    yield [d2]
    t.landed(7, land.at[other(dx=1)])
    t.landed(10, land.at[other(dz=1)])
    yield [other(dx=1), other(dz=1)]
    t.landed(13, land.at[other(dx=2)])
    yield [other(dx=2)]
    t.landed(8, land.at[zxm])
    t.send(14, land.at[zxm], land.at[zxm], core)
    t.landed(9, land.at[zxp])
    t.send(15, land.at[zxp], land.at[zxp], core)
    yield [zxm, zxp]
    t.landed(11, land.at[zd2, upper])
    t.send(16, land.at[zd2, upper], land.at[zd2, upper], core)
    t.landed(12, land.at[zd2, lower])
    t.send(17, land.at[zd2, lower], land.at[zd2, lower], core)
    t.landed(14, land.at[other(dx=-1, dz=1)])
    t.landed(15, land.at[other(dx=1, dz=1)])
    yield [other(dx=-1, dz=1), other(dx=1, dz=1), zd2]
    t.landed(16, land.at[other(dx=2, dz=1), upper])
    t.landed(17, land.at[other(dx=2, dz=1), lower])
    yield [other(dx=2, dz=1)]


def run_gather(a_ref, land, ss, rs, work, met=False, between=None):
    p = Place()
    t = Traffic(p, ss, rs)
    if not met:
        greet(p, [p.at(dc=1), p.at(dx=1), p.at(dx=-1), p.at(dz=1)])
    steps = gather_steps(p, t, a_ref, land)
    next(steps)
    if between is not None:
        between()
    land[p.s] = a_ref[...]
    ready = [p.s]
    for arrived in steps:
        ready += arrived
        for unused in range(min(2, len(ready))):
            work(ready.pop(0))
    for b in ready:
        work(b)
    return t


def save_blocks(land, all_ref, sem):
    R = land.shape[1]

    def start(b):
        pltpu.make_async_copy(land.at[b], all_ref.at[pl.ds(pl.multiple_of(b * R, 16), R)], sem.at[b]).start()

    def wait():
        for b in range(16):
            pltpu.make_async_copy(land.at[b], all_ref.at[pl.ds(b * R, R)], sem.at[b]).wait()

    return start, wait


def heads_of_blocks(land):
    R = land.shape[1]
    first = [land[b, 0:16, :].astype(F32)[0:1] for b in range(16)]
    before = [jnp.zeros_like(first[0])] + [land[b, R - 16 : R, :].astype(F32)[15:16] for b in range(15)]
    return jnp.concatenate(first, axis=0), jnp.concatenate(before, axis=0)


def shifted(n, same):
    rows = lax.broadcasted_iota(jnp.int32, n.shape, 0)
    before = jnp.where(rows == 0, 0.0, pltpu.roll(n, 1, 0))
    return before * same - n


def project_kernel(a_ref, w_ref, mu_ref, same_ref, all_ref, o_ref, land, ss, rs, ls):
    R = a_ref.shape[0]
    Q, cols = w_ref.shape[0], w_ref.shape[2]
    start, wait = save_blocks(land, all_ref, ls)

    def work(b):
        start(b)
        rows = pl.ds(pl.multiple_of(b * R, 16), R)
        n = land[b].astype(F32)
        shift = shifted(n, same_ref[rows, :])
        for q in range(Q):
            m = (n + shift * mu_ref[q : q + 1, :]).astype(BF)
            o_ref[rows, q * cols : (q + 1) * cols] = jnp.dot(m, w_ref[q], preferred_element_type=F32)

    t = run_gather(a_ref, land, ss, rs, work)
    first, before = heads_of_blocks(land)
    same = jnp.concatenate([same_ref[b * R : b * R + 1, :] for b in range(16)], axis=0)
    shift = before * same - first
    for q in range(Q):
        m = (first + shift * mu_ref[q : q + 1, :]).astype(BF)
        out = jnp.dot(m, w_ref[q], preferred_element_type=F32)
        for b in range(16):
            o_ref[b * R : b * R + 1, q * cols : (q + 1) * cols] = out[b : b + 1]
    wait()
    t.finish()


def project(a, w, mu, same, cid):
    R, C = a.shape
    Q, cols = w.shape[0], w.shape[2]
    return pl.pallas_call(
        project_kernel,
        out_shape=(jax.ShapeDtypeStruct((16 * R, C), BF), jax.ShapeDtypeStruct((16 * R, Q * cols), F32)),
        in_specs=[pl.BlockSpec(memory_space=VMEM)] * 4,
        out_specs=(pl.BlockSpec(memory_space=pl.ANY), pl.BlockSpec(memory_space=VMEM)),
        scratch_shapes=[VMEM((16, R, C), BF), DMA((18,)), DMA((18,)), DMA((16,))],
        compiler_params=pltpu.CompilerParams(collective_id=cid, has_side_effects=True, vmem_limit_bytes=48 * 2**20),
        name="gather_project",
    )(a, w, mu, same)


def key_kernel(a_ref, w_ref, nu_ref, same_ref, all_ref, in_ref, lift_ref, sq_ref, land, mixed, ss, rs, ls, ms):
    R = a_ref.shape[0]
    start, wait = save_blocks(land, all_ref, ls)

    def put(b, rows, m):
        e = jnp.maximum(jnp.dot(m, w_ref[...], preferred_element_type=F32), 0.0)
        lift_ref[rows, :] = e
        sq_ref[rows, :] = (e * e).astype(BF)

    def work(b):
        start(b)
        n = land[b].astype(F32)
        rows = pl.ds(pl.multiple_of(b * R, 16), R)
        m = (n + shifted(n, same_ref[rows, :]) * nu_ref[...]).astype(BF)
        mixed[b] = m
        put(b, rows, m)

    t = run_gather(a_ref, land, ss, rs, work)
    first, before = heads_of_blocks(land)
    same = jnp.concatenate([same_ref[b * R : b * R + 1, :] for b in range(16)], axis=0)
    head = first + (before * same - first) * nu_ref[...]
    e = jnp.maximum(jnp.dot(head.astype(BF), w_ref[...], preferred_element_type=F32), 0.0)
    sq = e * e
    copies = []
    for b in range(16):
        rows = slice(b * R, b * R + 16)
        top = lax.broadcasted_iota(jnp.int32, (16, 1), 0) == 0
        mixed[b, 0:16, :] = jnp.where(top, head[b : b + 1], mixed[b, 0:16, :].astype(F32)).astype(BF)
        lift_ref[b * R : b * R + 1, :] = e[b : b + 1]
        sq_ref[rows, :] = jnp.where(top, sq[b : b + 1], sq_ref[rows, :].astype(F32)).astype(BF)
        cp = pltpu.make_async_copy(mixed.at[b], in_ref.at[pl.ds(b * R, R)], ms.at[b])
        cp.start()
        copies.append(cp)
    for cp in copies:
        cp.wait()
    wait()
    t.finish()


def key_side(a, w, nu, same, cid):
    R, C = a.shape
    units = w.shape[1]
    return pl.pallas_call(
        key_kernel,
        out_shape=(
            jax.ShapeDtypeStruct((16 * R, C), BF),
            jax.ShapeDtypeStruct((16 * R, C), BF),
            jax.ShapeDtypeStruct((16 * R, units), F32),
            jax.ShapeDtypeStruct((16 * R, units), BF),
        ),
        in_specs=[pl.BlockSpec(memory_space=VMEM)] * 4,
        out_specs=(pl.BlockSpec(memory_space=pl.ANY), pl.BlockSpec(memory_space=pl.ANY), pl.BlockSpec(memory_space=VMEM), pl.BlockSpec(memory_space=VMEM)),
        scratch_shapes=[VMEM((16, R, C), BF), VMEM((16, R, C), BF), DMA((18,)), DMA((18,)), DMA((16,)), DMA((16,))],
        compiler_params=pltpu.CompilerParams(collective_id=cid, has_side_effects=True, vmem_limit_bytes=56 * 2**20),
        name="gather_key",
    )(a, w, nu, same)


def sum_steps(l_ref, w_ref, o_ref, pa, cb, zt, xs, zf, hv, xf, ss, rs, jobs=(), met=False):
    jobs = list(jobs) + [lambda: None] * (7 - len(jobs))
    p = Place()
    t = Traffic(p, ss, rs)
    R = o_ref.shape[0]
    H = R // 2
    core, xp, xm, zz = p.at(dc=1), p.at(dx=1), p.at(dx=-1), p.at(dz=1)
    order = [(2, 1), (-1, 1), (1, 1), (2, 0), (0, 1), (1, 0), (-1, 0), (0, 0)]
    if not met:
        greet(p, [core, xp, xm, zz])

    def term(i, dc):
        b = p.at(order[i][0], order[i][1], dc)
        rows = l_ref[pl.ds(pl.multiple_of(b * R, 16), R), :]
        return jnp.dot(rows, w_ref[...], preferred_element_type=F32)

    def give(i):
        pa[i, 0] = term(i, 1).astype(BF)
        t.send(i, pa.at[i, 0], cb.at[i], core)

    def pair(i):
        pa[i, 1] = term(i, 0).astype(BF)
        t.landed(i, cb.at[i])
        pa[i, 1] = (pa[i, 1].astype(F32) + cb[i].astype(F32)).astype(BF)

    upper, lower = pl.ds(0, H), pl.ds(H, H)
    give(0)
    give(1)
    pair(0)
    t.send(8, pa.at[0, 1], zt, zz)
    give(2)
    pair(1)
    t.send(9, pa.at[1, 1], xs.at[1], xm)
    give(3)
    pair(2)
    t.send(10, pa.at[2, 1], xs.at[0], xp)
    give(4)
    give(5)
    pair(3)
    give(6)
    pair(4)
    pair(5)
    t.send(11, pa.at[5, 1, lower], xf.at[0, lower], xp)
    give(7)
    pair(6)
    t.send(12, pa.at[6, 1, upper], xf.at[1, upper], xm)
    pair(7)
    jobs[0]()
    jobs[1]()
    t.landed(8, zt)
    pa[3, 1] = (pa[3, 1].astype(F32) + zt[...].astype(F32)).astype(BF)
    t.send(13, pa.at[3, 1, upper], hv.at[0], xp)
    t.send(14, pa.at[3, 1, lower], hv.at[1], xm)
    jobs[2]()
    t.landed(9, xs.at[1])
    t.landed(10, xs.at[0])
    pa[4, 1] = (pa[4, 1].astype(F32) + xs[0].astype(F32) + xs[1].astype(F32)).astype(BF)
    t.send(15, pa.at[4, 1], zf, zz)
    jobs[3]()
    t.landed(13, hv.at[0])
    pa[5, 1, upper] = (pa[5, 1, upper].astype(F32) + hv[0].astype(F32)).astype(BF)
    t.send(16, pa.at[5, 1, upper], xf.at[0, upper], xp)
    t.landed(14, hv.at[1])
    pa[6, 1, lower] = (pa[6, 1, lower].astype(F32) + hv[1].astype(F32)).astype(BF)
    t.send(17, pa.at[6, 1, lower], xf.at[1, lower], xm)
    jobs[4]()
    jobs[5]()
    t.landed(11, xf.at[0, lower])
    t.landed(12, xf.at[1, upper])
    t.landed(15, zf)
    o_ref[...] = pa[7, 1].astype(F32) + zf[...].astype(F32)
    jobs[6]()
    t.landed(16, xf.at[0, upper])
    t.landed(17, xf.at[1, lower])
    o_ref[...] = o_ref[...] + xf[0].astype(F32) + xf[1].astype(F32)
    t.finish()


def sum_kernel(*refs):
    sum_steps(*refs)


def sum_scratch(R, C):
    return [
        VMEM((8, 2, R, C), BF), VMEM((8, R, C), BF), VMEM((R, C), BF), VMEM((2, R, C), BF), VMEM((R, C), BF),
        VMEM((2, R // 2, C), BF), VMEM((2, R, C), BF),
    ]


def matmul_sum(l, w, cid):
    R, C = l.shape[0] // 16, w.shape[1]
    return pl.pallas_call(
        sum_kernel,
        out_shape=jax.ShapeDtypeStruct((R, C), F32),
        in_specs=[pl.BlockSpec(memory_space=VMEM)] * 2,
        out_specs=pl.BlockSpec(memory_space=VMEM),
        scratch_shapes=sum_scratch(R, C) + [DMA((18,)), DMA((18,))],
        compiler_params=pltpu.CompilerParams(collective_id=cid, has_side_effects=True, vmem_limit_bytes=48 * 2**20),
        name="matmul_sum",
    )(l, w)


def swap_kernel(a_ref, o_ref, ss, rs, ls):
    p = Place()
    n = 16
    greet(p, [(p.s + k) % n for k in range(1, n)])
    cps = []
    for k in range(1, n):
        to = (p.s + k) % n
        cp = pltpu.make_async_remote_copy(src_ref=a_ref.at[to], dst_ref=o_ref.at[p.s], send_sem=ss.at[k], recv_sem=rs.at[k], device_id=p.dev(to), device_id_type=MESH)
        cp.start()
        cps.append(cp)
    own = pltpu.make_async_copy(a_ref.at[p.s], o_ref.at[p.s], ls.at[0])
    own.start()
    own.wait()
    for cp in cps:
        cp.wait()


def swap(a, cid, space=VMEM):
    n = a.shape[0]
    return pl.pallas_call(
        swap_kernel,
        out_shape=jax.ShapeDtypeStruct(a.shape, a.dtype),
        in_specs=[pl.BlockSpec(memory_space=space)],
        out_specs=pl.BlockSpec(memory_space=space),
        scratch_shapes=[DMA((n,)), DMA((n,)), DMA((1,))],
        compiler_params=pltpu.CompilerParams(collective_id=cid, has_side_effects=True),
        name="swap_blocks",
    )(a)


CHUNK = 128


def halves(a):
    high = a.astype(BF)
    return high, (a - high.astype(F32)).astype(BF)


def dot3(a, b, dims):
    def one(x, y):
        return lax.dot_general(x, y, (dims, ((), ())), preferred_element_type=F32)

    return one(a[0], b[0]) + (one(a[0], b[1]) + one(a[1], b[0]))


NN, NT, TN = ((1,), (0,)), ((1,), (1,)), ((0,), (0,))


def head_sums(a, ones):
    high, rest = a.astype(BF), a - a.astype(BF).astype(F32)
    mid = rest.astype(BF)
    low = (rest - mid.astype(F32)).astype(BF)

    def one(x):
        return lax.dot_general(x, ones, (NN, ((), ())), preferred_element_type=F32)

    return one(high) + (one(mid) + one(low))


def iota(shape, dim):
    return lax.broadcasted_iota(jnp.int32, shape, dim)


def head_ones(width, dtype):
    return (iota((width, width), 0) // ATTENTION_WIDTH == iota((width, width), 1) // ATTENTION_WIDTH).astype(dtype)


def by_head(pair):
    lane = iota(pair[0].shape, 1) // ATTENTION_WIDTH
    heads = pair[0].shape[1] // ATTENTION_WIDTH
    zero = jnp.zeros_like(pair[0])
    return tuple(jnp.concatenate([jnp.where(lane == h, a, zero) for h in range(heads)], axis=0) for a in pair)


def pick_heads(a, rows):
    lane = iota((rows, a.shape[1]), 1) // ATTENTION_WIDTH
    out = a[:rows]
    for h in range(1, a.shape[1] // ATTENTION_WIDTH):
        out = jnp.where(lane == h, a[h * rows : (h + 1) * rows], out)
    return out


def powers(lam, tab):
    L = tab.shape[1]
    at = iota((L, 1), 0).astype(F32)
    mid = L // 2
    tab[0] = jnp.exp(lam * (at - mid))
    tab[1] = jnp.exp(-lam * (at + (1.0 - mid)))
    tab[2] = jnp.exp(lam * at)
    tab[3] = jnp.exp(lam * (L - 1.0 - at))


def chunk_mask(col, row):
    L = col.shape[0]
    return (iota((L, L), 1) < iota((L, L), 0)) & (col == row)


def forward_kernel(x_ref, col_ref, row_ref, keep_ref, vec_ref, z_ref, o_ref, s_ref, tab, state):
    chunks, L = row_ref.shape[0], row_ref.shape[2]
    W = vec_ref.shape[1]
    heads = W // ATTENTION_WIDTH
    lam, bonus, gain, bias = (vec_ref[q : q + 1, :] for q in range(4))
    powers(lam, tab)
    ones = head_ones(W, BF)
    diag = head_ones(W, F32)
    decay = vec_ref[8 : 8 + W, :]
    state[...] = jnp.zeros_like(state)

    def step(i, unused):
        rows = pl.ds(pl.multiple_of(i * L, L), L)
        r, k, v, p = (x_ref[rows, q * W : (q + 1) * W] for q in range(4))
        col = col_ref[rows, :]
        seg, kept, tail = col[:, 0:1], col[:, 1:2], col[:, 2:3]
        mask = chunk_mask(seg, row_ref[i])
        mask = jnp.concatenate([mask] * heads, axis=1)
        rs, ks = halves(r * tab[0]), halves(k * tab[1])
        scores = jnp.where(mask, dot3(rs, by_head(ks), NT), 0.0)
        vh = halves(v)
        out = dot3(halves(scores), by_head(vh), NN) + head_sums(r * k * bonus, ones) * v
        memory = state[...]
        s_ref[i] = memory
        out = out + kept * dot3(halves(r * tab[2]), halves(memory), NN)
        state[...] = keep_ref[i] * decay * memory + diag * dot3(halves(k * tab[3] * tail), vh, TN)
        o_ref[rows, :] = out
        center = out - head_sums(out, ones) * (1.0 / ATTENTION_WIDTH)
        spread = head_sums(center * center, ones) * (1.0 / ATTENTION_WIDTH)
        normed = center * lax.rsqrt(spread + 0.00064) * gain + bias
        z_ref[rows, :] = (normed * (p * (1.0 / (1.0 + jnp.exp(-p))))).astype(BF)
        return 0

    lax.fori_loop(0, chunks, step, 0, unroll=2)


def recurrence(x, cols, rows, keep, vec):
    T, W = x.shape[0], vec.shape[1]
    chunks, L = rows.shape[0], rows.shape[2]
    return pl.pallas_call(
        forward_kernel,
        out_shape=(jax.ShapeDtypeStruct((T, W), BF), jax.ShapeDtypeStruct((T, W), F32), jax.ShapeDtypeStruct((chunks, W, W), F32)),
        in_specs=[pl.BlockSpec(memory_space=VMEM)] * 3 + [pl.BlockSpec(memory_space=pltpu.SMEM), pl.BlockSpec(memory_space=VMEM)],
        out_specs=(pl.BlockSpec(memory_space=VMEM),) * 3,
        scratch_shapes=[VMEM((4, L, W), F32), VMEM((W, W), F32)],
        compiler_params=pltpu.CompilerParams(vmem_limit_bytes=40 * 2**20),
        name="recurrence",
    )(x, cols, rows, keep, vec)


def back_chunk(x_ref, o_ref, s_ref, gz_ref, col_ref, row_ref, keep_ref, vec_ref, g_ref, sums_ref, tab, grad_state, acc, carry, turned):
    chunks, L = row_ref.shape[0], row_ref.shape[2]
    W = vec_ref.shape[1]
    heads = W // ATTENTION_WIDTH
    lam, bonus, gain, bias = (vec_ref[q : q + 1, :] for q in range(4))
    powers(lam, tab)
    ones = head_ones(W, BF)
    diag = head_ones(W, F32)
    decay = vec_ref[8 : 8 + W, :]
    at = iota((L, 1), 0).astype(F32)
    mid = float(L // 2)
    grad_state[...] = jnp.zeros_like(grad_state)
    acc[...] = jnp.zeros_like(acc)
    carry[...] = jnp.zeros_like(carry)
    sums_ref[...] = jnp.zeros_like(sums_ref)

    def add(q, term):
        sums_ref[q : q + 1, :] += jnp.sum(term, axis=0, keepdims=True)

    def step(n):
        i = chunks - 1 - n
        rows = pl.ds(pl.multiple_of(i * L, L), L)
        r, k, v, p = (x_ref[rows, q * W : (q + 1) * W] for q in range(4))
        col = col_ref[rows, :]
        seg, kept, tail, same_next = col[:, 0:1], col[:, 1:2], col[:, 2:3], col[:, 3:4]
        o = o_ref[rows, :]
        gz = gz_ref[i].astype(F32)
        center = o - head_sums(o, ones) * (1.0 / ATTENTION_WIDTH)
        spread = head_sums(center * center, ones) * (1.0 / ATTENTION_WIDTH)
        scale = lax.rsqrt(spread + 0.00064)
        normed = center * scale
        gate = 1.0 / (1.0 + jnp.exp(-p))
        silu = p * gate
        gy = gz * silu
        gp = gz * (normed * gain + bias) * (gate * (1.0 + p * (1.0 - gate)))
        add(2, gy * normed)
        add(3, gy)
        gn = gy * gain
        go = scale * (
            gn
            - head_sums(gn, ones) * (1.0 / ATTENTION_WIDTH)
            - normed * (head_sums(gn * normed, ones) * (1.0 / ATTENTION_WIDTH))
        )
        mask = chunk_mask(seg, row_ref[i])
        mask = jnp.concatenate([mask] * heads, axis=1)
        rs_f, ks_f = r * tab[0], k * tab[1]
        r0_f, ke_f = r * tab[2] * kept, k * tab[3] * tail
        rs, ks, vh, goh = halves(rs_f), halves(ks_f), halves(v), halves(go)
        ks_by, v_by = by_head(ks), by_head(vh)
        scores = halves(jnp.where(mask, dot3(rs, ks_by, NT), 0.0))
        grad_scores = halves(jnp.where(mask, dot3(goh, v_by, NT), 0.0))
        memory = s_ref[i]
        gs = grad_state[...]
        mh, gsh = halves(memory), halves(gs)
        reward = head_sums(r * k * bonus, ones)
        grad_reward = head_sums(go * v, ones)
        g_rs = dot3(grad_scores, ks_by, NN)
        g_r0 = dot3(goh, mh, NT)
        g_ks = pick_heads(dot3(grad_scores, rs, TN), L)
        g_ke = dot3(vh, gsh, NT)
        gv = pick_heads(dot3(scores, goh, TN), L) + reward * go + dot3(halves(ke_f), gsh, NN)
        keep = keep_ref[i]
        acc[...] += keep * memory * gs
        grad_state[...] = keep * decay * gs + diag * dot3(halves(r0_f), goh, TN)
        gr = g_rs * tab[0] + g_r0 * (tab[2] * kept) + grad_reward * bonus * k
        gk = g_ks * tab[1] + g_ke * (tab[3] * tail) + grad_reward * bonus * r
        add(1, grad_reward * r * k)
        add(0, (at - mid) * (g_rs * rs_f) - (at + (1.0 - mid)) * (g_ks * ks_f) + at * (g_r0 * r0_f) + (L - 1.0 - at) * (g_ke * ke_f))
        grads = jnp.concatenate([gr, gk, gv, gp], axis=1).astype(BF).astype(F32)
        last = iota((L, 1), 0) == L - 1
        after = jnp.where(last, carry[0:1, :], pltpu.roll(grads, L - 1, 0)) * same_next
        carry[0:1, :] = grads[0:1, :]
        g_ref[rows, : 4 * W] = grads.astype(BF)
        g_ref[rows, 4 * W :] = after.astype(BF)
        turned[0 : 4 * W, rows] = grads.T.astype(BF)
        turned[4 * W :, rows] = after.T.astype(BF)

    return step


def back_finish(vec_ref, sums_ref, acc, L):
    W = vec_ref.shape[1]
    whole = dot3(halves(jnp.ones((8, W), F32)), halves(acc[...] * vec_ref[8 : 8 + W, :]), NT)
    sums_ref[0:1, :] = (sums_ref[0:1, :] + L * whole[0:1, :]) * vec_ref[0:1, :]


class Copies:
    def __init__(self, ss, rs):
        self.ss, self.rs, self.items = ss, rs, {}

    def add(self, k, src, dst, to):
        self.items[k] = (src, dst, to)

    def make(self, k, src, dst, to):
        return pltpu.make_async_remote_copy(
            src_ref=src, dst_ref=dst, send_sem=self.ss.at[k], recv_sem=self.rs.at[k], device_id=to, device_id_type=MESH
        )

    def start(self, *ks):
        for k in ks:
            self.make(k, *self.items[k]).start()

    def landed(self, k, ref):
        self.make(k, ref, ref, self.items[k][2]).wait_recv()

    def finish(self):
        for k in self.items:
            self.make(k, *self.items[k]).wait_send()


def meet(devices):
    barrier = pltpu.get_barrier_semaphore()
    for device in devices:
        pl.semaphore_signal(barrier, inc=1, device_id=device, device_id_type=MESH)
    pl.semaphore_wait(barrier, len(devices))


def ring_mates(p):
    return [p.dev((p.s + k) % 16) for k in range(1, 16)]


def dp_mates(p, nd):
    return [((p.dp + k) % nd, p.s) for k in range(1, nd)]


def swap_copies(p, c, base, src, dst):
    for k in range(1, 16):
        to = (p.s + k) % 16
        c.add(base + k - 1, src.at[to], dst.at[p.s], p.dev(to))
    keys = range(base, base + 15)

    def start():
        c.start(*keys)

    def wait():
        for k in range(1, 16):
            c.landed(base + k - 1, dst.at[(p.s + 16 - k) % 16])

    return start, wait


def gather_plan(p, c, base, a_ref, land):
    H = a_ref.shape[0] // 2
    up, lo = pl.ds(0, H), pl.ds(H, H)
    core, xp, xm, zz = p.at(dc=1), p.at(dx=1), p.at(dx=-1), p.at(dz=1)
    d2, zxm, zxp, zd2 = p.at(dx=2), p.at(dx=-1, dz=1), p.at(dx=1, dz=1), p.at(dx=2, dz=1)
    L = land.at

    def add(k, src, dst, to):
        c.add(base + k, src, dst, p.dev(to))

    def relay(k, ref, to):
        add(k, ref, ref, to)

    for k, to in enumerate((xp, xm, zz, core)):
        add(k, a_ref, L[p.s], to)
    relay(4, L[xm, up], xp)
    relay(5, L[xp, lo], xm)
    relay(6, L[xm], core)
    relay(7, L[xp], core)
    relay(8, L[zz], xp)
    relay(9, L[zz], xm)
    relay(10, L[zz], core)
    relay(11, L[d2, up], zz)
    relay(12, L[d2, lo], zz)
    relay(13, L[d2], core)
    relay(14, L[zxm], core)
    relay(15, L[zxp], core)
    relay(16, L[zd2, up], core)
    relay(17, L[zd2, lo], core)

    def start(*ks):
        c.start(*(base + k for k in ks))

    def landed(k, ref):
        c.landed(base + k, ref)

    def one():
        start(0, 1, 2, 3)

    def two():
        landed(0, L[xm])
        start(4)
        landed(1, L[xp])
        start(5, 6, 7)
        landed(2, L[zz])
        start(8, 9, 10)

    def three():
        landed(4, L[d2, up])
        start(11)
        landed(5, L[d2, lo])
        start(12, 13)

    def four():
        landed(8, L[zxm])
        start(14)
        landed(9, L[zxp])
        start(15)

    def five():
        landed(11, L[zd2, up])
        start(16)
        landed(12, L[zd2, lo])
        start(17)

    def other(**k):
        return p.at(dc=1, **k)

    def six():
        landed(3, L[core])
        landed(6, L[other(dx=-1)])
        landed(7, L[other(dx=1)])
        landed(10, L[other(dz=1)])
        landed(13, L[other(dx=2)])
        landed(14, L[other(dx=-1, dz=1)])
        landed(15, L[other(dx=1, dz=1)])
        landed(16, L[other(dx=2, dz=1), up])
        landed(17, L[other(dx=2, dz=1), lo])

    return [one, two, three, four, five, six]


def dp_scratch(J, C):
    return [VMEM((2, 2, J // 2, C), BF), VMEM((2, 2, J // 2, C), BF), VMEM((2, 2, J, C), BF), VMEM((2, J, C), BF)]


def dp_plan(p, nd, c, base, g_ref, o_ref, scratch):
    hv, stage, xf, zb = scratch
    J = g_ref.shape[1]
    H = J // 2
    up, lo = pl.ds(0, H), pl.ds(H, H)
    ny = nd // 2
    y, zl = p.dp // 2, p.dp % 2
    yp, ym, yo = (y + 1) % ny, (y + ny - 1) % ny, (y + 2) % ny

    def pay(at, rows):
        return g_ref.at[pl.ds(2 * at, 2), rows]

    to_p, to_m, to_z = (2 * yp + zl, p.s), (2 * ym + zl, p.s), (2 * y + 1 - zl, p.s)
    c.add(base, pay(yo, up), hv.at[0], to_p)
    c.add(base + 1, pay(yo, lo), hv.at[1], to_m)
    c.add(base + 2, pay(yp, lo), xf.at[0, :, lo], to_p)
    c.add(base + 3, pay(ym, up), xf.at[1, :, up], to_m)
    c.add(base + 4, stage.at[0], xf.at[0, :, up], to_p)
    c.add(base + 5, stage.at[1], xf.at[1, :, lo], to_m)
    c.add(base + 6, zb.at[0], zb.at[1], to_z)

    def one():
        c.start(base, base + 1, base + 2, base + 3)

    def two():
        c.landed(base, hv.at[0])
        stage[0] = (g_ref[pl.ds(2 * yp, 2), up].astype(F32) + hv[0].astype(F32)).astype(BF)
        c.start(base + 4)
        c.landed(base + 1, hv.at[1])
        stage[1] = (g_ref[pl.ds(2 * ym, 2), lo].astype(F32) + hv[1].astype(F32)).astype(BF)
        c.start(base + 5)

    def total(which):
        return g_ref[2 * y + which].astype(F32) + xf[0, which].astype(F32) + xf[1, which].astype(F32)

    def three():
        c.landed(base + 2, xf.at[0, :, lo])
        c.landed(base + 3, xf.at[1, :, up])
        c.landed(base + 4, xf.at[0, :, up])
        c.landed(base + 5, xf.at[1, :, lo])
        zb[0] = total(1 - zl).astype(BF)
        c.start(base + 6)
        o_ref[0] = total(zl)

    def four():
        c.landed(base + 6, zb.at[1])
        o_ref[0] += zb[1].astype(F32)

    return [one, two, three, four]


def value_back_kernel(a_ref, w_ref, lift_ref, gf_ref, all_ref, o_ref, rc_ref, land, ss, rs, ls, cs, cr):
    R = a_ref.shape[0]
    start, wait = save_blocks(land, all_ref, ls)
    p = Place()
    c = Copies(cs, cr)
    begin, end = swap_copies(p, c, 0, gf_ref, rc_ref)

    def work(b):
        start(b)
        rows = pl.ds(pl.multiple_of(b * R, 16), R)
        gs = jnp.dot(land[b], w_ref[...], preferred_element_type=F32)
        o_ref[rows, :] = (gs * 2.0 * lift_ref[rows, :]).astype(BF)

    meet(ring_mates(p))
    t = run_gather(a_ref, land, ss, rs, work, met=True, between=begin)
    rc_ref[p.s] = gf_ref[p.s]
    end()
    wait()
    t.finish()
    c.finish()


def value_back(a, w, lift, gf, cid):
    R, C = a.shape
    units = w.shape[1]
    return pl.pallas_call(
        value_back_kernel,
        out_shape=(
            jax.ShapeDtypeStruct((16 * R, C), BF),
            jax.ShapeDtypeStruct((16 * R, units), BF),
            jax.ShapeDtypeStruct(gf.shape, BF),
        ),
        in_specs=[pl.BlockSpec(memory_space=VMEM)] * 4,
        out_specs=(pl.BlockSpec(memory_space=pl.ANY), pl.BlockSpec(memory_space=VMEM), pl.BlockSpec(memory_space=VMEM)),
        scratch_shapes=[VMEM((16, R, C), BF), DMA((18,)), DMA((18,)), DMA((16,)), DMA((15,)), DMA((15,))],
        compiler_params=pltpu.CompilerParams(collective_id=cid, has_side_effects=True, vmem_limit_bytes=48 * 2**20),
        name="gather_value_back",
    )(a, w, lift, gf)


def column_tiles(refs, tile, sem):
    C = tile.shape[2]

    def copy(u, ref):
        return pltpu.make_async_copy(ref.at[:, pl.ds(pl.multiple_of((u % 8) * C, C), C)], tile.at[u % 2], sem.at[u % 2])

    def start(u, kind):
        copy(u, refs[kind]).start()

    def wait(u, kind):
        copy(u, refs[kind]).wait()

    return start, wait


def key_back_kernel(l_ref, w_ref, s_ref, rt_ref, nu_ref, gkv_hbm, in_hbm, n2_hbm, o_ref, gg_ref,
                    pa, cb, zt, xs, zf, hv, xf, lt, tile, ss, rs, ts):
    T, U = l_ref.shape
    K = rt_ref.shape[1] // 2
    C = tile.shape[2]
    refs = (gkv_hbm, in_hbm, n2_hbm)
    fetch, have = column_tiles(refs, tile, ts)
    fetch(0, 0)

    def turn():
        for r in range(0, T, 256):
            rows = slice(r, r + 256)
            lt[0:U, rows] = s_ref[rows, :].T
            lt[U : 2 * U, rows] = l_ref[rows, :].T
            lt[2 * U :, rows] = rt_ref[rows, :].T

    def grads(kind, lo, hi):
        def unit(d, unused):
            u = 8 * kind + d
            if hi < 8:
                fetch(u + 1, kind)
            elif kind < 2:
                @pl.when(d < 7)
                def _():
                    fetch(u + 1, kind)

                @pl.when(d == 7)
                def _():
                    fetch(u + 1, kind + 1)
            else:
                @pl.when(d < 7)
                def _():
                    fetch(u + 1, kind)
            have(u, kind)
            rhs = tile[d % 2]
            if kind < 2:
                out = jnp.dot(lt[kind * U : (kind + 1) * U, :], rhs, preferred_element_type=F32)
                gg_ref[d, kind * U : (kind + 1) * U, :] = out.astype(BF)
            else:
                out = jnp.dot(lt[2 * U :, :], rhs, preferred_element_type=F32)
                nu = nu_ref[:, pl.ds(pl.multiple_of(d * C, C), C)]
                gg_ref[d, 2 * U :, :] = (out[:K] + nu * (out[K:] - out[:K])).astype(BF)
            return 0

        lax.fori_loop(lo, hi, unit, 0)

    jobs = [turn] + [functools.partial(grads, kind, lo, lo + 4) for kind in range(3) for lo in (0, 4)]
    sum_steps(l_ref, w_ref, o_ref, pa, cb, zt, xs, zf, hv, xf, ss, rs, jobs)


def key_back(l, w, s, rt, nu, gkv_all, key_in, n2_all, cid):
    R, C = l.shape[0] // 16, w.shape[1]
    U, K = l.shape[1], rt.shape[1] // 2
    return pl.pallas_call(
        key_back_kernel,
        out_shape=(jax.ShapeDtypeStruct((R, C), F32), jax.ShapeDtypeStruct((8, 2 * U + K, C // 8), BF)),
        in_specs=[pl.BlockSpec(memory_space=VMEM)] * 5 + [pl.BlockSpec(memory_space=pl.ANY)] * 3,
        out_specs=(pl.BlockSpec(memory_space=VMEM),) * 2,
        scratch_shapes=sum_scratch(R, C)
        + [VMEM((2 * U + 2 * K, 16 * R), BF), VMEM((2, 16 * R, C // 8), BF), DMA((18,)), DMA((18,)), DMA((2,))],
        compiler_params=pltpu.CompilerParams(collective_id=cid, has_side_effects=True, vmem_limit_bytes=56 * 2**20),
        name="key_back",
    )(l, w, s, rt, nu, gkv_all, key_in, n2_all)


def time_back_kernel(nd, x_ref, o_ref, s_ref, gz_ref, col_ref, row_ref, keep_ref, vec_ref, gh_ref, z_ref, mixt_ref, mu_ref, early_ref,
                     n1_hbm, g_ref, sums_ref, gg_ref, mug_ref, dp_ref,
                     tab, grad_state, acc, carry, gz, land, turned, tile, d0, d1, d2, d3, cs, cr, ts):
    p = Place()
    c = Copies(cs, cr)
    W = vec_ref.shape[1]
    chunks, L = row_ref.shape[0], row_ref.shape[2]
    C = tile.shape[2]
    begin, end = swap_copies(p, c, 0, gz_ref, gz)
    gather = gather_plan(p, c, 15, gh_ref, land)
    fetch, have = column_tiles((n1_hbm,), tile, ts)
    mates = ring_mates(p)
    if nd > 1:
        sums = dp_plan(p, nd, c, 33, early_ref, dp_ref, (d0, d1, d2, d3))
        mates = mates + dp_mates(p, nd)
    else:
        sums = [lambda: None] * 3 + [lambda: dp_ref.__setitem__(Ellipsis, early_ref[...].astype(F32))]
    meet(mates)
    begin()
    gather[0]()
    sums[0]()
    fetch(0, 0)
    land[p.s] = gh_ref[...]
    gz[p.s] = gz_ref[p.s]
    when = {4: [gather[1]], 8: [gather[2]], 10: [sums[1]], 12: [gather[3]]}
    chunk = back_chunk(x_ref, o_ref, s_ref, gz, col_ref, row_ref, keep_ref, vec_ref, g_ref, sums_ref, tab, grad_state, acc, carry, turned)
    end()

    def step(n, unused):
        chunk(n)
        for at, parts in when.items():
            @pl.when(n == at)
            def _():
                for part in parts:
                    part()
        return 0

    lax.fori_loop(0, chunks, step, 0)
    gather[4]()
    sums[2]()
    back_finish(vec_ref, sums_ref, acc, L)
    mug_ref[...] = jnp.zeros_like(mug_ref)

    def mix(d, unused):
        @pl.when(d < 7)
        def _():
            fetch(d + 1, 0)

        have(d, 0)
        rhs = tile[d % 2]
        cols = pl.ds(pl.multiple_of(d * C, C), C)
        for q in range(4):
            a = jnp.dot(turned[q * W : (q + 1) * W, :], rhs, preferred_element_type=F32)
            b = jnp.dot(turned[(4 + q) * W : (5 + q) * W, :], rhs, preferred_element_type=F32)
            diff = b - a
            gg_ref[d, q * W : (q + 1) * W, :] = (a + mu_ref[q : q + 1, cols] * diff).astype(BF)
            mug_ref[q : q + 1, cols] = jnp.sum(mixt_ref[q * W : (q + 1) * W, cols].astype(F32) * diff, axis=0, keepdims=True)
        return 0

    lax.fori_loop(0, 8, mix, 0)
    gather[5]()
    sums[3]()
    T = x_ref.shape[0]
    for r in range(0, T, 256):
        turned[0:W, r : r + 256] = z_ref[r : r + 256, :].T

    def out(d, unused):
        cols = pl.ds(pl.multiple_of(d * C, C), C)
        rhs = jnp.concatenate([land[b, :, cols] for b in range(16)], axis=0)
        gg_ref[d, 4 * W :, :] = jnp.dot(turned[0:W, :], rhs, preferred_element_type=F32).astype(BF)
        return 0

    lax.fori_loop(0, 8, out, 0)
    c.finish()


def time_back(nd, x, o, states, gz, cols, rows, keep, vec, gh, z, mixt, mu, early, n1_all, cid):
    T, W = x.shape[0], vec.shape[1]
    L = rows.shape[2]
    R, C = gh.shape
    J = early.shape[1]
    vm, hbm = pl.BlockSpec(memory_space=VMEM), pl.BlockSpec(memory_space=pl.ANY)
    return pl.pallas_call(
        functools.partial(time_back_kernel, nd),
        out_shape=(
            jax.ShapeDtypeStruct((T, 8 * W), BF),
            jax.ShapeDtypeStruct((8, W), F32),
            jax.ShapeDtypeStruct((8, 5 * W, C // 8), BF),
            jax.ShapeDtypeStruct((4, C), F32),
            jax.ShapeDtypeStruct((8 // nd, J, C // 8), F32),
        ),
        in_specs=[vm] * 6 + [pl.BlockSpec(memory_space=pltpu.SMEM)] + [vm] * 6 + [hbm],
        out_specs=(vm,) * 5,
        scratch_shapes=[
            VMEM((4, L, W), F32), VMEM((W, W), F32), VMEM((W, W), F32), VMEM((8, 4 * W), F32),
            VMEM((16, R, W), BF), VMEM((16, R, C), BF), VMEM((8 * W, T), BF), VMEM((2, T, C // 8), BF),
        ]
        + dp_scratch(J, C // 8)
        + [DMA((40,)), DMA((40,)), DMA((2,))],
        compiler_params=pltpu.CompilerParams(collective_id=cid, has_side_effects=True, vmem_limit_bytes=60 * 2**20),
        name="time_back",
    )(x, o, states, gz, cols, rows, keep, vec, gh, z, mixt, mu, early, n1_all)


def last_kernel(nd, l_ref, w_ref, gg_ref, x_ref, gh_ref, gain_ref, terms_ref, ig_ref, dp_ref, v_ref,
                pa, cb, zt, xs, zf, hv, xf, o_ref, d0, d1, d2, d3, tv, b1, t1, b2, ss, rs, cs, cr):
    p = Place()
    c = Copies(cs, cr)
    mates = ring_mates(p)
    if nd > 1:
        sums = dp_plan(p, nd, c, 0, gg_ref, dp_ref, (d0, d1, d2, d3))
        mates = mates + dp_mates(p, nd)
    else:
        sums = [lambda: None] * 3 + [lambda: dp_ref.__setitem__(Ellipsis, gg_ref[...].astype(F32))]
    meet(mates)
    sums[0]()
    nothing = lambda: None
    sum_steps(l_ref, w_ref, o_ref, pa, cb, zt, xs, zf, hv, xf, ss, rs, [nothing, sums[1], nothing, sums[2], nothing, nothing, sums[3]], met=True)
    x = x_ref[...].astype(F32)
    gn = o_ref[...]
    width = x.shape[1]
    center = x - jnp.sum(x, axis=1, keepdims=True) * (1.0 / width)
    scale = lax.rsqrt(jnp.sum(center * center, axis=1, keepdims=True) * (1.0 / width) + 1e-05)
    normed = center * scale
    tv[...] = terms_ref[...]
    tv[0:1, :] = jnp.sum(gn * normed, axis=0, keepdims=True)
    tv[1:2, :] = jnp.sum(gn, axis=0, keepdims=True)
    C = width // nd
    for k in range(1, nd):
        to = (p.dp + k) % nd
        c.add(6 + k, tv.at[:, pl.ds(pl.multiple_of(to * C, 128), C)], b1.at[k - 1], (to, p.s))
        c.start(6 + k)
    gx = gn * gain_ref[...]
    inner = gx - jnp.sum(gx, axis=1, keepdims=True) * (1.0 / width)
    inner = inner - normed * (jnp.sum(gx * normed, axis=1, keepdims=True) * (1.0 / width))
    ig_ref[...] = gh_ref[...] + scale * inner
    total = tv[:, pl.ds(pl.multiple_of(p.dp * C, 128), C)]
    for k in range(1, nd):
        c.landed(6 + k, b1.at[k - 1])
        total = total + b1[k - 1]
    t1[...] = total
    for k in range(1, 16):
        c.add(14 + k, t1, b2.at[k - 1], p.dev((p.s + k) % 16))
        c.start(14 + k)
    for k in range(1, 16):
        c.landed(14 + k, b2.at[k - 1])
        total = total + b2[k - 1]
    v_ref[...] = total
    c.finish()


def last(nd, l, w, gg, x, gh, gain, terms, cid):
    R, C = x.shape
    J = gg.shape[1]
    vm = pl.BlockSpec(memory_space=VMEM)
    piece = (terms.shape[0], C // nd)
    return pl.pallas_call(
        functools.partial(last_kernel, nd),
        out_shape=(jax.ShapeDtypeStruct((R, C), F32), jax.ShapeDtypeStruct((8 // nd, J, C // 8), F32), jax.ShapeDtypeStruct(piece, F32)),
        in_specs=[vm] * 7,
        out_specs=(vm,) * 3,
        scratch_shapes=sum_scratch(R, C)
        + [VMEM((R, C), F32)]
        + dp_scratch(J, C // 8)
        + [VMEM(terms.shape, F32), VMEM((max(nd - 1, 1),) + piece, F32), VMEM(piece, F32), VMEM((15,) + piece, F32)]
        + [DMA((18,)), DMA((18,)), DMA((30,)), DMA((30,))],
        compiler_params=pltpu.CompilerParams(collective_id=cid, has_side_effects=True, vmem_limit_bytes=60 * 2**20),
        name="last_sums",
    )(l, w, gg, x, gh, gain, terms)


def layer_norm(tensor, gain_row, bias_row):
    center = tensor - jnp.mean(tensor, axis=-1, keepdims=True)
    spread = jnp.mean(center * center, axis=-1, keepdims=True)
    return center * lax.rsqrt(spread + 1e-05) * gain_row + bias_row


def earlier(tensor):
    return jnp.concatenate([tensor[1:], jnp.zeros_like(tensor[:1])], axis=0)


def contract(left, right, left_dim, right_dim):
    return lax.dot_general(left, right, (((left_dim,), (right_dim,)), ((), ())), preferred_element_type=F32)


def body(nd, inputs, cotangent, mix_weights, out_weight, key_weight, value_weight, recept_weight, vectors, segment_ids):
    tokens, width = inputs.shape
    group = segment_ids.shape[0]
    cols = mix_weights.shape[2]
    s = lax.axis_index("sp")
    ring = group // tokens
    own = lax.dynamic_slice_in_dim(vectors, s * cols, cols, 1)
    same = jnp.concatenate([jnp.zeros((1,), F32), (segment_ids[1:] == segment_ids[:-1]).astype(F32)])
    same_next = earlier(same)
    here = s * tokens
    same_here = lax.dynamic_slice_in_dim(same, here, tokens, 0)[:, None]
    mu = vectors[2:6]
    nu_k, nu_r = vectors[12], vectors[13]

    out_full = lax.all_gather(out_weight, "sp", axis=0, tiled=True)
    recept_full = lax.all_gather(recept_weight.T, "sp", axis=0, tiled=True)

    mix_f = mix_weights.astype(F32)
    folded = jnp.concatenate(
        [((1.0 - mu)[:, :, None] * mix_f).astype(BF), (mu[:, :, None] * mix_f).astype(BF)], axis=0
    )
    folded = folded.transpose(0, 2, 1).reshape(8 * cols, width)
    x = inputs.astype(F32)
    n1 = layer_norm(x, vectors[0], vectors[1]).astype(BF)
    half = 4 * cols
    n1_all, projected = project(n1, mix_weights, mu, same[:, None], 0)

    chunks = group // CHUNK
    seg = segment_ids.reshape(chunks, CHUNK)
    ending = seg[:, CHUNK - 1 :]
    prior = jnp.concatenate([jnp.full((1, 1), -1, jnp.int32), ending[:-1]], axis=0)
    tok_cols = jnp.stack(
        [t.astype(F32).reshape(group) for t in (seg, seg == prior, seg == ending, same_next.reshape(seg.shape))], axis=1
    )
    tok_rows = seg.astype(F32)[:, None, :]
    keep = (ending == prior).astype(F32).reshape(chunks)
    lam = -jnp.exp(own[6])
    decay = jnp.broadcast_to(jnp.exp(lam * CHUNK)[:, None], (cols, cols))
    vec = jnp.concatenate([lam[None], own[7:10], jnp.zeros((4, cols), F32), decay], axis=0)
    z, mixed_time, states = recurrence(projected, tok_cols, tok_rows, keep, vec)

    z_here = swap(z.reshape(ring, tokens, cols), 1).transpose(1, 0, 2).reshape(tokens, width)
    hidden = x + jnp.dot(z_here, out_full, preferred_element_type=F32)
    n2 = layer_norm(hidden, vectors[10], vectors[11]).astype(BF)

    n2_all, key_in, lifted, squared = key_side(n2, key_weight, nu_k[None], same[:, None], 2)
    before = lax.dynamic_slice_in_dim(n2_all, jnp.maximum(here - 1, 0), 1, 0)
    n2_f = n2.astype(F32)
    shift_here = jnp.concatenate([before, n2[:-1]], axis=0).astype(F32) * same_here - n2_f
    recept_in = (n2_f + shift_here * nu_r).astype(BF)
    value_here = matmul_sum(squared, value_weight, 3)
    gate = jax.nn.sigmoid(contract(recept_in, recept_full, 1, 1))
    channel = (gate * value_here).astype(BF)
    result = (hidden + channel.astype(F32)).astype(BF)

    g = cotangent.astype(F32)
    grad_value = (g * gate).astype(BF)
    grad_recept = (g * value_here * (gate * (1.0 - gate))).astype(BF)
    grad_value_all, grad_key, recept_cols = value_back(
        grad_value, value_weight.T, lifted, grad_recept.reshape(tokens, ring, cols).transpose(1, 0, 2), 4
    )
    recept_cols = recept_cols.reshape(group, cols)
    recept_two = jnp.concatenate([recept_cols, earlier(recept_cols) * same_next[:, None].astype(BF)], axis=1)
    key_sum, early = key_back(
        grad_key, key_weight.T, squared, recept_two, nu_r[None], grad_value_all, key_in, n2_all, 5
    )
    recept_back = contract(grad_recept, recept_full, 1, 0)
    nu_k_grad = jnp.sum(key_sum * shift_here, axis=0)
    nu_r_grad = jnp.sum(recept_back * shift_here, axis=0)
    moved = (key_sum * nu_k + recept_back * nu_r) * same_here
    after = lax.ppermute(moved[:1], "sp", [(i, i - 1) for i in range(1, ring)])
    grad_n2 = key_sum * (1.0 - nu_k) + recept_back * (1.0 - nu_r) + jnp.concatenate([moved[1:], after], axis=0)
    unused, pull_two = jax.vjp(layer_norm, hidden, vectors[10], vectors[11])
    grad_hidden, gain_two, bias_two = pull_two(grad_n2)
    grad_hidden = g + grad_hidden

    grad_hidden_b = grad_hidden.astype(BF)
    gz_here = contract(grad_hidden_b, out_full, 1, 1).astype(BF)
    gz = gz_here.reshape(tokens, ring, cols).transpose(1, 0, 2)
    mixt = mix_weights.transpose(0, 2, 1).reshape(4 * cols, width)
    grads_two, head_sums_grad, late, mu_grads, early_sum = time_back(
        nd, projected, mixed_time, states, gz, tok_cols, tok_rows, keep, vec, grad_hidden_b, z, mixt, mu, early, n1_all, 7
    )

    def place(part):
        return lax.dynamic_update_slice_in_dim(jnp.zeros((width,), F32), part, s * cols, 0)

    none = jnp.zeros((width,), F32)
    terms = jnp.stack(
        [none, none, mu_grads[0], mu_grads[1], mu_grads[2], mu_grads[3]]
        + [place(head_sums_grad[q]) for q in range(4)]
        + [gain_two, bias_two, nu_k_grad, nu_r_grad, none, none]
    )
    input_grad, late_sum, vector_sum = last(nd, grads_two, folded, late, inputs, grad_hidden, vectors[0:1], terms, 8)
    piece = width // (nd * ring)
    vectors_grad = lax.dynamic_slice_in_dim(vector_sum[:14], s * piece, piece, 1)

    def columns(part):
        return part.transpose(1, 0, 2).reshape(part.shape[1], width // nd)

    early_sum, late_sum = columns(early_sum), columns(late_sum)
    units = key_weight.shape[1]
    return (
        result,
        input_grad,
        late_sum[:half].reshape(4, cols, width // nd).transpose(0, 2, 1),
        late_sum[half:],
        early_sum[units : 2 * units].T,
        early_sum[:units],
        early_sum[2 * units :].T,
        vectors_grad,
    )


def solution(mesh):
    placed = (
        P(("dp", "sp"), None),
        P(("dp", "sp"), None),
        P(None, None, "sp"),
        P("sp", None),
        P(None, "sp"),
        P("sp", None),
        P(None, "sp"),
        P(),
        P("dp"),
    )
    return jax.shard_map(
        functools.partial(body, mesh.shape["dp"]),
        mesh=mesh,
        in_specs=placed,
        out_specs=(
            P(("dp", "sp"), None),
            P(("dp", "sp"), None),
            P(None, "dp", "sp"),
            P("sp", "dp"),
            P("dp", "sp"),
            P("sp", "dp"),
            P("dp", "sp"),
            P(None, ("dp", "sp")),
        ),
        check_vma=False,
    )
```

```python
import functools

import jax
import jax.numpy as jnp
from jax import lax
from jax.experimental import pallas as pl
from jax.experimental.pallas import tpu as pltpu
from jax.sharding import PartitionSpec as P

MESH = pl.DeviceIdType.MESH
VMEM = pltpu.VMEM
DMA = pltpu.SemaphoreType.DMA
BF = jnp.bfloat16
F32 = jnp.float32

ATTENTION_WIDTH = 64
CHUNK = 128
WHOLE = pl.BlockSpec(memory_space=VMEM)
FAR = pl.BlockSpec(memory_space=pl.ANY)


class Place:
    def __init__(self):
        self.dp = lax.axis_index("dp")
        s = lax.axis_index("sp")
        self.s = s
        self.x, self.z, self.c = s // 4, (s // 2) % 2, s % 2

    def at(self, dx=0, dz=0, dc=0):
        return ((self.x + dx) % 4) * 4 + ((self.z + dz) % 2) * 2 + (self.c + dc) % 2

    def dev(self, s):
        return (self.dp, s)


class Across:
    def __init__(self, p, nd):
        self.p, self.ny = p, nd // 2
        self.x, self.z, self.c = p.dp // 2, p.dp % 2, p.c
        self.s = p.dp * 2 + p.c

    def at(self, dx=0, dz=0, dc=0):
        return ((self.x + dx) % self.ny) * 4 + ((self.z + dz) % 2) * 2 + (self.c + dc) % 2

    def dev(self, i):
        return (i // 2, self.p.s - self.p.c + i % 2)


class Copies:
    def __init__(self, ss, rs):
        self.ss, self.rs, self.items = ss, rs, {}

    def add(self, k, src, dst, to):
        self.items[k] = (src, dst, to)

    def make(self, k, src, dst, to):
        return pltpu.make_async_remote_copy(
            src_ref=src, dst_ref=dst, send_sem=self.ss.at[k], recv_sem=self.rs.at[k], device_id=to, device_id_type=MESH
        )

    def start(self, *ks):
        for k in ks:
            self.make(k, *self.items[k]).start()

    def landed(self, k, ref):
        self.make(k, ref, ref, self.items[k][2]).wait_recv()

    def finish(self):
        for k in self.items:
            self.make(k, *self.items[k]).wait_send()


def meet(devices):
    barrier = pltpu.get_barrier_semaphore()
    for device in devices:
        pl.semaphore_signal(barrier, inc=1, device_id=device, device_id_type=MESH)
    pl.semaphore_wait(barrier, len(devices))


def near(p):
    return [p.dev(p.at(dc=1)), p.dev(p.at(dx=1)), p.dev(p.at(dx=-1)), p.dev(p.at(dz=1))]


def beside(p, nd):
    y, zl, ny = p.dp // 2, p.dp % 2, nd // 2
    if nd == 1:
        return []
    return [(2 * ((y + 1) % ny) + zl, p.s), (2 * ((y + ny - 1) % ny) + zl, p.s), (2 * y + 1 - zl, p.s)]


def chip_mates(p):
    return [p.dev(p.at(dx, dz)) for dz in range(2) for dx in range(4)][1:]


def ring_mates(p):
    return [p.dev((p.s + k) % 16) for k in range(1, 16)]


def dp_mates(p, nd):
    return [((p.dp + k) % nd, p.s) for k in range(1, nd)]


def params(cid, mib):
    return pltpu.CompilerParams(collective_id=cid, has_side_effects=True, vmem_limit_bytes=mib * 2**20)


class Swap:
    def __init__(self, p, src, dst, ss, rs):
        self.p, self.src, self.dst, self.ss, self.rs = p, src, dst, ss, rs

    def make(self, src, dst, at, to):
        return pltpu.make_async_remote_copy(
            src_ref=src, dst_ref=dst, send_sem=self.ss.at[to], recv_sem=self.rs.at[at], device_id=self.p.dev(to), device_id_type=MESH
        )

    def give(self, i):
        @pl.when(i != self.p.s)
        def _():
            self.make(self.src(i), self.dst.at[self.p.s], self.p.s, i).start()

        @pl.when(i == self.p.s)
        def _():
            self.dst[self.p.s] = self.src(i)[...]

    def take(self, i):
        @pl.when(i != self.p.s)
        def _():
            self.make(self.dst.at[i], self.dst.at[i], i, i).wait_recv()

    def sent(self, i):
        @pl.when(i != self.p.s)
        def _():
            self.make(self.src(i), self.dst.at[self.p.s], self.p.s, i).wait_send()

    def all(self, act):
        def step(i, unused):
            act(i)
            return 0

        lax.fori_loop(0, 16, step, 0)


def blocks_of(land):
    H = land.shape[1] // 2
    return lambda i, half=None: land.at[i] if half is None else land.at[i, pl.ds(half * H, H)]


def matrix_blocks(land):
    K = land.shape[1] // 2

    def blk(i, half=None):
        rows = K if half is None else K // 2
        return land.at[i // 2, pl.ds(pl.multiple_of((i % 2) * K + (half or 0) * rows, 16), rows)]

    return blk


def gather_plan(p, c, base, a_ref, blk, around=False):
    core, xp, xm, zz = p.at(dc=1), p.at(dx=1), p.at(dx=-1), p.at(dz=1)
    d2, zxm, zxp, zd2 = p.at(dx=2), p.at(dx=-1, dz=1), p.at(dx=1, dz=1), p.at(dx=2, dz=1)
    up, lo = 0, 1

    def relay(k, ref, to):
        c.add(base + k, ref, ref, p.dev(to))

    for k, to in enumerate((xp, xm, zz, core)):
        c.add(base + k, a_ref, blk(p.s), p.dev(to))
    relay(4, blk(xm, up), xp)
    relay(5, blk(xp, lo), xm)
    relay(6, blk(xm), core)
    relay(7, blk(xp), core)
    relay(8, blk(zz), xp)
    relay(9, blk(zz), xm)
    relay(10, blk(zz), core)
    if around:
        relay(11, blk(zxm, up), xp)
        relay(12, blk(zxp, lo), xm)
    else:
        relay(11, blk(d2, up), zz)
        relay(12, blk(d2, lo), zz)
    relay(13, blk(d2), core)
    relay(14, blk(zxm), core)
    relay(15, blk(zxp), core)
    relay(16, blk(zd2, up), core)
    relay(17, blk(zd2, lo), core)

    def start(*ks):
        c.start(*(base + k for k in ks))

    def landed(k, ref):
        c.landed(base + k, ref)

    def other(**k):
        return p.at(dc=1, **k)

    def one():
        start(0, 1, 2, 3)
        return []

    def own():
        landed(3, blk(core))
        return [core]

    def two():
        landed(0, blk(xm))
        start(4)
        landed(1, blk(xp))
        start(5, 6, 7)
        landed(2, blk(zz))
        start(8, 9, 10)
        return [xm, xp, zz]

    def third():
        landed(6, blk(other(dx=-1)))
        return [other(dx=-1)]

    def three():
        landed(4, blk(d2, up))
        if not around:
            start(11)
        landed(5, blk(d2, lo))
        if not around:
            start(12)
        start(13)
        return [d2]

    def third_more():
        landed(7, blk(other(dx=1)))
        landed(10, blk(other(dz=1)))
        return [other(dx=1), other(dz=1)]

    def fourth():
        landed(13, blk(other(dx=2)))
        return [other(dx=2)]

    def four():
        landed(8, blk(zxm))
        if around:
            start(11)
        landed(9, blk(zxp))
        if around:
            start(12)
        start(14, 15)
        return [zxm, zxp]

    def five():
        landed(11, blk(zd2, up))
        start(16)
        landed(12, blk(zd2, lo))
        start(17)
        landed(14, blk(other(dx=-1, dz=1)))
        landed(15, blk(other(dx=1, dz=1)))
        return [other(dx=-1, dz=1), other(dx=1, dz=1), zd2]

    def six():
        landed(16, blk(other(dx=2, dz=1), up))
        landed(17, blk(other(dx=2, dz=1), lo))
        return [other(dx=2, dz=1)]

    return [one, own, two, third, three, third_more, fourth, four, five, six]


def run_gather(plan, own, work, hooks):
    ready = [own]
    for n, step in enumerate(plan):
        ready += step()
        for hook in hooks.get(n, ()):
            hook()
        if n > 0:
            for unused in range(min(2, len(ready))):
                work(ready.pop(0))
    for b in ready:
        work(b)


def chip_plan(p, c, base, w_ref, part):
    R, C = w_ref.shape[0], part.shape[1]
    cols = pl.ds(pl.multiple_of(p.dp * C, C), C)
    mates = [(dx, dz) for dz in range(2) for dx in range(4)][1:]

    def rows(s):
        return pl.ds(pl.multiple_of((s // 2) * R, 16), R)

    for k, (dx, dz) in enumerate(mates):
        c.add(base + k, w_ref.at[:, cols], part.at[rows(p.s)], p.dev(p.at(dx, dz)))

    def begin():
        part[rows(p.s), :] = w_ref[:, cols]
        c.start(*range(base, base + 7))

    def end():
        for k, (dx, dz) in enumerate(mates):
            c.landed(base + k, part.at[rows(p.at(-dx, dz))])

    return begin, end


def across_plan(p, nd, c, base, part, land):
    q = Across(p, nd)
    K = part.shape[0]
    plan = gather_plan(q, c, base, part, matrix_blocks(land), around=True)

    def go(*ns):
        def run():
            for n in ns:
                if n == 0:
                    land[p.dp, pl.ds(pl.multiple_of(p.c * K, 16), K), :] = part[...]
                plan[n]()

        return run

    return go


def save_blocks(land, all_ref, sem):
    R = land.shape[1]

    def start(b):
        pltpu.make_async_copy(land.at[b], all_ref.at[pl.ds(pl.multiple_of(b * R, 16), R)], sem.at[b]).start()

    def wait():
        for b in range(16):
            pltpu.make_async_copy(land.at[b], all_ref.at[pl.ds(b * R, R)], sem.at[b]).wait()

    return start, wait


def heads_of_blocks(land):
    R = land.shape[1]
    first = [land[b, 0:16, :].astype(F32)[0:1] for b in range(16)]
    before = [jnp.zeros_like(first[0])] + [land[b, R - 16 : R, :].astype(F32)[15:16] for b in range(15)]
    return jnp.concatenate(first, axis=0), jnp.concatenate(before, axis=0)


def shifted(n, same):
    rows = lax.broadcasted_iota(jnp.int32, n.shape, 0)
    before = jnp.where(rows == 0, 0.0, pltpu.roll(n, 1, 0))
    return before * same - n


def norm_parts(a):
    width = a.shape[1]
    center = a - jnp.sum(a, axis=1, keepdims=True) * (1.0 / width)
    scale = lax.rsqrt(jnp.sum(center * center, axis=1, keepdims=True) * (1.0 / width) + 1e-05)
    return center, scale, center * scale


def norm_back(normed, scale, grad):
    width = grad.shape[1]
    inner = grad - jnp.sum(grad, axis=1, keepdims=True) * (1.0 / width)
    return scale * (inner - normed * (jnp.sum(grad * normed, axis=1, keepdims=True) * (1.0 / width)))


def sigmoid(a):
    return 1.0 / (1.0 + jnp.exp(-a))


CHUNK = 128


def halves(a):
    high = a.astype(BF)
    return high, (a - high.astype(F32)).astype(BF)


def dot3(a, b, dims):
    def one(x, y):
        return lax.dot_general(x, y, (dims, ((), ())), preferred_element_type=F32)

    return one(a[0], b[0]) + (one(a[0], b[1]) + one(a[1], b[0]))


NN, NT, TN = ((1,), (0,)), ((1,), (1,)), ((0,), (0,))


def head_sums(a, ones):
    high, rest = a.astype(BF), a - a.astype(BF).astype(F32)
    mid = rest.astype(BF)
    low = (rest - mid.astype(F32)).astype(BF)

    def one(x):
        return lax.dot_general(x, ones, (NN, ((), ())), preferred_element_type=F32)

    return one(high) + (one(mid) + one(low))


def iota(shape, dim):
    return lax.broadcasted_iota(jnp.int32, shape, dim)


def head_ones(width, dtype):
    return (iota((width, width), 0) // ATTENTION_WIDTH == iota((width, width), 1) // ATTENTION_WIDTH).astype(dtype)


def by_head(pair):
    lane = iota(pair[0].shape, 1) // ATTENTION_WIDTH
    heads = pair[0].shape[1] // ATTENTION_WIDTH
    zero = jnp.zeros_like(pair[0])
    return tuple(jnp.concatenate([jnp.where(lane == h, a, zero) for h in range(heads)], axis=0) for a in pair)


def pick_heads(a, rows):
    lane = iota((rows, a.shape[1]), 1) // ATTENTION_WIDTH
    out = a[:rows]
    for h in range(1, a.shape[1] // ATTENTION_WIDTH):
        out = jnp.where(lane == h, a[h * rows : (h + 1) * rows], out)
    return out


def powers(lam, tab):
    L = tab.shape[1]
    at = iota((L, 1), 0).astype(F32)
    mid = L // 2
    tab[0] = jnp.exp(lam * (at - mid))
    tab[1] = jnp.exp(-lam * (at + (1.0 - mid)))
    tab[2] = jnp.exp(lam * at)
    tab[3] = jnp.exp(lam * (L - 1.0 - at))


def chunk_mask(col, row):
    L = col.shape[0]
    return (iota((L, L), 1) < iota((L, L), 0)) & (col == row)


def forward_chunk(x_ref, col_ref, row_ref, keep_ref, vec_ref, z_ref, o_ref, s_ref, tab, state):
    chunks, L = row_ref.shape[0], row_ref.shape[2]
    W = vec_ref.shape[1]
    heads = W // ATTENTION_WIDTH
    lam, bonus, gain, bias = (vec_ref[q : q + 1, :] for q in range(4))
    powers(lam, tab)
    ones = head_ones(W, BF)
    diag = head_ones(W, F32)
    decay = vec_ref[8 : 8 + W, :]
    state[...] = jnp.zeros_like(state)

    def step(i):
        rows = pl.ds(pl.multiple_of(i * L, L), L)
        r, k, v, p = (x_ref[rows, q * W : (q + 1) * W] for q in range(4))
        col = col_ref[rows, :]
        seg, kept, tail = col[:, 0:1], col[:, 1:2], col[:, 2:3]
        mask = chunk_mask(seg, row_ref[i])
        mask = jnp.concatenate([mask] * heads, axis=1)
        rs, ks = halves(r * tab[0]), halves(k * tab[1])
        scores = jnp.where(mask, dot3(rs, by_head(ks), NT), 0.0)
        vh = halves(v)
        out = dot3(halves(scores), by_head(vh), NN) + head_sums(r * k * bonus, ones) * v
        memory = state[...]
        s_ref[i] = memory
        out = out + kept * dot3(halves(r * tab[2]), halves(memory), NN)
        state[...] = keep_ref[i] * decay * memory + diag * dot3(halves(k * tab[3] * tail), vh, TN)
        o_ref[rows, :] = out
        center = out - head_sums(out, ones) * (1.0 / ATTENTION_WIDTH)
        spread = head_sums(center * center, ones) * (1.0 / ATTENTION_WIDTH)
        normed = center * lax.rsqrt(spread + 0.00064) * gain + bias
        z_ref[rows, :] = (normed * (p * sigmoid(p))).astype(BF)

    return step


def back_chunk(x_ref, o_ref, s_ref, gz_ref, col_ref, row_ref, keep_ref, vec_ref, g_ref, sums_ref, tab, grad_state, acc, carry, turned):
    chunks, L = row_ref.shape[0], row_ref.shape[2]
    W = vec_ref.shape[1]
    heads = W // ATTENTION_WIDTH
    lam, bonus, gain, bias = (vec_ref[q : q + 1, :] for q in range(4))
    powers(lam, tab)
    ones = head_ones(W, BF)
    diag = head_ones(W, F32)
    decay = vec_ref[8 : 8 + W, :]
    at = iota((L, 1), 0).astype(F32)
    mid = float(L // 2)
    grad_state[...] = jnp.zeros_like(grad_state)
    acc[...] = jnp.zeros_like(acc)
    carry[...] = jnp.zeros_like(carry)
    sums_ref[...] = jnp.zeros_like(sums_ref)

    def add(q, term):
        sums_ref[q : q + 1, :] += jnp.sum(term, axis=0, keepdims=True)

    def step(n):
        i = chunks - 1 - n
        rows = pl.ds(pl.multiple_of(i * L, L), L)
        r, k, v, p = (x_ref[rows, q * W : (q + 1) * W] for q in range(4))
        col = col_ref[rows, :]
        seg, kept, tail, same_next = col[:, 0:1], col[:, 1:2], col[:, 2:3], col[:, 3:4]
        o = o_ref[rows, :]
        gz = gz_ref[i].astype(F32)
        center = o - head_sums(o, ones) * (1.0 / ATTENTION_WIDTH)
        spread = head_sums(center * center, ones) * (1.0 / ATTENTION_WIDTH)
        scale = lax.rsqrt(spread + 0.00064)
        normed = center * scale
        gate = sigmoid(p)
        silu = p * gate
        gy = gz * silu
        gp = gz * (normed * gain + bias) * (gate * (1.0 + p * (1.0 - gate)))
        add(2, gy * normed)
        add(3, gy)
        gn = gy * gain
        go = scale * (
            gn
            - head_sums(gn, ones) * (1.0 / ATTENTION_WIDTH)
            - normed * (head_sums(gn * normed, ones) * (1.0 / ATTENTION_WIDTH))
        )
        mask = chunk_mask(seg, row_ref[i])
        mask = jnp.concatenate([mask] * heads, axis=1)
        rs_f, ks_f = r * tab[0], k * tab[1]
        r0_f, ke_f = r * tab[2] * kept, k * tab[3] * tail
        rs, ks, vh, goh = halves(rs_f), halves(ks_f), halves(v), halves(go)
        ks_by, v_by = by_head(ks), by_head(vh)
        scores = halves(jnp.where(mask, dot3(rs, ks_by, NT), 0.0))
        grad_scores = halves(jnp.where(mask, dot3(goh, v_by, NT), 0.0))
        memory = s_ref[i]
        gs = grad_state[...]
        mh, gsh = halves(memory), halves(gs)
        reward = head_sums(r * k * bonus, ones)
        grad_reward = head_sums(go * v, ones)
        g_rs = dot3(grad_scores, ks_by, NN)
        g_r0 = dot3(goh, mh, NT)
        g_ks = pick_heads(dot3(grad_scores, rs, TN), L)
        g_ke = dot3(vh, gsh, NT)
        gv = pick_heads(dot3(scores, goh, TN), L) + reward * go + dot3(halves(ke_f), gsh, NN)
        keep = keep_ref[i]
        acc[...] += keep * memory * gs
        grad_state[...] = keep * decay * gs + diag * dot3(halves(r0_f), goh, TN)
        gr = g_rs * tab[0] + g_r0 * (tab[2] * kept) + grad_reward * bonus * k
        gk = g_ks * tab[1] + g_ke * (tab[3] * tail) + grad_reward * bonus * r
        add(1, grad_reward * r * k)
        add(0, (at - mid) * (g_rs * rs_f) - (at + (1.0 - mid)) * (g_ks * ks_f) + at * (g_r0 * r0_f) + (L - 1.0 - at) * (g_ke * ke_f))
        grads = jnp.concatenate([gr, gk, gv, gp], axis=1).astype(BF).astype(F32)
        last = iota((L, 1), 0) == L - 1
        after = jnp.where(last, carry[0:1, :], pltpu.roll(grads, L - 1, 0)) * same_next
        carry[0:1, :] = grads[0:1, :]
        g_ref[rows, : 4 * W] = grads.astype(BF)
        g_ref[rows, 4 * W :] = after.astype(BF)
        turned[0 : 4 * W, rows] = grads.T.astype(BF)
        turned[4 * W :, rows] = after.T.astype(BF)

    return step


def back_finish(vec_ref, sums_ref, acc, L):
    W = vec_ref.shape[1]
    whole = dot3(halves(jnp.ones((8, W), F32)), halves(acc[...] * vec_ref[8 : 8 + W, :]), NT)
    sums_ref[0:1, :] = (sums_ref[0:1, :] + L * whole[0:1, :]) * vec_ref[0:1, :]


def time_forward_kernel(nd, x_ref, w_ref, ow_ref, rw_ref, par_ref, col_ref, row_ref, keep_ref, vec_ref,
                        all_ref, proj_ref, z_ref, o_ref, s_ref, hid_ref, n2_ref, rp_ref, far_ref,
                        n1, land, op, lw, tab, state, zin, cs, cr, ss, rs, ls, ms):
    p = Place()
    c = Copies(cs, cr)
    R = x_ref.shape[0]
    Q, W = w_ref.shape[0], w_ref.shape[2]
    C = lw.shape[2]
    begin, end = chip_plan(p, c, 18, ow_ref, op)
    go = across_plan(p, nd, c, 25, op, lw)
    recept_begin, recept_end = chip_plan(p, c, 43, rw_ref, rp_ref)
    plan = gather_plan(p, c, 0, n1, blocks_of(land))
    start, wait = save_blocks(land, all_ref, ls)
    x = x_ref[...].astype(F32)
    n1[...] = (norm_parts(x)[2] * par_ref[0:1, :] + par_ref[1:2, :]).astype(BF)
    meet(chip_mates(p) + [p.dev(p.at(dc=1))] + beside(p, nd))
    land[p.s] = n1[...]

    def work(b):
        start(b)
        rows = pl.ds(pl.multiple_of(b * R, 16), R)
        n = land[b].astype(F32)
        shift = shifted(n, col_ref[rows, 4:5])
        for q in range(Q):
            m = (n + shift * par_ref[2 + q : 3 + q, :]).astype(BF)
            proj_ref[rows, q * W : (q + 1) * W] = jnp.dot(m, w_ref[q], preferred_element_type=F32)

    run_gather(plan, p.s, work, {0: [begin], 3: [end, go(0)], 8: [go(1, 2)]})
    recept_begin()
    first, before = heads_of_blocks(land)
    same = jnp.concatenate([col_ref[b * R : b * R + 1, 4:5] for b in range(16)], axis=0)
    shift = before * same - first
    for q in range(Q):
        m = (first + shift * par_ref[2 + q : 3 + q, :]).astype(BF)
        out = jnp.dot(m, w_ref[q], preferred_element_type=F32)
        for b in range(16):
            proj_ref[b * R : b * R + 1, q * W : (q + 1) * W] = out[b : b + 1]

    chunk = forward_chunk(proj_ref, col_ref, row_ref, keep_ref, vec_ref, z_ref, o_ref, s_ref, tab, state)
    swap = Swap(p, lambda i: z_ref.at[pl.ds(pl.multiple_of(i * R, 16), R)], zin, ss, rs)
    when = {3: go(3, 4), 6: go(5, 6, 7)}

    def step(n, unused):
        chunk(2 * n)
        chunk(2 * n + 1)
        swap.give(2 * n)
        swap.give(2 * n + 1)
        for at, act in when.items():
            pl.when(n == at)(act)
        return 0

    lax.fori_loop(0, row_ref.shape[0] // 2, step, 0)
    go(8, 9)()
    saved = pltpu.make_async_copy(lw, far_ref, ms.at[0])
    saved.start()
    swap.all(swap.take)
    recept_end()
    z_here = jnp.concatenate([zin[2 * k + core] for core in range(2) for k in range(8)], axis=1)
    for d in range(8):
        cols = slice(d * C, (d + 1) * C)
        hid_ref[:, cols] = x_ref[:, cols].astype(F32) + jnp.dot(z_here, lw[d], preferred_element_type=F32)
    n2_ref[...] = (norm_parts(hid_ref[...])[2] * par_ref[10:11, :] + par_ref[11:12, :]).astype(BF)
    wait()
    saved.wait()
    swap.all(swap.sent)
    c.finish()


def time_forward(nd, x, w, ow, rw, par, cols, rows, keep, vec, cid):
    R, C = x.shape
    T, W = 16 * R, w.shape[2]
    chunks, L = rows.shape[0], rows.shape[2]
    return pl.pallas_call(
        functools.partial(time_forward_kernel, nd),
        out_shape=(
            jax.ShapeDtypeStruct((T, C), BF),
            jax.ShapeDtypeStruct((T, 4 * W), F32),
            jax.ShapeDtypeStruct((T, W), BF),
            jax.ShapeDtypeStruct((T, W), F32),
            jax.ShapeDtypeStruct((chunks, W, W), F32),
            jax.ShapeDtypeStruct((R, C), F32),
            jax.ShapeDtypeStruct((R, C), BF),
            jax.ShapeDtypeStruct((8 * R, C // nd), BF),
            jax.ShapeDtypeStruct((8, 16 * R, C // 8), BF),
        ),
        in_specs=[WHOLE] * 7 + [pl.BlockSpec(memory_space=pltpu.SMEM), WHOLE],
        out_specs=(FAR,) + (WHOLE,) * 7 + (FAR,),
        scratch_shapes=[
            VMEM((R, C), BF), VMEM((16, R, C), BF), VMEM((8 * R, C // nd), BF), VMEM((8, 16 * R, C // 8), BF), VMEM((4, L, W), F32), VMEM((W, W), F32),
            VMEM((16, R, W), BF), DMA((50,)), DMA((50,)), DMA((16,)), DMA((16,)), DMA((16,)), DMA((1,)),
        ],
        compiler_params=params(cid, 56),
        name="time_forward",
    )(x, w, ow, rw, par, cols, rows, keep, vec)


def key_kernel(nd, a_ref, w_ref, rp_ref, par_ref, col_ref, vw_ref, mw_ref,
               all_ref, in_ref, lift_ref, sq_ref, rin_ref, sh_ref, vt_ref, kt_ref, mt_ref, fold_ref, far_ref,
               land, mixed, lw, cs, cr, ls, ms, fs):
    p = Place()
    c = Copies(cs, cr)
    R = a_ref.shape[0]
    go = across_plan(p, nd, c, 18, rp_ref, lw)
    plan = gather_plan(p, c, 0, a_ref, blocks_of(land))
    start, wait = save_blocks(land, all_ref, ls)
    meet(near(p) + beside(p, nd))
    land[p.s] = a_ref[...]
    nu_k, nu_r = par_ref[12:13, :], par_ref[13:14, :]
    Q, W = mw_ref.shape[0], mw_ref.shape[2]

    def turn():
        for k in range(0, w_ref.shape[0], 256):
            cols = slice(k, k + 256)
            kt_ref[:, cols] = w_ref[cols, :].T
            vt_ref[cols, :] = vw_ref[:, cols].T

    def fold(*qs):
        def run():
            for q in qs:
                for k in range(0, mw_ref.shape[1], 256):
                    cols, rows = slice(k, k + 256), slice(q * W, (q + 1) * W)
                    turned = mw_ref[q, cols, :].T
                    mt_ref[rows, cols] = turned
                    part = turned.astype(F32)
                    mu = par_ref[2 + q : 3 + q, cols]
                    fold_ref[rows, cols] = ((1.0 - mu) * part).astype(BF)
                    fold_ref[(Q + q) * W : (Q + q + 1) * W, cols] = (mu * part).astype(BF)

        return run

    def work(b):
        start(b)
        n = land[b].astype(F32)
        rows = pl.ds(pl.multiple_of(b * R, 16), R)
        m = (n + shifted(n, col_ref[rows, 4:5]) * nu_k).astype(BF)
        mixed[b] = m
        e = jnp.maximum(jnp.dot(m, w_ref[...], preferred_element_type=F32), 0.0)
        lift_ref[rows, :] = e
        sq_ref[rows, :] = (e * e).astype(BF)

    run_gather(plan, p.s, work, {0: [go(0), fold(0, 1)], 1: [turn], 3: [go(1, 2)], 4: [fold(2, 3)], 5: [go(3, 4)], 7: [go(5, 6, 7)]})
    first, before = heads_of_blocks(land)
    same = jnp.concatenate([col_ref[b * R : b * R + 1, 4:5] for b in range(16)], axis=0)
    shift = before * same - first
    head = first + shift * nu_k
    e = jnp.maximum(jnp.dot(head.astype(BF), w_ref[...], preferred_element_type=F32), 0.0)
    sq = e * e
    copies = []
    for b in range(16):
        rows = slice(b * R, b * R + 16)
        top = lax.broadcasted_iota(jnp.int32, (16, 1), 0) == 0
        mixed[b, 0:16, :] = jnp.where(top, head[b : b + 1], mixed[b, 0:16, :].astype(F32)).astype(BF)
        lift_ref[b * R : b * R + 1, :] = e[b : b + 1]
        sq_ref[rows, :] = jnp.where(top, sq[b : b + 1], sq_ref[rows, :].astype(F32)).astype(BF)
        cp = pltpu.make_async_copy(mixed.at[b], in_ref.at[pl.ds(b * R, R)], ms.at[b])
        cp.start()
        copies.append(cp)
    n = a_ref[...].astype(F32)
    mine = lax.broadcasted_iota(jnp.int32, (16, 1), 0) == p.s
    own_first = jnp.sum(jnp.where(mine, shift, 0.0), axis=0, keepdims=True)
    here = pl.ds(pl.multiple_of(p.s * R, 16), R)
    top = lax.broadcasted_iota(jnp.int32, (R, 1), 0) == 0
    moved = jnp.where(top, own_first, shifted(n, col_ref[here, 4:5]))
    sh_ref[...] = moved
    rin_ref[...] = (n + moved * nu_r).astype(BF)
    go(8, 9)()
    saved = pltpu.make_async_copy(lw, far_ref, fs.at[0])
    saved.start()
    for cp in copies:
        cp.wait()
    wait()
    saved.wait()
    c.finish()


def key_side(nd, a, w, part, par, cols, vw, mw, cid):
    R, C = a.shape
    T, units = 16 * R, w.shape[1]
    Q, W = mw.shape[0], mw.shape[2]
    return pl.pallas_call(
        functools.partial(key_kernel, nd),
        out_shape=(
            jax.ShapeDtypeStruct((T, C), BF),
            jax.ShapeDtypeStruct((T, C), BF),
            jax.ShapeDtypeStruct((T, units), F32),
            jax.ShapeDtypeStruct((T, units), BF),
            jax.ShapeDtypeStruct((R, C), BF),
            jax.ShapeDtypeStruct((R, C), F32),
            jax.ShapeDtypeStruct((C, units), BF),
            jax.ShapeDtypeStruct((units, C), BF),
            jax.ShapeDtypeStruct((Q * W, C), BF),
            jax.ShapeDtypeStruct((2 * Q * W, C), BF),
            jax.ShapeDtypeStruct((8, T, C // 8), BF),
        ),
        in_specs=[WHOLE] * 7,
        out_specs=(FAR, FAR) + (WHOLE,) * 8 + (FAR,),
        scratch_shapes=[
            VMEM((16, R, C), BF), VMEM((16, R, C), BF), VMEM((8, T, C // 8), BF),
            DMA((36,)), DMA((36,)), DMA((16,)), DMA((16,)), DMA((1,)),
        ],
        compiler_params=params(cid, 60),
        name="key_side",
    )(a, w, part, par, cols, vw, mw)


def column_tiles(refs, tile, sem):
    C = tile.shape[2]

    def copy(u, ref):
        if len(ref.shape) == 3:
            return pltpu.make_async_copy(ref.at[u % 8], tile.at[u % 2], sem.at[u % 2])
        return pltpu.make_async_copy(ref.at[:, pl.ds(pl.multiple_of((u % 8) * C, C), C)], tile.at[u % 2], sem.at[u % 2])

    def start(u, kind):
        copy(u, refs[kind]).start()

    def wait(u, kind):
        copy(u, refs[kind]).wait()

    return start, wait


def sum_scratch(R, C):
    return [
        VMEM((8, 2, R, C), BF), VMEM((8, R, C), BF), VMEM((R, C), BF), VMEM((2, R, C), BF), VMEM((R, C), BF),
        VMEM((2, R // 2, C), BF), VMEM((2, R, C), BF),
    ]


def sum_plan(p, c, base, l_ref, w_ref, o_ref, scratch):
    pa, cb, zt, xs, zf, hv, xf = scratch
    R = o_ref.shape[0]
    H = R // 2
    core, xp, xm, zz = (p.dev(i) for i in (p.at(dc=1), p.at(dx=1), p.at(dx=-1), p.at(dz=1)))
    upper, lower = pl.ds(0, H), pl.ds(H, H)
    order = [(2, 1), (-1, 1), (1, 1), (2, 0), (0, 1), (1, 0), (-1, 0), (0, 0)]

    def send(k, src, dst, to):
        c.add(base + k, src, dst, to)
        c.start(base + k)

    def landed(k, ref):
        c.landed(base + k, ref)

    def term(i, dc):
        b = p.at(order[i][0], order[i][1], dc)
        rows = l_ref[pl.ds(pl.multiple_of(b * R, 16), R), :]
        return jnp.dot(rows, w_ref[...], preferred_element_type=F32)

    def give(i):
        pa[i, 0] = term(i, 1).astype(BF)
        send(i, pa.at[i, 0], cb.at[i], core)

    def pair(i):
        mine = term(i, 0).astype(BF).astype(F32)
        landed(i, cb.at[i])
        pa[i, 1] = (mine + cb[i].astype(F32)).astype(BF)

    def one():
        give(0)
        give(1)
        pair(0)
        send(8, pa.at[0, 1], zt, zz)
        give(2)
        pair(1)
        send(9, pa.at[1, 1], xs.at[1], xm)
        give(3)
        pair(2)
        send(10, pa.at[2, 1], xs.at[0], xp)
        give(4)
        give(5)
        pair(3)
        give(6)
        pair(4)
        pair(5)
        send(11, pa.at[5, 1, lower], xf.at[0, lower], xp)
        give(7)
        pair(6)
        send(12, pa.at[6, 1, upper], xf.at[1, upper], xm)
        pair(7)

    def two():
        landed(8, zt)
        pa[3, 1] = (pa[3, 1].astype(F32) + zt[...].astype(F32)).astype(BF)
        send(13, pa.at[3, 1, upper], hv.at[0], xp)
        send(14, pa.at[3, 1, lower], hv.at[1], xm)

    def three():
        landed(9, xs.at[1])
        landed(10, xs.at[0])
        pa[4, 1] = (pa[4, 1].astype(F32) + xs[0].astype(F32) + xs[1].astype(F32)).astype(BF)
        send(15, pa.at[4, 1], zf, zz)

    def four():
        landed(13, hv.at[0])
        pa[5, 1, upper] = (pa[5, 1, upper].astype(F32) + hv[0].astype(F32)).astype(BF)
        send(16, pa.at[5, 1, upper], xf.at[0, upper], xp)
        landed(14, hv.at[1])
        pa[6, 1, lower] = (pa[6, 1, lower].astype(F32) + hv[1].astype(F32)).astype(BF)
        send(17, pa.at[6, 1, lower], xf.at[1, lower], xm)

    def five():
        landed(11, xf.at[0, lower])
        landed(12, xf.at[1, upper])
        landed(15, zf)
        o_ref[...] = pa[7, 1].astype(F32) + zf[...].astype(F32)

    def six():
        landed(16, xf.at[0, upper])
        landed(17, xf.at[1, lower])
        o_ref[...] = o_ref[...] + xf[0].astype(F32) + xf[1].astype(F32)

    return [one, two, three, four, five, six]


def value_kernel(l_ref, w_ref, vt_ref, lift_ref, rin_ref, hid_ref, g_ref, far_ref,
                 all_ref, res_ref, gf_ref, rc_ref, ge_ref, get_ref, st_ref, *rest):
    scratch, (o_ref, f_ref, gate_ref, gkv, land, tile, cs, cr, ss, rs, ls, ts) = rest[:7], rest[7:]
    p = Place()
    c = Copies(cs, cr)
    R = o_ref.shape[0]
    T = l_ref.shape[0]
    W = gf_ref.shape[2]
    C = tile.shape[2]
    fetch, have = column_tiles((far_ref,), tile, ts)
    fetch(0, 0)
    sums = sum_plan(p, c, 0, l_ref, w_ref, o_ref, scratch)
    plan = gather_plan(p, c, 18, gkv, blocks_of(land))
    save, saved = save_blocks(land, all_ref, ls)
    swap = Swap(p, lambda i: gf_ref.at[i], rc_ref, ss, rs)
    meet(near(p))
    sums[0]()

    def unit(d, unused):
        pl.when(d < 7)(lambda: fetch(d + 1, 0))
        have(d, 0)
        cols = pl.ds(pl.multiple_of(d * C, C), C)
        part = lax.dot_general(rin_ref[:, cols], tile[d % 2], (NT, ((), ())), preferred_element_type=F32)

        @pl.when(d == 0)
        def _():
            f_ref[...] = part

        @pl.when(d > 0)
        def _():
            f_ref[...] += part

        return 0

    lax.fori_loop(0, 8, unit, 0)
    for s in range(16):
        at = ((s % 2) * 8 + s // 2) * W
        cols = slice(s * W, (s + 1) * W)
        gate = sigmoid(f_ref[:, at : at + W])
        gate_ref[:, cols] = gate
        gkv[:, cols] = (g_ref[:, cols].astype(F32) * gate).astype(BF)
    plan[0]()
    land[p.s] = gkv[...]

    def work(*blocks):
        for b in blocks:
            save(b)
            rows = pl.ds(pl.multiple_of(b * R, 16), R)
            gs = jnp.dot(land[b], vt_ref[...], preferred_element_type=F32)
            ge = gs * 2.0 * lift_ref[rows, :]
            ge_ref[rows, :] = ge.astype(BF)
            get_ref[:, pl.ds(pl.multiple_of(b * R, 128), R)] = ge.T.astype(BF)

    def turn(lo, hi):
        for r in range(lo, hi, 256):
            st_ref[:, r : r + 256] = l_ref[r : r + 256, :].T

    sums[1]()
    sums[2]()
    work(p.s)
    work(*plan[1]())
    sums[3]()
    ready = plan[2]()
    work(ready[0])
    turn(0, T // 2)
    ready = ready[1:] + plan[3]()
    sums[4]()
    ready += plan[4]()
    work(ready[0])
    turn(T // 2, T)
    sums[5]()
    kv, gate = o_ref[...], gate_ref[...]
    gf = g_ref[...].astype(F32) * kv * (gate * (1.0 - gate))
    for s in range(16):
        gf_ref[s] = gf[:, s * W : (s + 1) * W].astype(BF)
    swap.all(swap.give)
    res_ref[...] = (hid_ref[...] + (gate * kv).astype(BF).astype(F32)).astype(BF)
    ready = ready[1:]
    for n in range(5, 10):
        ready += plan[n]()
        work(*ready[:2])
        ready = ready[2:]
    work(*ready)
    swap.all(swap.take)
    saved()
    swap.all(swap.sent)
    c.finish()


def value_side(l, w, vt, lift, rin, hidden, g, far, cid):
    R, C = hidden.shape
    T, U = l.shape
    W = C // 16
    return pl.pallas_call(
        value_kernel,
        out_shape=(
            jax.ShapeDtypeStruct((T, C), BF),
            jax.ShapeDtypeStruct((R, C), BF),
            jax.ShapeDtypeStruct((16, R, W), BF),
            jax.ShapeDtypeStruct((16, R, W), BF),
            jax.ShapeDtypeStruct((T, U), BF),
            jax.ShapeDtypeStruct((U, T), BF),
            jax.ShapeDtypeStruct((U, T), BF),
        ),
        in_specs=[WHOLE] * 7 + [FAR],
        out_specs=(FAR,) + (WHOLE,) * 6,
        scratch_shapes=sum_scratch(R, C)
        + [VMEM((R, C), F32), VMEM((R, C), F32), VMEM((R, C), F32), VMEM((R, C), BF), VMEM((16, R, C), BF), VMEM((2, T, C // 8), BF)]
        + [DMA((36,)), DMA((36,)), DMA((16,)), DMA((16,)), DMA((16,)), DMA((2,))],
        compiler_params=params(cid, 60),
        name="value_side",
    )(l, w, vt, lift, rin, hidden, g, far)


def dp_scratch(J, C):
    return [VMEM((2, 2, J // 2, C), BF), VMEM((2, 2, J // 2, C), BF), VMEM((2, 2, J, C), BF), VMEM((2, J, C), BF)]


def dp_plan(p, nd, c, base, g_ref, o_ref, scratch):
    hv, stage, xf, zb = scratch
    J = g_ref.shape[1]
    H = J // 2
    up, lo = pl.ds(0, H), pl.ds(H, H)
    ny = nd // 2
    y, zl = p.dp // 2, p.dp % 2
    yp, ym, yo = (y + 1) % ny, (y + ny - 1) % ny, (y + 2) % ny

    def pay(at, rows):
        return g_ref.at[pl.ds(2 * at, 2), rows]

    to_p, to_m, to_z = (2 * yp + zl, p.s), (2 * ym + zl, p.s), (2 * y + 1 - zl, p.s)
    c.add(base, pay(yo, up), hv.at[0], to_p)
    c.add(base + 1, pay(yo, lo), hv.at[1], to_m)
    c.add(base + 2, pay(yp, lo), xf.at[0, :, lo], to_p)
    c.add(base + 3, pay(ym, up), xf.at[1, :, up], to_m)
    c.add(base + 4, stage.at[0], xf.at[0, :, up], to_p)
    c.add(base + 5, stage.at[1], xf.at[1, :, lo], to_m)
    c.add(base + 6, zb.at[0], zb.at[1], to_z)

    def one():
        c.start(base, base + 1, base + 2, base + 3)

    def two():
        c.landed(base, hv.at[0])
        stage[0] = (g_ref[pl.ds(2 * yp, 2), up].astype(F32) + hv[0].astype(F32)).astype(BF)
        c.start(base + 4)
        c.landed(base + 1, hv.at[1])
        stage[1] = (g_ref[pl.ds(2 * ym, 2), lo].astype(F32) + hv[1].astype(F32)).astype(BF)
        c.start(base + 5)

    def total(which):
        return g_ref[2 * y + which].astype(F32) + xf[0, which].astype(F32) + xf[1, which].astype(F32)

    def three():
        c.landed(base + 2, xf.at[0, :, lo])
        c.landed(base + 3, xf.at[1, :, up])
        c.landed(base + 4, xf.at[0, :, up])
        c.landed(base + 5, xf.at[1, :, lo])
        zb[0] = total(1 - zl).astype(BF)
        c.start(base + 6)
        o_ref[0] = total(zl)

    def four():
        c.landed(base + 6, zb.at[1])
        o_ref[0] += zb[1].astype(F32)

    return [one, two, three, four]


def no_sums(g_ref, o_ref):
    def copy():
        o_ref[...] = g_ref[...].astype(F32)

    return [lambda: None] * 3 + [copy]


def key_back_kernel(l_ref, w_ref, st_ref, lt_ref, rc_ref, gf_ref, par_ref, col_ref, hid_ref, sh_ref, g_ref,
                    gkv_hbm, in_hbm, n2_hbm, far_ref, out_far, gh_ref, ghb_ref, rows_ref, gg_ref, gz_ref, *rest):
    scratch, (o_ref, rt, gfp, ga_ref, gzp, halo, tile, strip, cs, cr, ss, rs, ts, os) = rest[:7], rest[7:]
    p = Place()
    c = Copies(cs, cr)
    T, U = l_ref.shape
    R, width = o_ref.shape
    W = rc_ref.shape[2]
    C = tile.shape[2]
    fetch, have = column_tiles((gkv_hbm, in_hbm, n2_hbm, far_ref), tile, ts)
    fetch(0, 0)

    def strip_copy(n):
        return pltpu.make_async_copy(out_far.at[:, pl.ds(pl.multiple_of(n * 2 * W, 16), 2 * W)], strip.at[n % 2], os.at[n % 2])

    c.add(18, halo.at[0], halo.at[1], p.dev((p.s + 15) % 16))
    sums = sum_plan(p, c, 0, l_ref, w_ref, o_ref, scratch)
    swap = Swap(p, lambda i: gzp.at[i], gz_ref, ss, rs)
    meet(near(p) + [p.dev((p.s + 1) % 16), p.dev((p.s + 15) % 16)])
    nu_k, nu_r = par_ref[12:13, :], par_ref[13:14, :]

    def turn():
        last = lax.broadcasted_iota(jnp.int32, (R, 1), 0) == R - 1
        for b in range(16):
            part = rc_ref[b].astype(F32)
            after = rc_ref[b + 1, 0:16, :].astype(F32)[0:1] if b < 15 else jnp.zeros((1, W), F32)
            moved = jnp.where(last, after, pltpu.roll(part, R - 1, 0)) * col_ref[b * R : (b + 1) * R, 3:4]
            rt[0:W, b * R : (b + 1) * R] = part.T.astype(BF)
            rt[W:, b * R : (b + 1) * R] = moved.T.astype(BF)
        for s in range(16):
            at = ((s % 2) * 8 + s // 2) * W
            gfp[:, at : at + W] = gf_ref[s]

    def units(kind, lo, hi):
        def unit(d, unused):
            u = 8 * kind + d
            if hi < 8:
                fetch(u + 1, kind)
            else:
                pl.when(d < 7)(lambda: fetch(u + 1, kind))
                if kind < 3:
                    pl.when(d == 7)(lambda: fetch(u + 1, kind + 1))
            have(u, kind)
            rhs = tile[d % 2]
            cols = pl.ds(pl.multiple_of(d * C, C), C)
            if kind < 2:
                lhs = (st_ref, lt_ref)[kind]
                gg_ref[d, kind * U : (kind + 1) * U, :] = jnp.dot(lhs[...], rhs, preferred_element_type=F32).astype(BF)
            elif kind == 2:
                out = jnp.dot(rt[...], rhs, preferred_element_type=F32)
                gg_ref[d, 2 * U :, :] = (out[:W] + par_ref[13:14, cols] * (out[W:] - out[:W])).astype(BF)
            else:
                ga_ref[:, cols] = jnp.dot(gfp[...], rhs, preferred_element_type=F32)
            return 0

        lax.fori_loop(lo, hi, unit, 0)

    sums[0]()
    units(0, 0, 5)
    sums[1]()
    sums[2]()
    units(0, 5, 8)
    turn()
    sums[3]()
    units(1, 0, 8)
    units(2, 0, 8)
    sums[4]()
    units(3, 0, 8)
    strip_copy(0).start()
    sums[5]()
    ga_k, ga_r, shift = o_ref[...], ga_ref[...], sh_ref[...]
    here = pl.ds(pl.multiple_of(p.s * R, 16), R)
    moved = (ga_k * nu_k + ga_r * nu_r) * col_ref[here, 4:5]
    halo[0] = moved[0:8]
    c.start(18)
    unused, scale, normed = norm_parts(hid_ref[...])
    c.landed(18, halo.at[1])
    last = lax.broadcasted_iota(jnp.int32, (R, 1), 0) == R - 1
    grad = ga_k - ga_k * nu_k + (ga_r - ga_r * nu_r) + jnp.where(last, halo[1, 0:1, :], pltpu.roll(moved, R - 1, 0))
    gh = g_ref[...].astype(F32) + norm_back(normed, scale, grad * par_ref[10:11, :])
    gh_ref[...] = gh
    ghb_ref[...] = gh.astype(BF)

    def back_out(n, unused):
        pl.when(n < 7)(lambda: strip_copy(n + 1).start())
        strip_copy(n).wait()
        part = lax.dot_general(ghb_ref[:, 0:C], strip[n % 2, 0], (NT, ((), ())), preferred_element_type=F32)
        for d in range(1, 8):
            part = part + lax.dot_general(
                ghb_ref[:, d * C : (d + 1) * C], strip[n % 2, d], (NT, ((), ())), preferred_element_type=F32
            )
        for k in range(2):
            to = 2 * ((2 * n + k) % 8) + (2 * n + k) // 8
            gzp[to] = part[:, k * W : (k + 1) * W].astype(BF)
            swap.give(to)
        return 0

    lax.fori_loop(0, 8, back_out, 0)
    rows_ref[...] = jnp.zeros_like(rows_ref)
    rows_ref[0:1, :] = jnp.sum(grad * normed, axis=0, keepdims=True)
    rows_ref[1:2, :] = jnp.sum(grad, axis=0, keepdims=True)
    rows_ref[2:3, :] = jnp.sum(ga_k * shift, axis=0, keepdims=True)
    rows_ref[3:4, :] = jnp.sum(ga_r * shift, axis=0, keepdims=True)
    swap.all(swap.take)
    swap.all(swap.sent)
    c.finish()


def key_back(l, w, st, lt, rc, gf, par, cols, hidden, sh, g, gkv_all, key_in, n2_all, far, out_far, cid):
    R, C = hidden.shape
    T, U, W = 16 * R, l.shape[1], rc.shape[2]
    return pl.pallas_call(
        key_back_kernel,
        out_shape=(
            jax.ShapeDtypeStruct((R, C), F32),
            jax.ShapeDtypeStruct((R, C), BF),
            jax.ShapeDtypeStruct((8, C), F32),
            jax.ShapeDtypeStruct((8, 2 * U + W, C // 8), BF),
            jax.ShapeDtypeStruct((16, R, W), BF),
        ),
        in_specs=[WHOLE] * 11 + [FAR] * 5,
        out_specs=(WHOLE,) * 5,
        scratch_shapes=sum_scratch(R, C)
        + [VMEM((R, C), F32), VMEM((2 * W, T), BF), VMEM((R, C), BF), VMEM((R, C), F32), VMEM((16, R, W), BF), VMEM((2, 8, C), F32)]
        + [VMEM((2, T, C // 8), BF), VMEM((2, 8, 2 * W, C // 8), BF)]
        + [DMA((19,)), DMA((19,)), DMA((16,)), DMA((16,)), DMA((2,)), DMA((2,))],
        compiler_params=params(cid, 60),
        name="key_back",
    )(l, w, st, lt, rc, gf, par, cols, hidden, sh, g, gkv_all, key_in, n2_all, far, out_far)


def time_back_kernel(nd, x_ref, o_ref, s_ref, gz, col_ref, row_ref, keep_ref, vec_ref, gh_ref, z_ref, mixt_ref, mu_ref, early_ref,
                     n1_hbm, g_ref, sums_ref, gg_ref, mug_ref, dp_ref,
                     tab, grad_state, acc, carry, land, turned, tile, d0, d1, d2, d3, cs, cr, ts):
    p = Place()
    c = Copies(cs, cr)
    W = vec_ref.shape[1]
    chunks, L = row_ref.shape[0], row_ref.shape[2]
    C = tile.shape[2]
    fetch, have = column_tiles((n1_hbm,), tile, ts)
    fetch(0, 0)
    plan = gather_plan(p, c, 0, gh_ref, blocks_of(land))
    sums = dp_plan(p, nd, c, 18, early_ref, dp_ref, (d0, d1, d2, d3)) if nd > 1 else no_sums(early_ref, dp_ref)
    meet(near(p) + beside(p, nd))
    plan[0]()
    sums[0]()
    land[p.s] = gh_ref[...]
    when = {6: [plan[1], plan[2]], 9: [sums[1]], 11: [plan[3], plan[4]], 14: [plan[5], plan[6], plan[7]]}
    chunk = back_chunk(x_ref, o_ref, s_ref, gz, col_ref, row_ref, keep_ref, vec_ref, g_ref, sums_ref, tab, grad_state, acc, carry, turned)

    def step(n, unused):
        chunk(n)
        for at, parts in when.items():
            @pl.when(n == at)
            def _():
                for part in parts:
                    part()
        return 0

    lax.fori_loop(0, chunks, step, 0)
    sums[2]()
    back_finish(vec_ref, sums_ref, acc, L)
    mug_ref[...] = jnp.zeros_like(mug_ref)

    def mix(d, unused):
        pl.when(d < 7)(lambda: fetch(d + 1, 0))
        have(d, 0)
        rhs = tile[d % 2]
        cols = pl.ds(pl.multiple_of(d * C, C), C)
        a = jnp.dot(turned[: 4 * W, :], rhs, preferred_element_type=F32)
        b = jnp.dot(turned[4 * W :, :], rhs, preferred_element_type=F32)
        for q in range(4):
            rows = slice(q * W, (q + 1) * W)
            diff = b[rows] - a[rows]
            gg_ref[d, rows, :] = (a[rows] + mu_ref[q : q + 1, cols] * diff).astype(BF)
            mug_ref[q : q + 1, cols] = jnp.sum(mixt_ref[rows, cols].astype(F32) * diff, axis=0, keepdims=True)
        return 0

    lax.fori_loop(0, 4, mix, 0)
    plan[8]()
    lax.fori_loop(4, 8, mix, 0)
    sums[3]()
    T = x_ref.shape[0]
    for r in range(0, T, 256):
        turned[0:W, r : r + 256] = z_ref[r : r + 256, :].T
    plan[9]()

    def out(d, unused):
        cols = pl.ds(pl.multiple_of(d * C, C), C)
        rhs = jnp.concatenate([land[b, :, cols] for b in range(16)], axis=0)
        gg_ref[d, 4 * W :, :] = jnp.dot(turned[0:W, :], rhs, preferred_element_type=F32).astype(BF)
        return 0

    lax.fori_loop(0, 8, out, 0)
    c.finish()


def time_back(nd, x, o, states, gz, cols, rows, keep, vec, gh, z, mixt, mu, early, n1_all, cid):
    T, W = x.shape[0], vec.shape[1]
    L = rows.shape[2]
    R, C = gh.shape
    J = early.shape[1]
    return pl.pallas_call(
        functools.partial(time_back_kernel, nd),
        out_shape=(
            jax.ShapeDtypeStruct((T, 8 * W), BF),
            jax.ShapeDtypeStruct((8, W), F32),
            jax.ShapeDtypeStruct((8, 5 * W, C // 8), BF),
            jax.ShapeDtypeStruct((4, C), F32),
            jax.ShapeDtypeStruct((8 // nd, J, C // 8), F32),
        ),
        in_specs=[WHOLE] * 6 + [pl.BlockSpec(memory_space=pltpu.SMEM)] + [WHOLE] * 6 + [FAR],
        out_specs=(WHOLE,) * 5,
        scratch_shapes=[
            VMEM((4, L, W), F32), VMEM((W, W), F32), VMEM((W, W), F32), VMEM((8, 4 * W), F32),
            VMEM((16, R, C), BF), VMEM((8 * W, T), BF), VMEM((2, T, C // 8), BF),
        ]
        + dp_scratch(J, C // 8)
        + [DMA((25,)), DMA((25,)), DMA((2,))],
        compiler_params=params(cid, 60),
        name="time_back",
    )(x, o, states, gz, cols, rows, keep, vec, gh, z, mixt, mu, early, n1_all)


def last_kernel(nd, l_ref, w_ref, gg_ref, x_ref, gh_ref, par_ref, mug_ref, head_ref, norm_ref, ig_ref, dp_ref, v_ref, *rest):
    scratch, (o_ref, d0, d1, d2, d3, tv, b1, t1, b2, cs, cr) = rest[:7], rest[7:]
    p = Place()
    c = Copies(cs, cr)
    sums = dp_plan(p, nd, c, 18, gg_ref, dp_ref, (d0, d1, d2, d3)) if nd > 1 else no_sums(gg_ref, dp_ref)
    steps = sum_plan(p, c, 0, l_ref, w_ref, o_ref, scratch)
    meet(near(p) + beside(p, nd))
    sums[0]()
    steps[0]()
    sums[1]()
    steps[1]()
    steps[2]()
    steps[3]()
    sums[2]()
    W = head_ref.shape[1]
    tv[...] = jnp.zeros_like(tv)
    tv[2:6, :] = mug_ref[...]
    tv[6:10, pl.ds(pl.multiple_of(p.s * W, 128), W)] = head_ref[0:4, :]
    tv[10:14, :] = norm_ref[0:4, :]
    unused, scale, normed = norm_parts(x_ref[...].astype(F32))
    sums[3]()
    steps[4]()
    steps[5]()
    gn = o_ref[...]
    tv[0:1, :] = jnp.sum(gn * normed, axis=0, keepdims=True)
    tv[1:2, :] = jnp.sum(gn, axis=0, keepdims=True)
    C = b1.shape[2]
    for k in range(1, nd):
        to = (p.dp + k) % nd
        c.add(24 + k, tv.at[:, pl.ds(pl.multiple_of(to * C, 128), C)], b1.at[k - 1], (to, p.s))
        c.start(24 + k)
    ig_ref[...] = gh_ref[...] + norm_back(normed, scale, gn * par_ref[0:1, :])
    total = tv[:, pl.ds(pl.multiple_of(p.dp * C, 128), C)]
    for k in range(1, nd):
        c.landed(24 + k, b1.at[k - 1])
        total = total + b1[k - 1]
    t1[...] = total
    for k in range(1, 16):
        c.add(31 + k, t1, b2.at[k - 1], p.dev((p.s + k) % 16))
        c.start(31 + k)
    for k in range(1, 16):
        c.landed(31 + k, b2.at[k - 1])
        total = total + b2[k - 1]
    v_ref[...] = total
    c.finish()


def last_sums(nd, l, w, gg, x, gh, par, mug, head, norm, cid):
    R, C = x.shape
    J = gg.shape[1]
    piece = (16, C // nd)
    return pl.pallas_call(
        functools.partial(last_kernel, nd),
        out_shape=(jax.ShapeDtypeStruct((R, C), F32), jax.ShapeDtypeStruct((8 // nd, J, C // 8), F32), jax.ShapeDtypeStruct(piece, F32)),
        in_specs=[WHOLE] * 9,
        out_specs=(WHOLE,) * 3,
        scratch_shapes=sum_scratch(R, C)
        + [VMEM((R, C), F32)]
        + dp_scratch(J, C // 8)
        + [VMEM((16, C), F32), VMEM((max(nd - 1, 1),) + piece, F32), VMEM(piece, F32), VMEM((15,) + piece, F32)]
        + [DMA((47,)), DMA((47,))],
        compiler_params=params(cid, 60),
        name="last_sums",
    )(l, w, gg, x, gh, par, mug, head, norm)


def body(nd, inputs, cotangent, mix_weights, out_weight, key_weight, value_weight, recept_weight, vectors, segment_ids):
    tokens, width = inputs.shape
    group = segment_ids.shape[0]
    cols = mix_weights.shape[2]
    units = key_weight.shape[1]
    s = lax.axis_index("sp")
    ring = group // tokens
    own = lax.dynamic_slice_in_dim(vectors, s * cols, cols, 1)

    chunks = group // CHUNK
    seg = segment_ids.reshape(chunks, CHUNK)
    ending = seg[:, CHUNK - 1 :]
    prior = jnp.concatenate([jnp.full((1, 1), -1, jnp.int32), ending[:-1]], axis=0)
    joined = segment_ids[1:] == segment_ids[:-1]
    edge = jnp.zeros((1,), bool)
    same, same_next = jnp.concatenate([edge, joined]), jnp.concatenate([joined, edge])
    tok_cols = jnp.stack(
        [t.astype(F32).reshape(group) for t in (seg, seg == prior, seg == ending, same_next, same)], axis=1
    )
    tok_rows = seg.astype(F32)[:, None, :]
    keep = (ending == prior).astype(F32).reshape(chunks)
    lam = -jnp.exp(own[6])
    decay = jnp.broadcast_to(jnp.exp(lam * CHUNK)[:, None], (cols, cols))
    vec = jnp.concatenate([lam[None], own[7:10], jnp.zeros((4, cols), F32), decay], axis=0)

    n1_all, projected, z, mixed_time, states, hidden, n2, recept_part, out_far = time_forward(
        nd, inputs, mix_weights, out_weight, recept_weight.T, vectors, tok_cols, tok_rows, keep, vec, 0
    )
    n2_all, key_in, lifted, squared, recept_in, shift, value_t, key_t, mixt, folded, recept_far = key_side(
        nd, n2, key_weight, recept_part, vectors, tok_cols, value_weight, mix_weights, 1
    )
    grad_value_all, result, grad_recept, recept_cols, grad_key, grad_key_t, squared_t = value_side(
        squared, value_weight, value_t, lifted, recept_in, hidden, cotangent, recept_far, 2
    )
    grad_hidden, grad_hidden_b, norm_rows, early, gz = key_back(
        grad_key, key_t, squared_t, grad_key_t, recept_cols, grad_recept, vectors, tok_cols, hidden, shift, cotangent,
        grad_value_all, key_in, n2_all, recept_far, out_far, 3,
    )
    grads_two, head_rows, late, mu_rows, early_sum = time_back(
        nd, projected, mixed_time, states, gz, tok_cols, tok_rows, keep, vec, grad_hidden_b, z, mixt, vectors[2:6], early, n1_all, 4
    )
    input_grad, late_sum, vector_sum = last_sums(
        nd, grads_two, folded, late, inputs, grad_hidden, vectors, mu_rows, head_rows, norm_rows, 5
    )
    piece = width // (nd * ring)
    vectors_grad = lax.dynamic_slice_in_dim(vector_sum[:14], s * piece, piece, 1)

    def columns(part):
        return part.transpose(1, 0, 2).reshape(part.shape[1], width // nd)

    early_sum, late_sum = columns(early_sum), columns(late_sum)
    return (
        result,
        input_grad,
        late_sum[: 4 * cols].reshape(4, cols, width // nd).transpose(0, 2, 1),
        late_sum[4 * cols :],
        early_sum[units : 2 * units].T,
        early_sum[:units],
        early_sum[2 * units :].T,
        vectors_grad,
    )


def solution(mesh):
    placed = (
        P(("dp", "sp"), None),
        P(("dp", "sp"), None),
        P(None, None, "sp"),
        P("sp", None),
        P(None, "sp"),
        P("sp", None),
        P(None, "sp"),
        P(),
        P("dp"),
    )
    return jax.shard_map(
        functools.partial(body, mesh.shape["dp"]),
        mesh=mesh,
        in_specs=placed,
        out_specs=(
            P(("dp", "sp"), None),
            P(("dp", "sp"), None),
            P(None, "dp", "sp"),
            P("sp", "dp"),
            P("dp", "sp"),
            P("sp", "dp"),
            P("dp", "sp"),
            P(None, ("dp", "sp")),
        ),
        check_vma=False,
    )
```

```python
import functools

import jax
import jax.numpy as jnp
from jax import lax
from jax.experimental import pallas as pl
from jax.experimental.pallas import tpu as pltpu
from jax.sharding import PartitionSpec as P

MESH = pl.DeviceIdType.MESH
VMEM = pltpu.VMEM
DMA = pltpu.SemaphoreType.DMA
BF = jnp.bfloat16
F32 = jnp.float32

ATTENTION_WIDTH = 64
CHUNK = 128
WHOLE = pl.BlockSpec(memory_space=VMEM)
FAR = pl.BlockSpec(memory_space=pl.ANY)


class Place:
    def __init__(self):
        self.dp = lax.axis_index("dp")
        s = lax.axis_index("sp")
        self.s = s
        self.x, self.z, self.c = s // 4, (s // 2) % 2, s % 2

    def at(self, dx=0, dz=0, dc=0):
        return ((self.x + dx) % 4) * 4 + ((self.z + dz) % 2) * 2 + (self.c + dc) % 2

    def dev(self, s):
        return (self.dp, s)


class Across:
    def __init__(self, p, nd):
        self.p, self.ny = p, nd // 2
        self.x, self.z, self.c = p.dp // 2, p.dp % 2, p.c
        self.s = p.dp * 2 + p.c

    def at(self, dx=0, dz=0, dc=0):
        return ((self.x + dx) % self.ny) * 4 + ((self.z + dz) % 2) * 2 + (self.c + dc) % 2

    def dev(self, i):
        return (i // 2, self.p.s - self.p.c + i % 2)


class Copies:
    def __init__(self, ss, rs):
        self.ss, self.rs, self.items = ss, rs, {}

    def add(self, k, src, dst, to):
        self.items[k] = (src, dst, to)

    def make(self, k, src, dst, to):
        return pltpu.make_async_remote_copy(
            src_ref=src, dst_ref=dst, send_sem=self.ss.at[k], recv_sem=self.rs.at[k], device_id=to, device_id_type=MESH
        )

    def start(self, *ks):
        for k in ks:
            self.make(k, *self.items[k]).start()

    def landed(self, k, ref):
        self.make(k, ref, ref, self.items[k][2]).wait_recv()

    def finish(self):
        for k in self.items:
            self.make(k, *self.items[k]).wait_send()


def meet(devices):
    barrier = pltpu.get_barrier_semaphore()
    for device in devices:
        pl.semaphore_signal(barrier, inc=1, device_id=device, device_id_type=MESH)
    pl.semaphore_wait(barrier, len(devices))


def near(p):
    return [p.dev(p.at(dc=1)), p.dev(p.at(dx=1)), p.dev(p.at(dx=-1)), p.dev(p.at(dz=1))]


def beside(p, nd):
    y, zl, ny = p.dp // 2, p.dp % 2, nd // 2
    if nd == 1:
        return []
    return [(2 * ((y + 1) % ny) + zl, p.s), (2 * ((y + ny - 1) % ny) + zl, p.s), (2 * y + 1 - zl, p.s)]


def chip_mates(p):
    return [p.dev(p.at(dx, dz)) for dz in range(2) for dx in range(4)][1:]


def ring_mates(p):
    return [p.dev((p.s + k) % 16) for k in range(1, 16)]


def dp_mates(p, nd):
    return [((p.dp + k) % nd, p.s) for k in range(1, nd)]


def params(cid, mib):
    return pltpu.CompilerParams(collective_id=cid, has_side_effects=True, vmem_limit_bytes=mib * 2**20)


class Swap:
    def __init__(self, p, src, dst, ss, rs):
        self.p, self.src, self.dst, self.ss, self.rs = p, src, dst, ss, rs

    def make(self, src, dst, at, to):
        return pltpu.make_async_remote_copy(
            src_ref=src, dst_ref=dst, send_sem=self.ss.at[to], recv_sem=self.rs.at[at], device_id=self.p.dev(to), device_id_type=MESH
        )

    def give(self, i):
        @pl.when(i != self.p.s)
        def _():
            self.make(self.src(i), self.dst.at[self.p.s], self.p.s, i).start()

        @pl.when(i == self.p.s)
        def _():
            self.dst[self.p.s] = self.src(i)[...]

    def take(self, i):
        @pl.when(i != self.p.s)
        def _():
            self.make(self.dst.at[i], self.dst.at[i], i, i).wait_recv()

    def sent(self, i):
        @pl.when(i != self.p.s)
        def _():
            self.make(self.src(i), self.dst.at[self.p.s], self.p.s, i).wait_send()

    def all(self, act):
        def step(i, unused):
            act(i)
            return 0

        lax.fori_loop(0, 16, step, 0)


class Moves:
    def __init__(self, sem):
        self.sem, self.n = sem, 0

    def start(self, src, dst):
        cp = pltpu.make_async_copy(src, dst, self.sem.at[self.n])
        self.n += 1
        cp.start()
        return cp


def equal(a, b):
    return jnp.where(a == b, 1.0, 0.0)


def blocks_of(land):
    H = land.shape[1] // 2
    return lambda i, half=None: land.at[i] if half is None else land.at[i, pl.ds(half * H, H)]


def rows_of(land):
    R = land.shape[0] // 16

    def blk(i, half=None):
        rows = R if half is None else R // 2
        return land.at[pl.ds(pl.multiple_of(i * R + (half or 0) * rows, 16), rows)]

    return blk


def matrix_blocks(land):
    K = land.shape[1] // 2

    def blk(i, half=None):
        rows = K if half is None else K // 2
        return land.at[i // 2, pl.ds(pl.multiple_of((i % 2) * K + (half or 0) * rows, 16), rows)]

    return blk


def gather_plan(p, c, base, a_ref, blk, around=False):
    core, xp, xm, zz = p.at(dc=1), p.at(dx=1), p.at(dx=-1), p.at(dz=1)
    d2, zxm, zxp, zd2 = p.at(dx=2), p.at(dx=-1, dz=1), p.at(dx=1, dz=1), p.at(dx=2, dz=1)
    up, lo = 0, 1

    def relay(k, ref, to):
        c.add(base + k, ref, ref, p.dev(to))

    for k, to in enumerate((xp, xm, zz, core)):
        c.add(base + k, a_ref, blk(p.s), p.dev(to))
    relay(4, blk(xm, up), xp)
    relay(5, blk(xp, lo), xm)
    relay(6, blk(xm), core)
    relay(7, blk(xp), core)
    relay(8, blk(zz), xp)
    relay(9, blk(zz), xm)
    relay(10, blk(zz), core)
    if around:
        relay(11, blk(zxm, up), xp)
        relay(12, blk(zxp, lo), xm)
    else:
        relay(11, blk(d2, up), zz)
        relay(12, blk(d2, lo), zz)
    relay(13, blk(d2), core)
    relay(14, blk(zxm), core)
    relay(15, blk(zxp), core)
    relay(16, blk(zd2, up), core)
    relay(17, blk(zd2, lo), core)

    def start(*ks):
        c.start(*(base + k for k in ks))

    def landed(k, ref):
        c.landed(base + k, ref)

    def other(**k):
        return p.at(dc=1, **k)

    def one():
        start(0, 1, 2, 3)
        return []

    def own():
        landed(3, blk(core))
        return [core]

    def two():
        landed(0, blk(xm))
        start(4)
        landed(1, blk(xp))
        start(5, 6, 7)
        landed(2, blk(zz))
        start(8, 9, 10)
        return [xm, xp, zz]

    def third():
        landed(6, blk(other(dx=-1)))
        return [other(dx=-1)]

    def three():
        landed(4, blk(d2, up))
        if not around:
            start(11)
        landed(5, blk(d2, lo))
        if not around:
            start(12)
        start(13)
        return [d2]

    def third_more():
        landed(7, blk(other(dx=1)))
        landed(10, blk(other(dz=1)))
        return [other(dx=1), other(dz=1)]

    def fourth():
        landed(13, blk(other(dx=2)))
        return [other(dx=2)]

    def four():
        landed(8, blk(zxm))
        if around:
            start(11)
        landed(9, blk(zxp))
        if around:
            start(12)
        start(14, 15)
        return [zxm, zxp]

    def five():
        landed(11, blk(zd2, up))
        start(16)
        landed(12, blk(zd2, lo))
        start(17)
        landed(14, blk(other(dx=-1, dz=1)))
        landed(15, blk(other(dx=1, dz=1)))
        return [other(dx=-1, dz=1), other(dx=1, dz=1), zd2]

    def six():
        landed(16, blk(other(dx=2, dz=1), up))
        landed(17, blk(other(dx=2, dz=1), lo))
        return [other(dx=2, dz=1)]

    return [one, own, two, third, three, third_more, fourth, four, five, six]


def run_gather(plan, own, work, hooks):
    ready = [own]
    for n, step in enumerate(plan):
        ready += step()
        for hook in hooks.get(n, ()):
            hook()
        if n > 0:
            for unused in range(min(2, len(ready))):
                work(ready.pop(0))
    for b in ready:
        work(b)


def chip_plan(p, c, base, w_ref, part):
    R, C = w_ref.shape[0], part.shape[1]
    cols = pl.ds(pl.multiple_of(p.dp * C, C), C)
    mates = [(dx, dz) for dz in range(2) for dx in range(4)][1:]

    def rows(s):
        return pl.ds(pl.multiple_of((s // 2) * R, 16), R)

    for k, (dx, dz) in enumerate(mates):
        c.add(base + k, w_ref.at[:, cols], part.at[rows(p.s)], p.dev(p.at(dx, dz)))

    def begin():
        part[rows(p.s), :] = w_ref[:, cols]
        c.start(*range(base, base + 7))

    def end():
        for k, (dx, dz) in enumerate(mates):
            c.landed(base + k, part.at[rows(p.at(-dx, dz))])

    return begin, end


def across_plan(p, nd, c, base, part, land):
    q = Across(p, nd)
    K = part.shape[0]
    plan = gather_plan(q, c, base, part, matrix_blocks(land), around=True)

    def go(*ns):
        def run():
            for n in ns:
                plan[n]()

        return run

    return go, land.at[p.dp, pl.ds(pl.multiple_of(p.c * K, 16), K)]


def save_blocks(land, all_ref, sem):
    R = land.shape[1]

    def start(b):
        pltpu.make_async_copy(land.at[b], all_ref.at[pl.ds(pl.multiple_of(b * R, 16), R)], sem.at[b]).start()

    def wait():
        for b in range(16):
            pltpu.make_async_copy(land.at[b], all_ref.at[pl.ds(b * R, R)], sem.at[b]).wait()

    return start, wait


def heads_of_blocks(land, col):
    R = land.shape[1]
    first = [land[b, 0:16, :].astype(F32)[0:1] for b in range(16)]
    before = [jnp.zeros_like(first[0])] + [land[b, R - 16 : R, :].astype(F32)[15:16] for b in range(15)]
    heads = jnp.concatenate([col[b * R : b * R + 1, :] for b in range(16)], axis=0)
    first = jnp.concatenate(first, axis=0)
    return first, jnp.concatenate(before, axis=0) * equal(heads[:, 0:1], heads[:, 1:2]) - first


def shifted(n, col):
    same = equal(col[:, 0:1], col[:, 1:2])
    rows = lax.broadcasted_iota(jnp.int32, n.shape, 0)
    before = jnp.where(rows == 0, 0.0, pltpu.roll(n, 1, 0))
    return before * same - n


def norm_parts(a):
    width = a.shape[1]
    center = a - jnp.sum(a, axis=1, keepdims=True) * (1.0 / width)
    scale = lax.rsqrt(jnp.sum(center * center, axis=1, keepdims=True) * (1.0 / width) + 1e-05)
    return center, scale, center * scale


def norm_back(normed, scale, grad):
    width = grad.shape[1]
    inner = grad - jnp.sum(grad, axis=1, keepdims=True) * (1.0 / width)
    return scale * (inner - normed * (jnp.sum(grad * normed, axis=1, keepdims=True) * (1.0 / width)))


def sigmoid(a):
    return 1.0 / (1.0 + jnp.exp(-a))


CHUNK = 128


def halves(a):
    high = a.astype(BF)
    return high, (a - high.astype(F32)).astype(BF)


def dot3(a, b, dims):
    def one(x, y):
        return lax.dot_general(x, y, (dims, ((), ())), preferred_element_type=F32)

    return one(a[0], b[0]) + (one(a[0], b[1]) + one(a[1], b[0]))


NN, NT, TN = ((1,), (0,)), ((1,), (1,)), ((0,), (0,))


def head_sums(a, ones):
    high, rest = a.astype(BF), a - a.astype(BF).astype(F32)
    mid = rest.astype(BF)
    low = (rest - mid.astype(F32)).astype(BF)

    def one(x):
        return lax.dot_general(x, ones, (NN, ((), ())), preferred_element_type=F32)

    return one(high) + (one(mid) + one(low))


def iota(shape, dim):
    return lax.broadcasted_iota(jnp.int32, shape, dim)


def head_ones(width, dtype):
    return (iota((width, width), 0) // ATTENTION_WIDTH == iota((width, width), 1) // ATTENTION_WIDTH).astype(dtype)


def by_head(pair):
    lane = iota(pair[0].shape, 1) // ATTENTION_WIDTH
    heads = pair[0].shape[1] // ATTENTION_WIDTH
    zero = jnp.zeros_like(pair[0])
    return tuple(jnp.concatenate([jnp.where(lane == h, a, zero) for h in range(heads)], axis=0) for a in pair)


def pick_heads(a, rows):
    lane = iota((rows, a.shape[1]), 1) // ATTENTION_WIDTH
    out = a[:rows]
    for h in range(1, a.shape[1] // ATTENTION_WIDTH):
        out = jnp.where(lane == h, a[h * rows : (h + 1) * rows], out)
    return out


def powers(lam, tab):
    L = tab.shape[1]
    at = iota((L, 1), 0).astype(F32)
    mid = L // 2
    tab[0] = jnp.exp(lam * (at - mid))
    tab[1] = jnp.exp(-lam * (at + (1.0 - mid)))
    tab[2] = jnp.exp(lam * at)
    tab[3] = jnp.exp(lam * (L - 1.0 - at))


def own_vectors(p, par_ref, vec):
    W = vec.shape[1]
    own = par_ref[6:10, pl.ds(pl.multiple_of(p.s * W, 128), W)]
    lam = -jnp.exp(own[0:1])
    vec[0:1, :] = lam
    vec[1:4, :] = own[1:4]
    vec[8:, :] = jnp.broadcast_to(jnp.exp(lam * CHUNK), (W, W)).T


def chunk_mask(col, row):
    L = col.shape[0]
    return (iota((L, L), 1) < iota((L, L), 0)) & (col == row)


def forward_chunk(x_ref, col_ref, row_ref, bound_ref, vec_ref, z_ref, zt_ref, o_ref, s_ref, tab, state):
    chunks, L = row_ref.shape[0], row_ref.shape[2]
    W = vec_ref.shape[1]
    heads = W // ATTENTION_WIDTH
    lam, bonus, gain, bias = (vec_ref[q : q + 1, :] for q in range(4))
    powers(lam, tab)
    ones = head_ones(W, BF)
    diag = head_ones(W, F32)
    decay = vec_ref[8 : 8 + W, :]
    state[...] = jnp.zeros_like(state)

    def step(i):
        rows = pl.ds(pl.multiple_of(i * L, L), L)
        r, k, v, p = (x_ref[rows, q * W : (q + 1) * W] for q in range(4))
        col = col_ref[rows, :]
        seg = col[:, 0:1]
        kept, tail = equal(seg, bound_ref[0, i]), equal(seg, bound_ref[0, i + 1])
        mask = chunk_mask(seg, row_ref[i])
        mask = jnp.concatenate([mask] * heads, axis=1)
        rs, ks = halves(r * tab[0]), halves(k * tab[1])
        scores = jnp.where(mask, dot3(rs, by_head(ks), NT), 0.0)
        vh = halves(v)
        out = dot3(halves(scores), by_head(vh), NN) + head_sums(r * k * bonus, ones) * v
        memory = state[...]
        s_ref[i] = memory
        out = out + kept * dot3(halves(r * tab[2]), halves(memory), NN)
        state[...] = bound_ref[1, i] * decay * memory + diag * dot3(halves(k * tab[3] * tail), vh, TN)
        o_ref[rows, :] = out
        center = out - head_sums(out, ones) * (1.0 / ATTENTION_WIDTH)
        spread = head_sums(center * center, ones) * (1.0 / ATTENTION_WIDTH)
        normed = center * lax.rsqrt(spread + 0.00064) * gain + bias
        z = (normed * (p * sigmoid(p))).astype(BF).astype(F32)
        z_ref[rows, :] = z.astype(BF)
        zt_ref[:, rows] = z.T.astype(BF)

    return step


def back_chunk(x_ref, o_ref, s_ref, gz_ref, col_ref, row_ref, bound_ref, vec_ref, g_ref, sums_ref, tab, grad_state, acc, carry, turned):
    chunks, L = row_ref.shape[0], row_ref.shape[2]
    W = vec_ref.shape[1]
    heads = W // ATTENTION_WIDTH
    lam, bonus, gain, bias = (vec_ref[q : q + 1, :] for q in range(4))
    powers(lam, tab)
    ones = head_ones(W, BF)
    diag = head_ones(W, F32)
    decay = vec_ref[8 : 8 + W, :]
    at = iota((L, 1), 0).astype(F32)
    mid = float(L // 2)
    grad_state[...] = jnp.zeros_like(grad_state)
    acc[...] = jnp.zeros_like(acc)
    carry[...] = jnp.zeros_like(carry)
    sums_ref[...] = jnp.zeros_like(sums_ref)

    def add(q, term):
        sums_ref[q : q + 1, :] += jnp.sum(term, axis=0, keepdims=True)

    def step(n):
        i = chunks - 1 - n
        rows = pl.ds(pl.multiple_of(i * L, L), L)
        r, k, v, p = (x_ref[rows, q * W : (q + 1) * W] for q in range(4))
        col = col_ref[rows, :]
        seg = col[:, 0:1]
        kept, tail = equal(seg, bound_ref[0, i]), equal(seg, bound_ref[0, i + 1])
        same_next = equal(seg, col[:, 2:3])
        o = o_ref[rows, :]
        gz = gz_ref[i].astype(F32)
        center = o - head_sums(o, ones) * (1.0 / ATTENTION_WIDTH)
        spread = head_sums(center * center, ones) * (1.0 / ATTENTION_WIDTH)
        scale = lax.rsqrt(spread + 0.00064)
        normed = center * scale
        gate = sigmoid(p)
        silu = p * gate
        gy = gz * silu
        gp = gz * (normed * gain + bias) * (gate * (1.0 + p * (1.0 - gate)))
        add(2, gy * normed)
        add(3, gy)
        gn = gy * gain
        go = scale * (
            gn
            - head_sums(gn, ones) * (1.0 / ATTENTION_WIDTH)
            - normed * (head_sums(gn * normed, ones) * (1.0 / ATTENTION_WIDTH))
        )
        mask = chunk_mask(seg, row_ref[i])
        mask = jnp.concatenate([mask] * heads, axis=1)
        rs_f, ks_f = r * tab[0], k * tab[1]
        r0_f, ke_f = r * tab[2] * kept, k * tab[3] * tail
        rs, ks, vh, goh = halves(rs_f), halves(ks_f), halves(v), halves(go)
        ks_by, v_by = by_head(ks), by_head(vh)
        scores = halves(jnp.where(mask, dot3(rs, ks_by, NT), 0.0))
        grad_scores = halves(jnp.where(mask, dot3(goh, v_by, NT), 0.0))
        memory = s_ref[i]
        gs = grad_state[...]
        mh, gsh = halves(memory), halves(gs)
        reward = head_sums(r * k * bonus, ones)
        grad_reward = head_sums(go * v, ones)
        g_rs = dot3(grad_scores, ks_by, NN)
        g_r0 = dot3(goh, mh, NT)
        g_ks = pick_heads(dot3(grad_scores, rs, TN), L)
        g_ke = dot3(vh, gsh, NT)
        gv = pick_heads(dot3(scores, goh, TN), L) + reward * go + dot3(halves(ke_f), gsh, NN)
        keep = bound_ref[1, i]
        acc[...] += keep * memory * gs
        grad_state[...] = keep * decay * gs + diag * dot3(halves(r0_f), goh, TN)
        gr = g_rs * tab[0] + g_r0 * (tab[2] * kept) + grad_reward * bonus * k
        gk = g_ks * tab[1] + g_ke * (tab[3] * tail) + grad_reward * bonus * r
        add(1, grad_reward * r * k)
        add(0, (at - mid) * (g_rs * rs_f) - (at + (1.0 - mid)) * (g_ks * ks_f) + at * (g_r0 * r0_f) + (L - 1.0 - at) * (g_ke * ke_f))
        grads = jnp.concatenate([gr, gk, gv, gp], axis=1).astype(BF).astype(F32)
        last = iota((L, 1), 0) == L - 1
        after = jnp.where(last, carry[0:1, :], pltpu.roll(grads, L - 1, 0)) * same_next
        carry[0:1, :] = grads[0:1, :]
        g_ref[rows, : 4 * W] = grads.astype(BF)
        g_ref[rows, 4 * W :] = after.astype(BF)
        turned[0 : 4 * W, rows] = grads.T.astype(BF)
        turned[4 * W :, rows] = after.T.astype(BF)

    return step


def back_finish(vec_ref, sums_ref, acc, L):
    W = vec_ref.shape[1]
    whole = dot3(halves(jnp.ones((8, W), F32)), halves(acc[...] * vec_ref[8 : 8 + W, :]), NT)
    sums_ref[0:1, :] = (sums_ref[0:1, :] + L * whole[0:1, :]) * vec_ref[0:1, :]


def time_forward_kernel(nd, x_ref, par_ref, row_ref, bound_ref, w_far, ow_far, rw_far, col_far,
                        all_ref, proj_far, zt_far, o_far, s_far, hid_ref, n2_ref, rp_ref, far_ref,
                        n1, land, op, lw, tab, state, zin, w_ref, ow_ref, rw_ref, rt_ref, col_ref, proj_ref, z_ref, zt_ref,
                        o_ref, s_ref, vec, cs, cr, ss, rs, ls, ms):
    p = Place()
    c = Copies(cs, cr)
    moves = Moves(ms)
    ow_in, w_in, col_in, rw_in = (
        moves.start(a, b) for a, b in ((ow_far, ow_ref), (w_far, w_ref), (col_far, col_ref), (rw_far, rw_ref))
    )
    R = x_ref.shape[0]
    Q, W = w_ref.shape[0], w_ref.shape[2]
    C = lw.shape[2]
    begin, end = chip_plan(p, c, 18, ow_ref, op)
    go, own_part = across_plan(p, nd, c, 25, op, lw)
    recept_begin, recept_end = chip_plan(p, c, 43, rt_ref, rp_ref)
    plan = gather_plan(p, c, 0, n1, blocks_of(land))
    start, wait = save_blocks(land, all_ref, ls)
    n1[...] = (norm_parts(x_ref[...].astype(F32))[2] * par_ref[0:1, :] + par_ref[1:2, :]).astype(BF)
    meet(chip_mates(p) + [p.dev(p.at(dc=1))] + beside(p, nd))

    def ready():
        begin()
        land[p.s] = n1[...]
        own_vectors(p, par_ref, vec)
        w_in.wait()
        col_in.wait()

    def turn():
        rw_in.wait()
        for k in range(0, rw_ref.shape[0], 256):
            rt_ref[:, k : k + 256] = rw_ref[k : k + 256, :].T

    def across():
        own_part[...] = op[...]
        go(0)()

    def work(b):
        start(b)
        rows = pl.ds(pl.multiple_of(b * R, 16), R)
        n = land[b].astype(F32)
        shift = shifted(n, col_ref[rows, :])
        for q in range(Q):
            m = (n + shift * par_ref[2 + q : 3 + q, :]).astype(BF)
            proj_ref[rows, q * W : (q + 1) * W] = jnp.dot(m, w_ref[q], preferred_element_type=F32)

    ow_in.wait()
    run_gather(plan, p.s, work, {0: [ready], 1: [turn], 3: [end, across], 8: [go(1, 2)]})
    recept_begin()
    first, shift = heads_of_blocks(land, col_ref)
    for q in range(Q):
        m = (first + shift * par_ref[2 + q : 3 + q, :]).astype(BF)
        out = jnp.dot(m, w_ref[q], preferred_element_type=F32)
        for b in range(16):
            proj_ref[b * R : b * R + 1, q * W : (q + 1) * W] = out[b : b + 1]
    saves = [moves.start(proj_ref, proj_far)]

    chunk = forward_chunk(proj_ref, col_ref, row_ref, bound_ref, vec, z_ref, zt_ref, o_ref, s_ref, tab, state)
    swap = Swap(p, lambda i: z_ref.at[pl.ds(pl.multiple_of(i * R, 16), R)], zin, ss, rs)
    when = {3: go(3, 4), 6: go(5, 6, 7)}

    def step(n, unused):
        chunk(2 * n)
        chunk(2 * n + 1)
        swap.give(2 * n)
        swap.give(2 * n + 1)
        for at, act in when.items():
            pl.when(n == at)(act)
        return 0

    lax.fori_loop(0, row_ref.shape[0] // 2, step, 0)
    saves += [moves.start(a, b) for a, b in ((zt_ref, zt_far), (o_ref, o_far), (s_ref, s_far))]
    go(8, 9)()
    saves.append(moves.start(lw, far_ref))
    swap.all(swap.take)
    z_here = jnp.concatenate([zin[2 * k + core] for core in range(2) for k in range(8)], axis=1)
    for d in range(8):
        cols = slice(d * C, (d + 1) * C)
        hid_ref[:, cols] = x_ref[:, cols].astype(F32) + jnp.dot(z_here, lw[d], preferred_element_type=F32)
    n2_ref[...] = (norm_parts(hid_ref[...])[2] * par_ref[10:11, :] + par_ref[11:12, :]).astype(BF)
    recept_end()
    wait()
    for cp in saves:
        cp.wait()
    swap.all(swap.sent)
    c.finish()


def time_forward(nd, x, par, rows, bounds, w, ow, rw, cols, cid):
    R, C = x.shape
    T, W = 16 * R, w.shape[2]
    chunks, L = rows.shape[0], rows.shape[2]
    return pl.pallas_call(
        functools.partial(time_forward_kernel, nd),
        out_shape=(
            jax.ShapeDtypeStruct((T, C), BF),
            jax.ShapeDtypeStruct((T, 4 * W), F32),
            jax.ShapeDtypeStruct((W, T), BF),
            jax.ShapeDtypeStruct((T, W), F32),
            jax.ShapeDtypeStruct((chunks, W, W), F32),
            jax.ShapeDtypeStruct((R, C), F32),
            jax.ShapeDtypeStruct((R, C), BF),
            jax.ShapeDtypeStruct((8 * R, C // nd), BF),
            jax.ShapeDtypeStruct((8, 16 * R, C // 8), BF),
        ),
        in_specs=[WHOLE] * 3 + [pl.BlockSpec(memory_space=pltpu.SMEM)] + [FAR] * 4,
        out_specs=(FAR,) * 5 + (WHOLE,) * 3 + (FAR,),
        scratch_shapes=[
            VMEM((R, C), BF), VMEM((16, R, C), BF), VMEM((8 * R, C // nd), BF), VMEM((8, 16 * R, C // 8), BF), VMEM((4, L, W), F32),
            VMEM((W, W), F32), VMEM((16, R, W), BF), VMEM(w.shape, BF), VMEM((R, C), BF), VMEM((C, W), BF), VMEM((W, C), BF),
            VMEM(cols.shape, F32), VMEM((T, 4 * W), F32), VMEM((T, W), BF), VMEM((W, T), BF), VMEM((T, W), F32),
            VMEM((chunks, W, W), F32), VMEM((8 + W, W), F32),
            DMA((50,)), DMA((50,)), DMA((16,)), DMA((16,)), DMA((16,)), DMA((9,)),
        ],
        compiler_params=params(cid, 56),
        name="time_forward",
    )(x, par, rows, bounds, w, ow, rw, cols)


def key_kernel(nd, a_ref, rp_ref, par_ref, k_far, col_far, vw_far, mw_far,
               all_ref, in_ref, lift_far, sq_far, rin_ref, sh_ref, vt_far, mt_far, fold_far, far_ref,
               land, mixed, k_ref, w_ref, col_ref, vw_ref, mw_ref, lift_ref, sq_ref, vt_ref, mt_ref, fold_ref,
               cs, cr, ls, ms, ks):
    p = Place()
    c = Copies(cs, cr)
    moves = Moves(ms)
    col_in, k_in, mw_in, vw_in = (
        moves.start(a, b) for a, b in ((col_far, col_ref), (k_far, k_ref), (mw_far, mw_ref), (vw_far, vw_ref))
    )
    R = a_ref.shape[0]
    go, own_part = across_plan(p, nd, c, 18, rp_ref, far_ref)
    saves = [moves.start(rp_ref, own_part)]
    plan = gather_plan(p, c, 0, a_ref, blocks_of(land))
    start, wait = save_blocks(land, all_ref, ls)
    meet(near(p) + beside(p, nd))
    nu_k, nu_r = par_ref[12:13, :], par_ref[13:14, :]
    Q, W = mw_ref.shape[0], mw_ref.shape[2]

    def ready():
        go(0)()
        land[p.s] = a_ref[...]
        k_in.wait()
        for k in range(0, w_ref.shape[0], 256):
            w_ref[k : k + 256, :] = k_ref[:, k : k + 256].T
        col_in.wait()

    def turn():
        vw_in.wait()
        for k in range(0, w_ref.shape[0], 256):
            vt_ref[k : k + 256, :] = vw_ref[:, k : k + 256].T
        saves.append(moves.start(vt_ref, vt_far))

    def fold(*qs):
        def run():
            if qs[0] == 0:
                mw_in.wait()
            for q in qs:
                for k in range(0, mw_ref.shape[1], 256):
                    cols, rows = slice(k, k + 256), slice(q * W, (q + 1) * W)
                    turned = mw_ref[q, cols, :].T
                    mt_ref[rows, cols] = turned
                    part = turned.astype(F32)
                    mu = par_ref[2 + q : 3 + q, cols]
                    fold_ref[rows, cols] = ((1.0 - mu) * part).astype(BF)
                    fold_ref[(Q + q) * W : (Q + q + 1) * W, cols] = (mu * part).astype(BF)
            if qs[-1] == Q - 1:
                saves.append(moves.start(mt_ref, mt_far))
                saves.append(moves.start(fold_ref, fold_far))

        return run

    def tail_copy(b):
        return pltpu.make_async_copy(mixed.at[b, pl.ds(16, R - 16)], in_ref.at[b, pl.ds(16, R - 16)], ks.at[b])

    def work(b):
        start(b)
        n = land[b].astype(F32)
        rows = pl.ds(pl.multiple_of(b * R, 16), R)
        m = (n + shifted(n, col_ref[rows, :]) * nu_k).astype(BF)
        mixed[b] = m
        e = jnp.maximum(jnp.dot(m, w_ref[...], preferred_element_type=F32), 0.0)
        lift_ref[rows, :] = e
        sq_ref[rows, :] = (e * e).astype(BF)
        tail_copy(b).start()

    run_gather(
        plan, p.s, work, {0: [ready], 1: [turn], 3: [go(1, 2)], 4: [fold(0, 1)], 5: [go(3, 4)], 6: [fold(2, 3)], 7: [go(5, 6, 7)]}
    )
    first, shift = heads_of_blocks(land, col_ref)
    head = first + shift * nu_k
    e = jnp.maximum(jnp.dot(head.astype(BF), w_ref[...], preferred_element_type=F32), 0.0)
    sq = e * e
    top = lax.broadcasted_iota(jnp.int32, (16, 1), 0) == 0
    for b in range(16):
        rows = slice(b * R, b * R + 16)
        mixed[b, 0:16, :] = jnp.where(top, head[b : b + 1], mixed[b, 0:16, :].astype(F32)).astype(BF)
        lift_ref[b * R : b * R + 1, :] = e[b : b + 1]
        sq_ref[rows, :] = jnp.where(top, sq[b : b + 1], sq_ref[rows, :].astype(F32)).astype(BF)
    saves.append(moves.start(lift_ref, lift_far))
    saves.append(moves.start(sq_ref, sq_far))
    saves.append(moves.start(mixed.at[:, pl.ds(0, 16)], in_ref.at[:, pl.ds(0, 16)]))
    n = a_ref[...].astype(F32)
    mine = lax.broadcasted_iota(jnp.int32, (16, 1), 0) == p.s
    own_first = jnp.sum(jnp.where(mine, shift, 0.0), axis=0, keepdims=True)
    here = pl.ds(pl.multiple_of(p.s * R, 16), R)
    topmost = lax.broadcasted_iota(jnp.int32, (R, 1), 0) == 0
    moved = jnp.where(topmost, own_first, shifted(n, col_ref[here, :]))
    sh_ref[...] = moved
    rin_ref[...] = (n + moved * nu_r).astype(BF)
    go(8, 9)()
    for b in range(16):
        tail_copy(b).wait()
    wait()
    for cp in saves:
        cp.wait()
    c.finish()


def key_side(nd, a, part, par, kt, cols, vw, mw, cid):
    R, C = a.shape
    T, units = 16 * R, kt.shape[0]
    Q, W = mw.shape[0], mw.shape[2]
    return pl.pallas_call(
        functools.partial(key_kernel, nd),
        out_shape=(
            jax.ShapeDtypeStruct((T, C), BF),
            jax.ShapeDtypeStruct((16, R, C), BF),
            jax.ShapeDtypeStruct((T, units), F32),
            jax.ShapeDtypeStruct((T, units), BF),
            jax.ShapeDtypeStruct((R, C), BF),
            jax.ShapeDtypeStruct((R, C), F32),
            jax.ShapeDtypeStruct((C, units), BF),
            jax.ShapeDtypeStruct((Q * W, C), BF),
            jax.ShapeDtypeStruct((2 * Q * W, C), BF),
            jax.ShapeDtypeStruct((8, T, C // 8), BF),
        ),
        in_specs=[WHOLE] * 3 + [FAR] * 4,
        out_specs=(FAR,) * 4 + (WHOLE,) * 2 + (FAR,) * 4,
        scratch_shapes=[
            VMEM((16, R, C), BF), VMEM((16, R, C), BF), VMEM((units, C), BF), VMEM((C, units), BF), VMEM(cols.shape, F32),
            VMEM((units, C), BF), VMEM(mw.shape, BF), VMEM((T, units), F32), VMEM((T, units), BF), VMEM((C, units), BF),
            VMEM((Q * W, C), BF), VMEM((2 * Q * W, C), BF),
            DMA((36,)), DMA((36,)), DMA((16,)), DMA((12,)), DMA((16,)),
        ],
        compiler_params=params(cid, 60),
        name="key_side",
    )(a, part, par, kt, cols, vw, mw)


def column_tiles(refs, tile, sem):
    C = tile.shape[2]

    def copy(u, ref):
        if len(ref.shape) == 3:
            return pltpu.make_async_copy(ref.at[u % 8], tile.at[u % 2], sem.at[u % 2])
        return pltpu.make_async_copy(ref.at[:, pl.ds(pl.multiple_of((u % 8) * C, C), C)], tile.at[u % 2], sem.at[u % 2])

    def start(u, kind):
        copy(u, refs[kind]).start()

    def wait(u, kind):
        copy(u, refs[kind]).wait()

    return start, wait


def sum_scratch(R, C):
    return [
        VMEM((8, 2, R, C), BF), VMEM((8, R, C), BF), VMEM((R, C), BF), VMEM((2, R, C), BF), VMEM((R, C), BF),
        VMEM((2, R // 2, C), BF), VMEM((2, R, C), BF),
    ]


def sum_plan(p, c, base, l_ref, w_ref, o_ref, scratch):
    pa, cb, zt, xs, zf, hv, xf = scratch
    R = o_ref.shape[0]
    H = R // 2
    core, xp, xm, zz = (p.dev(i) for i in (p.at(dc=1), p.at(dx=1), p.at(dx=-1), p.at(dz=1)))
    upper, lower = pl.ds(0, H), pl.ds(H, H)
    order = [(2, 1), (-1, 1), (1, 1), (2, 0), (0, 1), (1, 0), (-1, 0), (0, 0)]

    def send(k, src, dst, to):
        c.add(base + k, src, dst, to)
        c.start(base + k)

    def landed(k, ref):
        c.landed(base + k, ref)

    def term(i, dc):
        b = p.at(order[i][0], order[i][1], dc)
        rows = l_ref[pl.ds(pl.multiple_of(b * R, 16), R), :]
        return jnp.dot(rows, w_ref[...], preferred_element_type=F32)

    def give(i):
        pa[i, 0] = term(i, 1).astype(BF)
        send(i, pa.at[i, 0], cb.at[i], core)

    def pair(i):
        mine = term(i, 0).astype(BF).astype(F32)
        landed(i, cb.at[i])
        pa[i, 1] = (mine + cb[i].astype(F32)).astype(BF)

    def one():
        give(0)
        give(1)
        pair(0)
        send(8, pa.at[0, 1], zt, zz)
        give(2)
        pair(1)
        send(9, pa.at[1, 1], xs.at[1], xm)
        give(3)
        pair(2)
        send(10, pa.at[2, 1], xs.at[0], xp)
        give(4)
        give(5)
        pair(3)
        give(6)
        pair(4)
        pair(5)
        send(11, pa.at[5, 1, lower], xf.at[0, lower], xp)
        give(7)
        pair(6)
        send(12, pa.at[6, 1, upper], xf.at[1, upper], xm)
        pair(7)

    def two():
        landed(8, zt)
        pa[3, 1] = (pa[3, 1].astype(F32) + zt[...].astype(F32)).astype(BF)
        send(13, pa.at[3, 1, upper], hv.at[0], xp)
        send(14, pa.at[3, 1, lower], hv.at[1], xm)

    def three():
        landed(9, xs.at[1])
        landed(10, xs.at[0])
        pa[4, 1] = (pa[4, 1].astype(F32) + xs[0].astype(F32) + xs[1].astype(F32)).astype(BF)
        send(15, pa.at[4, 1], zf, zz)

    def four():
        landed(13, hv.at[0])
        pa[5, 1, upper] = (pa[5, 1, upper].astype(F32) + hv[0].astype(F32)).astype(BF)
        send(16, pa.at[5, 1, upper], xf.at[0, upper], xp)
        landed(14, hv.at[1])
        pa[6, 1, lower] = (pa[6, 1, lower].astype(F32) + hv[1].astype(F32)).astype(BF)
        send(17, pa.at[6, 1, lower], xf.at[1, lower], xm)

    def five():
        landed(11, xf.at[0, lower])
        landed(12, xf.at[1, upper])
        landed(15, zf)
        o_ref[...] = pa[7, 1].astype(F32) + zf[...].astype(F32)

    def six():
        landed(16, xf.at[0, upper])
        landed(17, xf.at[1, lower])
        o_ref[...] = o_ref[...] + xf[0].astype(F32) + xf[1].astype(F32)

    return [one, two, three, four, five, six]


def value_kernel(rin_ref, g_ref, hid_ref, l_far, w_far, vt_far, lift_far, far_ref,
                 res_ref, gf_ref, rc_ref, ge_far, get_far, vg_far, *rest):
    scratch = rest[:7]
    (o_ref, f_ref, gate_ref, gkv, land, tile, l_ref, w_ref, vt_ref, lift_ref, ge_ref, get_ref, st_ref, acc,
     cs, cr, ss, rs, ts, ms) = rest[7:]
    p = Place()
    c = Copies(cs, cr)
    moves = Moves(ms)
    R = o_ref.shape[0]
    T, U = l_ref.shape
    W = gf_ref.shape[2]
    C = tile.shape[2]
    fetch, have = column_tiles((far_ref,), tile, ts)
    fetch(0, 0)
    l_in, w_in, vt_in, lift_in = (
        moves.start(a, b) for a, b in ((l_far, l_ref), (w_far, w_ref), (vt_far, vt_ref), (lift_far, lift_ref))
    )
    sums = sum_plan(p, c, 0, l_ref, w_ref, o_ref, scratch)
    plan = gather_plan(p, c, 18, gkv, blocks_of(land))
    swap = Swap(p, lambda i: gf_ref.at[i], rc_ref, ss, rs)
    meet(near(p))

    def unit(d, unused):
        pl.when(d < 7)(lambda: fetch(d + 1, 0))
        have(d, 0)
        cols = pl.ds(pl.multiple_of(d * C, C), C)
        part = lax.dot_general(rin_ref[:, cols], tile[d % 2], (NT, ((), ())), preferred_element_type=F32)

        @pl.when(d == 0)
        def _():
            f_ref[...] = part

        @pl.when(d > 0)
        def _():
            f_ref[...] += part

        return 0

    lax.fori_loop(0, 8, unit, 0)
    for s in range(16):
        at = ((s % 2) * 8 + s // 2) * W
        cols = slice(s * W, (s + 1) * W)
        gate = sigmoid(f_ref[:, at : at + W])
        gate_ref[:, cols] = gate
        gkv[:, cols] = (g_ref[:, cols].astype(F32) * gate).astype(BF)
    plan[0]()
    l_in.wait()
    w_in.wait()
    sums[0]()
    land[p.s] = gkv[...]
    acc[...] = jnp.zeros_like(acc)
    for r in range(0, T, 256):
        st_ref[:, r : r + 256] = l_ref[r : r + 256, :].T
    vt_in.wait()
    lift_in.wait()

    def work(*blocks):
        for b in blocks:
            rows = pl.ds(pl.multiple_of(b * R, 16), R)
            cols = pl.ds(pl.multiple_of(b * R, 128), R)
            gs = jnp.dot(land[b], vt_ref[...], preferred_element_type=F32)
            ge = gs * 2.0 * lift_ref[rows, :]
            ge_ref[rows, :] = ge.astype(BF)
            get_ref[:, cols] = ge.T.astype(BF)
            acc[...] += jnp.dot(st_ref[:, cols], land[b], preferred_element_type=F32)

    sums[1]()
    sums[2]()
    ready = [p.s] + plan[1]()
    work(ready.pop(0))
    sums[3]()
    ready += plan[2]()
    work(ready.pop(0))
    ready += plan[3]()
    work(ready.pop(0))
    sums[4]()
    ready += plan[4]()
    work(ready.pop(0))
    sums[5]()
    kv, gate = o_ref[...], gate_ref[...]
    gf = g_ref[...].astype(F32) * kv * (gate * (1.0 - gate))
    for s in range(16):
        gf_ref[s] = gf[:, s * W : (s + 1) * W].astype(BF)
    swap.all(swap.give)
    res_ref[...] = (hid_ref[...] + (gate * kv).astype(BF).astype(F32)).astype(BF)
    for n in range(5, 10):
        ready += plan[n]()
        work(*ready[:2])
        ready = ready[2:]
    work(*ready)
    saves = [moves.start(ge_ref, ge_far), moves.start(get_ref, get_far)]
    for d in range(8):
        rows = slice((d % 4) * U, (d % 4 + 1) * U)
        tile[d // 4, rows, :] = acc[:, d * C : (d + 1) * C].astype(BF)
        saves.append(moves.start(tile.at[d // 4, pl.ds((d % 4) * U, U)], vg_far.at[d]))
    swap.all(swap.take)
    for cp in saves:
        cp.wait()
    swap.all(swap.sent)
    c.finish()


def value_side(rin, g, hidden, l, w, vt, lift, far, cid):
    R, C = hidden.shape
    T, U = l.shape
    W = C // 16
    return pl.pallas_call(
        value_kernel,
        out_shape=(
            jax.ShapeDtypeStruct((R, C), BF),
            jax.ShapeDtypeStruct((16, R, W), BF),
            jax.ShapeDtypeStruct((16, R, W), BF),
            jax.ShapeDtypeStruct((T, U), BF),
            jax.ShapeDtypeStruct((U, T), BF),
            jax.ShapeDtypeStruct((8, U, C // 8), BF),
        ),
        in_specs=[WHOLE] * 3 + [FAR] * 5,
        out_specs=(WHOLE,) * 3 + (FAR,) * 3,
        scratch_shapes=sum_scratch(R, C)
        + [VMEM((R, C), F32), VMEM((R, C), F32), VMEM((R, C), F32), VMEM((R, C), BF), VMEM((16, R, C), BF), VMEM((2, T, C // 8), BF)]
        + [VMEM((T, U), BF), VMEM((U, C), BF), VMEM((C, U), BF), VMEM((T, U), F32)]
        + [VMEM((T, U), BF), VMEM((U, T), BF), VMEM((U, T), BF), VMEM((U, C), F32)]
        + [DMA((36,)), DMA((36,)), DMA((16,)), DMA((16,)), DMA((2,)), DMA((14,))],
        compiler_params=params(cid, 62),
        name="value_side",
    )(rin, g, hidden, l, w, vt, lift, far)


def dp_scratch(J, C):
    return [VMEM((2, 2, J // 2, C), BF), VMEM((2, 2, J // 2, C), BF), VMEM((2, 2, J, C), BF), VMEM((2, J, C), BF)]


def dp_plan(p, nd, c, base, g_ref, o_ref, scratch):
    hv, stage, xf, zb = scratch
    J = g_ref.shape[1]
    H = J // 2
    up, lo = pl.ds(0, H), pl.ds(H, H)
    ny = nd // 2
    y, zl = p.dp // 2, p.dp % 2
    yp, ym, yo = (y + 1) % ny, (y + ny - 1) % ny, (y + 2) % ny

    def pay(at, rows):
        return g_ref.at[pl.ds(2 * at, 2), rows]

    to_p, to_m, to_z = (2 * yp + zl, p.s), (2 * ym + zl, p.s), (2 * y + 1 - zl, p.s)
    c.add(base, pay(yo, up), hv.at[0], to_p)
    c.add(base + 1, pay(yo, lo), hv.at[1], to_m)
    c.add(base + 2, pay(yp, lo), xf.at[0, :, lo], to_p)
    c.add(base + 3, pay(ym, up), xf.at[1, :, up], to_m)
    c.add(base + 4, stage.at[0], xf.at[0, :, up], to_p)
    c.add(base + 5, stage.at[1], xf.at[1, :, lo], to_m)
    c.add(base + 6, zb.at[0], zb.at[1], to_z)

    def one():
        c.start(base, base + 1, base + 2, base + 3)

    def two():
        c.landed(base, hv.at[0])
        stage[0] = (g_ref[pl.ds(2 * yp, 2), up].astype(F32) + hv[0].astype(F32)).astype(BF)
        c.start(base + 4)
        c.landed(base + 1, hv.at[1])
        stage[1] = (g_ref[pl.ds(2 * ym, 2), lo].astype(F32) + hv[1].astype(F32)).astype(BF)
        c.start(base + 5)

    def total(which):
        return g_ref[2 * y + which].astype(F32) + xf[0, which].astype(F32) + xf[1, which].astype(F32)

    def three():
        c.landed(base + 2, xf.at[0, :, lo])
        c.landed(base + 3, xf.at[1, :, up])
        c.landed(base + 4, xf.at[0, :, up])
        c.landed(base + 5, xf.at[1, :, lo])
        zb[0] = total(1 - zl).astype(BF)
        c.start(base + 6)
        o_ref[0] = total(zl)

    def four():
        c.landed(base + 6, zb.at[1])
        o_ref[0] += zb[1].astype(F32)

    return [one, two, three, four]


def no_sums(g_ref, o_ref):
    def copy():
        o_ref[...] = g_ref[...].astype(F32)

    return [lambda: None] * 3 + [copy]


def key_back_kernel(rc_ref, gf_ref, par_ref, g_ref, l_far, w_far, lt_far, col_far, hid_far, sh_far, vg_far,
                    in_hbm, n2_hbm, far_ref, out_far, gh_ref, ghb_ref, rows_ref, gg_far, gz_ref, *rest):
    scratch = rest[:7]
    (o_ref, rt, gfp, ga_ref, gzp, halo, tile, strip, l_ref, w_ref, lt_ref, col_ref, hid_ref, sh_ref, gg_ref,
     cs, cr, ss, rs, ts, os, ms) = rest[7:]
    p = Place()
    c = Copies(cs, cr)
    moves = Moves(ms)
    T, U = l_ref.shape
    R, width = o_ref.shape
    W = rc_ref.shape[2]
    C = tile.shape[2]
    l_in, w_in, lt_in, col_in, hid_in, sh_in, vg_in = (
        moves.start(a, b)
        for a, b in (
            (l_far, l_ref), (w_far, w_ref), (lt_far, lt_ref), (col_far, col_ref), (hid_far, hid_ref), (sh_far, sh_ref),
            (vg_far, gg_ref.at[:, pl.ds(0, U)]),
        )
    )
    fetch, have = column_tiles((in_hbm, n2_hbm, far_ref), tile, ts)
    fetch(0, 0)

    def strip_copy(n):
        return pltpu.make_async_copy(out_far.at[:, pl.ds(pl.multiple_of(n * 2 * W, 16), 2 * W)], strip.at[n % 2], os.at[n % 2])

    c.add(18, halo.at[0], halo.at[1], p.dev((p.s + 15) % 16))
    sums = sum_plan(p, c, 0, l_ref, w_ref, o_ref, scratch)
    swap = Swap(p, lambda i: gzp.at[i], gz_ref, ss, rs)
    meet(near(p) + [p.dev((p.s + 1) % 16), p.dev((p.s + 15) % 16)])
    nu_k, nu_r = par_ref[12:13, :], par_ref[13:14, :]

    def turn():
        last = lax.broadcasted_iota(jnp.int32, (R, 1), 0) == R - 1
        for b in range(16):
            part = rc_ref[b].astype(F32)
            after = rc_ref[b + 1, 0:16, :].astype(F32)[0:1] if b < 15 else jnp.zeros((1, W), F32)
            col = col_ref[b * R : (b + 1) * R, :]
            moved = jnp.where(last, after, pltpu.roll(part, R - 1, 0)) * equal(col[:, 0:1], col[:, 2:3])
            rt[0:W, b * R : (b + 1) * R] = part.T.astype(BF)
            rt[W:, b * R : (b + 1) * R] = moved.T.astype(BF)
        for s in range(16):
            at = ((s % 2) * 8 + s // 2) * W
            gfp[:, at : at + W] = gf_ref[s]

    def units(kind, lo, hi):
        def unit(d, unused):
            u = 8 * kind + d
            if hi < 8:
                fetch(u + 1, kind)
            else:
                pl.when(d < 7)(lambda: fetch(u + 1, kind))
                if kind < 2:
                    pl.when(d == 7)(lambda: fetch(u + 1, kind + 1))
            have(u, kind)
            rhs = tile[d % 2]
            cols = pl.ds(pl.multiple_of(d * C, C), C)
            if kind == 0:
                gg_ref[d, U : 2 * U, :] = jnp.dot(lt_ref[...], rhs, preferred_element_type=F32).astype(BF)
            elif kind == 1:
                out = jnp.dot(rt[...], rhs, preferred_element_type=F32)
                gg_ref[d, 2 * U :, :] = (out[:W] + par_ref[13:14, cols] * (out[W:] - out[:W])).astype(BF)
            else:
                ga_ref[:, cols] = jnp.dot(gfp[...], rhs, preferred_element_type=F32)
            return 0

        lax.fori_loop(lo, hi, unit, 0)

    l_in.wait()
    w_in.wait()
    sums[0]()
    lt_in.wait()
    units(0, 0, 4)
    sums[1]()
    sums[2]()
    units(0, 4, 8)
    sums[3]()
    col_in.wait()
    turn()
    units(1, 0, 8)
    vg_in.wait()
    saves = [moves.start(gg_ref, gg_far)]
    sums[4]()
    units(2, 0, 8)
    strip_copy(0).start()
    hid_in.wait()
    sh_in.wait()
    unused, scale, normed = norm_parts(hid_ref[...])
    sums[5]()
    ga_k, ga_r, shift = o_ref[...], ga_ref[...], sh_ref[...]
    here = pl.ds(pl.multiple_of(p.s * R, 16), R)
    col = col_ref[here, :]
    moved = (ga_k * nu_k + ga_r * nu_r) * equal(col[:, 0:1], col[:, 1:2])
    halo[0] = moved[0:8]
    c.start(18)
    held = ga_k - ga_k * nu_k + (ga_r - ga_r * nu_r)
    rows_ref[...] = jnp.zeros_like(rows_ref)
    rows_ref[2:3, :] = jnp.sum(ga_k * shift, axis=0, keepdims=True)
    rows_ref[3:4, :] = jnp.sum(ga_r * shift, axis=0, keepdims=True)
    c.landed(18, halo.at[1])
    last = lax.broadcasted_iota(jnp.int32, (R, 1), 0) == R - 1
    grad = held + jnp.where(last, halo[1, 0:1, :], pltpu.roll(moved, R - 1, 0))
    gh = g_ref[...].astype(F32) + norm_back(normed, scale, grad * par_ref[10:11, :])
    gh_ref[...] = gh
    ghb_ref[...] = gh.astype(BF)

    def back_out(n, unused):
        pl.when(n < 7)(lambda: strip_copy(n + 1).start())
        strip_copy(n).wait()
        part = lax.dot_general(ghb_ref[:, 0:C], strip[n % 2, 0], (NT, ((), ())), preferred_element_type=F32)
        for d in range(1, 8):
            part = part + lax.dot_general(
                ghb_ref[:, d * C : (d + 1) * C], strip[n % 2, d], (NT, ((), ())), preferred_element_type=F32
            )
        for k in range(2):
            to = 2 * ((2 * n + k) % 8) + (2 * n + k) // 8
            gzp[to] = part[:, k * W : (k + 1) * W].astype(BF)
            swap.give(to)
        return 0

    lax.fori_loop(0, 8, back_out, 0)
    rows_ref[0:1, :] = jnp.sum(grad * normed, axis=0, keepdims=True)
    rows_ref[1:2, :] = jnp.sum(grad, axis=0, keepdims=True)
    for cp in saves:
        cp.wait()
    swap.all(swap.take)
    swap.all(swap.sent)
    c.finish()


def key_back(rc, gf, par, g, l, w, lt, cols, hidden, sh, vg, key_in, n2_all, far, out_far, cid):
    R, C = hidden.shape
    T, U, W = 16 * R, l.shape[1], rc.shape[2]
    return pl.pallas_call(
        key_back_kernel,
        out_shape=(
            jax.ShapeDtypeStruct((R, C), F32),
            jax.ShapeDtypeStruct((R, C), BF),
            jax.ShapeDtypeStruct((8, C), F32),
            jax.ShapeDtypeStruct((8, 2 * U + W, C // 8), BF),
            jax.ShapeDtypeStruct((16, R, W), BF),
        ),
        in_specs=[WHOLE] * 4 + [FAR] * 11,
        out_specs=(WHOLE,) * 3 + (FAR, WHOLE),
        scratch_shapes=sum_scratch(R, C)
        + [VMEM((R, C), F32), VMEM((2 * W, T), BF), VMEM((R, C), BF), VMEM((R, C), F32), VMEM((16, R, W), BF), VMEM((2, 8, C), F32)]
        + [VMEM((2, T, C // 8), BF), VMEM((2, 8, 2 * W, C // 8), BF), VMEM((T, U), BF), VMEM((U, C), BF), VMEM((U, T), BF)]
        + [VMEM(cols.shape, F32), VMEM((R, C), F32), VMEM((R, C), F32), VMEM((8, 2 * U + W, C // 8), BF)]
        + [DMA((19,)), DMA((19,)), DMA((16,)), DMA((16,)), DMA((2,)), DMA((2,)), DMA((8,))],
        compiler_params=params(cid, 60),
        name="key_back",
    )(rc, gf, par, g, l, w, lt, cols, hidden, sh, vg, key_in, n2_all, far, out_far)


def time_back_kernel(nd, gh_ref, gz_ref, par_ref, row_ref, bound_ref, early_far, x_far, o_far, s_far, col_far, zt_far, mixt_far, n1_hbm,
                     g_far, gg_far, sums_ref, mug_ref, dp_ref,
                     tab, grad_state, acc, carry, land, turned, tile, vec, early_ref, x_ref, o_ref, s_ref, col_ref, zt_ref, mixt_ref,
                     g_ref, gg_ref, d0, d1, d2, d3, cs, cr, ts, ms):
    p = Place()
    c = Copies(cs, cr)
    moves = Moves(ms)
    W = vec.shape[1]
    chunks, L = row_ref.shape[0], row_ref.shape[2]
    C = tile.shape[2]
    early_in, x_in, o_in, s_in, col_in, zt_in, mixt_in = (
        moves.start(a, b)
        for a, b in (
            (early_far, early_ref), (x_far, x_ref), (o_far, o_ref), (s_far, s_ref), (col_far, col_ref), (zt_far, zt_ref),
            (mixt_far, mixt_ref),
        )
    )
    fetch, have = column_tiles((n1_hbm,), tile, ts)
    fetch(0, 0)
    blk = rows_of(land)
    plan = gather_plan(p, c, 0, gh_ref, blk)
    sums = dp_plan(p, nd, c, 18, early_ref, dp_ref, (d0, d1, d2, d3)) if nd > 1 else no_sums(early_ref, dp_ref)
    own_vectors(p, par_ref, vec)
    meet(near(p) + beside(p, nd))
    plan[0]()
    early_in.wait()
    sums[0]()
    blk(p.s)[...] = gh_ref[...]
    when = {6: [plan[1], plan[2]], 9: [sums[1]], 11: [plan[3], plan[4]], 14: [plan[5], plan[6], plan[7]]}
    for cp in (x_in, o_in, s_in, col_in):
        cp.wait()
    chunk = back_chunk(x_ref, o_ref, s_ref, gz_ref, col_ref, row_ref, bound_ref, vec, g_ref, sums_ref, tab, grad_state, acc, carry, turned)

    def step(n, unused):
        chunk(n)
        for at, parts in when.items():
            @pl.when(n == at)
            def _():
                for part in parts:
                    part()
        return 0

    lax.fori_loop(0, chunks, step, 0)
    saves = [moves.start(g_ref, g_far)]
    sums[2]()
    back_finish(vec, sums_ref, acc, L)
    mug_ref[...] = jnp.zeros_like(mug_ref)
    mixt_in.wait()

    def mix(d, unused):
        pl.when(d < 7)(lambda: fetch(d + 1, 0))
        have(d, 0)
        rhs = tile[d % 2]
        cols = pl.ds(pl.multiple_of(d * C, C), C)
        a = jnp.dot(turned[: 4 * W, :], rhs, preferred_element_type=F32)
        b = jnp.dot(turned[4 * W :, :], rhs, preferred_element_type=F32)
        for q in range(4):
            rows = slice(q * W, (q + 1) * W)
            diff = b[rows] - a[rows]
            gg_ref[d, rows, :] = (a[rows] + par_ref[2 + q : 3 + q, cols] * diff).astype(BF)
            mug_ref[q : q + 1, cols] = jnp.sum(mixt_ref[rows, cols].astype(F32) * diff, axis=0, keepdims=True)
        return 0

    lax.fori_loop(0, 4, mix, 0)
    plan[8]()
    lax.fori_loop(4, 8, mix, 0)
    sums[3]()
    zt_in.wait()
    plan[9]()

    def out(d, unused):
        cols = pl.ds(pl.multiple_of(d * C, C), C)
        gg_ref[d, 4 * W :, :] = jnp.dot(zt_ref[...], land[:, cols], preferred_element_type=F32).astype(BF)
        return 0

    lax.fori_loop(0, 8, out, 0)
    saves.append(moves.start(gg_ref, gg_far))
    for cp in saves:
        cp.wait()
    c.finish()


def time_back(nd, gh, gz, par, rows, bounds, early, x, o, states, cols, zt, mixt, n1_all, cid):
    T, W = o.shape
    L = rows.shape[2]
    R, C = gh.shape
    J = early.shape[1]
    return pl.pallas_call(
        functools.partial(time_back_kernel, nd),
        out_shape=(
            jax.ShapeDtypeStruct((T, 8 * W), BF),
            jax.ShapeDtypeStruct((8, 5 * W, C // 8), BF),
            jax.ShapeDtypeStruct((8, W), F32),
            jax.ShapeDtypeStruct((4, C), F32),
            jax.ShapeDtypeStruct((8 // nd, J, C // 8), F32),
        ),
        in_specs=[WHOLE] * 4 + [pl.BlockSpec(memory_space=pltpu.SMEM)] + [FAR] * 8,
        out_specs=(FAR,) * 2 + (WHOLE,) * 3,
        scratch_shapes=[
            VMEM((4, L, W), F32), VMEM((W, W), F32), VMEM((W, W), F32), VMEM((8, 4 * W), F32),
            VMEM((T, C), BF), VMEM((8 * W, T), BF), VMEM((2, T, C // 8), BF), VMEM((8 + W, W), F32),
            VMEM(early.shape, BF), VMEM(x.shape, F32), VMEM((T, W), F32), VMEM(states.shape, F32), VMEM(cols.shape, F32),
            VMEM((W, T), BF), VMEM(mixt.shape, BF), VMEM((T, 8 * W), BF), VMEM((8, 5 * W, C // 8), BF),
        ]
        + dp_scratch(J, C // 8)
        + [DMA((25,)), DMA((25,)), DMA((2,)), DMA((9,))],
        compiler_params=params(cid, 60),
        name="time_back",
    )(gh, gz, par, rows, bounds, early, x, o, states, cols, zt, mixt, n1_all)


def last_kernel(nd, x_ref, par_ref, mug_ref, head_ref, norm_ref, gg_far, l_far, w_far, gh_far, ig_ref, dp_ref, v_ref, *rest):
    scratch = rest[:7]
    o_ref, d0, d1, d2, d3, tv, b1, t1, b2, gg_ref, l_ref, w_ref, gh_ref, cs, cr, ms = rest[7:]
    p = Place()
    c = Copies(cs, cr)
    moves = Moves(ms)
    l_in, w_in, gg_in, gh_in = (
        moves.start(a, b) for a, b in ((l_far, l_ref), (w_far, w_ref), (gg_far, gg_ref), (gh_far, gh_ref))
    )
    sums = dp_plan(p, nd, c, 18, gg_ref, dp_ref, (d0, d1, d2, d3)) if nd > 1 else no_sums(gg_ref, dp_ref)
    steps = sum_plan(p, c, 0, l_ref, w_ref, o_ref, scratch)
    W = head_ref.shape[1]
    tv[...] = jnp.zeros_like(tv)
    tv[2:6, :] = mug_ref[...]
    tv[6:10, pl.ds(pl.multiple_of(p.s * W, 128), W)] = head_ref[0:4, :]
    tv[10:14, :] = norm_ref[0:4, :]
    meet(near(p) + beside(p, nd))
    for cp in (l_in, w_in, gg_in):
        cp.wait()
    sums[0]()
    steps[0]()
    sums[1]()
    steps[1]()
    steps[2]()
    steps[3]()
    sums[2]()
    unused, scale, normed = norm_parts(x_ref[...].astype(F32))
    sums[3]()
    gh_in.wait()
    steps[4]()
    steps[5]()
    gn = o_ref[...]
    tv[0:1, :] = jnp.sum(gn * normed, axis=0, keepdims=True)
    tv[1:2, :] = jnp.sum(gn, axis=0, keepdims=True)
    C = b1.shape[2]
    for k in range(1, nd):
        to = (p.dp + k) % nd
        c.add(24 + k, tv.at[:, pl.ds(pl.multiple_of(to * C, 128), C)], b1.at[k - 1], (to, p.s))
        c.start(24 + k)
    ig_ref[...] = gh_ref[...] + norm_back(normed, scale, gn * par_ref[0:1, :])
    total = tv[:, pl.ds(pl.multiple_of(p.dp * C, 128), C)]
    for k in range(1, nd):
        c.landed(24 + k, b1.at[k - 1])
        total = total + b1[k - 1]
    t1[...] = total
    for k in range(1, 16):
        c.add(31 + k, t1, b2.at[k - 1], p.dev((p.s + k) % 16))
        c.start(31 + k)
    for k in range(1, 16):
        c.landed(31 + k, b2.at[k - 1])
        total = total + b2[k - 1]
    v_ref[...] = total
    c.finish()


def last_sums(nd, x, par, mug, head, norm, gg, l, w, gh, cid):
    R, C = x.shape
    J = gg.shape[1]
    piece = (16, C // nd)
    return pl.pallas_call(
        functools.partial(last_kernel, nd),
        out_shape=(jax.ShapeDtypeStruct((R, C), F32), jax.ShapeDtypeStruct((8 // nd, J, C // 8), F32), jax.ShapeDtypeStruct(piece, F32)),
        in_specs=[WHOLE] * 5 + [FAR] * 4,
        out_specs=(WHOLE,) * 3,
        scratch_shapes=sum_scratch(R, C)
        + [VMEM((R, C), F32)]
        + dp_scratch(J, C // 8)
        + [VMEM((16, C), F32), VMEM((max(nd - 1, 1),) + piece, F32), VMEM(piece, F32), VMEM((15,) + piece, F32)]
        + [VMEM(gg.shape, BF), VMEM(l.shape, BF), VMEM(w.shape, BF), VMEM((R, C), F32)]
        + [DMA((47,)), DMA((47,)), DMA((4,))],
        compiler_params=params(cid, 60),
        name="last_sums",
    )(x, par, mug, head, norm, gg, l, w, gh)


def body(nd, inputs, cotangent, mix_weights, out_weight, key_weight, value_weight, recept_weight, vectors, segment_ids):
    tokens, width = inputs.shape
    group = segment_ids.shape[0]
    cols = mix_weights.shape[2]
    units = key_weight.shape[1]
    s = lax.axis_index("sp")
    ring = group // tokens
    chunks = group // CHUNK

    edge = jnp.full((1,), -1.0, F32)
    seg = jnp.concatenate([edge, segment_ids.astype(F32), edge])
    tok_cols = jnp.stack([seg[1:-1], seg[:-2], seg[2:]], axis=1)
    tok_rows = seg[1:-1].reshape(chunks, 1, CHUNK)
    ends = seg[: group + 1 : CHUNK]
    bounds = jnp.stack([ends, jnp.concatenate([(ends[1:] == ends[:-1]).astype(F32), edge])])

    n1_all, projected, z_t, mixed_time, states, hidden, n2, recept_part, out_far = time_forward(
        nd, inputs, vectors, tok_rows, bounds, mix_weights, out_weight, recept_weight, tok_cols, 0
    )
    n2_all, key_in, lifted, squared, recept_in, shift, value_t, mixt, folded, recept_far = key_side(
        nd, n2, recept_part, vectors, key_weight.T, tok_cols, value_weight, mix_weights, 1
    )
    result, grad_recept, recept_cols, grad_key, grad_key_t, value_grad = value_side(
        recept_in, cotangent, hidden, squared, value_weight, value_t, lifted, recept_far, 2
    )
    grad_hidden, grad_hidden_b, norm_rows, early, gz = key_back(
        recept_cols, grad_recept, vectors, cotangent, grad_key, key_weight.T, grad_key_t, tok_cols, hidden, shift, value_grad,
        key_in.reshape(group, width), n2_all, recept_far, out_far, 3,
    )
    grads_two, late, head_rows, mu_rows, early_sum = time_back(
        nd, grad_hidden_b, gz, vectors, tok_rows, bounds, early, projected, mixed_time, states, tok_cols, z_t, mixt, n1_all, 4
    )
    input_grad, late_sum, vector_sum = last_sums(
        nd, inputs, vectors, mu_rows, head_rows, norm_rows, late, grads_two, folded, grad_hidden, 5
    )
    piece = width // (nd * ring)
    vectors_grad = lax.dynamic_slice_in_dim(vector_sum[:14], s * piece, piece, 1)

    def columns(part):
        return part.transpose(1, 0, 2).reshape(part.shape[1], width // nd)

    early_sum, late_sum = columns(early_sum), columns(late_sum)
    return (
        result,
        input_grad,
        late_sum[: 4 * cols].reshape(4, cols, width // nd).transpose(0, 2, 1),
        late_sum[4 * cols :],
        early_sum[units : 2 * units].T,
        early_sum[:units],
        early_sum[2 * units :].T,
        vectors_grad,
    )


def solution(mesh):
    placed = (
        P(("dp", "sp"), None),
        P(("dp", "sp"), None),
        P(None, None, "sp"),
        P("sp", None),
        P(None, "sp"),
        P("sp", None),
        P(None, "sp"),
        P(),
        P("dp"),
    )
    return jax.shard_map(
        functools.partial(body, mesh.shape["dp"]),
        mesh=mesh,
        in_specs=placed,
        out_specs=(
            P(("dp", "sp"), None),
            P(("dp", "sp"), None),
            P(None, "dp", "sp"),
            P("sp", "dp"),
            P("dp", "sp"),
            P("sp", "dp"),
            P("dp", "sp"),
            P(None, ("dp", "sp")),
        ),
        check_vma=False,
    )
```

```python
import functools

import jax
import jax.numpy as jnp
from jax import lax
from jax.experimental import pallas as pl
from jax.experimental.pallas import tpu as pltpu
from jax.sharding import PartitionSpec as P

MESH = pl.DeviceIdType.MESH
VMEM = pltpu.VMEM
DMA = pltpu.SemaphoreType.DMA
BF = jnp.bfloat16
F32 = jnp.float32

ATTENTION_WIDTH = 64
CHUNK = 128
WHOLE = pl.BlockSpec(memory_space=VMEM)
FAR = pl.BlockSpec(memory_space=pl.ANY)


class Place:
    def __init__(self):
        self.dp = lax.axis_index("dp")
        s = lax.axis_index("sp")
        self.s = s
        self.x, self.z, self.c = s // 4, (s // 2) % 2, s % 2

    def at(self, dx=0, dz=0, dc=0):
        return ((self.x + dx) % 4) * 4 + ((self.z + dz) % 2) * 2 + (self.c + dc) % 2

    def dev(self, s):
        return (self.dp, s)


class Across:
    def __init__(self, p, nd):
        self.p, self.ny = p, nd // 2
        self.x, self.z, self.c = p.dp // 2, p.dp % 2, p.c
        self.s = p.dp * 2 + p.c

    def at(self, dx=0, dz=0, dc=0):
        return ((self.x + dx) % self.ny) * 4 + ((self.z + dz) % 2) * 2 + (self.c + dc) % 2

    def dev(self, i):
        return (i // 2, self.p.s - self.p.c + i % 2)


class Copies:
    def __init__(self, ss, rs):
        self.ss, self.rs, self.items = ss, rs, {}

    def add(self, k, src, dst, to):
        self.items[k] = (src, dst, to)

    def make(self, k, src, dst, to):
        return pltpu.make_async_remote_copy(
            src_ref=src, dst_ref=dst, send_sem=self.ss.at[k], recv_sem=self.rs.at[k], device_id=to, device_id_type=MESH
        )

    def start(self, *ks):
        for k in ks:
            self.make(k, *self.items[k]).start()

    def landed(self, k, ref):
        self.make(k, ref, ref, self.items[k][2]).wait_recv()

    def finish(self):
        for k in self.items:
            self.make(k, *self.items[k]).wait_send()


def meet(devices):
    barrier = pltpu.get_barrier_semaphore()
    for device in devices:
        pl.semaphore_signal(barrier, inc=1, device_id=device, device_id_type=MESH)
    pl.semaphore_wait(barrier, len(devices))


def near(p):
    return [p.dev(p.at(dc=1)), p.dev(p.at(dx=1)), p.dev(p.at(dx=-1)), p.dev(p.at(dz=1))]


def beside(p, nd):
    y, zl, ny = p.dp // 2, p.dp % 2, nd // 2
    if nd == 1:
        return []
    return [(2 * ((y + 1) % ny) + zl, p.s), (2 * ((y + ny - 1) % ny) + zl, p.s), (2 * y + 1 - zl, p.s)]


def chip_mates(p):
    return [p.dev(p.at(dx, dz)) for dz in range(2) for dx in range(4)][1:]


def ring_mates(p):
    return [p.dev((p.s + k) % 16) for k in range(1, 16)]


def dp_mates(p, nd):
    return [((p.dp + k) % nd, p.s) for k in range(1, nd)]


def params(cid, mib):
    return pltpu.CompilerParams(collective_id=cid, has_side_effects=True, vmem_limit_bytes=mib * 2**20)


class Swap:
    def __init__(self, p, src, dst, ss, rs):
        self.p, self.src, self.dst, self.ss, self.rs = p, src, dst, ss, rs

    def make(self, src, dst, at, to):
        return pltpu.make_async_remote_copy(
            src_ref=src, dst_ref=dst, send_sem=self.ss.at[to], recv_sem=self.rs.at[at], device_id=self.p.dev(to), device_id_type=MESH
        )

    def give(self, i):
        @pl.when(i != self.p.s)
        def _():
            self.make(self.src(i), self.dst.at[self.p.s], self.p.s, i).start()

        @pl.when(i == self.p.s)
        def _():
            self.dst[self.p.s] = self.src(i)[...]

    def take(self, i):
        @pl.when(i != self.p.s)
        def _():
            self.make(self.dst.at[i], self.dst.at[i], i, i).wait_recv()

    def sent(self, i):
        @pl.when(i != self.p.s)
        def _():
            self.make(self.src(i), self.dst.at[self.p.s], self.p.s, i).wait_send()

    def all(self, act):
        def step(i, unused):
            act(i)
            return 0

        lax.fori_loop(0, 16, step, 0)


class Moves:
    def __init__(self, sem):
        self.sem, self.n = sem, 0

    def start(self, src, dst):
        cp = pltpu.make_async_copy(src, dst, self.sem.at[self.n])
        self.n += 1
        cp.start()
        return cp


def equal(a, b):
    return jnp.where(a == b, 1.0, 0.0)


def blocks_of(land):
    R = land.shape[1] // 2

    def blk(i, half=None):
        rows = R if half is None else R // 2
        return land.at[i // 2, pl.ds(pl.multiple_of((i % 2) * R + (half or 0) * rows, 16), rows)]

    return blk


def rows_of(land):
    R = land.shape[0] // 16

    def blk(i, half=None):
        rows = R if half is None else R // 2
        return land.at[pl.ds(pl.multiple_of(i * R + (half or 0) * rows, 16), rows)]

    return blk


def matrix_blocks(land):
    K = land.shape[1] // 2

    def blk(i, half=None):
        rows = K if half is None else K // 2
        return land.at[i // 2, pl.ds(pl.multiple_of((i % 2) * K + (half or 0) * rows, 16), rows)]

    return blk


def gather_plan(p, c, base, a_ref, blk, around=False):
    core, xp, xm, zz = p.at(dc=1), p.at(dx=1), p.at(dx=-1), p.at(dz=1)
    d2, zxm, zxp, zd2 = p.at(dx=2), p.at(dx=-1, dz=1), p.at(dx=1, dz=1), p.at(dx=2, dz=1)
    up, lo = 0, 1

    def relay(k, ref, to):
        c.add(base + k, ref, ref, p.dev(to))

    for k, to in enumerate((xp, xm, zz, core)):
        c.add(base + k, a_ref, blk(p.s), p.dev(to))
    relay(4, blk(xm, up), xp)
    relay(5, blk(xp, lo), xm)
    relay(6, blk(xm), core)
    relay(7, blk(xp), core)
    relay(8, blk(zz), xp)
    relay(9, blk(zz), xm)
    relay(10, blk(zz), core)
    if around:
        relay(11, blk(zxm, up), xp)
        relay(12, blk(zxp, lo), xm)
    else:
        relay(11, blk(d2, up), zz)
        relay(12, blk(d2, lo), zz)
    relay(13, blk(d2), core)
    relay(14, blk(zxm), core)
    relay(15, blk(zxp), core)
    relay(16, blk(zd2, up), core)
    relay(17, blk(zd2, lo), core)

    def start(*ks):
        c.start(*(base + k for k in ks))

    def landed(k, ref):
        c.landed(base + k, ref)

    def other(**k):
        return p.at(dc=1, **k)

    def one():
        start(0, 1, 2, 3)
        return []

    def own():
        landed(3, blk(core))
        return [core // 2]

    def two():
        landed(0, blk(xm))
        start(4)
        landed(1, blk(xp))
        start(5, 6, 7)
        landed(2, blk(zz))
        start(8, 9, 10)
        return []

    def third():
        landed(6, blk(other(dx=-1)))
        return [xm // 2]

    def three():
        landed(4, blk(d2, up))
        if not around:
            start(11)
        landed(5, blk(d2, lo))
        if not around:
            start(12)
        start(13)
        return []

    def third_more():
        landed(7, blk(other(dx=1)))
        landed(10, blk(other(dz=1)))
        return [xp // 2, zz // 2]

    def fourth():
        landed(13, blk(other(dx=2)))
        return [d2 // 2]

    def four():
        landed(8, blk(zxm))
        if around:
            start(11)
        landed(9, blk(zxp))
        if around:
            start(12)
        start(14, 15)
        return []

    def five():
        landed(11, blk(zd2, up))
        start(16)
        landed(12, blk(zd2, lo))
        start(17)
        landed(14, blk(other(dx=-1, dz=1)))
        landed(15, blk(other(dx=1, dz=1)))
        return [zxm // 2, zxp // 2]

    def six():
        landed(16, blk(other(dx=2, dz=1), up))
        landed(17, blk(other(dx=2, dz=1), lo))
        return [zd2 // 2]

    return [one, own, two, third, three, third_more, fourth, four, five, six]


def run_gather(plan, work, hooks):
    ready = []
    for n, step in enumerate(plan):
        ready += step()
        for hook in hooks.get(n, ()):
            hook()
        if ready:
            work(ready.pop(0))
    for chip in ready:
        work(chip)


def chip_plan(p, c, base, w_ref, part):
    R, C = w_ref.shape[0], part.shape[1]
    cols = pl.ds(pl.multiple_of(p.dp * C, C), C)
    mates = [(dx, dz) for dz in range(2) for dx in range(4)][1:]

    def rows(s):
        return pl.ds(pl.multiple_of((s // 2) * R, 16), R)

    for k, (dx, dz) in enumerate(mates):
        c.add(base + k, w_ref.at[:, cols], part.at[rows(p.s)], p.dev(p.at(dx, dz)))

    def begin():
        part[rows(p.s), :] = w_ref[:, cols]
        c.start(*range(base, base + 7))

    def end():
        for k, (dx, dz) in enumerate(mates):
            c.landed(base + k, part.at[rows(p.at(-dx, dz))])

    return begin, end


def across_plan(p, nd, c, base, part, land):
    q = Across(p, nd)
    K = part.shape[0]
    plan = gather_plan(q, c, base, part, matrix_blocks(land), around=True)

    def go(*ns):
        def run():
            for n in ns:
                plan[n]()

        return run

    return go, land.at[p.dp, pl.ds(pl.multiple_of(p.c * K, 16), K)]


def save_blocks(land, all_ref, sem):
    R = land.shape[1]

    def copy(k):
        return pltpu.make_async_copy(land.at[k], all_ref.at[pl.ds(pl.multiple_of(k * R, 16), R)], sem.at[k])

    def wait():
        for k in range(8):
            copy(k).wait()

    return lambda k: copy(k).start(), wait


def heads_of_blocks(land, col):
    R = land.shape[1] // 2

    def row(b, at):
        at += (b % 2) * R
        return land[b // 2, at // 16 * 16 : at // 16 * 16 + 16, :].astype(F32)[at % 16 : at % 16 + 1]

    first = jnp.concatenate([row(b, 0) for b in range(16)], axis=0)
    before = jnp.concatenate([jnp.zeros_like(first[0:1])] + [row(b, R - 1) for b in range(15)], axis=0)
    heads = jnp.concatenate([col[b * R : b * R + 1, :] for b in range(16)], axis=0)
    return first, before * equal(heads[:, 0:1], heads[:, 1:2]) - first


def shifted(n, col):
    same = equal(col[:, 0:1], col[:, 1:2])
    rows = lax.broadcasted_iota(jnp.int32, n.shape, 0)
    before = jnp.where(rows == 0, 0.0, pltpu.roll(n, 1, 0))
    return before * same - n


def norm_parts(a):
    width = a.shape[1]
    center = a - jnp.sum(a, axis=1, keepdims=True) * (1.0 / width)
    scale = lax.rsqrt(jnp.sum(center * center, axis=1, keepdims=True) * (1.0 / width) + 1e-05)
    return center, scale, center * scale


def norm_back(normed, scale, grad):
    width = grad.shape[1]
    inner = grad - jnp.sum(grad, axis=1, keepdims=True) * (1.0 / width)
    return scale * (inner - normed * (jnp.sum(grad * normed, axis=1, keepdims=True) * (1.0 / width)))


def sigmoid(a):
    return 1.0 / (1.0 + jnp.exp(-a))


CHUNK = 128


def halves(a):
    high = a.astype(BF)
    return high, (a - high.astype(F32)).astype(BF)


def dot3(a, b, dims):
    def one(x, y):
        return lax.dot_general(x, y, (dims, ((), ())), preferred_element_type=F32)

    return one(a[0], b[0]) + (one(a[0], b[1]) + one(a[1], b[0]))


NN, NT, TN = ((1,), (0,)), ((1,), (1,)), ((0,), (0,))


def head_sums(a, ones):
    high, rest = a.astype(BF), a - a.astype(BF).astype(F32)
    mid = rest.astype(BF)
    low = (rest - mid.astype(F32)).astype(BF)

    def one(x):
        return lax.dot_general(x, ones, (NN, ((), ())), preferred_element_type=F32)

    return one(high) + (one(mid) + one(low))


def iota(shape, dim):
    return lax.broadcasted_iota(jnp.int32, shape, dim)


def head_ones(width, dtype):
    return (iota((width, width), 0) // ATTENTION_WIDTH == iota((width, width), 1) // ATTENTION_WIDTH).astype(dtype)


def by_head(pair):
    lane = iota(pair[0].shape, 1) // ATTENTION_WIDTH
    heads = pair[0].shape[1] // ATTENTION_WIDTH
    zero = jnp.zeros_like(pair[0])
    return tuple(jnp.concatenate([jnp.where(lane == h, a, zero) for h in range(heads)], axis=0) for a in pair)


def pick_heads(a, rows):
    lane = iota((rows, a.shape[1]), 1) // ATTENTION_WIDTH
    out = a[:rows]
    for h in range(1, a.shape[1] // ATTENTION_WIDTH):
        out = jnp.where(lane == h, a[h * rows : (h + 1) * rows], out)
    return out


def powers(lam, tab):
    L = tab.shape[1]
    at = iota((L, 1), 0).astype(F32)
    mid = L // 2
    tab[0] = jnp.exp(lam * (at - mid))
    tab[1] = jnp.exp(-lam * (at + (1.0 - mid)))
    tab[2] = jnp.exp(lam * at)
    tab[3] = jnp.exp(lam * (L - 1.0 - at))


def own_vectors(p, par_ref, vec):
    W = vec.shape[1]
    own = par_ref[6:10, pl.ds(pl.multiple_of(p.s * W, 128), W)]
    lam = -jnp.exp(own[0:1])
    vec[0:1, :] = lam
    vec[1:4, :] = own[1:4]
    vec[8:, :] = jnp.broadcast_to(jnp.exp(lam * CHUNK), (W, W)).T


def chunk_mask(col, row):
    L = col.shape[0]
    return (iota((L, L), 1) < iota((L, L), 0)) & (col == row)


def forward_chunk(x_ref, col_ref, row_ref, bound_ref, vec_ref, z_ref, zt_ref, o_ref, s_ref, tab, state):
    chunks, L = row_ref.shape[0], row_ref.shape[2]
    W = vec_ref.shape[1]
    heads = W // ATTENTION_WIDTH
    lam, bonus, gain, bias = (vec_ref[q : q + 1, :] for q in range(4))
    powers(lam, tab)
    ones = head_ones(W, BF)
    diag = head_ones(W, F32)
    decay = vec_ref[8 : 8 + W, :]
    state[...] = jnp.zeros_like(state)

    def step(i):
        rows = pl.ds(pl.multiple_of(i * L, L), L)
        r, k, v, p = (x_ref[rows, q * W : (q + 1) * W] for q in range(4))
        col = col_ref[rows, :]
        seg = col[:, 0:1]
        kept, tail = equal(seg, bound_ref[0, i]), equal(seg, bound_ref[0, i + 1])
        mask = chunk_mask(seg, row_ref[i])
        mask = jnp.concatenate([mask] * heads, axis=1)
        rs, ks = halves(r * tab[0]), halves(k * tab[1])
        scores = jnp.where(mask, dot3(rs, by_head(ks), NT), 0.0)
        vh = halves(v)
        out = dot3(halves(scores), by_head(vh), NN) + head_sums(r * k * bonus, ones) * v
        memory = state[...]
        s_ref[i] = memory
        out = out + kept * dot3(halves(r * tab[2]), halves(memory), NN)
        state[...] = bound_ref[1, i] * decay * memory + diag * dot3(halves(k * tab[3] * tail), vh, TN)
        o_ref[rows, :] = out
        center = out - head_sums(out, ones) * (1.0 / ATTENTION_WIDTH)
        spread = head_sums(center * center, ones) * (1.0 / ATTENTION_WIDTH)
        normed = center * lax.rsqrt(spread + 0.00064) * gain + bias
        z = (normed * (p * sigmoid(p))).astype(BF).astype(F32)
        z_ref[rows, :] = z.astype(BF)
        zt_ref[:, rows] = z.T.astype(BF)

    return step


def back_chunk(x_ref, o_ref, s_ref, gz_ref, col_ref, row_ref, bound_ref, vec_ref, g_ref, sums_ref, tab, grad_state, acc, carry, turned):
    chunks, L = row_ref.shape[0], row_ref.shape[2]
    W = vec_ref.shape[1]
    heads = W // ATTENTION_WIDTH
    lam, bonus, gain, bias = (vec_ref[q : q + 1, :] for q in range(4))
    powers(lam, tab)
    ones = head_ones(W, BF)
    diag = head_ones(W, F32)
    decay = vec_ref[8 : 8 + W, :]
    at = iota((L, 1), 0).astype(F32)
    mid = float(L // 2)
    grad_state[...] = jnp.zeros_like(grad_state)
    acc[...] = jnp.zeros_like(acc)
    carry[...] = jnp.zeros_like(carry)
    sums_ref[...] = jnp.zeros_like(sums_ref)

    def add(q, term):
        sums_ref[q : q + 1, :] += jnp.sum(term, axis=0, keepdims=True)

    def step(n):
        i = chunks - 1 - n
        rows = pl.ds(pl.multiple_of(i * L, L), L)
        r, k, v, p = (x_ref[rows, q * W : (q + 1) * W] for q in range(4))
        col = col_ref[rows, :]
        seg = col[:, 0:1]
        kept, tail = equal(seg, bound_ref[0, i]), equal(seg, bound_ref[0, i + 1])
        same_next = equal(seg, col[:, 2:3])
        o = o_ref[rows, :]
        gz = gz_ref[i].astype(F32)
        center = o - head_sums(o, ones) * (1.0 / ATTENTION_WIDTH)
        spread = head_sums(center * center, ones) * (1.0 / ATTENTION_WIDTH)
        scale = lax.rsqrt(spread + 0.00064)
        normed = center * scale
        gate = sigmoid(p)
        silu = p * gate
        gy = gz * silu
        gp = gz * (normed * gain + bias) * (gate * (1.0 + p * (1.0 - gate)))
        add(2, gy * normed)
        add(3, gy)
        gn = gy * gain
        go = scale * (
            gn
            - head_sums(gn, ones) * (1.0 / ATTENTION_WIDTH)
            - normed * (head_sums(gn * normed, ones) * (1.0 / ATTENTION_WIDTH))
        )
        mask = chunk_mask(seg, row_ref[i])
        mask = jnp.concatenate([mask] * heads, axis=1)
        rs_f, ks_f = r * tab[0], k * tab[1]
        r0_f, ke_f = r * tab[2] * kept, k * tab[3] * tail
        rs, ks, vh, goh = halves(rs_f), halves(ks_f), halves(v), halves(go)
        ks_by, v_by = by_head(ks), by_head(vh)
        scores = halves(jnp.where(mask, dot3(rs, ks_by, NT), 0.0))
        grad_scores = halves(jnp.where(mask, dot3(goh, v_by, NT), 0.0))
        memory = s_ref[i]
        gs = grad_state[...]
        mh, gsh = halves(memory), halves(gs)
        reward = head_sums(r * k * bonus, ones)
        grad_reward = head_sums(go * v, ones)
        g_rs = dot3(grad_scores, ks_by, NN)
        g_r0 = dot3(goh, mh, NT)
        g_ks = pick_heads(dot3(grad_scores, rs, TN), L)
        g_ke = dot3(vh, gsh, NT)
        gv = pick_heads(dot3(scores, goh, TN), L) + reward * go + dot3(halves(ke_f), gsh, NN)
        keep = bound_ref[1, i]
        acc[...] += keep * memory * gs
        grad_state[...] = keep * decay * gs + diag * dot3(halves(r0_f), goh, TN)
        gr = g_rs * tab[0] + g_r0 * (tab[2] * kept) + grad_reward * bonus * k
        gk = g_ks * tab[1] + g_ke * (tab[3] * tail) + grad_reward * bonus * r
        add(1, grad_reward * r * k)
        add(0, (at - mid) * (g_rs * rs_f) - (at + (1.0 - mid)) * (g_ks * ks_f) + at * (g_r0 * r0_f) + (L - 1.0 - at) * (g_ke * ke_f))
        grads = jnp.concatenate([gr, gk, gv, gp], axis=1).astype(BF).astype(F32)
        last = iota((L, 1), 0) == L - 1
        after = jnp.where(last, carry[0:1, :], pltpu.roll(grads, L - 1, 0)) * same_next
        carry[0:1, :] = grads[0:1, :]
        g_ref[rows, : 4 * W] = grads.astype(BF)
        g_ref[rows, 4 * W :] = after.astype(BF)
        turned[0 : 4 * W, rows] = grads.T.astype(BF)
        turned[4 * W :, rows] = after.T.astype(BF)

    return step


def back_finish(vec_ref, sums_ref, acc, L):
    W = vec_ref.shape[1]
    whole = dot3(halves(jnp.ones((8, W), F32)), halves(acc[...] * vec_ref[8 : 8 + W, :]), NT)
    sums_ref[0:1, :] = (sums_ref[0:1, :] + L * whole[0:1, :]) * vec_ref[0:1, :]


def time_forward_kernel(nd, x_ref, par_ref, row_ref, bound_ref, w_far, ow_far, rw_far, col_far,
                        all_ref, proj_far, zt_far, o_far, s_far, hid_ref, n2_ref, rp_ref, far_ref,
                        n1, land, op, lw, tab, state, zin, w_ref, ow_ref, rw_ref, rt_ref, col_ref, proj_ref, z_ref, zt_ref,
                        o_ref, s_ref, vec, cs, cr, ss, rs, ls, ms):
    p = Place()
    c = Copies(cs, cr)
    moves = Moves(ms)
    ow_in, w_in, col_in, rw_in = (
        moves.start(a, b) for a, b in ((ow_far, ow_ref), (w_far, w_ref), (col_far, col_ref), (rw_far, rw_ref))
    )
    R = x_ref.shape[0]
    Q, W = w_ref.shape[0], w_ref.shape[2]
    C = lw.shape[2]
    begin, end = chip_plan(p, c, 18, ow_ref, op)
    go, own_part = across_plan(p, nd, c, 25, op, lw)
    recept_begin, recept_end = chip_plan(p, c, 43, rt_ref, rp_ref)
    blk = blocks_of(land)
    plan = gather_plan(p, c, 0, n1, blk)
    start, wait = save_blocks(land, all_ref, ls)
    n1[...] = (norm_parts(x_ref[...].astype(F32))[2] * par_ref[0:1, :] + par_ref[1:2, :]).astype(BF)
    meet(chip_mates(p) + [p.dev(p.at(dc=1))] + beside(p, nd))

    def ready():
        begin()
        blk(p.s)[...] = n1[...]
        own_vectors(p, par_ref, vec)
        w_in.wait()
        col_in.wait()

    def turn():
        rw_in.wait()
        for k in range(0, rw_ref.shape[0], 256):
            rt_ref[:, k : k + 256] = rw_ref[k : k + 256, :].T

    def across():
        own_part[...] = op[...]
        go(0)()

    def work(k):
        start(k)
        rows = pl.ds(pl.multiple_of(k * 2 * R, 16), 2 * R)
        n = land[k].astype(F32)
        shift = shifted(n, col_ref[rows, :])
        for q in range(Q):
            m = (n + shift * par_ref[2 + q : 3 + q, :]).astype(BF)
            proj_ref[rows, q * W : (q + 1) * W] = jnp.dot(m, w_ref[q], preferred_element_type=F32)

    ow_in.wait()
    run_gather(plan, work, {0: [ready], 1: [turn], 3: [end, across], 8: [go(1, 2)]})
    recept_begin()
    first, shift = heads_of_blocks(land, col_ref)
    for q in range(Q):
        m = (first + shift * par_ref[2 + q : 3 + q, :]).astype(BF)
        out = jnp.dot(m, w_ref[q], preferred_element_type=F32)
        for b in range(0, 16, 2):
            proj_ref[b * R : b * R + 1, q * W : (q + 1) * W] = out[b : b + 1]
    saves = [moves.start(proj_ref, proj_far)]

    chunk = forward_chunk(proj_ref, col_ref, row_ref, bound_ref, vec, z_ref, zt_ref, o_ref, s_ref, tab, state)
    swap = Swap(p, lambda i: z_ref.at[pl.ds(pl.multiple_of(i * R, 16), R)], zin, ss, rs)
    when = {3: go(3, 4), 6: go(5, 6, 7)}

    def step(n, unused):
        chunk(2 * n)
        chunk(2 * n + 1)
        swap.give(2 * n)
        swap.give(2 * n + 1)
        for at, act in when.items():
            pl.when(n == at)(act)
        return 0

    lax.fori_loop(0, row_ref.shape[0] // 2, step, 0)
    saves += [moves.start(a, b) for a, b in ((zt_ref, zt_far), (o_ref, o_far), (s_ref, s_far))]
    go(8, 9)()
    saves.append(moves.start(lw, far_ref))
    swap.all(swap.take)
    z_here = jnp.concatenate([zin[2 * k + core] for core in range(2) for k in range(8)], axis=1)
    for d in range(8):
        cols = slice(d * C, (d + 1) * C)
        hid_ref[:, cols] = x_ref[:, cols].astype(F32) + jnp.dot(z_here, lw[d], preferred_element_type=F32)
    n2_ref[...] = (norm_parts(hid_ref[...])[2] * par_ref[10:11, :] + par_ref[11:12, :]).astype(BF)
    recept_end()
    wait()
    for cp in saves:
        cp.wait()
    swap.all(swap.sent)
    c.finish()


def time_forward(nd, x, par, rows, bounds, w, ow, rw, cols, cid):
    R, C = x.shape
    T, W = 16 * R, w.shape[2]
    chunks, L = rows.shape[0], rows.shape[2]
    return pl.pallas_call(
        functools.partial(time_forward_kernel, nd),
        out_shape=(
            jax.ShapeDtypeStruct((T, C), BF),
            jax.ShapeDtypeStruct((T, 4 * W), F32),
            jax.ShapeDtypeStruct((W, T), BF),
            jax.ShapeDtypeStruct((T, W), F32),
            jax.ShapeDtypeStruct((chunks, W, W), F32),
            jax.ShapeDtypeStruct((R, C), F32),
            jax.ShapeDtypeStruct((R, C), BF),
            jax.ShapeDtypeStruct((8 * R, C // nd), BF),
            jax.ShapeDtypeStruct((8, 16 * R, C // 8), BF),
        ),
        in_specs=[WHOLE] * 3 + [pl.BlockSpec(memory_space=pltpu.SMEM)] + [FAR] * 4,
        out_specs=(FAR,) * 5 + (WHOLE,) * 3 + (FAR,),
        scratch_shapes=[
            VMEM((R, C), BF), VMEM((8, 2 * R, C), BF), VMEM((8 * R, C // nd), BF), VMEM((8, 16 * R, C // 8), BF), VMEM((4, L, W), F32),
            VMEM((W, W), F32), VMEM((16, R, W), BF), VMEM(w.shape, BF), VMEM((R, C), BF), VMEM((C, W), BF), VMEM((W, C), BF),
            VMEM(cols.shape, F32), VMEM((T, 4 * W), F32), VMEM((T, W), BF), VMEM((W, T), BF), VMEM((T, W), F32),
            VMEM((chunks, W, W), F32), VMEM((8 + W, W), F32),
            DMA((50,)), DMA((50,)), DMA((16,)), DMA((16,)), DMA((16,)), DMA((9,)),
        ],
        compiler_params=params(cid, 56),
        name="time_forward",
    )(x, par, rows, bounds, w, ow, rw, cols)


def key_kernel(nd, a_ref, rp_ref, par_ref, k_far, col_far, vw_far, mw_far,
               all_ref, in_ref, lift_far, sq_far, rin_ref, sh_ref, vt_far, mt_far, fold_far, far_ref,
               land, mixed, k_ref, w_ref, col_ref, vw_ref, mw_ref, lift_ref, sq_ref, vt_ref, mt_ref, fold_ref,
               cs, cr, ls, ms, ks):
    p = Place()
    c = Copies(cs, cr)
    moves = Moves(ms)
    col_in, k_in, mw_in, vw_in = (
        moves.start(a, b) for a, b in ((col_far, col_ref), (k_far, k_ref), (mw_far, mw_ref), (vw_far, vw_ref))
    )
    R = a_ref.shape[0]
    go, own_part = across_plan(p, nd, c, 18, rp_ref, far_ref)
    saves = [moves.start(rp_ref, own_part)]
    blk = blocks_of(land)
    plan = gather_plan(p, c, 0, a_ref, blk)
    start, wait = save_blocks(land, all_ref, ls)
    meet(near(p) + beside(p, nd))
    nu_k, nu_r = par_ref[12:13, :], par_ref[13:14, :]
    Q, W = mw_ref.shape[0], mw_ref.shape[2]

    def ready():
        go(0)()
        blk(p.s)[...] = a_ref[...]
        k_in.wait()
        for k in range(0, w_ref.shape[0], 256):
            w_ref[k : k + 256, :] = k_ref[:, k : k + 256].T
        col_in.wait()

    def turn():
        vw_in.wait()
        for k in range(0, w_ref.shape[0], 256):
            vt_ref[k : k + 256, :] = vw_ref[:, k : k + 256].T
        saves.append(moves.start(vt_ref, vt_far))

    def fold(*qs):
        def run():
            if qs[0] == 0:
                mw_in.wait()
            for q in qs:
                for k in range(0, mw_ref.shape[1], 256):
                    cols, rows = slice(k, k + 256), slice(q * W, (q + 1) * W)
                    turned = mw_ref[q, cols, :].T
                    mt_ref[rows, cols] = turned
                    part = turned.astype(F32)
                    mu = par_ref[2 + q : 3 + q, cols]
                    fold_ref[rows, cols] = ((1.0 - mu) * part).astype(BF)
                    fold_ref[(Q + q) * W : (Q + q + 1) * W, cols] = (mu * part).astype(BF)
            if qs[-1] == Q - 1:
                saves.append(moves.start(mt_ref, mt_far))
                saves.append(moves.start(fold_ref, fold_far))

        return run

    def tail_copy(k):
        rows = pl.ds(16, 2 * R - 16)
        return pltpu.make_async_copy(mixed.at[k, rows], in_ref.at[k, rows], ks.at[k])

    def work(k):
        start(k)
        n = land[k].astype(F32)
        rows = pl.ds(pl.multiple_of(k * 2 * R, 16), 2 * R)
        m = (n + shifted(n, col_ref[rows, :]) * nu_k).astype(BF)
        mixed[k] = m
        e = jnp.maximum(jnp.dot(m, w_ref[...], preferred_element_type=F32), 0.0)
        lift_ref[rows, :] = e
        sq_ref[rows, :] = (e * e).astype(BF)
        tail_copy(k).start()

    run_gather(plan, work, {0: [ready], 1: [turn], 3: [go(1, 2)], 4: [fold(0, 1)], 5: [go(3, 4)], 6: [fold(2, 3)], 7: [go(5, 6, 7)]})
    first, shift = heads_of_blocks(land, col_ref)
    head = first + shift * nu_k
    e = jnp.maximum(jnp.dot(head.astype(BF), w_ref[...], preferred_element_type=F32), 0.0)
    sq = e * e
    top = lax.broadcasted_iota(jnp.int32, (16, 1), 0) == 0
    for b in range(0, 16, 2):
        rows = slice(b * R, b * R + 16)
        mixed[b // 2, 0:16, :] = jnp.where(top, head[b : b + 1], mixed[b // 2, 0:16, :].astype(F32)).astype(BF)
        lift_ref[b * R : b * R + 1, :] = e[b : b + 1]
        sq_ref[rows, :] = jnp.where(top, sq[b : b + 1], sq_ref[rows, :].astype(F32)).astype(BF)
    saves.append(moves.start(lift_ref, lift_far))
    saves.append(moves.start(sq_ref, sq_far))
    saves.append(moves.start(mixed.at[:, pl.ds(0, 16)], in_ref.at[:, pl.ds(0, 16)]))
    n = a_ref[...].astype(F32)
    mine = lax.broadcasted_iota(jnp.int32, (16, 1), 0) == p.s
    own_first = jnp.sum(jnp.where(mine, shift, 0.0), axis=0, keepdims=True)
    here = pl.ds(pl.multiple_of(p.s * R, 16), R)
    topmost = lax.broadcasted_iota(jnp.int32, (R, 1), 0) == 0
    moved = jnp.where(topmost, own_first, shifted(n, col_ref[here, :]))
    sh_ref[...] = moved
    rin_ref[...] = (n + moved * nu_r).astype(BF)
    go(8, 9)()
    for k in range(8):
        tail_copy(k).wait()
    wait()
    for cp in saves:
        cp.wait()
    c.finish()


def key_side(nd, a, part, par, kt, cols, vw, mw, cid):
    R, C = a.shape
    T, units = 16 * R, kt.shape[0]
    Q, W = mw.shape[0], mw.shape[2]
    return pl.pallas_call(
        functools.partial(key_kernel, nd),
        out_shape=(
            jax.ShapeDtypeStruct((T, C), BF),
            jax.ShapeDtypeStruct((8, 2 * R, C), BF),
            jax.ShapeDtypeStruct((T, units), F32),
            jax.ShapeDtypeStruct((T, units), BF),
            jax.ShapeDtypeStruct((R, C), BF),
            jax.ShapeDtypeStruct((R, C), F32),
            jax.ShapeDtypeStruct((C, units), BF),
            jax.ShapeDtypeStruct((Q * W, C), BF),
            jax.ShapeDtypeStruct((2 * Q * W, C), BF),
            jax.ShapeDtypeStruct((8, T, C // 8), BF),
        ),
        in_specs=[WHOLE] * 3 + [FAR] * 4,
        out_specs=(FAR,) * 4 + (WHOLE,) * 2 + (FAR,) * 4,
        scratch_shapes=[
            VMEM((8, 2 * R, C), BF), VMEM((8, 2 * R, C), BF), VMEM((units, C), BF), VMEM((C, units), BF), VMEM(cols.shape, F32),
            VMEM((units, C), BF), VMEM(mw.shape, BF), VMEM((T, units), F32), VMEM((T, units), BF), VMEM((C, units), BF),
            VMEM((Q * W, C), BF), VMEM((2 * Q * W, C), BF),
            DMA((36,)), DMA((36,)), DMA((16,)), DMA((12,)), DMA((16,)),
        ],
        compiler_params=params(cid, 60),
        name="key_side",
    )(a, part, par, kt, cols, vw, mw)


def column_tiles(refs, tile, sem):
    C = tile.shape[2]

    def copy(u, ref):
        if len(ref.shape) == 3:
            return pltpu.make_async_copy(ref.at[u % 8], tile.at[u % 2], sem.at[u % 2])
        return pltpu.make_async_copy(ref.at[:, pl.ds(pl.multiple_of((u % 8) * C, C), C)], tile.at[u % 2], sem.at[u % 2])

    def start(u, kind):
        copy(u, refs[kind]).start()

    def wait(u, kind):
        copy(u, refs[kind]).wait()

    return start, wait


def sum_scratch(R, C):
    return [
        VMEM((8, 2, R, C), BF), VMEM((8, R, C), BF), VMEM((R, C), BF), VMEM((2, R, C), BF), VMEM((R, C), BF),
        VMEM((2, R // 2, C), BF), VMEM((2, R, C), BF),
    ]


def sum_plan(p, c, base, l_ref, w_ref, o_ref, scratch):
    pa, cb, zt, xs, zf, hv, xf = scratch
    R = o_ref.shape[0]
    H = R // 2
    core, xp, xm, zz = (p.dev(i) for i in (p.at(dc=1), p.at(dx=1), p.at(dx=-1), p.at(dz=1)))
    upper, lower = pl.ds(0, H), pl.ds(H, H)
    order = [(2, 1), (-1, 1), (1, 1), (2, 0), (0, 1), (1, 0), (-1, 0), (0, 0)]

    def send(k, src, dst, to):
        c.add(base + k, src, dst, to)
        c.start(base + k)

    def landed(k, ref):
        c.landed(base + k, ref)

    def give(i):
        k = p.at(*order[i]) // 2
        rows = l_ref[pl.ds(pl.multiple_of(k * 2 * R, 16), 2 * R), :]
        pa[i] = jnp.dot(rows, w_ref[...], preferred_element_type=F32).astype(BF).reshape(2, R, -1)
        send(i, pa.at[i, 1 - p.c], cb.at[i], core)

    def pair(i):
        landed(i, cb.at[i])
        pa[i, p.c] = (pa[i, p.c].astype(F32) + cb[i].astype(F32)).astype(BF)

    def one():
        give(0)
        give(1)
        pair(0)
        send(8, pa.at[0, p.c], zt, zz)
        give(2)
        pair(1)
        send(9, pa.at[1, p.c], xs.at[1], xm)
        give(3)
        pair(2)
        send(10, pa.at[2, p.c], xs.at[0], xp)
        give(5)
        pair(3)
        give(6)
        pair(5)
        send(11, pa.at[5, p.c, lower], xf.at[0, lower], xp)
        give(4)
        pair(6)
        send(12, pa.at[6, p.c, upper], xf.at[1, upper], xm)
        give(7)
        pair(4)
        pair(7)

    def two():
        landed(8, zt)
        pa[3, p.c] = (pa[3, p.c].astype(F32) + zt[...].astype(F32)).astype(BF)
        send(13, pa.at[3, p.c, upper], hv.at[0], xp)
        send(14, pa.at[3, p.c, lower], hv.at[1], xm)

    def three():
        landed(9, xs.at[1])
        landed(10, xs.at[0])
        pa[4, p.c] = (pa[4, p.c].astype(F32) + xs[0].astype(F32) + xs[1].astype(F32)).astype(BF)
        send(15, pa.at[4, p.c], zf, zz)

    def four():
        landed(13, hv.at[0])
        pa[5, p.c, upper] = (pa[5, p.c, upper].astype(F32) + hv[0].astype(F32)).astype(BF)
        send(16, pa.at[5, p.c, upper], xf.at[0, upper], xp)
        landed(14, hv.at[1])
        pa[6, p.c, lower] = (pa[6, p.c, lower].astype(F32) + hv[1].astype(F32)).astype(BF)
        send(17, pa.at[6, p.c, lower], xf.at[1, lower], xm)

    def five():
        landed(11, xf.at[0, lower])
        landed(12, xf.at[1, upper])
        landed(15, zf)
        o_ref[...] = pa[7, p.c].astype(F32) + zf[...].astype(F32)

    def six():
        landed(16, xf.at[0, upper])
        landed(17, xf.at[1, lower])
        o_ref[...] = o_ref[...] + xf[0].astype(F32) + xf[1].astype(F32)

    return [one, two, three, four, five, six]


def value_kernel(rin_ref, g_ref, hid_ref, l_far, w_far, vt_far, lift_far, far_ref,
                 res_ref, gf_ref, rc_ref, ge_far, get_far, vg_far, *rest):
    scratch = rest[:7]
    (o_ref, f_ref, gate_ref, gkv, land, tile, l_ref, w_ref, vt_ref, lift_ref, ge_ref, get_ref, st_ref, acc,
     cs, cr, ss, rs, ts, ms) = rest[7:]
    p = Place()
    c = Copies(cs, cr)
    moves = Moves(ms)
    R = o_ref.shape[0]
    T, U = l_ref.shape
    W = gf_ref.shape[2]
    C = tile.shape[2]
    fetch, have = column_tiles((far_ref,), tile, ts)
    fetch(0, 0)
    l_in, w_in, vt_in, lift_in = (
        moves.start(a, b) for a, b in ((l_far, l_ref), (w_far, w_ref), (vt_far, vt_ref), (lift_far, lift_ref))
    )
    sums = sum_plan(p, c, 0, l_ref, w_ref, o_ref, scratch)
    blk = blocks_of(land)
    plan = gather_plan(p, c, 18, gkv, blk)
    swap = Swap(p, lambda i: gf_ref.at[i], rc_ref, ss, rs)
    meet(near(p))

    def unit(d, unused):
        pl.when(d < 7)(lambda: fetch(d + 1, 0))
        have(d, 0)
        cols = pl.ds(pl.multiple_of(d * C, C), C)
        part = lax.dot_general(rin_ref[:, cols], tile[d % 2], (NT, ((), ())), preferred_element_type=F32)

        @pl.when(d == 0)
        def _():
            f_ref[...] = part

        @pl.when(d > 0)
        def _():
            f_ref[...] += part

        return 0

    lax.fori_loop(0, 8, unit, 0)
    for s in range(16):
        at = ((s % 2) * 8 + s // 2) * W
        cols = slice(s * W, (s + 1) * W)
        gate = sigmoid(f_ref[:, at : at + W])
        gate_ref[:, cols] = gate
        gkv[:, cols] = (g_ref[:, cols].astype(F32) * gate).astype(BF)
    plan[0]()
    l_in.wait()
    w_in.wait()
    sums[0]()
    blk(p.s)[...] = gkv[...]
    acc[...] = jnp.zeros_like(acc)
    for r in range(0, T, 256):
        st_ref[:, r : r + 256] = l_ref[r : r + 256, :].T
    vt_in.wait()
    lift_in.wait()

    def work(k):
        rows = pl.ds(pl.multiple_of(k * 2 * R, 16), 2 * R)
        cols = pl.ds(pl.multiple_of(k * 2 * R, 128), 2 * R)
        gs = jnp.dot(land[k], vt_ref[...], preferred_element_type=F32)
        ge = gs * 2.0 * lift_ref[rows, :]
        ge_ref[rows, :] = ge.astype(BF)
        get_ref[:, cols] = ge.T.astype(BF)
        acc[...] += jnp.dot(st_ref[:, cols], land[k], preferred_element_type=F32)

    ready = plan[1]() + plan[2]()
    work(ready.pop(0))
    sums[1]()
    sums[2]()
    ready += plan[3]() + plan[4]()
    work(ready.pop(0))
    sums[3]()
    ready += plan[5]()
    work(ready.pop(0))
    sums[4]()
    ready += plan[6]()
    work(ready.pop(0))
    sums[5]()
    kv, gate = o_ref[...], gate_ref[...]
    gf = g_ref[...].astype(F32) * kv * (gate * (1.0 - gate))
    for s in range(16):
        gf_ref[s] = gf[:, s * W : (s + 1) * W].astype(BF)
    swap.all(swap.give)
    res_ref[...] = (hid_ref[...] + (gate * kv).astype(BF).astype(F32)).astype(BF)
    for n in range(7, 10):
        ready += plan[n]()
        work(ready.pop(0))
    for k in ready:
        work(k)
    saves = [moves.start(ge_ref, ge_far), moves.start(get_ref, get_far)]
    for d in range(8):
        rows = slice((d % 4) * U, (d % 4 + 1) * U)
        tile[d // 4, rows, :] = acc[:, d * C : (d + 1) * C].astype(BF)
        saves.append(moves.start(tile.at[d // 4, pl.ds((d % 4) * U, U)], vg_far.at[d]))
    swap.all(swap.take)
    for cp in saves:
        cp.wait()
    swap.all(swap.sent)
    c.finish()


def value_side(rin, g, hidden, l, w, vt, lift, far, cid):
    R, C = hidden.shape
    T, U = l.shape
    W = C // 16
    return pl.pallas_call(
        value_kernel,
        out_shape=(
            jax.ShapeDtypeStruct((R, C), BF),
            jax.ShapeDtypeStruct((16, R, W), BF),
            jax.ShapeDtypeStruct((16, R, W), BF),
            jax.ShapeDtypeStruct((T, U), BF),
            jax.ShapeDtypeStruct((U, T), BF),
            jax.ShapeDtypeStruct((8, U, C // 8), BF),
        ),
        in_specs=[WHOLE] * 3 + [FAR] * 5,
        out_specs=(WHOLE,) * 3 + (FAR,) * 3,
        scratch_shapes=sum_scratch(R, C)
        + [VMEM((R, C), F32), VMEM((R, C), F32), VMEM((R, C), F32), VMEM((R, C), BF), VMEM((8, 2 * R, C), BF), VMEM((2, T, C // 8), BF)]
        + [VMEM((T, U), BF), VMEM((U, C), BF), VMEM((C, U), BF), VMEM((T, U), F32)]
        + [VMEM((T, U), BF), VMEM((U, T), BF), VMEM((U, T), BF), VMEM((U, C), F32)]
        + [DMA((36,)), DMA((36,)), DMA((16,)), DMA((16,)), DMA((2,)), DMA((14,))],
        compiler_params=params(cid, 62),
        name="value_side",
    )(rin, g, hidden, l, w, vt, lift, far)


def dp_scratch(J, C):
    return [VMEM((2, 2, J // 2, C), BF), VMEM((2, 2, J // 2, C), BF), VMEM((2, 2, J, C), BF), VMEM((2, J, C), BF)]


def dp_plan(p, nd, c, base, g_ref, o_ref, scratch):
    hv, stage, xf, zb = scratch
    J = g_ref.shape[1]
    H = J // 2
    up, lo = pl.ds(0, H), pl.ds(H, H)
    ny = nd // 2
    y, zl = p.dp // 2, p.dp % 2
    yp, ym, yo = (y + 1) % ny, (y + ny - 1) % ny, (y + 2) % ny

    def pay(at, rows):
        return g_ref.at[pl.ds(2 * at, 2), rows]

    to_p, to_m, to_z = (2 * yp + zl, p.s), (2 * ym + zl, p.s), (2 * y + 1 - zl, p.s)
    c.add(base, pay(yo, up), hv.at[0], to_p)
    c.add(base + 1, pay(yo, lo), hv.at[1], to_m)
    c.add(base + 2, pay(yp, lo), xf.at[0, :, lo], to_p)
    c.add(base + 3, pay(ym, up), xf.at[1, :, up], to_m)
    c.add(base + 4, stage.at[0], xf.at[0, :, up], to_p)
    c.add(base + 5, stage.at[1], xf.at[1, :, lo], to_m)
    c.add(base + 6, zb.at[0], zb.at[1], to_z)

    def one():
        c.start(base, base + 1)

    def two():
        c.landed(base, hv.at[0])
        stage[0] = (g_ref[pl.ds(2 * yp, 2), up].astype(F32) + hv[0].astype(F32)).astype(BF)
        c.start(base + 4)
        c.landed(base + 1, hv.at[1])
        stage[1] = (g_ref[pl.ds(2 * ym, 2), lo].astype(F32) + hv[1].astype(F32)).astype(BF)
        c.start(base + 5, base + 2, base + 3)

    def total(which):
        return g_ref[2 * y + which].astype(F32) + xf[0, which].astype(F32) + xf[1, which].astype(F32)

    def three():
        c.landed(base + 2, xf.at[0, :, lo])
        c.landed(base + 3, xf.at[1, :, up])
        c.landed(base + 4, xf.at[0, :, up])
        c.landed(base + 5, xf.at[1, :, lo])
        zb[0] = total(1 - zl).astype(BF)
        c.start(base + 6)
        o_ref[0] = total(zl)

    def four():
        c.landed(base + 6, zb.at[1])
        o_ref[0] += zb[1].astype(F32)

    return [one, two, three, four]


def no_sums(g_ref, o_ref):
    def copy():
        o_ref[...] = g_ref[...].astype(F32)

    return [lambda: None] * 3 + [copy]


def key_back_kernel(rc_ref, gf_ref, par_ref, g_ref, l_far, w_far, lt_far, col_far, hid_far, sh_far, vg_far,
                    in_hbm, n2_hbm, far_ref, out_far, gh_ref, ghb_ref, rows_ref, gg_far, gz_ref, *rest):
    scratch = rest[:7]
    (o_ref, rt, gfp, ga_ref, gzp, halo, tile, strip, l_ref, w_ref, lt_ref, col_ref, hid_ref, sh_ref, gg_ref,
     cs, cr, ss, rs, ts, os, ms) = rest[7:]
    p = Place()
    c = Copies(cs, cr)
    moves = Moves(ms)
    T, U = l_ref.shape
    R, width = o_ref.shape
    W = rc_ref.shape[2]
    C = tile.shape[2]
    l_in, w_in, lt_in, col_in, hid_in, sh_in, vg_in = (
        moves.start(a, b)
        for a, b in (
            (l_far, l_ref), (w_far, w_ref), (lt_far, lt_ref), (col_far, col_ref), (hid_far, hid_ref), (sh_far, sh_ref),
            (vg_far, gg_ref.at[:, pl.ds(0, U)]),
        )
    )
    fetch, have = column_tiles((in_hbm, n2_hbm, far_ref), tile, ts)
    fetch(0, 0)

    def strip_copy(n):
        return pltpu.make_async_copy(out_far.at[:, pl.ds(pl.multiple_of(n * 2 * W, 16), 2 * W)], strip.at[n % 2], os.at[n % 2])

    c.add(18, halo.at[0], halo.at[1], p.dev((p.s + 15) % 16))
    sums = sum_plan(p, c, 0, l_ref, w_ref, o_ref, scratch)
    swap = Swap(p, lambda i: gzp.at[i], gz_ref, ss, rs)
    meet(near(p) + [p.dev((p.s + 1) % 16), p.dev((p.s + 15) % 16)])
    nu_k, nu_r = par_ref[12:13, :], par_ref[13:14, :]

    def turn():
        last = lax.broadcasted_iota(jnp.int32, (R, 1), 0) == R - 1
        for b in range(16):
            part = rc_ref[b].astype(F32)
            after = rc_ref[b + 1, 0:16, :].astype(F32)[0:1] if b < 15 else jnp.zeros((1, W), F32)
            col = col_ref[b * R : (b + 1) * R, :]
            moved = jnp.where(last, after, pltpu.roll(part, R - 1, 0)) * equal(col[:, 0:1], col[:, 2:3])
            rt[0:W, b * R : (b + 1) * R] = part.T.astype(BF)
            rt[W:, b * R : (b + 1) * R] = moved.T.astype(BF)
        for s in range(16):
            at = ((s % 2) * 8 + s // 2) * W
            gfp[:, at : at + W] = gf_ref[s]

    def units(kind, lo, hi):
        def unit(d, unused):
            u = 8 * kind + d
            if hi < 8:
                fetch(u + 1, kind)
            else:
                pl.when(d < 7)(lambda: fetch(u + 1, kind))
                if kind < 2:
                    pl.when(d == 7)(lambda: fetch(u + 1, kind + 1))
            have(u, kind)
            rhs = tile[d % 2]
            cols = pl.ds(pl.multiple_of(d * C, C), C)
            if kind == 0:
                gg_ref[d, U : 2 * U, :] = jnp.dot(lt_ref[...], rhs, preferred_element_type=F32).astype(BF)
            elif kind == 1:
                out = jnp.dot(rt[...], rhs, preferred_element_type=F32)
                gg_ref[d, 2 * U :, :] = (out[:W] + par_ref[13:14, cols] * (out[W:] - out[:W])).astype(BF)
            else:
                ga_ref[:, cols] = jnp.dot(gfp[...], rhs, preferred_element_type=F32)
            return 0

        lax.fori_loop(lo, hi, unit, 0)

    l_in.wait()
    w_in.wait()
    sums[0]()
    lt_in.wait()
    units(0, 0, 4)
    sums[1]()
    sums[2]()
    units(0, 4, 8)
    sums[3]()
    col_in.wait()
    turn()
    units(1, 0, 8)
    vg_in.wait()
    saves = [moves.start(gg_ref, gg_far)]
    sums[4]()
    units(2, 0, 8)
    strip_copy(0).start()
    hid_in.wait()
    sh_in.wait()
    unused, scale, normed = norm_parts(hid_ref[...])
    sums[5]()
    ga_k, ga_r, shift = o_ref[...], ga_ref[...], sh_ref[...]
    here = pl.ds(pl.multiple_of(p.s * R, 16), R)
    col = col_ref[here, :]
    moved = (ga_k * nu_k + ga_r * nu_r) * equal(col[:, 0:1], col[:, 1:2])
    halo[0] = moved[0:8]
    c.start(18)
    held = ga_k - ga_k * nu_k + (ga_r - ga_r * nu_r)
    rows_ref[...] = jnp.zeros_like(rows_ref)
    rows_ref[2:3, :] = jnp.sum(ga_k * shift, axis=0, keepdims=True)
    rows_ref[3:4, :] = jnp.sum(ga_r * shift, axis=0, keepdims=True)
    c.landed(18, halo.at[1])
    last = lax.broadcasted_iota(jnp.int32, (R, 1), 0) == R - 1
    grad = held + jnp.where(last, halo[1, 0:1, :], pltpu.roll(moved, R - 1, 0))
    gh = g_ref[...].astype(F32) + norm_back(normed, scale, grad * par_ref[10:11, :])
    gh_ref[...] = gh
    ghb_ref[...] = gh.astype(BF)

    def back_out(n, unused):
        pl.when(n < 7)(lambda: strip_copy(n + 1).start())
        strip_copy(n).wait()
        part = lax.dot_general(ghb_ref[:, 0:C], strip[n % 2, 0], (NT, ((), ())), preferred_element_type=F32)
        for d in range(1, 8):
            part = part + lax.dot_general(
                ghb_ref[:, d * C : (d + 1) * C], strip[n % 2, d], (NT, ((), ())), preferred_element_type=F32
            )
        for k in range(2):
            to = 2 * ((2 * n + k) % 8) + (2 * n + k) // 8
            gzp[to] = part[:, k * W : (k + 1) * W].astype(BF)
            swap.give(to)
        return 0

    lax.fori_loop(0, 8, back_out, 0)
    rows_ref[0:1, :] = jnp.sum(grad * normed, axis=0, keepdims=True)
    rows_ref[1:2, :] = jnp.sum(grad, axis=0, keepdims=True)
    for cp in saves:
        cp.wait()
    swap.all(swap.take)
    swap.all(swap.sent)
    c.finish()


def key_back(rc, gf, par, g, l, w, lt, cols, hidden, sh, vg, key_in, n2_all, far, out_far, cid):
    R, C = hidden.shape
    T, U, W = 16 * R, l.shape[1], rc.shape[2]
    return pl.pallas_call(
        key_back_kernel,
        out_shape=(
            jax.ShapeDtypeStruct((R, C), F32),
            jax.ShapeDtypeStruct((R, C), BF),
            jax.ShapeDtypeStruct((8, C), F32),
            jax.ShapeDtypeStruct((8, 2 * U + W, C // 8), BF),
            jax.ShapeDtypeStruct((16, R, W), BF),
        ),
        in_specs=[WHOLE] * 4 + [FAR] * 11,
        out_specs=(WHOLE,) * 3 + (FAR, WHOLE),
        scratch_shapes=sum_scratch(R, C)
        + [VMEM((R, C), F32), VMEM((2 * W, T), BF), VMEM((R, C), BF), VMEM((R, C), F32), VMEM((16, R, W), BF), VMEM((2, 8, C), F32)]
        + [VMEM((2, T, C // 8), BF), VMEM((2, 8, 2 * W, C // 8), BF), VMEM((T, U), BF), VMEM((U, C), BF), VMEM((U, T), BF)]
        + [VMEM(cols.shape, F32), VMEM((R, C), F32), VMEM((R, C), F32), VMEM((8, 2 * U + W, C // 8), BF)]
        + [DMA((19,)), DMA((19,)), DMA((16,)), DMA((16,)), DMA((2,)), DMA((2,)), DMA((8,))],
        compiler_params=params(cid, 60),
        name="key_back",
    )(rc, gf, par, g, l, w, lt, cols, hidden, sh, vg, key_in, n2_all, far, out_far)


def time_back_kernel(nd, gh_ref, gz_ref, par_ref, row_ref, bound_ref, early_far, x_far, o_far, s_far, col_far, zt_far, mixt_far, n1_hbm,
                     g_far, gg_far, sums_ref, mug_ref, dp_ref,
                     tab, grad_state, acc, carry, land, turned, tile, vec, early_ref, x_ref, o_ref, s_ref, col_ref, zt_ref, mixt_ref,
                     g_ref, gg_ref, d0, d1, d2, d3, cs, cr, ts, ms):
    p = Place()
    c = Copies(cs, cr)
    moves = Moves(ms)
    W = vec.shape[1]
    chunks, L = row_ref.shape[0], row_ref.shape[2]
    C = tile.shape[2]
    early_in, x_in, o_in, s_in, col_in, zt_in, mixt_in = (
        moves.start(a, b)
        for a, b in (
            (early_far, early_ref), (x_far, x_ref), (o_far, o_ref), (s_far, s_ref), (col_far, col_ref), (zt_far, zt_ref),
            (mixt_far, mixt_ref),
        )
    )
    fetch, have = column_tiles((n1_hbm,), tile, ts)
    fetch(0, 0)
    blk = rows_of(land)
    plan = gather_plan(p, c, 0, gh_ref, blk)
    sums = dp_plan(p, nd, c, 18, early_ref, dp_ref, (d0, d1, d2, d3)) if nd > 1 else no_sums(early_ref, dp_ref)
    own_vectors(p, par_ref, vec)
    meet(near(p) + beside(p, nd))
    plan[0]()
    early_in.wait()
    sums[0]()
    blk(p.s)[...] = gh_ref[...]
    when = {6: [plan[1], plan[2]], 9: [sums[1]], 11: [plan[3], plan[4]], 14: [plan[5], plan[6], plan[7]]}
    for cp in (x_in, o_in, s_in, col_in):
        cp.wait()
    chunk = back_chunk(x_ref, o_ref, s_ref, gz_ref, col_ref, row_ref, bound_ref, vec, g_ref, sums_ref, tab, grad_state, acc, carry, turned)

    def step(n, unused):
        chunk(n)
        for at, parts in when.items():
            @pl.when(n == at)
            def _():
                for part in parts:
                    part()
        return 0

    lax.fori_loop(0, chunks, step, 0)
    saves = [moves.start(g_ref, g_far)]
    back_finish(vec, sums_ref, acc, L)
    mug_ref[...] = jnp.zeros_like(mug_ref)
    mixt_in.wait()

    def mix(d, unused):
        pl.when(d < 7)(lambda: fetch(d + 1, 0))
        have(d, 0)
        rhs = tile[d % 2]
        cols = pl.ds(pl.multiple_of(d * C, C), C)
        a = jnp.dot(turned[: 4 * W, :], rhs, preferred_element_type=F32)
        b = jnp.dot(turned[4 * W :, :], rhs, preferred_element_type=F32)
        for q in range(4):
            rows = slice(q * W, (q + 1) * W)
            diff = b[rows] - a[rows]
            gg_ref[d, rows, :] = (a[rows] + par_ref[2 + q : 3 + q, cols] * diff).astype(BF)
            mug_ref[q : q + 1, cols] = jnp.sum(mixt_ref[rows, cols].astype(F32) * diff, axis=0, keepdims=True)
        return 0

    lax.fori_loop(0, 4, mix, 0)
    plan[8]()
    lax.fori_loop(4, 8, mix, 0)
    sums[2]()
    zt_in.wait()
    plan[9]()

    def out(d, unused):
        cols = pl.ds(pl.multiple_of(d * C, C), C)
        gg_ref[d, 4 * W :, :] = jnp.dot(zt_ref[...], land[:, cols], preferred_element_type=F32).astype(BF)
        return 0

    lax.fori_loop(0, 8, out, 0)
    saves.append(moves.start(gg_ref, gg_far))
    sums[3]()
    for cp in saves:
        cp.wait()
    c.finish()


def time_back(nd, gh, gz, par, rows, bounds, early, x, o, states, cols, zt, mixt, n1_all, cid):
    T, W = o.shape
    L = rows.shape[2]
    R, C = gh.shape
    J = early.shape[1]
    return pl.pallas_call(
        functools.partial(time_back_kernel, nd),
        out_shape=(
            jax.ShapeDtypeStruct((T, 8 * W), BF),
            jax.ShapeDtypeStruct((8, 5 * W, C // 8), BF),
            jax.ShapeDtypeStruct((8, W), F32),
            jax.ShapeDtypeStruct((4, C), F32),
            jax.ShapeDtypeStruct((8 // nd, J, C // 8), F32),
        ),
        in_specs=[WHOLE] * 4 + [pl.BlockSpec(memory_space=pltpu.SMEM)] + [FAR] * 8,
        out_specs=(FAR,) * 2 + (WHOLE,) * 3,
        scratch_shapes=[
            VMEM((4, L, W), F32), VMEM((W, W), F32), VMEM((W, W), F32), VMEM((8, 4 * W), F32),
            VMEM((T, C), BF), VMEM((8 * W, T), BF), VMEM((2, T, C // 8), BF), VMEM((8 + W, W), F32),
            VMEM(early.shape, BF), VMEM(x.shape, F32), VMEM((T, W), F32), VMEM(states.shape, F32), VMEM(cols.shape, F32),
            VMEM((W, T), BF), VMEM(mixt.shape, BF), VMEM((T, 8 * W), BF), VMEM((8, 5 * W, C // 8), BF),
        ]
        + dp_scratch(J, C // 8)
        + [DMA((25,)), DMA((25,)), DMA((2,)), DMA((9,))],
        compiler_params=params(cid, 60),
        name="time_back",
    )(gh, gz, par, rows, bounds, early, x, o, states, cols, zt, mixt, n1_all)


def last_kernel(nd, x_ref, par_ref, mug_ref, head_ref, norm_ref, gg_far, l_far, w_far, gh_far, ig_ref, dp_ref, v_ref, *rest):
    scratch = rest[:7]
    o_ref, d0, d1, d2, d3, tv, b1, t1, b2, gg_ref, l_ref, w_ref, gh_ref, cs, cr, ms = rest[7:]
    p = Place()
    c = Copies(cs, cr)
    moves = Moves(ms)
    l_in, w_in, gg_in, gh_in = (
        moves.start(a, b) for a, b in ((l_far, l_ref), (w_far, w_ref), (gg_far, gg_ref), (gh_far, gh_ref))
    )
    sums = dp_plan(p, nd, c, 18, gg_ref, dp_ref, (d0, d1, d2, d3)) if nd > 1 else no_sums(gg_ref, dp_ref)
    steps = sum_plan(p, c, 0, l_ref, w_ref, o_ref, scratch)
    W = head_ref.shape[1]
    tv[...] = jnp.zeros_like(tv)
    tv[2:6, :] = mug_ref[...]
    tv[6:10, pl.ds(pl.multiple_of(p.s * W, 128), W)] = head_ref[0:4, :]
    tv[10:14, :] = norm_ref[0:4, :]
    meet(near(p) + beside(p, nd))
    for cp in (l_in, w_in, gg_in):
        cp.wait()
    sums[0]()
    steps[0]()
    sums[1]()
    steps[1]()
    steps[2]()
    steps[3]()
    sums[2]()
    unused, scale, normed = norm_parts(x_ref[...].astype(F32))
    sums[3]()
    gh_in.wait()
    steps[4]()
    steps[5]()
    gn = o_ref[...]
    tv[0:1, :] = jnp.sum(gn * normed, axis=0, keepdims=True)
    tv[1:2, :] = jnp.sum(gn, axis=0, keepdims=True)
    C = b1.shape[2]
    for k in range(1, nd):
        to = (p.dp + k) % nd
        c.add(24 + k, tv.at[:, pl.ds(pl.multiple_of(to * C, 128), C)], b1.at[k - 1], (to, p.s))
        c.start(24 + k)
    ig_ref[...] = gh_ref[...] + norm_back(normed, scale, gn * par_ref[0:1, :])
    total = tv[:, pl.ds(pl.multiple_of(p.dp * C, 128), C)]
    for k in range(1, nd):
        c.landed(24 + k, b1.at[k - 1])
        total = total + b1[k - 1]
    t1[...] = total
    for k in range(1, 16):
        c.add(31 + k, t1, b2.at[k - 1], p.dev((p.s + k) % 16))
        c.start(31 + k)
    for k in range(1, 16):
        c.landed(31 + k, b2.at[k - 1])
        total = total + b2[k - 1]
    v_ref[...] = total
    c.finish()


def last_sums(nd, x, par, mug, head, norm, gg, l, w, gh, cid):
    R, C = x.shape
    J = gg.shape[1]
    piece = (16, C // nd)
    return pl.pallas_call(
        functools.partial(last_kernel, nd),
        out_shape=(jax.ShapeDtypeStruct((R, C), F32), jax.ShapeDtypeStruct((8 // nd, J, C // 8), F32), jax.ShapeDtypeStruct(piece, F32)),
        in_specs=[WHOLE] * 5 + [FAR] * 4,
        out_specs=(WHOLE,) * 3,
        scratch_shapes=sum_scratch(R, C)
        + [VMEM((R, C), F32)]
        + dp_scratch(J, C // 8)
        + [VMEM((16, C), F32), VMEM((max(nd - 1, 1),) + piece, F32), VMEM(piece, F32), VMEM((15,) + piece, F32)]
        + [VMEM(gg.shape, BF), VMEM(l.shape, BF), VMEM(w.shape, BF), VMEM((R, C), F32)]
        + [DMA((47,)), DMA((47,)), DMA((4,))],
        compiler_params=params(cid, 60),
        name="last_sums",
    )(x, par, mug, head, norm, gg, l, w, gh)


def body(nd, inputs, cotangent, mix_weights, out_weight, key_weight, value_weight, recept_weight, vectors, segment_ids):
    tokens, width = inputs.shape
    group = segment_ids.shape[0]
    cols = mix_weights.shape[2]
    units = key_weight.shape[1]
    s = lax.axis_index("sp")
    ring = group // tokens
    chunks = group // CHUNK

    edge = jnp.full((1,), -1.0, F32)
    seg = jnp.concatenate([edge, segment_ids.astype(F32), edge])
    tok_cols = jnp.stack([seg[1:-1], seg[:-2], seg[2:]], axis=1)
    tok_rows = seg[1:-1].reshape(chunks, 1, CHUNK)
    ends = seg[: group + 1 : CHUNK]
    bounds = jnp.stack([ends, jnp.concatenate([(ends[1:] == ends[:-1]).astype(F32), edge])])

    n1_all, projected, z_t, mixed_time, states, hidden, n2, recept_part, out_far = time_forward(
        nd, inputs, vectors, tok_rows, bounds, mix_weights, out_weight, recept_weight, tok_cols, 0
    )
    n2_all, key_in, lifted, squared, recept_in, shift, value_t, mixt, folded, recept_far = key_side(
        nd, n2, recept_part, vectors, key_weight.T, tok_cols, value_weight, mix_weights, 1
    )
    result, grad_recept, recept_cols, grad_key, grad_key_t, value_grad = value_side(
        recept_in, cotangent, hidden, squared, value_weight, value_t, lifted, recept_far, 2
    )
    grad_hidden, grad_hidden_b, norm_rows, early, gz = key_back(
        recept_cols, grad_recept, vectors, cotangent, grad_key, key_weight.T, grad_key_t, tok_cols, hidden, shift, value_grad,
        key_in.reshape(group, width), n2_all, recept_far, out_far, 3,
    )
    grads_two, late, head_rows, mu_rows, early_sum = time_back(
        nd, grad_hidden_b, gz, vectors, tok_rows, bounds, early, projected, mixed_time, states, tok_cols, z_t, mixt, n1_all, 4
    )
    input_grad, late_sum, vector_sum = last_sums(
        nd, inputs, vectors, mu_rows, head_rows, norm_rows, late, grads_two, folded, grad_hidden, 5
    )
    piece = width // (nd * ring)
    vectors_grad = lax.dynamic_slice_in_dim(vector_sum[:14], s * piece, piece, 1)

    def columns(part):
        return part.transpose(1, 0, 2).reshape(part.shape[1], width // nd)

    early_sum, late_sum = columns(early_sum), columns(late_sum)
    return (
        result,
        input_grad,
        late_sum[: 4 * cols].reshape(4, cols, width // nd).transpose(0, 2, 1),
        late_sum[4 * cols :],
        early_sum[units : 2 * units].T,
        early_sum[:units],
        early_sum[2 * units :].T,
        vectors_grad,
    )


def solution(mesh):
    placed = (
        P(("dp", "sp"), None),
        P(("dp", "sp"), None),
        P(None, None, "sp"),
        P("sp", None),
        P(None, "sp"),
        P("sp", None),
        P(None, "sp"),
        P(),
        P("dp"),
    )
    return jax.shard_map(
        functools.partial(body, mesh.shape["dp"]),
        mesh=mesh,
        in_specs=placed,
        out_specs=(
            P(("dp", "sp"), None),
            P(("dp", "sp"), None),
            P(None, "dp", "sp"),
            P("sp", "dp"),
            P("dp", "sp"),
            P("sp", "dp"),
            P("dp", "sp"),
            P(None, ("dp", "sp")),
        ),
        check_vma=False,
    )
```

```python
import functools

import jax
import jax.numpy as jnp
from jax import lax
from jax.experimental import pallas as pl
from jax.experimental.pallas import tpu as pltpu
from jax.sharding import PartitionSpec as P

MESH = pl.DeviceIdType.MESH
VMEM = pltpu.VMEM
DMA = pltpu.SemaphoreType.DMA
BF = jnp.bfloat16
F32 = jnp.float32

ATTENTION_WIDTH = 64
CHUNK = 128
WHOLE = pl.BlockSpec(memory_space=VMEM)
FAR = pl.BlockSpec(memory_space=pl.ANY)


class Place:
    def __init__(self):
        self.dp = lax.axis_index("dp")
        s = lax.axis_index("sp")
        self.s = s
        self.x, self.z, self.c = s // 4, (s // 2) % 2, s % 2

    def at(self, dx=0, dz=0, dc=0):
        return ((self.x + dx) % 4) * 4 + ((self.z + dz) % 2) * 2 + (self.c + dc) % 2

    def dev(self, s):
        return (self.dp, s)


class Across:
    def __init__(self, p, nd):
        self.p, self.ny = p, nd // 2
        self.x, self.z, self.c = p.dp // 2, p.dp % 2, p.c
        self.s = p.dp * 2 + p.c

    def at(self, dx=0, dz=0, dc=0):
        return ((self.x + dx) % self.ny) * 4 + ((self.z + dz) % 2) * 2 + (self.c + dc) % 2

    def dev(self, i):
        return (i // 2, self.p.s - self.p.c + i % 2)


class Copies:
    def __init__(self, ss, rs):
        self.ss, self.rs, self.items = ss, rs, {}

    def add(self, k, src, dst, to):
        self.items[k] = (src, dst, to)

    def make(self, k, src, dst, to):
        return pltpu.make_async_remote_copy(
            src_ref=src, dst_ref=dst, send_sem=self.ss.at[k], recv_sem=self.rs.at[k], device_id=to, device_id_type=MESH
        )

    def start(self, *ks):
        for k in ks:
            self.make(k, *self.items[k]).start()

    def landed(self, k, ref):
        self.make(k, ref, ref, self.items[k][2]).wait_recv()

    def finish(self):
        for k in self.items:
            self.make(k, *self.items[k]).wait_send()


def greet(devices):
    barrier = pltpu.get_barrier_semaphore()
    for device in devices:
        pl.semaphore_signal(barrier, inc=1, device_id=device, device_id_type=MESH)
    return lambda: pl.semaphore_wait(barrier, len(devices))


def near(p):
    return [p.dev(p.at(dc=1)), p.dev(p.at(dx=1)), p.dev(p.at(dx=-1)), p.dev(p.at(dz=1))]


def beside(p, nd):
    y, zl, ny = p.dp // 2, p.dp % 2, nd // 2
    if nd == 1:
        return []
    return [(2 * ((y + 1) % ny) + zl, p.s), (2 * ((y + ny - 1) % ny) + zl, p.s), (2 * y + 1 - zl, p.s)]


def chip_mates(p):
    return [p.dev(p.at(dx, dz)) for dz in range(2) for dx in range(4)][1:]


def ring_mates(p):
    return [p.dev((p.s + k) % 16) for k in range(1, 16)]


def dp_mates(p, nd):
    return [((p.dp + k) % nd, p.s) for k in range(1, nd)]


def params(cid, mib):
    return pltpu.CompilerParams(collective_id=cid, has_side_effects=True, vmem_limit_bytes=mib * 2**20)


class Swap:
    def __init__(self, p, src, dst, ss, rs):
        self.p, self.src, self.dst, self.ss, self.rs = p, src, dst, ss, rs

    def make(self, src, dst, at, to):
        return pltpu.make_async_remote_copy(
            src_ref=src, dst_ref=dst, send_sem=self.ss.at[to], recv_sem=self.rs.at[at], device_id=self.p.dev(to), device_id_type=MESH
        )

    def give(self, i):
        @pl.when(i != self.p.s)
        def _():
            self.make(self.src(i), self.dst.at[self.p.s], self.p.s, i).start()

        @pl.when(i == self.p.s)
        def _():
            self.dst[self.p.s] = self.src(i)[...]

    def take(self, i):
        @pl.when(i != self.p.s)
        def _():
            self.make(self.dst.at[i], self.dst.at[i], i, i).wait_recv()

    def sent(self, i):
        @pl.when(i != self.p.s)
        def _():
            self.make(self.src(i), self.dst.at[self.p.s], self.p.s, i).wait_send()

    def all(self, act):
        def step(i, unused):
            act(i)
            return 0

        lax.fori_loop(0, 16, step, 0)


class Moves:
    def __init__(self, sem):
        self.sem, self.n = sem, 0

    def start(self, src, dst):
        cp = pltpu.make_async_copy(src, dst, self.sem.at[self.n])
        self.n += 1
        cp.start()
        return cp


def equal(a, b):
    return jnp.where(a == b, 1.0, 0.0)


def blocks_of(land):
    R = land.shape[1] // 2

    def blk(i, half=None):
        rows = R if half is None else R // 2
        return land.at[i // 2, pl.ds(pl.multiple_of((i % 2) * R + (half or 0) * rows, 16), rows)]

    return blk


def rows_of(land):
    R = land.shape[0] // 16

    def blk(i, half=None):
        rows = R if half is None else R // 2
        return land.at[pl.ds(pl.multiple_of(i * R + (half or 0) * rows, 16), rows)]

    return blk


def matrix_blocks(land):
    K = land.shape[1] // 2

    def blk(i, half=None):
        rows = K if half is None else K // 2
        return land.at[i // 2, pl.ds(pl.multiple_of((i % 2) * K + (half or 0) * rows, 16), rows)]

    return blk


def gather_plan(p, c, base, a_ref, blk, around=False):
    core, xp, xm, zz = p.at(dc=1), p.at(dx=1), p.at(dx=-1), p.at(dz=1)
    d2, zxm, zxp, zd2 = p.at(dx=2), p.at(dx=-1, dz=1), p.at(dx=1, dz=1), p.at(dx=2, dz=1)
    up, lo = 0, 1

    def relay(k, ref, to):
        c.add(base + k, ref, ref, p.dev(to))

    for k, to in enumerate((xp, xm, zz, core)):
        c.add(base + k, a_ref, blk(p.s), p.dev(to))
    relay(4, blk(xm, up), xp)
    relay(5, blk(xp, lo), xm)
    relay(6, blk(xm), core)
    relay(7, blk(xp), core)
    relay(8, blk(zz), xp)
    relay(9, blk(zz), xm)
    relay(10, blk(zz), core)
    if around:
        relay(11, blk(zxm, up), xp)
        relay(12, blk(zxp, lo), xm)
    else:
        relay(11, blk(d2, up), zz)
        relay(12, blk(d2, lo), zz)
    relay(13, blk(d2), core)
    relay(14, blk(zxm), core)
    relay(15, blk(zxp), core)
    relay(16, blk(zd2, up), core)
    relay(17, blk(zd2, lo), core)

    def start(*ks):
        c.start(*(base + k for k in ks))

    def landed(k, ref):
        c.landed(base + k, ref)

    def other(**k):
        return p.at(dc=1, **k)

    def one():
        start(0, 1, 2, 3)
        return []

    def own():
        landed(3, blk(core))
        return [core // 2]

    def two():
        landed(0, blk(xm))
        start(4)
        landed(1, blk(xp))
        start(5, 6, 7)
        landed(2, blk(zz))
        start(8, 9, 10)
        return []

    def third():
        landed(6, blk(other(dx=-1)))
        return [xm // 2]

    def three():
        landed(4, blk(d2, up))
        if not around:
            start(11)
        landed(5, blk(d2, lo))
        if not around:
            start(12)
        start(13)
        return []

    def third_more():
        landed(7, blk(other(dx=1)))
        landed(10, blk(other(dz=1)))
        return [xp // 2, zz // 2]

    def fourth():
        landed(13, blk(other(dx=2)))
        return [d2 // 2]

    def four():
        landed(8, blk(zxm))
        if around:
            start(11)
        landed(9, blk(zxp))
        if around:
            start(12)
        start(14, 15)
        return []

    def five():
        landed(11, blk(zd2, up))
        start(16)
        landed(12, blk(zd2, lo))
        start(17)
        landed(14, blk(other(dx=-1, dz=1)))
        landed(15, blk(other(dx=1, dz=1)))
        return [zxm // 2, zxp // 2]

    def six():
        landed(16, blk(other(dx=2, dz=1), up))
        landed(17, blk(other(dx=2, dz=1), lo))
        return [zd2 // 2]

    return [one, own, two, third, three, third_more, fourth, four, five, six]


def run_gather(plan, work, hooks):
    ready = []
    for n, step in enumerate(plan):
        ready += step()
        for hook in hooks.get(n, ()):
            hook()
        if ready:
            work(ready.pop(0))
    for chip in ready:
        work(chip)


def chip_plan(p, c, base, w_ref, part):
    R, C = w_ref.shape[0], part.shape[1]
    cols = pl.ds(pl.multiple_of(p.dp * C, C), C)
    mates = [(dx, dz) for dz in range(2) for dx in range(4)][1:]

    def rows(s):
        return pl.ds(pl.multiple_of((s // 2) * R, 16), R)

    for k, (dx, dz) in enumerate(mates):
        c.add(base + k, w_ref.at[:, cols], part.at[rows(p.s)], p.dev(p.at(dx, dz)))

    def begin():
        part[rows(p.s), :] = w_ref[:, cols]
        c.start(*range(base, base + 7))

    def end():
        for k, (dx, dz) in enumerate(mates):
            c.landed(base + k, part.at[rows(p.at(-dx, dz))])

    return begin, end


def across_plan(p, nd, c, base, part, land):
    q = Across(p, nd)
    K = part.shape[0]
    plan = gather_plan(q, c, base, part, matrix_blocks(land), around=True)

    def go(*ns):
        def run():
            for n in ns:
                plan[n]()

        return run

    return go, land.at[p.dp, pl.ds(pl.multiple_of(p.c * K, 16), K)]


def save_blocks(land, all_ref, sem):
    R = land.shape[1]

    def copy(k):
        return pltpu.make_async_copy(land.at[k], all_ref.at[pl.ds(pl.multiple_of(k * R, 16), R)], sem.at[k])

    def wait():
        for k in range(8):
            copy(k).wait()

    return lambda k: copy(k).start(), wait


def heads_of_blocks(land, col):
    R = land.shape[1] // 2

    def row(b, at):
        at += (b % 2) * R
        return land[b // 2, at // 16 * 16 : at // 16 * 16 + 16, :].astype(F32)[at % 16 : at % 16 + 1]

    first = jnp.concatenate([row(b, 0) for b in range(16)], axis=0)
    before = jnp.concatenate([jnp.zeros_like(first[0:1])] + [row(b, R - 1) for b in range(15)], axis=0)
    heads = jnp.concatenate([col[b * R : b * R + 1, :] for b in range(16)], axis=0)
    return first, before * equal(heads[:, 0:1], heads[:, 1:2]) - first


def shifted(n, col):
    same = equal(col[:, 0:1], col[:, 1:2])
    rows = lax.broadcasted_iota(jnp.int32, n.shape, 0)
    before = jnp.where(rows == 0, 0.0, pltpu.roll(n, 1, 0))
    return before * same - n


def norm_parts(a):
    width = a.shape[1]
    center = a - jnp.sum(a, axis=1, keepdims=True) * (1.0 / width)
    scale = lax.rsqrt(jnp.sum(center * center, axis=1, keepdims=True) * (1.0 / width) + 1e-05)
    return center, scale, center * scale


def norm_back(normed, scale, grad):
    width = grad.shape[1]
    inner = grad - jnp.sum(grad, axis=1, keepdims=True) * (1.0 / width)
    return scale * (inner - normed * (jnp.sum(grad * normed, axis=1, keepdims=True) * (1.0 / width)))


def sigmoid(a):
    return 1.0 / (1.0 + jnp.exp(-a))


CHUNK = 128


def halves(a):
    high = a.astype(BF)
    return high, (a - high.astype(F32)).astype(BF)


def dot3(a, b, dims):
    def one(x, y):
        return lax.dot_general(x, y, (dims, ((), ())), preferred_element_type=F32)

    return one(a[0], b[0]) + (one(a[0], b[1]) + one(a[1], b[0]))


NN, NT, TN = ((1,), (0,)), ((1,), (1,)), ((0,), (0,))


def head_sums(a, ones):
    high, rest = a.astype(BF), a - a.astype(BF).astype(F32)
    mid = rest.astype(BF)
    low = (rest - mid.astype(F32)).astype(BF)

    def one(x):
        return lax.dot_general(x, ones, (NN, ((), ())), preferred_element_type=F32)

    return one(high) + (one(mid) + one(low))


def iota(shape, dim):
    return lax.broadcasted_iota(jnp.int32, shape, dim)


def head_ones(width, dtype):
    return (iota((width, width), 0) // ATTENTION_WIDTH == iota((width, width), 1) // ATTENTION_WIDTH).astype(dtype)


def by_head(pair):
    lane = iota(pair[0].shape, 1) // ATTENTION_WIDTH
    heads = pair[0].shape[1] // ATTENTION_WIDTH
    zero = jnp.zeros_like(pair[0])
    return tuple(jnp.concatenate([jnp.where(lane == h, a, zero) for h in range(heads)], axis=0) for a in pair)


def pick_heads(a, rows):
    lane = iota((rows, a.shape[1]), 1) // ATTENTION_WIDTH
    out = a[:rows]
    for h in range(1, a.shape[1] // ATTENTION_WIDTH):
        out = jnp.where(lane == h, a[h * rows : (h + 1) * rows], out)
    return out


def powers(lam, tab):
    L = tab.shape[1]
    at = iota((L, 1), 0).astype(F32)
    mid = L // 2
    tab[0] = jnp.exp(lam * (at - mid))
    tab[1] = jnp.exp(-lam * (at + (1.0 - mid)))
    tab[2] = jnp.exp(lam * at)
    tab[3] = jnp.exp(lam * (L - 1.0 - at))


def own_vectors(p, par_ref, vec):
    W = vec.shape[1]
    own = par_ref[6:10, pl.ds(pl.multiple_of(p.s * W, 128), W)]
    lam = -jnp.exp(own[0:1])
    vec[0:1, :] = lam
    vec[1:4, :] = own[1:4]
    vec[8:, :] = jnp.broadcast_to(jnp.exp(lam * CHUNK), (W, W)).T


def chunk_mask(col, row):
    L = col.shape[0]
    return (iota((L, L), 1) < iota((L, L), 0)) & (col == row)


def forward_chunk(x_ref, col_ref, row_ref, bound_ref, vec_ref, z_ref, zt_ref, o_ref, s_ref, tab, state):
    chunks, L = row_ref.shape[0], row_ref.shape[2]
    W = vec_ref.shape[1]
    heads = W // ATTENTION_WIDTH
    lam, bonus, gain, bias = (vec_ref[q : q + 1, :] for q in range(4))
    powers(lam, tab)
    ones = head_ones(W, BF)
    diag = head_ones(W, F32)
    decay = vec_ref[8 : 8 + W, :]
    state[...] = jnp.zeros_like(state)

    def step(i):
        rows = pl.ds(pl.multiple_of(i * L, L), L)
        r, k, v, p = (x_ref[rows, q * W : (q + 1) * W] for q in range(4))
        col = col_ref[rows, :]
        seg = col[:, 0:1]
        kept, tail = equal(seg, bound_ref[0, i]), equal(seg, bound_ref[0, i + 1])
        mask = chunk_mask(seg, row_ref[i])
        mask = jnp.concatenate([mask] * heads, axis=1)
        rs, ks = halves(r * tab[0]), halves(k * tab[1])
        scores = jnp.where(mask, dot3(rs, by_head(ks), NT), 0.0)
        vh = halves(v)
        out = dot3(halves(scores), by_head(vh), NN) + head_sums(r * k * bonus, ones) * v
        memory = state[...]
        s_ref[i] = memory
        out = out + kept * dot3(halves(r * tab[2]), halves(memory), NN)
        state[...] = bound_ref[1, i] * decay * memory + diag * dot3(halves(k * tab[3] * tail), vh, TN)
        o_ref[rows, :] = out
        center = out - head_sums(out, ones) * (1.0 / ATTENTION_WIDTH)
        spread = head_sums(center * center, ones) * (1.0 / ATTENTION_WIDTH)
        normed = center * lax.rsqrt(spread + 0.00064) * gain + bias
        z = (normed * (p * sigmoid(p))).astype(BF).astype(F32)
        z_ref[rows, :] = z.astype(BF)
        zt_ref[:, rows] = z.T.astype(BF)

    return step


def back_chunk(x_ref, o_ref, s_ref, gz_ref, col_ref, row_ref, bound_ref, vec_ref, g_ref, sums_ref, tab, grad_state, acc, carry, turned):
    chunks, L = row_ref.shape[0], row_ref.shape[2]
    W = vec_ref.shape[1]
    heads = W // ATTENTION_WIDTH
    lam, bonus, gain, bias = (vec_ref[q : q + 1, :] for q in range(4))
    powers(lam, tab)
    ones = head_ones(W, BF)
    diag = head_ones(W, F32)
    decay = vec_ref[8 : 8 + W, :]
    at = iota((L, 1), 0).astype(F32)
    mid = float(L // 2)
    grad_state[...] = jnp.zeros_like(grad_state)
    acc[...] = jnp.zeros_like(acc)
    carry[...] = jnp.zeros_like(carry)
    sums_ref[...] = jnp.zeros_like(sums_ref)

    def add(q, term):
        sums_ref[q : q + 1, :] += jnp.sum(term, axis=0, keepdims=True)

    def step(n):
        i = chunks - 1 - n
        rows = pl.ds(pl.multiple_of(i * L, L), L)
        r, k, v, p = (x_ref[rows, q * W : (q + 1) * W] for q in range(4))
        col = col_ref[rows, :]
        seg = col[:, 0:1]
        kept, tail = equal(seg, bound_ref[0, i]), equal(seg, bound_ref[0, i + 1])
        same_next = equal(seg, col[:, 2:3])
        o = o_ref[rows, :]
        gz = gz_ref[i].astype(F32)
        center = o - head_sums(o, ones) * (1.0 / ATTENTION_WIDTH)
        spread = head_sums(center * center, ones) * (1.0 / ATTENTION_WIDTH)
        scale = lax.rsqrt(spread + 0.00064)
        normed = center * scale
        gate = sigmoid(p)
        silu = p * gate
        gy = gz * silu
        gp = gz * (normed * gain + bias) * (gate * (1.0 + p * (1.0 - gate)))
        add(2, gy * normed)
        add(3, gy)
        gn = gy * gain
        go = scale * (
            gn
            - head_sums(gn, ones) * (1.0 / ATTENTION_WIDTH)
            - normed * (head_sums(gn * normed, ones) * (1.0 / ATTENTION_WIDTH))
        )
        mask = chunk_mask(seg, row_ref[i])
        mask = jnp.concatenate([mask] * heads, axis=1)
        rs_f, ks_f = r * tab[0], k * tab[1]
        r0_f, ke_f = r * tab[2] * kept, k * tab[3] * tail
        rs, ks, vh, goh = halves(rs_f), halves(ks_f), halves(v), halves(go)
        ks_by, v_by = by_head(ks), by_head(vh)
        scores = halves(jnp.where(mask, dot3(rs, ks_by, NT), 0.0))
        grad_scores = halves(jnp.where(mask, dot3(goh, v_by, NT), 0.0))
        memory = s_ref[i]
        gs = grad_state[...]
        mh, gsh = halves(memory), halves(gs)
        reward = head_sums(r * k * bonus, ones)
        grad_reward = head_sums(go * v, ones)
        g_rs = dot3(grad_scores, ks_by, NN)
        g_r0 = dot3(goh, mh, NT)
        g_ks = pick_heads(dot3(grad_scores, rs, TN), L)
        g_ke = dot3(vh, gsh, NT)
        gv = pick_heads(dot3(scores, goh, TN), L) + reward * go + dot3(halves(ke_f), gsh, NN)
        keep = bound_ref[1, i]
        acc[...] += keep * memory * gs
        grad_state[...] = keep * decay * gs + diag * dot3(halves(r0_f), goh, TN)
        gr = g_rs * tab[0] + g_r0 * (tab[2] * kept) + grad_reward * bonus * k
        gk = g_ks * tab[1] + g_ke * (tab[3] * tail) + grad_reward * bonus * r
        add(1, grad_reward * r * k)
        add(0, (at - mid) * (g_rs * rs_f) - (at + (1.0 - mid)) * (g_ks * ks_f) + at * (g_r0 * r0_f) + (L - 1.0 - at) * (g_ke * ke_f))
        grads = jnp.concatenate([gr, gk, gv, gp], axis=1).astype(BF).astype(F32)
        last = iota((L, 1), 0) == L - 1
        after = jnp.where(last, carry[0:1, :], pltpu.roll(grads, L - 1, 0)) * same_next
        carry[0:1, :] = grads[0:1, :]
        g_ref[rows, : 4 * W] = grads.astype(BF)
        g_ref[rows, 4 * W :] = after.astype(BF)
        turned[0 : 4 * W, rows] = grads.T.astype(BF)
        turned[4 * W :, rows] = after.T.astype(BF)

    return step


def back_finish(vec_ref, sums_ref, acc, L):
    W = vec_ref.shape[1]
    whole = dot3(halves(jnp.ones((8, W), F32)), halves(acc[...] * vec_ref[8 : 8 + W, :]), NT)
    sums_ref[0:1, :] = (sums_ref[0:1, :] + L * whole[0:1, :]) * vec_ref[0:1, :]


def time_forward_kernel(nd, x_ref, par_ref, row_ref, bound_ref, w_far, ow_far, rw_far, col_far,
                        all_ref, proj_far, zt_far, o_far, s_far, hid_ref, n2_ref, rp_ref, far_ref,
                        n1, land, op, lw, tab, state, zin, w_ref, ow_ref, rw_ref, rt_ref, col_ref, proj_ref, z_ref, zt_ref,
                        o_ref, s_ref, vec, cs, cr, ss, rs, ls, ms):
    p = Place()
    met = greet(chip_mates(p) + [p.dev(p.at(dc=1))] + beside(p, nd))
    c = Copies(cs, cr)
    moves = Moves(ms)
    ow_in, w_in, col_in, rw_in = (
        moves.start(a, b) for a, b in ((ow_far, ow_ref), (w_far, w_ref), (col_far, col_ref), (rw_far, rw_ref))
    )
    R = x_ref.shape[0]
    Q, W = w_ref.shape[0], w_ref.shape[2]
    C = lw.shape[2]
    begin, end = chip_plan(p, c, 18, ow_ref, op)
    go, own_part = across_plan(p, nd, c, 25, op, lw)
    recept_begin, recept_end = chip_plan(p, c, 43, rt_ref, rp_ref)
    blk = blocks_of(land)
    plan = gather_plan(p, c, 0, n1, blk)
    start, wait = save_blocks(land, all_ref, ls)
    n1[...] = (norm_parts(x_ref[...].astype(F32))[2] * par_ref[0:1, :] + par_ref[1:2, :]).astype(BF)
    met()

    def ready():
        begin()
        blk(p.s)[...] = n1[...]
        own_vectors(p, par_ref, vec)
        w_in.wait()
        col_in.wait()

    def turn():
        rw_in.wait()
        for k in range(0, rw_ref.shape[0], 256):
            rt_ref[:, k : k + 256] = rw_ref[k : k + 256, :].T

    def across():
        own_part[...] = op[...]
        go(0)()

    def work(k):
        start(k)
        rows = pl.ds(pl.multiple_of(k * 2 * R, 16), 2 * R)
        n = land[k].astype(F32)
        shift = shifted(n, col_ref[rows, :])
        for q in range(Q):
            m = (n + shift * par_ref[2 + q : 3 + q, :]).astype(BF)
            proj_ref[rows, q * W : (q + 1) * W] = jnp.dot(m, w_ref[q], preferred_element_type=F32)

    ow_in.wait()
    run_gather(plan, work, {0: [ready], 1: [turn], 3: [end, across], 8: [go(1, 2)]})
    recept_begin()
    first, shift = heads_of_blocks(land, col_ref)
    for q in range(Q):
        m = (first + shift * par_ref[2 + q : 3 + q, :]).astype(BF)
        out = jnp.dot(m, w_ref[q], preferred_element_type=F32)
        for b in range(0, 16, 2):
            proj_ref[b * R : b * R + 1, q * W : (q + 1) * W] = out[b : b + 1]
    saves = [moves.start(proj_ref, proj_far)]

    chunk = forward_chunk(proj_ref, col_ref, row_ref, bound_ref, vec, z_ref, zt_ref, o_ref, s_ref, tab, state)
    swap = Swap(p, lambda i: z_ref.at[pl.ds(pl.multiple_of(i * R, 16), R)], zin, ss, rs)
    when = {3: go(3, 4), 6: go(5, 6, 7)}

    def step(n, unused):
        chunk(2 * n)
        chunk(2 * n + 1)
        swap.give(2 * n)
        swap.give(2 * n + 1)
        for at, act in when.items():
            pl.when(n == at)(act)
        return 0

    lax.fori_loop(0, row_ref.shape[0] // 2, step, 0)
    saves += [moves.start(a, b) for a, b in ((zt_ref, zt_far), (o_ref, o_far), (s_ref, s_far))]
    go(8, 9)()
    saves.append(moves.start(lw, far_ref))
    swap.all(swap.take)
    z_here = jnp.concatenate([zin[2 * k + core] for core in range(2) for k in range(8)], axis=1)
    for d in range(8):
        cols = slice(d * C, (d + 1) * C)
        hid_ref[:, cols] = x_ref[:, cols].astype(F32) + jnp.dot(z_here, lw[d], preferred_element_type=F32)
    n2_ref[...] = (norm_parts(hid_ref[...])[2] * par_ref[10:11, :] + par_ref[11:12, :]).astype(BF)
    recept_end()
    wait()
    for cp in saves:
        cp.wait()
    swap.all(swap.sent)
    c.finish()


def time_forward(nd, x, par, rows, bounds, w, ow, rw, cols, cid):
    R, C = x.shape
    T, W = 16 * R, w.shape[2]
    chunks, L = rows.shape[0], rows.shape[2]
    return pl.pallas_call(
        functools.partial(time_forward_kernel, nd),
        out_shape=(
            jax.ShapeDtypeStruct((T, C), BF),
            jax.ShapeDtypeStruct((T, 4 * W), F32),
            jax.ShapeDtypeStruct((W, T), BF),
            jax.ShapeDtypeStruct((T, W), F32),
            jax.ShapeDtypeStruct((chunks, W, W), F32),
            jax.ShapeDtypeStruct((R, C), F32),
            jax.ShapeDtypeStruct((R, C), BF),
            jax.ShapeDtypeStruct((8 * R, C // nd), BF),
            jax.ShapeDtypeStruct((8, 16 * R, C // 8), BF),
        ),
        in_specs=[WHOLE] * 3 + [pl.BlockSpec(memory_space=pltpu.SMEM)] + [FAR] * 4,
        out_specs=(FAR,) * 5 + (WHOLE,) * 3 + (FAR,),
        scratch_shapes=[
            VMEM((R, C), BF), VMEM((8, 2 * R, C), BF), VMEM((8 * R, C // nd), BF), VMEM((8, 16 * R, C // 8), BF), VMEM((4, L, W), F32),
            VMEM((W, W), F32), VMEM((16, R, W), BF), VMEM(w.shape, BF), VMEM((R, C), BF), VMEM((C, W), BF), VMEM((W, C), BF),
            VMEM(cols.shape, F32), VMEM((T, 4 * W), F32), VMEM((T, W), BF), VMEM((W, T), BF), VMEM((T, W), F32),
            VMEM((chunks, W, W), F32), VMEM((8 + W, W), F32),
            DMA((50,)), DMA((50,)), DMA((16,)), DMA((16,)), DMA((16,)), DMA((9,)),
        ],
        compiler_params=params(cid, 56),
        name="time_forward",
    )(x, par, rows, bounds, w, ow, rw, cols)


def key_kernel(nd, a_ref, rp_ref, par_ref, k_far, col_far, vw_far, mw_far,
               all_ref, in_ref, lift_far, sq_far, rin_ref, sh_ref, vt_far, mt_far, fold_far, far_ref,
               land, mixed, k_ref, w_ref, col_ref, vw_ref, mw_ref, lift_ref, sq_ref, vt_ref, mt_ref, fold_ref,
               cs, cr, ls, ms, ks):
    p = Place()
    met = greet(near(p) + beside(p, nd))
    c = Copies(cs, cr)
    moves = Moves(ms)
    col_in, k_in, mw_in, vw_in = (
        moves.start(a, b) for a, b in ((col_far, col_ref), (k_far, k_ref), (mw_far, mw_ref), (vw_far, vw_ref))
    )
    R = a_ref.shape[0]
    go, own_part = across_plan(p, nd, c, 18, rp_ref, far_ref)
    saves = [moves.start(rp_ref, own_part)]
    blk = blocks_of(land)
    plan = gather_plan(p, c, 0, a_ref, blk)
    start, wait = save_blocks(land, all_ref, ls)
    met()
    nu_k, nu_r = par_ref[12:13, :], par_ref[13:14, :]
    Q, W = mw_ref.shape[0], mw_ref.shape[2]

    def ready():
        go(0)()
        blk(p.s)[...] = a_ref[...]
        k_in.wait()
        for k in range(0, w_ref.shape[0], 256):
            w_ref[k : k + 256, :] = k_ref[:, k : k + 256].T
        col_in.wait()

    def turn():
        vw_in.wait()
        for k in range(0, w_ref.shape[0], 256):
            vt_ref[k : k + 256, :] = vw_ref[:, k : k + 256].T
        saves.append(moves.start(vt_ref, vt_far))

    def fold(*qs):
        def run():
            if qs[0] == 0:
                mw_in.wait()
            for q in qs:
                for k in range(0, mw_ref.shape[1], 256):
                    cols, rows = slice(k, k + 256), slice(q * W, (q + 1) * W)
                    turned = mw_ref[q, cols, :].T
                    mt_ref[rows, cols] = turned
                    part = turned.astype(F32)
                    mu = par_ref[2 + q : 3 + q, cols]
                    fold_ref[rows, cols] = ((1.0 - mu) * part).astype(BF)
                    fold_ref[(Q + q) * W : (Q + q + 1) * W, cols] = (mu * part).astype(BF)
            if qs[-1] == Q - 1:
                saves.append(moves.start(mt_ref, mt_far))
                saves.append(moves.start(fold_ref, fold_far))

        return run

    def tail_copy(k):
        rows = pl.ds(16, 2 * R - 16)
        return pltpu.make_async_copy(mixed.at[k, rows], in_ref.at[k, rows], ks.at[k])

    def work(k):
        start(k)
        n = land[k].astype(F32)
        rows = pl.ds(pl.multiple_of(k * 2 * R, 16), 2 * R)
        m = (n + shifted(n, col_ref[rows, :]) * nu_k).astype(BF)
        mixed[k] = m
        e = jnp.maximum(jnp.dot(m, w_ref[...], preferred_element_type=F32), 0.0)
        lift_ref[rows, :] = e
        sq_ref[rows, :] = (e * e).astype(BF)
        tail_copy(k).start()

    run_gather(plan, work, {0: [ready], 1: [turn], 3: [go(1, 2)], 4: [fold(0, 1)], 5: [go(3, 4)], 6: [fold(2, 3)], 7: [go(5, 6, 7)]})
    first, shift = heads_of_blocks(land, col_ref)
    head = first + shift * nu_k
    e = jnp.maximum(jnp.dot(head.astype(BF), w_ref[...], preferred_element_type=F32), 0.0)
    sq = e * e
    top = lax.broadcasted_iota(jnp.int32, (16, 1), 0) == 0
    for b in range(0, 16, 2):
        rows = slice(b * R, b * R + 16)
        mixed[b // 2, 0:16, :] = jnp.where(top, head[b : b + 1], mixed[b // 2, 0:16, :].astype(F32)).astype(BF)
        lift_ref[b * R : b * R + 1, :] = e[b : b + 1]
        sq_ref[rows, :] = jnp.where(top, sq[b : b + 1], sq_ref[rows, :].astype(F32)).astype(BF)
    saves.append(moves.start(lift_ref, lift_far))
    saves.append(moves.start(sq_ref, sq_far))
    saves.append(moves.start(mixed.at[:, pl.ds(0, 16)], in_ref.at[:, pl.ds(0, 16)]))
    n = a_ref[...].astype(F32)
    mine = lax.broadcasted_iota(jnp.int32, (16, 1), 0) == p.s
    own_first = jnp.sum(jnp.where(mine, shift, 0.0), axis=0, keepdims=True)
    here = pl.ds(pl.multiple_of(p.s * R, 16), R)
    topmost = lax.broadcasted_iota(jnp.int32, (R, 1), 0) == 0
    moved = jnp.where(topmost, own_first, shifted(n, col_ref[here, :]))
    sh_ref[...] = moved
    rin_ref[...] = (n + moved * nu_r).astype(BF)
    go(8, 9)()
    for k in range(8):
        tail_copy(k).wait()
    wait()
    for cp in saves:
        cp.wait()
    c.finish()


def key_side(nd, a, part, par, kt, cols, vw, mw, cid):
    R, C = a.shape
    T, units = 16 * R, kt.shape[0]
    Q, W = mw.shape[0], mw.shape[2]
    return pl.pallas_call(
        functools.partial(key_kernel, nd),
        out_shape=(
            jax.ShapeDtypeStruct((T, C), BF),
            jax.ShapeDtypeStruct((8, 2 * R, C), BF),
            jax.ShapeDtypeStruct((T, units), F32),
            jax.ShapeDtypeStruct((T, units), BF),
            jax.ShapeDtypeStruct((R, C), BF),
            jax.ShapeDtypeStruct((R, C), F32),
            jax.ShapeDtypeStruct((C, units), BF),
            jax.ShapeDtypeStruct((Q * W, C), BF),
            jax.ShapeDtypeStruct((2 * Q * W, C), BF),
            jax.ShapeDtypeStruct((8, T, C // 8), BF),
        ),
        in_specs=[WHOLE] * 3 + [FAR] * 4,
        out_specs=(FAR,) * 4 + (WHOLE,) * 2 + (FAR,) * 4,
        scratch_shapes=[
            VMEM((8, 2 * R, C), BF), VMEM((8, 2 * R, C), BF), VMEM((units, C), BF), VMEM((C, units), BF), VMEM(cols.shape, F32),
            VMEM((units, C), BF), VMEM(mw.shape, BF), VMEM((T, units), F32), VMEM((T, units), BF), VMEM((C, units), BF),
            VMEM((Q * W, C), BF), VMEM((2 * Q * W, C), BF),
            DMA((36,)), DMA((36,)), DMA((16,)), DMA((12,)), DMA((16,)),
        ],
        compiler_params=params(cid, 60),
        name="key_side",
    )(a, part, par, kt, cols, vw, mw)


def column_tiles(refs, tile, sem):
    C = tile.shape[2]

    def copy(u, ref):
        if len(ref.shape) == 3:
            return pltpu.make_async_copy(ref.at[u % 8], tile.at[u % 2], sem.at[u % 2])
        return pltpu.make_async_copy(ref.at[:, pl.ds(pl.multiple_of((u % 8) * C, C), C)], tile.at[u % 2], sem.at[u % 2])

    def start(u, kind):
        copy(u, refs[kind]).start()

    def wait(u, kind):
        copy(u, refs[kind]).wait()

    return start, wait


def sum_scratch(R, C):
    return [
        VMEM((8, 2, R, C), BF), VMEM((8, R, C), BF), VMEM((R, C), BF), VMEM((2, R, C), BF), VMEM((R, C), BF),
        VMEM((2, R // 2, C), BF), VMEM((2, R, C), BF),
    ]


def sum_plan(p, c, base, l_ref, w_ref, o_ref, scratch):
    pa, cb, zt, xs, zf, hv, xf = scratch
    R = o_ref.shape[0]
    H = R // 2
    core, xp, xm, zz = (p.dev(i) for i in (p.at(dc=1), p.at(dx=1), p.at(dx=-1), p.at(dz=1)))
    upper, lower = pl.ds(0, H), pl.ds(H, H)
    order = [(2, 1), (-1, 1), (1, 1), (2, 0), (0, 1), (1, 0), (-1, 0), (0, 0)]

    def send(k, src, dst, to):
        c.add(base + k, src, dst, to)
        c.start(base + k)

    def landed(k, ref):
        c.landed(base + k, ref)

    def give(i):
        k = p.at(*order[i]) // 2
        rows = l_ref[pl.ds(pl.multiple_of(k * 2 * R, 16), 2 * R), :]
        pa[i] = jnp.dot(rows, w_ref[...], preferred_element_type=F32).astype(BF).reshape(2, R, -1)
        send(i, pa.at[i, 1 - p.c], cb.at[i], core)

    def pair(i):
        landed(i, cb.at[i])
        pa[i, p.c] = (pa[i, p.c].astype(F32) + cb[i].astype(F32)).astype(BF)

    def one():
        give(0)
        give(1)
        pair(0)
        send(8, pa.at[0, p.c], zt, zz)
        give(2)
        pair(1)
        send(9, pa.at[1, p.c], xs.at[1], xm)
        pair(2)
        send(10, pa.at[2, p.c], xs.at[0], xp)

    def more():
        give(3)
        give(5)
        pair(3)
        give(6)
        pair(5)
        send(11, pa.at[5, p.c, lower], xf.at[0, lower], xp)
        give(4)
        pair(6)
        send(12, pa.at[6, p.c, upper], xf.at[1, upper], xm)
        give(7)
        pair(4)
        pair(7)

    def two():
        landed(8, zt)
        pa[3, p.c] = (pa[3, p.c].astype(F32) + zt[...].astype(F32)).astype(BF)
        send(13, pa.at[3, p.c, upper], hv.at[0], xp)
        send(14, pa.at[3, p.c, lower], hv.at[1], xm)

    def three():
        landed(9, xs.at[1])
        landed(10, xs.at[0])
        pa[4, p.c] = (pa[4, p.c].astype(F32) + xs[0].astype(F32) + xs[1].astype(F32)).astype(BF)
        send(15, pa.at[4, p.c], zf, zz)

    def four():
        landed(13, hv.at[0])
        pa[5, p.c, upper] = (pa[5, p.c, upper].astype(F32) + hv[0].astype(F32)).astype(BF)
        send(16, pa.at[5, p.c, upper], xf.at[0, upper], xp)
        landed(14, hv.at[1])
        pa[6, p.c, lower] = (pa[6, p.c, lower].astype(F32) + hv[1].astype(F32)).astype(BF)
        send(17, pa.at[6, p.c, lower], xf.at[1, lower], xm)

    def five():
        landed(11, xf.at[0, lower])
        landed(12, xf.at[1, upper])
        landed(15, zf)
        o_ref[...] = pa[7, p.c].astype(F32) + zf[...].astype(F32)

    def six():
        landed(16, xf.at[0, upper])
        landed(17, xf.at[1, lower])
        o_ref[...] = o_ref[...] + xf[0].astype(F32) + xf[1].astype(F32)

    return [one, more, two, three, four, five, six]


def value_kernel(rin_ref, g_ref, hid_ref, l_far, w_far, vt_far, lift_far, far_ref,
                 res_ref, gf_ref, rc_ref, ge_far, get_far, vg_far, *rest):
    scratch = rest[:7]
    (o_ref, f_ref, gate_ref, gkv, land, tile, l_ref, w_ref, vt_ref, lift_ref, ge_ref, get_ref, st_ref, acc,
     cs, cr, ss, rs, ts, ms) = rest[7:]
    p = Place()
    met = greet(near(p))
    c = Copies(cs, cr)
    moves = Moves(ms)
    R = o_ref.shape[0]
    T, U = l_ref.shape
    W = gf_ref.shape[2]
    C = tile.shape[2]
    fetch, have = column_tiles((far_ref,), tile, ts)
    l_in, w_in, vt_in, lift_in = (
        moves.start(a, b) for a, b in ((l_far, l_ref), (w_far, w_ref), (vt_far, vt_ref), (lift_far, lift_ref))
    )
    fetch(0, 0)
    sums = sum_plan(p, c, 0, l_ref, w_ref, o_ref, scratch)
    blk = blocks_of(land)
    plan = gather_plan(p, c, 18, gkv, blk)
    swap = Swap(p, lambda i: gf_ref.at[i], rc_ref, ss, rs)
    met()
    l_in.wait()
    w_in.wait()
    sums[0]()

    def unit(d, unused):
        pl.when(d < 7)(lambda: fetch(d + 1, 0))
        have(d, 0)
        cols = pl.ds(pl.multiple_of(d * C, C), C)
        part = lax.dot_general(rin_ref[:, cols], tile[d % 2], (NT, ((), ())), preferred_element_type=F32)

        @pl.when(d == 0)
        def _():
            f_ref[...] = part

        @pl.when(d > 0)
        def _():
            f_ref[...] += part

        return 0

    lax.fori_loop(0, 8, unit, 0)
    for s in range(16):
        at = ((s % 2) * 8 + s // 2) * W
        cols = slice(s * W, (s + 1) * W)
        gate = sigmoid(f_ref[:, at : at + W])
        gate_ref[:, cols] = gate
        gkv[:, cols] = (g_ref[:, cols].astype(F32) * gate).astype(BF)
    plan[0]()
    sums[1]()
    blk(p.s)[...] = gkv[...]
    acc[...] = jnp.zeros_like(acc)
    for r in range(0, T, 256):
        st_ref[:, r : r + 256] = l_ref[r : r + 256, :].T
    vt_in.wait()
    lift_in.wait()

    saves = []

    def work(k):
        rows = pl.ds(pl.multiple_of(k * 2 * R, 16), 2 * R)
        cols = pl.ds(pl.multiple_of(k * 2 * R, 128), 2 * R)
        gs = jnp.dot(land[k], vt_ref[...], preferred_element_type=F32)
        ge = gs * 2.0 * lift_ref[rows, :]
        ge_ref[rows, :] = ge.astype(BF)
        get_ref[:, cols] = ge.T.astype(BF)
        acc[...] += jnp.dot(st_ref[:, cols], land[k], preferred_element_type=F32)
        saves.append(moves.start(ge_ref.at[rows], ge_far.at[rows]))
        saves.append(moves.start(get_ref.at[:, cols], get_far.at[:, cols]))

    ready = plan[1]() + plan[2]()
    work(ready.pop(0))
    sums[2]()
    sums[3]()
    ready += plan[3]() + plan[4]()
    work(ready.pop(0))
    sums[4]()
    ready += plan[5]()
    work(ready.pop(0))
    sums[5]()
    ready += plan[6]()
    work(ready.pop(0))
    sums[6]()
    kv, gate = o_ref[...], gate_ref[...]
    gf = g_ref[...].astype(F32) * kv * (gate * (1.0 - gate))
    for s in range(16):
        gf_ref[s] = gf[:, s * W : (s + 1) * W].astype(BF)
    swap.all(swap.give)
    res_ref[...] = (hid_ref[...] + (gate * kv).astype(BF).astype(F32)).astype(BF)
    for n in range(7, 10):
        ready += plan[n]()
        work(ready.pop(0))
    for k in ready:
        work(k)
    for d in range(8):
        rows = slice((d % 4) * U, (d % 4 + 1) * U)
        tile[d // 4, rows, :] = acc[:, d * C : (d + 1) * C].astype(BF)
        saves.append(moves.start(tile.at[d // 4, pl.ds((d % 4) * U, U)], vg_far.at[d]))
    swap.all(swap.take)
    for cp in saves:
        cp.wait()
    swap.all(swap.sent)
    c.finish()


def value_side(rin, g, hidden, l, w, vt, lift, far, cid):
    R, C = hidden.shape
    T, U = l.shape
    W = C // 16
    return pl.pallas_call(
        value_kernel,
        out_shape=(
            jax.ShapeDtypeStruct((R, C), BF),
            jax.ShapeDtypeStruct((16, R, W), BF),
            jax.ShapeDtypeStruct((16, R, W), BF),
            jax.ShapeDtypeStruct((T, U), BF),
            jax.ShapeDtypeStruct((U, T), BF),
            jax.ShapeDtypeStruct((8, U, C // 8), BF),
        ),
        in_specs=[WHOLE] * 3 + [FAR] * 5,
        out_specs=(WHOLE,) * 3 + (FAR,) * 3,
        scratch_shapes=sum_scratch(R, C)
        + [VMEM((R, C), F32), VMEM((R, C), F32), VMEM((R, C), F32), VMEM((R, C), BF), VMEM((8, 2 * R, C), BF), VMEM((2, T, C // 8), BF)]
        + [VMEM((T, U), BF), VMEM((U, C), BF), VMEM((C, U), BF), VMEM((T, U), F32)]
        + [VMEM((T, U), BF), VMEM((U, T), BF), VMEM((U, T), BF), VMEM((U, C), F32)]
        + [DMA((36,)), DMA((36,)), DMA((16,)), DMA((16,)), DMA((2,)), DMA((28,))],
        compiler_params=params(cid, 62),
        name="value_side",
    )(rin, g, hidden, l, w, vt, lift, far)


def dp_scratch(J, C):
    return [VMEM((2, 2, J // 2, C), BF), VMEM((2, 2, J // 2, C), BF), VMEM((2, 2, J, C), BF), VMEM((2, J, C), BF)]


def dp_plan(p, nd, c, base, g_ref, o_ref, scratch):
    hv, stage, xf, zb = scratch
    J = g_ref.shape[1]
    H = J // 2
    up, lo = pl.ds(0, H), pl.ds(H, H)
    ny = nd // 2
    y, zl = p.dp // 2, p.dp % 2
    yp, ym, yo = (y + 1) % ny, (y + ny - 1) % ny, (y + 2) % ny

    def pay(at, rows):
        return g_ref.at[pl.ds(2 * at, 2), rows]

    to_p, to_m, to_z = (2 * yp + zl, p.s), (2 * ym + zl, p.s), (2 * y + 1 - zl, p.s)
    c.add(base, pay(yo, up), hv.at[0], to_p)
    c.add(base + 1, pay(yo, lo), hv.at[1], to_m)
    c.add(base + 2, pay(yp, lo), xf.at[0, :, lo], to_p)
    c.add(base + 3, pay(ym, up), xf.at[1, :, up], to_m)
    c.add(base + 4, stage.at[0], xf.at[0, :, up], to_p)
    c.add(base + 5, stage.at[1], xf.at[1, :, lo], to_m)
    c.add(base + 6, zb.at[0], zb.at[1], to_z)

    def one():
        c.start(base, base + 1)

    def two():
        c.landed(base, hv.at[0])
        stage[0] = (g_ref[pl.ds(2 * yp, 2), up].astype(F32) + hv[0].astype(F32)).astype(BF)
        c.start(base + 4)
        c.landed(base + 1, hv.at[1])
        stage[1] = (g_ref[pl.ds(2 * ym, 2), lo].astype(F32) + hv[1].astype(F32)).astype(BF)
        c.start(base + 5, base + 2, base + 3)

    def total(which):
        return g_ref[2 * y + which].astype(F32) + xf[0, which].astype(F32) + xf[1, which].astype(F32)

    def three():
        c.landed(base + 2, xf.at[0, :, lo])
        c.landed(base + 3, xf.at[1, :, up])
        c.landed(base + 4, xf.at[0, :, up])
        c.landed(base + 5, xf.at[1, :, lo])
        zb[0] = total(1 - zl).astype(BF)
        c.start(base + 6)
        o_ref[0] = total(zl)

    def four():
        c.landed(base + 6, zb.at[1])
        o_ref[0] += zb[1].astype(F32)

    return [one, two, three, four]


def no_sums(g_ref, o_ref):
    def copy():
        o_ref[...] = g_ref[...].astype(F32)

    return [lambda: None] * 3 + [copy]


def key_back_kernel(rc_ref, gf_ref, par_ref, g_ref, l_far, w_far, lt_far, col_far, hid_far, sh_far, vg_far,
                    in_hbm, n2_hbm, far_ref, out_far, gh_ref, ghb_ref, rows_ref, gg_far, gz_ref, *rest):
    scratch = rest[:7]
    (o_ref, rt, gfp, ga_ref, gzp, halo, tile, strip, l_ref, w_ref, lt_ref, col_ref, hid_ref, sh_ref, gg_ref,
     cs, cr, ss, rs, ts, os, ms) = rest[7:]
    p = Place()
    met = greet(near(p) + [p.dev((p.s + 1) % 16), p.dev((p.s + 15) % 16)])
    c = Copies(cs, cr)
    moves = Moves(ms)
    T, U = l_ref.shape
    R, width = o_ref.shape
    W = rc_ref.shape[2]
    C = tile.shape[2]
    l_in, w_in, lt_in, col_in, hid_in, sh_in, vg_in = (
        moves.start(a, b)
        for a, b in (
            (l_far, l_ref), (w_far, w_ref), (lt_far, lt_ref), (col_far, col_ref), (hid_far, hid_ref), (sh_far, sh_ref),
            (vg_far, gg_ref.at[:, pl.ds(0, U)]),
        )
    )
    fetch, have = column_tiles((in_hbm, n2_hbm, far_ref), tile, ts)
    fetch(0, 0)

    def strip_copy(n):
        return pltpu.make_async_copy(out_far.at[:, pl.ds(pl.multiple_of(n * 2 * W, 16), 2 * W)], strip.at[n % 2], os.at[n % 2])

    c.add(18, halo.at[0], halo.at[1], p.dev((p.s + 15) % 16))
    sums = sum_plan(p, c, 0, l_ref, w_ref, o_ref, scratch)
    swap = Swap(p, lambda i: gzp.at[i], gz_ref, ss, rs)
    met()
    nu_k, nu_r = par_ref[12:13, :], par_ref[13:14, :]

    def turn():
        last = lax.broadcasted_iota(jnp.int32, (R, 1), 0) == R - 1
        for b in range(16):
            part = rc_ref[b].astype(F32)
            after = rc_ref[b + 1, 0:16, :].astype(F32)[0:1] if b < 15 else jnp.zeros((1, W), F32)
            col = col_ref[b * R : (b + 1) * R, :]
            moved = jnp.where(last, after, pltpu.roll(part, R - 1, 0)) * equal(col[:, 0:1], col[:, 2:3])
            rt[0:W, b * R : (b + 1) * R] = part.T.astype(BF)
            rt[W:, b * R : (b + 1) * R] = moved.T.astype(BF)
        for s in range(16):
            at = ((s % 2) * 8 + s // 2) * W
            gfp[:, at : at + W] = gf_ref[s]

    def units(kind, lo, hi):
        def unit(d, unused):
            u = 8 * kind + d
            if hi < 8:
                fetch(u + 1, kind)
            else:
                pl.when(d < 7)(lambda: fetch(u + 1, kind))
                if kind < 2:
                    pl.when(d == 7)(lambda: fetch(u + 1, kind + 1))
            have(u, kind)
            rhs = tile[d % 2]
            cols = pl.ds(pl.multiple_of(d * C, C), C)
            if kind == 0:
                gg_ref[d, U : 2 * U, :] = jnp.dot(lt_ref[...], rhs, preferred_element_type=F32).astype(BF)
            elif kind == 1:
                out = jnp.dot(rt[...], rhs, preferred_element_type=F32)
                gg_ref[d, 2 * U :, :] = (out[:W] + par_ref[13:14, cols] * (out[W:] - out[:W])).astype(BF)
            else:
                ga_ref[:, cols] = jnp.dot(gfp[...], rhs, preferred_element_type=F32)
            return 0

        lax.fori_loop(lo, hi, unit, 0)

    l_in.wait()
    w_in.wait()
    sums[0]()
    sums[1]()
    lt_in.wait()
    units(0, 0, 4)
    sums[2]()
    sums[3]()
    units(0, 4, 8)
    sums[4]()
    col_in.wait()
    turn()
    units(1, 0, 8)
    vg_in.wait()
    saves = [moves.start(gg_ref, gg_far)]
    sums[5]()
    units(2, 0, 8)
    strip_copy(0).start()
    hid_in.wait()
    sh_in.wait()
    unused, scale, normed = norm_parts(hid_ref[...])
    sums[6]()
    ga_k, ga_r, shift = o_ref[...], ga_ref[...], sh_ref[...]
    here = pl.ds(pl.multiple_of(p.s * R, 16), R)
    col = col_ref[here, :]
    moved = (ga_k * nu_k + ga_r * nu_r) * equal(col[:, 0:1], col[:, 1:2])
    halo[0] = moved[0:8]
    c.start(18)
    held = ga_k - ga_k * nu_k + (ga_r - ga_r * nu_r)
    rows_ref[...] = jnp.zeros_like(rows_ref)
    rows_ref[2:3, :] = jnp.sum(ga_k * shift, axis=0, keepdims=True)
    rows_ref[3:4, :] = jnp.sum(ga_r * shift, axis=0, keepdims=True)
    c.landed(18, halo.at[1])
    last = lax.broadcasted_iota(jnp.int32, (R, 1), 0) == R - 1
    grad = held + jnp.where(last, halo[1, 0:1, :], pltpu.roll(moved, R - 1, 0))
    gh = g_ref[...].astype(F32) + norm_back(normed, scale, grad * par_ref[10:11, :])
    gh_ref[...] = gh
    ghb_ref[...] = gh.astype(BF)

    def back_out(n, unused):
        pl.when(n < 7)(lambda: strip_copy(n + 1).start())
        strip_copy(n).wait()
        part = lax.dot_general(ghb_ref[:, 0:C], strip[n % 2, 0], (NT, ((), ())), preferred_element_type=F32)
        for d in range(1, 8):
            part = part + lax.dot_general(
                ghb_ref[:, d * C : (d + 1) * C], strip[n % 2, d], (NT, ((), ())), preferred_element_type=F32
            )
        for k in range(2):
            to = 2 * ((2 * n + k) % 8) + (2 * n + k) // 8
            gzp[to] = part[:, k * W : (k + 1) * W].astype(BF)
            swap.give(to)
        return 0

    lax.fori_loop(0, 8, back_out, 0)
    rows_ref[0:1, :] = jnp.sum(grad * normed, axis=0, keepdims=True)
    rows_ref[1:2, :] = jnp.sum(grad, axis=0, keepdims=True)
    for cp in saves:
        cp.wait()
    swap.all(swap.take)
    swap.all(swap.sent)
    c.finish()


def key_back(rc, gf, par, g, l, w, lt, cols, hidden, sh, vg, key_in, n2_all, far, out_far, cid):
    R, C = hidden.shape
    T, U, W = 16 * R, l.shape[1], rc.shape[2]
    return pl.pallas_call(
        key_back_kernel,
        out_shape=(
            jax.ShapeDtypeStruct((R, C), F32),
            jax.ShapeDtypeStruct((R, C), BF),
            jax.ShapeDtypeStruct((8, C), F32),
            jax.ShapeDtypeStruct((8, 2 * U + W, C // 8), BF),
            jax.ShapeDtypeStruct((16, R, W), BF),
        ),
        in_specs=[WHOLE] * 4 + [FAR] * 11,
        out_specs=(WHOLE,) * 3 + (FAR, WHOLE),
        scratch_shapes=sum_scratch(R, C)
        + [VMEM((R, C), F32), VMEM((2 * W, T), BF), VMEM((R, C), BF), VMEM((R, C), F32), VMEM((16, R, W), BF), VMEM((2, 8, C), F32)]
        + [VMEM((2, T, C // 8), BF), VMEM((2, 8, 2 * W, C // 8), BF), VMEM((T, U), BF), VMEM((U, C), BF), VMEM((U, T), BF)]
        + [VMEM(cols.shape, F32), VMEM((R, C), F32), VMEM((R, C), F32), VMEM((8, 2 * U + W, C // 8), BF)]
        + [DMA((19,)), DMA((19,)), DMA((16,)), DMA((16,)), DMA((2,)), DMA((2,)), DMA((8,))],
        compiler_params=params(cid, 60),
        name="key_back",
    )(rc, gf, par, g, l, w, lt, cols, hidden, sh, vg, key_in, n2_all, far, out_far)


def time_back_kernel(nd, gh_ref, gz_ref, par_ref, row_ref, bound_ref, early_far, x_far, o_far, s_far, col_far, zt_far, mixt_far, n1_hbm,
                     g_far, gg_far, sums_ref, mug_ref, dp_ref,
                     tab, grad_state, acc, carry, land, turned, tile, vec, early_ref, x_ref, o_ref, s_ref, col_ref, zt_ref, mixt_ref,
                     g_ref, gg_ref, d0, d1, d2, d3, cs, cr, ts, ms):
    p = Place()
    met = greet(near(p) + beside(p, nd))
    c = Copies(cs, cr)
    moves = Moves(ms)
    W = vec.shape[1]
    chunks, L = row_ref.shape[0], row_ref.shape[2]
    C = tile.shape[2]
    J = early_ref.shape[1]
    early_in, x_in, o_in, s_in, col_in, zt_in, mixt_in, left_in = (
        moves.start(a, b)
        for a, b in (
            (early_far.at[:, pl.ds(0, J)], early_ref), (x_far, x_ref), (o_far, o_ref), (s_far, s_ref), (col_far, col_ref), (zt_far, zt_ref),
            (mixt_far, mixt_ref), (early_far.at[:, pl.ds(J, early_far.shape[1] - J)], gg_ref.at[:, pl.ds(5 * W, J - 5 * W)]),
        )
    )
    fetch, have = column_tiles((n1_hbm,), tile, ts)
    fetch(0, 0)
    blk = rows_of(land)
    plan = gather_plan(p, c, 0, gh_ref, blk)
    sums = dp_plan(p, nd, c, 18, early_ref, dp_ref, (d0, d1, d2, d3)) if nd > 1 else no_sums(early_ref, dp_ref)
    own_vectors(p, par_ref, vec)
    met()
    plan[0]()
    early_in.wait()
    sums[0]()
    blk(p.s)[...] = gh_ref[...]
    when = {6: [plan[1], plan[2]], 7: [sums[1]], 11: [plan[3], plan[4]], 14: [plan[5], plan[6], plan[7]]}
    for cp in (x_in, o_in, s_in, col_in):
        cp.wait()
    chunk = back_chunk(x_ref, o_ref, s_ref, gz_ref, col_ref, row_ref, bound_ref, vec, g_ref, sums_ref, tab, grad_state, acc, carry, turned)

    def step(n, unused):
        chunk(n)
        for at, parts in when.items():
            @pl.when(n == at)
            def _():
                for part in parts:
                    part()
        return 0

    lax.fori_loop(0, chunks, step, 0)
    saves = [moves.start(g_ref, g_far)]
    back_finish(vec, sums_ref, acc, L)
    mug_ref[...] = jnp.zeros_like(mug_ref)
    mixt_in.wait()

    def mix(d, unused):
        pl.when(d < 7)(lambda: fetch(d + 1, 0))
        have(d, 0)
        rhs = tile[d % 2]
        cols = pl.ds(pl.multiple_of(d * C, C), C)
        a = jnp.dot(turned[: 4 * W, :], rhs, preferred_element_type=F32)
        b = jnp.dot(turned[4 * W :, :], rhs, preferred_element_type=F32)
        for q in range(4):
            rows = slice(q * W, (q + 1) * W)
            diff = b[rows] - a[rows]
            gg_ref[d, rows, :] = (a[rows] + par_ref[2 + q : 3 + q, cols] * diff).astype(BF)
            mug_ref[q : q + 1, cols] = jnp.sum(mixt_ref[rows, cols].astype(F32) * diff, axis=0, keepdims=True)
        return 0

    lax.fori_loop(0, 4, mix, 0)
    plan[8]()
    sums[2]()
    lax.fori_loop(4, 8, mix, 0)
    zt_in.wait()
    plan[9]()

    def out(d, unused):
        cols = pl.ds(pl.multiple_of(d * C, C), C)
        gg_ref[d, 4 * W : 5 * W, :] = jnp.dot(zt_ref[...], land[:, cols], preferred_element_type=F32).astype(BF)
        return 0

    lax.fori_loop(0, 8, out, 0)
    left_in.wait()
    saves.append(moves.start(gg_ref, gg_far))
    sums[3]()
    for cp in saves:
        cp.wait()
    c.finish()


def time_back(nd, gh, gz, par, rows, bounds, early, x, o, states, cols, zt, mixt, n1_all, cid):
    T, W = o.shape
    L = rows.shape[2]
    R, C = gh.shape
    J = (early.shape[1] + 5 * W) // 2
    return pl.pallas_call(
        functools.partial(time_back_kernel, nd),
        out_shape=(
            jax.ShapeDtypeStruct((T, 8 * W), BF),
            jax.ShapeDtypeStruct((8, J, C // 8), BF),
            jax.ShapeDtypeStruct((8, W), F32),
            jax.ShapeDtypeStruct((4, C), F32),
            jax.ShapeDtypeStruct((8 // nd, J, C // 8), F32),
        ),
        in_specs=[WHOLE] * 4 + [pl.BlockSpec(memory_space=pltpu.SMEM)] + [FAR] * 8,
        out_specs=(FAR,) * 2 + (WHOLE,) * 3,
        scratch_shapes=[
            VMEM((4, L, W), F32), VMEM((W, W), F32), VMEM((W, W), F32), VMEM((8, 4 * W), F32),
            VMEM((T, C), BF), VMEM((8 * W, T), BF), VMEM((2, T, C // 8), BF), VMEM((8 + W, W), F32),
            VMEM((8, J, C // 8), BF), VMEM(x.shape, F32), VMEM((T, W), F32), VMEM(states.shape, F32), VMEM(cols.shape, F32),
            VMEM((W, T), BF), VMEM(mixt.shape, BF), VMEM((T, 8 * W), BF), VMEM((8, J, C // 8), BF),
        ]
        + dp_scratch(J, C // 8)
        + [DMA((25,)), DMA((25,)), DMA((2,)), DMA((10,))],
        compiler_params=params(cid, 60),
        name="time_back",
    )(gh, gz, par, rows, bounds, early, x, o, states, cols, zt, mixt, n1_all)


def last_kernel(nd, x_ref, par_ref, mug_ref, head_ref, norm_ref, gg_far, l_far, w_far, gh_far, ig_ref, dp_ref, v_ref, *rest):
    scratch = rest[:7]
    o_ref, d0, d1, d2, d3, tv, b1, t1, b2, gg_ref, l_ref, w_ref, gh_ref, cs, cr, ms = rest[7:]
    p = Place()
    met = greet(near(p) + beside(p, nd))
    c = Copies(cs, cr)
    moves = Moves(ms)
    gg_in, w_in, l_in, gh_in = (
        moves.start(a, b) for a, b in ((gg_far, gg_ref), (w_far, w_ref), (l_far, l_ref), (gh_far, gh_ref))
    )
    sums = dp_plan(p, nd, c, 18, gg_ref, dp_ref, (d0, d1, d2, d3)) if nd > 1 else no_sums(gg_ref, dp_ref)
    steps = sum_plan(p, c, 0, l_ref, w_ref, o_ref, scratch)
    W = head_ref.shape[1]
    tv[...] = jnp.zeros_like(tv)
    tv[2:6, :] = mug_ref[...]
    tv[6:10, pl.ds(pl.multiple_of(p.s * W, 128), W)] = head_ref[0:4, :]
    tv[10:14, :] = norm_ref[0:4, :]
    met()
    gg_in.wait()
    sums[0]()
    l_in.wait()
    w_in.wait()
    steps[0]()
    steps[1]()
    sums[1]()
    steps[2]()
    steps[3]()
    steps[4]()
    sums[2]()
    unused, scale, normed = norm_parts(x_ref[...].astype(F32))
    gh_in.wait()
    steps[5]()
    steps[6]()
    gn = o_ref[...]
    tv[0:1, :] = jnp.sum(gn * normed, axis=0, keepdims=True)
    tv[1:2, :] = jnp.sum(gn, axis=0, keepdims=True)
    sums[3]()
    C = b1.shape[2]
    for k in range(1, nd):
        to = (p.dp + k) % nd
        c.add(24 + k, tv.at[:, pl.ds(pl.multiple_of(to * C, 128), C)], b1.at[k - 1], (to, p.s))
        c.start(24 + k)
    ig_ref[...] = gh_ref[...] + norm_back(normed, scale, gn * par_ref[0:1, :])
    total = tv[:, pl.ds(pl.multiple_of(p.dp * C, 128), C)]
    for k in range(1, nd):
        c.landed(24 + k, b1.at[k - 1])
        total = total + b1[k - 1]
    t1[...] = total
    for k in range(1, 16):
        c.add(31 + k, t1, b2.at[k - 1], p.dev((p.s + k) % 16))
        c.start(31 + k)
    for k in range(1, 16):
        c.landed(31 + k, b2.at[k - 1])
        total = total + b2[k - 1]
    v_ref[...] = total
    c.finish()


def last_sums(nd, x, par, mug, head, norm, gg, l, w, gh, cid):
    R, C = x.shape
    J = gg.shape[1]
    piece = (16, C // nd)
    return pl.pallas_call(
        functools.partial(last_kernel, nd),
        out_shape=(jax.ShapeDtypeStruct((R, C), F32), jax.ShapeDtypeStruct((8 // nd, J, C // 8), F32), jax.ShapeDtypeStruct(piece, F32)),
        in_specs=[WHOLE] * 5 + [FAR] * 4,
        out_specs=(WHOLE,) * 3,
        scratch_shapes=sum_scratch(R, C)
        + [VMEM((R, C), F32)]
        + dp_scratch(J, C // 8)
        + [VMEM((16, C), F32), VMEM((max(nd - 1, 1),) + piece, F32), VMEM(piece, F32), VMEM((15,) + piece, F32)]
        + [VMEM(gg.shape, BF), VMEM(l.shape, BF), VMEM(w.shape, BF), VMEM((R, C), F32)]
        + [DMA((47,)), DMA((47,)), DMA((4,))],
        compiler_params=params(cid, 60),
        name="last_sums",
    )(x, par, mug, head, norm, gg, l, w, gh)


def body(nd, inputs, cotangent, mix_weights, out_weight, key_weight, value_weight, recept_weight, vectors, segment_ids):
    tokens, width = inputs.shape
    group = segment_ids.shape[0]
    cols = mix_weights.shape[2]
    units = key_weight.shape[1]
    s = lax.axis_index("sp")
    ring = group // tokens
    chunks = group // CHUNK

    edge = jnp.full((1,), -1.0, F32)
    seg = jnp.concatenate([edge, segment_ids.astype(F32), edge])
    tok_cols = jnp.stack([seg[1:-1], seg[:-2], seg[2:]], axis=1)
    tok_rows = seg[1:-1].reshape(chunks, 1, CHUNK)
    ends = seg[: group + 1 : CHUNK]
    bounds = jnp.stack([ends, jnp.concatenate([(ends[1:] == ends[:-1]).astype(F32), edge])])

    n1_all, projected, z_t, mixed_time, states, hidden, n2, recept_part, out_far = time_forward(
        nd, inputs, vectors, tok_rows, bounds, mix_weights, out_weight, recept_weight, tok_cols, 0
    )
    n2_all, key_in, lifted, squared, recept_in, shift, value_t, mixt, folded, recept_far = key_side(
        nd, n2, recept_part, vectors, key_weight.T, tok_cols, value_weight, mix_weights, 1
    )
    result, grad_recept, recept_cols, grad_key, grad_key_t, value_grad = value_side(
        recept_in, cotangent, hidden, squared, value_weight, value_t, lifted, recept_far, 2
    )
    grad_hidden, grad_hidden_b, norm_rows, early, gz = key_back(
        recept_cols, grad_recept, vectors, cotangent, grad_key, key_weight.T, grad_key_t, tok_cols, hidden, shift, value_grad,
        key_in.reshape(group, width), n2_all, recept_far, out_far, 3,
    )
    grads_two, late, head_rows, mu_rows, early_sum = time_back(
        nd, grad_hidden_b, gz, vectors, tok_rows, bounds, early, projected, mixed_time, states, tok_cols, z_t, mixt, n1_all, 4
    )
    input_grad, late_sum, vector_sum = last_sums(
        nd, inputs, vectors, mu_rows, head_rows, norm_rows, late, grads_two, folded, grad_hidden, 5
    )
    piece = width // (nd * ring)
    vectors_grad = lax.dynamic_slice_in_dim(vector_sum[:14], s * piece, piece, 1)

    def columns(part):
        return part.transpose(1, 0, 2).reshape(part.shape[1], width // nd)

    early_sum, late_sum = columns(early_sum), columns(late_sum)
    rest = jnp.concatenate([early_sum[units:], late_sum[5 * cols :]], axis=0)
    return (
        result,
        input_grad,
        late_sum[: 4 * cols].reshape(4, cols, width // nd).transpose(0, 2, 1),
        late_sum[4 * cols : 5 * cols],
        rest[:units].T,
        early_sum[:units],
        rest[units:].T,
        vectors_grad,
    )


def solution(mesh):
    placed = (
        P(("dp", "sp"), None),
        P(("dp", "sp"), None),
        P(None, None, "sp"),
        P("sp", None),
        P(None, "sp"),
        P("sp", None),
        P(None, "sp"),
        P(),
        P("dp"),
    )
    return jax.shard_map(
        functools.partial(body, mesh.shape["dp"]),
        mesh=mesh,
        in_specs=placed,
        out_specs=(
            P(("dp", "sp"), None),
            P(("dp", "sp"), None),
            P(None, "dp", "sp"),
            P("sp", "dp"),
            P("dp", "sp"),
            P("sp", "dp"),
            P("dp", "sp"),
            P(None, ("dp", "sp")),
        ),
        check_vma=False,
    )
```

```python
import functools

import jax
import jax.numpy as jnp
from jax import lax
from jax.experimental import pallas as pl
from jax.experimental.pallas import tpu as pltpu
from jax.sharding import PartitionSpec as P

MESH = pl.DeviceIdType.MESH
VMEM = pltpu.VMEM
DMA = pltpu.SemaphoreType.DMA
BF = jnp.bfloat16
F32 = jnp.float32

ATTENTION_WIDTH = 64
CHUNK = 128
WHOLE = pl.BlockSpec(memory_space=VMEM)
FAR = pl.BlockSpec(memory_space=pl.ANY)


class Place:
    def __init__(self):
        self.dp = lax.axis_index("dp")
        s = lax.axis_index("sp")
        self.s = s
        self.x, self.z, self.c = s // 4, (s // 2) % 2, s % 2

    def at(self, dx=0, dz=0, dc=0):
        return ((self.x + dx) % 4) * 4 + ((self.z + dz) % 2) * 2 + (self.c + dc) % 2

    def dev(self, s):
        return (self.dp, s)


class Across:
    def __init__(self, p, nd):
        self.p, self.ny = p, nd // 2
        self.x, self.z, self.c = p.dp // 2, p.dp % 2, p.c
        self.s = p.dp * 2 + p.c

    def at(self, dx=0, dz=0, dc=0):
        return ((self.x + dx) % self.ny) * 4 + ((self.z + dz) % 2) * 2 + (self.c + dc) % 2

    def dev(self, i):
        return (i // 2, self.p.s - self.p.c + i % 2)


class Copies:
    def __init__(self, ss, rs):
        self.ss, self.rs, self.items = ss, rs, {}

    def add(self, k, src, dst, to):
        self.items[k] = (src, dst, to)

    def make(self, k, src, dst, to):
        return pltpu.make_async_remote_copy(
            src_ref=src, dst_ref=dst, send_sem=self.ss.at[k], recv_sem=self.rs.at[k], device_id=to, device_id_type=MESH
        )

    def start(self, *ks):
        for k in ks:
            self.make(k, *self.items[k]).start()

    def landed(self, k, ref):
        self.make(k, ref, ref, self.items[k][2]).wait_recv()

    def finish(self):
        for k in self.items:
            self.make(k, *self.items[k]).wait_send()


def greet(devices):
    barrier = pltpu.get_barrier_semaphore()
    for device in devices:
        pl.semaphore_signal(barrier, inc=1, device_id=device, device_id_type=MESH)
    return lambda: pl.semaphore_wait(barrier, len(devices))


def near(p):
    return [p.dev(p.at(dc=1)), p.dev(p.at(dx=1)), p.dev(p.at(dx=-1)), p.dev(p.at(dz=1))]


def beside(p, nd):
    y, zl, ny = p.dp // 2, p.dp % 2, nd // 2
    if nd == 1:
        return []
    return [(2 * ((y + 1) % ny) + zl, p.s), (2 * ((y + ny - 1) % ny) + zl, p.s), (2 * y + 1 - zl, p.s)]


def chip_mates(p):
    return [p.dev(p.at(dx, dz)) for dz in range(2) for dx in range(4)][1:]


def ring_mates(p):
    return [p.dev((p.s + k) % 16) for k in range(1, 16)]


def dp_mates(p, nd):
    return [((p.dp + k) % nd, p.s) for k in range(1, nd)]


def params(cid, mib):
    return pltpu.CompilerParams(collective_id=cid, has_side_effects=True, vmem_limit_bytes=mib * 2**20)


class Swap:
    def __init__(self, p, src, dst, ss, rs):
        self.p, self.src, self.dst, self.ss, self.rs = p, src, dst, ss, rs

    def make(self, src, dst, at, to):
        return pltpu.make_async_remote_copy(
            src_ref=src, dst_ref=dst, send_sem=self.ss.at[to], recv_sem=self.rs.at[at], device_id=self.p.dev(to), device_id_type=MESH
        )

    def give(self, i):
        @pl.when(i != self.p.s)
        def _():
            self.make(self.src(i), self.dst.at[self.p.s], self.p.s, i).start()

        @pl.when(i == self.p.s)
        def _():
            self.dst[self.p.s] = self.src(i)[...]

    def take(self, i):
        @pl.when(i != self.p.s)
        def _():
            self.make(self.dst.at[i], self.dst.at[i], i, i).wait_recv()

    def sent(self, i):
        @pl.when(i != self.p.s)
        def _():
            self.make(self.src(i), self.dst.at[self.p.s], self.p.s, i).wait_send()

    def all(self, act):
        def step(i, unused):
            act(i)
            return 0

        lax.fori_loop(0, 16, step, 0)


class Moves:
    def __init__(self, sem):
        self.sem, self.n = sem, 0

    def start(self, src, dst):
        cp = pltpu.make_async_copy(src, dst, self.sem.at[self.n])
        self.n += 1
        cp.start()
        return cp


def equal(a, b):
    return jnp.where(a == b, 1.0, 0.0)


def blocks_of(land):
    R = land.shape[1] // 2

    def blk(i, half=None):
        rows = R if half is None else R // 2
        return land.at[i // 2, pl.ds(pl.multiple_of((i % 2) * R + (half or 0) * rows, 16), rows)]

    return blk


def rows_of(land):
    R = land.shape[0] // 16

    def blk(i, half=None):
        rows = R if half is None else R // 2
        return land.at[pl.ds(pl.multiple_of(i * R + (half or 0) * rows, 16), rows)]

    return blk


def matrix_blocks(land):
    K = land.shape[1] // 2

    def blk(i, half=None):
        rows = K if half is None else K // 2
        return land.at[i // 2, pl.ds(pl.multiple_of((i % 2) * K + (half or 0) * rows, 16), rows)]

    return blk


def gather_plan(p, c, base, a_ref, blk, around=False):
    core, xp, xm, zz = p.at(dc=1), p.at(dx=1), p.at(dx=-1), p.at(dz=1)
    d2, zxm, zxp, zd2 = p.at(dx=2), p.at(dx=-1, dz=1), p.at(dx=1, dz=1), p.at(dx=2, dz=1)
    up, lo = 0, 1

    def relay(k, ref, to):
        c.add(base + k, ref, ref, p.dev(to))

    for k, to in enumerate((xp, xm, zz, core)):
        c.add(base + k, a_ref, blk(p.s), p.dev(to))
    relay(4, blk(xm, up), xp)
    relay(5, blk(xp, lo), xm)
    relay(6, blk(xm), core)
    relay(7, blk(xp), core)
    relay(8, blk(zz), xp)
    relay(9, blk(zz), xm)
    relay(10, blk(zz), core)
    if around:
        relay(11, blk(zxm, up), xp)
        relay(12, blk(zxp, lo), xm)
    else:
        relay(11, blk(d2, up), zz)
        relay(12, blk(d2, lo), zz)
    relay(13, blk(d2), core)
    relay(14, blk(zxm), core)
    relay(15, blk(zxp), core)
    relay(16, blk(zd2, up), core)
    relay(17, blk(zd2, lo), core)

    def start(*ks):
        c.start(*(base + k for k in ks))

    def landed(k, ref):
        c.landed(base + k, ref)

    def other(**k):
        return p.at(dc=1, **k)

    def one():
        start(0, 1, 2, 3)
        return []

    def own():
        landed(3, blk(core))
        return [core // 2]

    def two():
        landed(0, blk(xm))
        start(4)
        landed(1, blk(xp))
        start(5, 6, 7)
        landed(2, blk(zz))
        start(8, 9, 10)
        return []

    def third():
        landed(6, blk(other(dx=-1)))
        return [xm // 2]

    def three():
        landed(4, blk(d2, up))
        if not around:
            start(11)
        landed(5, blk(d2, lo))
        if not around:
            start(12)
        start(13)
        return []

    def third_more():
        landed(7, blk(other(dx=1)))
        landed(10, blk(other(dz=1)))
        return [xp // 2, zz // 2]

    def fourth():
        landed(13, blk(other(dx=2)))
        return [d2 // 2]

    def four():
        landed(8, blk(zxm))
        if around:
            start(11)
        landed(9, blk(zxp))
        if around:
            start(12)
        start(14, 15)
        return []

    def five():
        landed(11, blk(zd2, up))
        start(16)
        landed(12, blk(zd2, lo))
        start(17)
        landed(14, blk(other(dx=-1, dz=1)))
        landed(15, blk(other(dx=1, dz=1)))
        return [zxm // 2, zxp // 2]

    def six():
        landed(16, blk(other(dx=2, dz=1), up))
        landed(17, blk(other(dx=2, dz=1), lo))
        return [zd2 // 2]

    return [one, own, two, third, three, third_more, fourth, four, five, six]


def run_gather(plan, work, hooks):
    ready = []
    for n, step in enumerate(plan):
        ready += step()
        for hook in hooks.get(n, ()):
            hook()
        if ready:
            work(ready.pop(0))
    for chip in ready:
        work(chip)


def chip_plan(p, c, base, w_ref, part):
    R, C = w_ref.shape[0], part.shape[1]
    cols = pl.ds(pl.multiple_of(p.dp * C, C), C)
    mates = [(dx, dz) for dz in range(2) for dx in range(4)][1:]

    def rows(s):
        return pl.ds(pl.multiple_of((s // 2) * R, 16), R)

    for k, (dx, dz) in enumerate(mates):
        c.add(base + k, w_ref.at[:, cols], part.at[rows(p.s)], p.dev(p.at(dx, dz)))

    def begin():
        part[rows(p.s), :] = w_ref[:, cols]
        c.start(*range(base, base + 7))

    def end():
        for k, (dx, dz) in enumerate(mates):
            c.landed(base + k, part.at[rows(p.at(-dx, dz))])

    return begin, end


def across_plan(p, nd, c, base, part, land):
    q = Across(p, nd)
    K = part.shape[0]
    plan = gather_plan(q, c, base, part, matrix_blocks(land), around=True)

    def go(*ns):
        def run():
            for n in ns:
                plan[n]()

        return run

    return go, land.at[p.dp, pl.ds(pl.multiple_of(p.c * K, 16), K)]


def save_blocks(land, all_ref, sem):
    R = land.shape[1]

    def copy(k):
        return pltpu.make_async_copy(land.at[k], all_ref.at[pl.ds(pl.multiple_of(k * R, 16), R)], sem.at[k])

    def wait():
        for k in range(8):
            copy(k).wait()

    return lambda k: copy(k).start(), wait


def heads_of_blocks(land, col):
    R = land.shape[1] // 2

    def row(b, at):
        at += (b % 2) * R
        return land[b // 2, at // 16 * 16 : at // 16 * 16 + 16, :].astype(F32)[at % 16 : at % 16 + 1]

    first = jnp.concatenate([row(b, 0) for b in range(16)], axis=0)
    before = jnp.concatenate([jnp.zeros_like(first[0:1])] + [row(b, R - 1) for b in range(15)], axis=0)
    heads = jnp.concatenate([col[b * R : b * R + 1, :] for b in range(16)], axis=0)
    return first, before * equal(heads[:, 0:1], heads[:, 1:2]) - first


def shifted(n, col):
    same = equal(col[:, 0:1], col[:, 1:2])
    rows = lax.broadcasted_iota(jnp.int32, n.shape, 0)
    before = jnp.where(rows == 0, 0.0, pltpu.roll(n, 1, 0))
    return before * same - n


def norm_parts(a):
    width = a.shape[1]
    center = a - jnp.sum(a, axis=1, keepdims=True) * (1.0 / width)
    scale = lax.rsqrt(jnp.sum(center * center, axis=1, keepdims=True) * (1.0 / width) + 1e-05)
    return center, scale, center * scale


def norm_back(normed, scale, grad):
    width = grad.shape[1]
    inner = grad - jnp.sum(grad, axis=1, keepdims=True) * (1.0 / width)
    return scale * (inner - normed * (jnp.sum(grad * normed, axis=1, keepdims=True) * (1.0 / width)))


def sigmoid(a):
    return 1.0 / (1.0 + jnp.exp(-a))


CHUNK = 128


def halves(a):
    high = a.astype(BF)
    return high, (a - high.astype(F32)).astype(BF)


def dot3(a, b, dims):
    def one(x, y):
        return lax.dot_general(x, y, (dims, ((), ())), preferred_element_type=F32)

    return one(a[0], b[0]) + (one(a[0], b[1]) + one(a[1], b[0]))


NN, NT, TN = ((1,), (0,)), ((1,), (1,)), ((0,), (0,))


def head_sums(a, ones):
    high, rest = a.astype(BF), a - a.astype(BF).astype(F32)
    mid = rest.astype(BF)
    low = (rest - mid.astype(F32)).astype(BF)

    def one(x):
        return lax.dot_general(x, ones, (NN, ((), ())), preferred_element_type=F32)

    return one(high) + (one(mid) + one(low))


def iota(shape, dim):
    return lax.broadcasted_iota(jnp.int32, shape, dim)


def head_ones(width, dtype):
    return (iota((width, width), 0) // ATTENTION_WIDTH == iota((width, width), 1) // ATTENTION_WIDTH).astype(dtype)


def by_head(pair):
    lane = iota(pair[0].shape, 1) // ATTENTION_WIDTH
    heads = pair[0].shape[1] // ATTENTION_WIDTH
    zero = jnp.zeros_like(pair[0])
    return tuple(jnp.concatenate([jnp.where(lane == h, a, zero) for h in range(heads)], axis=0) for a in pair)


def pick_heads(a, rows):
    lane = iota((rows, a.shape[1]), 1) // ATTENTION_WIDTH
    out = a[:rows]
    for h in range(1, a.shape[1] // ATTENTION_WIDTH):
        out = jnp.where(lane == h, a[h * rows : (h + 1) * rows], out)
    return out


def powers(lam, tab):
    L = tab.shape[1]
    at = iota((L, 1), 0).astype(F32)
    mid = L // 2
    tab[0] = jnp.exp(lam * (at - mid))
    tab[1] = jnp.exp(-lam * (at + (1.0 - mid)))
    tab[2] = jnp.exp(lam * at)
    tab[3] = jnp.exp(lam * (L - 1.0 - at))


def own_vectors(p, par_ref, vec):
    W = vec.shape[1]
    own = par_ref[6:10, pl.ds(pl.multiple_of(p.s * W, 128), W)]
    lam = -jnp.exp(own[0:1])
    vec[0:1, :] = lam
    vec[1:4, :] = own[1:4]
    vec[8:, :] = jnp.broadcast_to(jnp.exp(lam * CHUNK), (W, W)).T


def chunk_mask(col, row):
    L = col.shape[0]
    return (iota((L, L), 1) < iota((L, L), 0)) & (col == row)


def forward_chunk(x_ref, col_ref, row_ref, bound_ref, vec_ref, z_ref, zt_ref, o_ref, s_ref, tab, state):
    chunks, L = row_ref.shape[0], row_ref.shape[2]
    W = vec_ref.shape[1]
    heads = W // ATTENTION_WIDTH
    lam, bonus, gain, bias = (vec_ref[q : q + 1, :] for q in range(4))
    powers(lam, tab)
    ones = head_ones(W, BF)
    diag = head_ones(W, F32)
    decay = vec_ref[8 : 8 + W, :]
    state[...] = jnp.zeros_like(state)

    def step(i):
        rows = pl.ds(pl.multiple_of(i * L, L), L)
        r, k, v, p = (x_ref[rows, q * W : (q + 1) * W] for q in range(4))
        col = col_ref[rows, :]
        seg = col[:, 0:1]
        kept, tail = equal(seg, bound_ref[0, i]), equal(seg, bound_ref[0, i + 1])
        mask = chunk_mask(seg, row_ref[i])
        mask = jnp.concatenate([mask] * heads, axis=1)
        rs, ks = halves(r * tab[0]), halves(k * tab[1])
        scores = jnp.where(mask, dot3(rs, by_head(ks), NT), 0.0)
        vh = halves(v)
        out = dot3(halves(scores), by_head(vh), NN) + head_sums(r * k * bonus, ones) * v
        memory = state[...]
        s_ref[i] = memory
        out = out + kept * dot3(halves(r * tab[2]), halves(memory), NN)
        state[...] = bound_ref[1, i] * decay * memory + diag * dot3(halves(k * tab[3] * tail), vh, TN)
        o_ref[rows, :] = out
        center = out - head_sums(out, ones) * (1.0 / ATTENTION_WIDTH)
        spread = head_sums(center * center, ones) * (1.0 / ATTENTION_WIDTH)
        normed = center * lax.rsqrt(spread + 0.00064) * gain + bias
        z = (normed * (p * sigmoid(p))).astype(BF).astype(F32)
        z_ref[rows, :] = z.astype(BF)
        zt_ref[:, rows] = z.T.astype(BF)

    return step


def back_chunk(x_ref, o_ref, s_ref, gz_ref, col_ref, row_ref, bound_ref, vec_ref, g_ref, sums_ref, tab, grad_state, acc, carry, turned):
    chunks, L = row_ref.shape[0], row_ref.shape[2]
    W = vec_ref.shape[1]
    heads = W // ATTENTION_WIDTH
    lam, bonus, gain, bias = (vec_ref[q : q + 1, :] for q in range(4))
    powers(lam, tab)
    ones = head_ones(W, BF)
    diag = head_ones(W, F32)
    decay = vec_ref[8 : 8 + W, :]
    at = iota((L, 1), 0).astype(F32)
    mid = float(L // 2)
    grad_state[...] = jnp.zeros_like(grad_state)
    acc[...] = jnp.zeros_like(acc)
    carry[...] = jnp.zeros_like(carry)
    sums_ref[...] = jnp.zeros_like(sums_ref)

    def add(q, term):
        sums_ref[q : q + 1, :] += jnp.sum(term, axis=0, keepdims=True)

    def step(n):
        i = chunks - 1 - n
        rows = pl.ds(pl.multiple_of(i * L, L), L)
        r, k, v, p = (x_ref[rows, q * W : (q + 1) * W] for q in range(4))
        col = col_ref[rows, :]
        seg = col[:, 0:1]
        kept, tail = equal(seg, bound_ref[0, i]), equal(seg, bound_ref[0, i + 1])
        same_next = equal(seg, col[:, 2:3])
        o = o_ref[rows, :]
        gz = gz_ref[i].astype(F32)
        center = o - head_sums(o, ones) * (1.0 / ATTENTION_WIDTH)
        spread = head_sums(center * center, ones) * (1.0 / ATTENTION_WIDTH)
        scale = lax.rsqrt(spread + 0.00064)
        normed = center * scale
        gate = sigmoid(p)
        silu = p * gate
        gy = gz * silu
        gp = gz * (normed * gain + bias) * (gate * (1.0 + p * (1.0 - gate)))
        add(2, gy * normed)
        add(3, gy)
        gn = gy * gain
        go = scale * (
            gn
            - head_sums(gn, ones) * (1.0 / ATTENTION_WIDTH)
            - normed * (head_sums(gn * normed, ones) * (1.0 / ATTENTION_WIDTH))
        )
        mask = chunk_mask(seg, row_ref[i])
        mask = jnp.concatenate([mask] * heads, axis=1)
        rs_f, ks_f = r * tab[0], k * tab[1]
        r0_f, ke_f = r * tab[2] * kept, k * tab[3] * tail
        rs, ks, vh, goh = halves(rs_f), halves(ks_f), halves(v), halves(go)
        ks_by, v_by = by_head(ks), by_head(vh)
        scores = halves(jnp.where(mask, dot3(rs, ks_by, NT), 0.0))
        grad_scores = halves(jnp.where(mask, dot3(goh, v_by, NT), 0.0))
        memory = s_ref[i]
        gs = grad_state[...]
        mh, gsh = halves(memory), halves(gs)
        reward = head_sums(r * k * bonus, ones)
        grad_reward = head_sums(go * v, ones)
        g_rs = dot3(grad_scores, ks_by, NN)
        g_r0 = dot3(goh, mh, NT)
        g_ks = pick_heads(dot3(grad_scores, rs, TN), L)
        g_ke = dot3(vh, gsh, NT)
        gv = pick_heads(dot3(scores, goh, TN), L) + reward * go + dot3(halves(ke_f), gsh, NN)
        keep = bound_ref[1, i]
        acc[...] += keep * memory * gs
        grad_state[...] = keep * decay * gs + diag * dot3(halves(r0_f), goh, TN)
        gr = g_rs * tab[0] + g_r0 * (tab[2] * kept) + grad_reward * bonus * k
        gk = g_ks * tab[1] + g_ke * (tab[3] * tail) + grad_reward * bonus * r
        add(1, grad_reward * r * k)
        add(0, (at - mid) * (g_rs * rs_f) - (at + (1.0 - mid)) * (g_ks * ks_f) + at * (g_r0 * r0_f) + (L - 1.0 - at) * (g_ke * ke_f))
        grads = jnp.concatenate([gr, gk, gv, gp], axis=1).astype(BF).astype(F32)
        last = iota((L, 1), 0) == L - 1
        after = jnp.where(last, carry[0:1, :], pltpu.roll(grads, L - 1, 0)) * same_next
        carry[0:1, :] = grads[0:1, :]
        g_ref[rows, : 4 * W] = grads.astype(BF)
        g_ref[rows, 4 * W :] = after.astype(BF)
        turned[0 : 4 * W, rows] = grads.T.astype(BF)
        turned[4 * W :, rows] = after.T.astype(BF)

    return step


def back_finish(vec_ref, sums_ref, acc, L):
    W = vec_ref.shape[1]
    whole = dot3(halves(jnp.ones((8, W), F32)), halves(acc[...] * vec_ref[8 : 8 + W, :]), NT)
    sums_ref[0:1, :] = (sums_ref[0:1, :] + L * whole[0:1, :]) * vec_ref[0:1, :]


def time_forward_kernel(nd, x_ref, par_ref, row_ref, bound_ref, w_far, ow_far, rw_far, col_far,
                        all_ref, proj_far, zt_far, o_far, s_far, hid_ref, n2_ref, rp_ref, far_ref,
                        n1, land, op, lw, tab, state, zin, w_ref, ow_ref, rw_ref, rt_ref, col_ref, proj_ref, z_ref, zt_ref,
                        o_ref, s_ref, vec, cs, cr, ss, rs, ls, ms):
    p = Place()
    met = greet(chip_mates(p) + [p.dev(p.at(dc=1))] + beside(p, nd))
    c = Copies(cs, cr)
    moves = Moves(ms)
    ow_in, w_in, col_in, rw_in = (
        moves.start(a, b) for a, b in ((ow_far, ow_ref), (w_far, w_ref), (col_far, col_ref), (rw_far, rw_ref))
    )
    R = x_ref.shape[0]
    Q, W = w_ref.shape[0], w_ref.shape[2]
    C = lw.shape[2]
    begin, end = chip_plan(p, c, 18, ow_ref, op)
    go, own_part = across_plan(p, nd, c, 25, op, lw)
    recept_begin, recept_end = chip_plan(p, c, 43, rt_ref, rp_ref)
    blk = blocks_of(land)
    plan = gather_plan(p, c, 0, n1, blk, around=True)
    start, wait = save_blocks(land, all_ref, ls)
    n1[...] = (norm_parts(x_ref[...].astype(F32))[2] * par_ref[0:1, :] + par_ref[1:2, :]).astype(BF)
    met()

    def ready():
        begin()
        blk(p.s)[...] = n1[...]
        own_vectors(p, par_ref, vec)
        w_in.wait()
        col_in.wait()

    def turn():
        rw_in.wait()
        for k in range(0, rw_ref.shape[0], 256):
            rt_ref[:, k : k + 256] = rw_ref[k : k + 256, :].T

    def across():
        own_part[...] = op[...]
        go(0)()

    def work(k):
        start(k)
        rows = pl.ds(pl.multiple_of(k * 2 * R, 16), 2 * R)
        n = land[k].astype(F32)
        shift = shifted(n, col_ref[rows, :])
        for q in range(Q):
            m = (n + shift * par_ref[2 + q : 3 + q, :]).astype(BF)
            proj_ref[rows, q * W : (q + 1) * W] = jnp.dot(m, w_ref[q], preferred_element_type=F32)

    ow_in.wait()
    run_gather(plan, work, {0: [ready], 1: [turn], 3: [end, across], 7: [go(1, 2)]})
    recept_begin()
    first, shift = heads_of_blocks(land, col_ref)
    for q in range(Q):
        m = (first + shift * par_ref[2 + q : 3 + q, :]).astype(BF)
        out = jnp.dot(m, w_ref[q], preferred_element_type=F32)
        for b in range(0, 16, 2):
            proj_ref[b * R : b * R + 1, q * W : (q + 1) * W] = out[b : b + 1]
    saves = [moves.start(proj_ref, proj_far)]

    chunk = forward_chunk(proj_ref, col_ref, row_ref, bound_ref, vec, z_ref, zt_ref, o_ref, s_ref, tab, state)
    swap = Swap(p, lambda i: z_ref.at[pl.ds(pl.multiple_of(i * R, 16), R)], zin, ss, rs)
    when = {0: go(3, 4), 2: go(5, 6, 7)}

    def step(n, unused):
        chunk(2 * n)
        chunk(2 * n + 1)
        swap.give(2 * n)
        swap.give(2 * n + 1)
        for at, act in when.items():
            pl.when(n == at)(act)
        return 0

    lax.fori_loop(0, row_ref.shape[0] // 2, step, 0)
    saves += [moves.start(a, b) for a, b in ((zt_ref, zt_far), (o_ref, o_far), (s_ref, s_far))]
    go(8, 9)()
    saves.append(moves.start(lw, far_ref))
    swap.all(swap.take)
    z_here = jnp.concatenate([zin[2 * k + core] for core in range(2) for k in range(8)], axis=1)
    for d in range(8):
        cols = slice(d * C, (d + 1) * C)
        hid_ref[:, cols] = x_ref[:, cols].astype(F32) + jnp.dot(z_here, lw[d], preferred_element_type=F32)
    n2_ref[...] = (norm_parts(hid_ref[...])[2] * par_ref[10:11, :] + par_ref[11:12, :]).astype(BF)
    recept_end()
    wait()
    for cp in saves:
        cp.wait()
    swap.all(swap.sent)
    c.finish()


def time_forward(nd, x, par, rows, bounds, w, ow, rw, cols, cid):
    R, C = x.shape
    T, W = 16 * R, w.shape[2]
    chunks, L = rows.shape[0], rows.shape[2]
    return pl.pallas_call(
        functools.partial(time_forward_kernel, nd),
        out_shape=(
            jax.ShapeDtypeStruct((T, C), BF),
            jax.ShapeDtypeStruct((T, 4 * W), F32),
            jax.ShapeDtypeStruct((W, T), BF),
            jax.ShapeDtypeStruct((T, W), F32),
            jax.ShapeDtypeStruct((chunks, W, W), F32),
            jax.ShapeDtypeStruct((R, C), F32),
            jax.ShapeDtypeStruct((R, C), BF),
            jax.ShapeDtypeStruct((8 * R, C // nd), BF),
            jax.ShapeDtypeStruct((8, 16 * R, C // 8), BF),
        ),
        in_specs=[WHOLE] * 3 + [pl.BlockSpec(memory_space=pltpu.SMEM)] + [FAR] * 4,
        out_specs=(FAR,) * 5 + (WHOLE,) * 3 + (FAR,),
        scratch_shapes=[
            VMEM((R, C), BF), VMEM((8, 2 * R, C), BF), VMEM((8 * R, C // nd), BF), VMEM((8, 16 * R, C // 8), BF), VMEM((4, L, W), F32),
            VMEM((W, W), F32), VMEM((16, R, W), BF), VMEM(w.shape, BF), VMEM((R, C), BF), VMEM((C, W), BF), VMEM((W, C), BF),
            VMEM(cols.shape, F32), VMEM((T, 4 * W), F32), VMEM((T, W), BF), VMEM((W, T), BF), VMEM((T, W), F32),
            VMEM((chunks, W, W), F32), VMEM((8 + W, W), F32),
            DMA((50,)), DMA((50,)), DMA((16,)), DMA((16,)), DMA((16,)), DMA((9,)),
        ],
        compiler_params=params(cid, 56),
        name="time_forward",
    )(x, par, rows, bounds, w, ow, rw, cols)


def key_kernel(nd, a_ref, rp_ref, par_ref, k_far, col_far, vw_far, mw_far,
               all_ref, in_ref, lift_far, sq_far, rin_ref, sh_ref, vt_far, mt_far, fold_far, far_ref,
               land, mixed, k_ref, w_ref, col_ref, vw_ref, mw_ref, lift_ref, sq_ref, vt_ref, mt_ref, fold_ref,
               cs, cr, ls, ms, ks):
    p = Place()
    met = greet(near(p) + beside(p, nd))
    c = Copies(cs, cr)
    moves = Moves(ms)
    col_in, k_in, mw_in, vw_in = (
        moves.start(a, b) for a, b in ((col_far, col_ref), (k_far, k_ref), (mw_far, mw_ref), (vw_far, vw_ref))
    )
    R = a_ref.shape[0]
    go, own_part = across_plan(p, nd, c, 18, rp_ref, far_ref)
    saves = [moves.start(rp_ref, own_part)]
    blk = blocks_of(land)
    plan = gather_plan(p, c, 0, a_ref, blk, around=True)
    start, wait = save_blocks(land, all_ref, ls)
    met()
    nu_k, nu_r = par_ref[12:13, :], par_ref[13:14, :]
    Q, W = mw_ref.shape[0], mw_ref.shape[2]

    def ready():
        c.start(18, 19, 21)
        blk(p.s)[...] = a_ref[...]
        k_in.wait()
        for k in range(0, w_ref.shape[0], 256):
            w_ref[k : k + 256, :] = k_ref[:, k : k + 256].T
        col_in.wait()

    def turn():
        vw_in.wait()
        for k in range(0, w_ref.shape[0], 256):
            vt_ref[k : k + 256, :] = vw_ref[:, k : k + 256].T
        saves.append(moves.start(vt_ref, vt_far))

    def fold(*qs):
        def run():
            if qs[0] == 0:
                mw_in.wait()
            for q in qs:
                for k in range(0, mw_ref.shape[1], 256):
                    cols, rows = slice(k, k + 256), slice(q * W, (q + 1) * W)
                    turned = mw_ref[q, cols, :].T
                    mt_ref[rows, cols] = turned
                    part = turned.astype(F32)
                    mu = par_ref[2 + q : 3 + q, cols]
                    fold_ref[rows, cols] = ((1.0 - mu) * part).astype(BF)
                    fold_ref[(Q + q) * W : (Q + q + 1) * W, cols] = (mu * part).astype(BF)
            if qs[-1] == Q - 1:
                saves.append(moves.start(mt_ref, mt_far))
                saves.append(moves.start(fold_ref, fold_far))

        return run

    def tail_copy(k):
        rows = pl.ds(16, 2 * R - 16)
        return pltpu.make_async_copy(mixed.at[k, rows], in_ref.at[k, rows], ks.at[k])

    def work(k):
        start(k)
        n = land[k].astype(F32)
        rows = pl.ds(pl.multiple_of(k * 2 * R, 16), 2 * R)
        m = (n + shifted(n, col_ref[rows, :]) * nu_k).astype(BF)
        mixed[k] = m
        e = jnp.maximum(jnp.dot(m, w_ref[...], preferred_element_type=F32), 0.0)
        lift_ref[rows, :] = e
        sq_ref[rows, :] = (e * e).astype(BF)
        tail_copy(k).start()

    run_gather(plan, work, {0: [ready], 1: [turn], 2: [lambda: c.start(20)], 4: [fold(0, 1)], 6: [fold(2, 3)], 7: [go(1, 2)], 9: [go(3, 4)]})
    first, shift = heads_of_blocks(land, col_ref)
    head = first + shift * nu_k
    e = jnp.maximum(jnp.dot(head.astype(BF), w_ref[...], preferred_element_type=F32), 0.0)
    sq = e * e
    top = lax.broadcasted_iota(jnp.int32, (16, 1), 0) == 0
    for b in range(0, 16, 2):
        rows = slice(b * R, b * R + 16)
        mixed[b // 2, 0:16, :] = jnp.where(top, head[b : b + 1], mixed[b // 2, 0:16, :].astype(F32)).astype(BF)
        lift_ref[b * R : b * R + 1, :] = e[b : b + 1]
        sq_ref[rows, :] = jnp.where(top, sq[b : b + 1], sq_ref[rows, :].astype(F32)).astype(BF)
    go(5, 6, 7)()
    saves.append(moves.start(lift_ref, lift_far))
    saves.append(moves.start(sq_ref, sq_far))
    saves.append(moves.start(mixed.at[:, pl.ds(0, 16)], in_ref.at[:, pl.ds(0, 16)]))
    n = a_ref[...].astype(F32)
    mine = lax.broadcasted_iota(jnp.int32, (16, 1), 0) == p.s
    own_first = jnp.sum(jnp.where(mine, shift, 0.0), axis=0, keepdims=True)
    here = pl.ds(pl.multiple_of(p.s * R, 16), R)
    topmost = lax.broadcasted_iota(jnp.int32, (R, 1), 0) == 0
    moved = jnp.where(topmost, own_first, shifted(n, col_ref[here, :]))
    sh_ref[...] = moved
    rin_ref[...] = (n + moved * nu_r).astype(BF)
    go(8, 9)()
    for k in range(8):
        tail_copy(k).wait()
    wait()
    for cp in saves:
        cp.wait()
    c.finish()


def key_side(nd, a, part, par, kt, cols, vw, mw, cid):
    R, C = a.shape
    T, units = 16 * R, kt.shape[0]
    Q, W = mw.shape[0], mw.shape[2]
    return pl.pallas_call(
        functools.partial(key_kernel, nd),
        out_shape=(
            jax.ShapeDtypeStruct((T, C), BF),
            jax.ShapeDtypeStruct((8, 2 * R, C), BF),
            jax.ShapeDtypeStruct((T, units), F32),
            jax.ShapeDtypeStruct((T, units), BF),
            jax.ShapeDtypeStruct((R, C), BF),
            jax.ShapeDtypeStruct((R, C), F32),
            jax.ShapeDtypeStruct((C, units), BF),
            jax.ShapeDtypeStruct((Q * W, C), BF),
            jax.ShapeDtypeStruct((2 * Q * W, C), BF),
            jax.ShapeDtypeStruct((8, T, C // 8), BF),
        ),
        in_specs=[WHOLE] * 3 + [FAR] * 4,
        out_specs=(FAR,) * 4 + (WHOLE,) * 2 + (FAR,) * 4,
        scratch_shapes=[
            VMEM((8, 2 * R, C), BF), VMEM((8, 2 * R, C), BF), VMEM((units, C), BF), VMEM((C, units), BF), VMEM(cols.shape, F32),
            VMEM((units, C), BF), VMEM(mw.shape, BF), VMEM((T, units), F32), VMEM((T, units), BF), VMEM((C, units), BF),
            VMEM((Q * W, C), BF), VMEM((2 * Q * W, C), BF),
            DMA((36,)), DMA((36,)), DMA((16,)), DMA((12,)), DMA((16,)),
        ],
        compiler_params=params(cid, 60),
        name="key_side",
    )(a, part, par, kt, cols, vw, mw)


def column_tiles(refs, tile, sem):
    C = tile.shape[2]

    def copy(u, ref):
        if len(ref.shape) == 3:
            return pltpu.make_async_copy(ref.at[u % 8], tile.at[u % 2], sem.at[u % 2])
        return pltpu.make_async_copy(ref.at[:, pl.ds(pl.multiple_of((u % 8) * C, C), C)], tile.at[u % 2], sem.at[u % 2])

    def start(u, kind):
        copy(u, refs[kind]).start()

    def wait(u, kind):
        copy(u, refs[kind]).wait()

    return start, wait


def sum_scratch(R, C):
    return [
        VMEM((8, 2, R, C), BF), VMEM((8, R, C), BF), VMEM((R, C), BF), VMEM((2, R, C), BF), VMEM((R, C), BF),
        VMEM((2, R // 2, C), BF), VMEM((2, R, C), BF),
    ]


def sum_plan(p, c, base, l_ref, w_ref, o_ref, scratch):
    pa, cb, zt, xs, zf, hv, xf = scratch
    R = o_ref.shape[0]
    H = R // 2
    core, xp, xm, zz = (p.dev(i) for i in (p.at(dc=1), p.at(dx=1), p.at(dx=-1), p.at(dz=1)))
    upper, lower = pl.ds(0, H), pl.ds(H, H)
    order = [(2, 1), (-1, 1), (1, 1), (2, 0), (0, 1), (1, 0), (-1, 0), (0, 0)]

    def send(k, src, dst, to):
        c.add(base + k, src, dst, to)
        c.start(base + k)

    def landed(k, ref):
        c.landed(base + k, ref)

    def give(i):
        k = p.at(*order[i]) // 2
        rows = l_ref[pl.ds(pl.multiple_of(k * 2 * R, 16), 2 * R), :]
        pa[i] = jnp.dot(rows, w_ref[...], preferred_element_type=F32).astype(BF).reshape(2, R, -1)
        send(i, pa.at[i, 1 - p.c], cb.at[i], core)

    def pair(i):
        landed(i, cb.at[i])
        pa[i, p.c] = (pa[i, p.c].astype(F32) + cb[i].astype(F32)).astype(BF)

    def one():
        give(0)
        give(1)
        pair(0)
        send(8, pa.at[0, p.c], zt, zz)
        give(2)
        pair(1)
        send(9, pa.at[1, p.c], xs.at[1], xm)
        pair(2)
        send(10, pa.at[2, p.c], xs.at[0], xp)

    def more():
        give(3)
        give(5)
        pair(3)
        give(6)
        pair(5)
        send(11, pa.at[5, p.c, lower], xf.at[0, lower], xp)
        give(4)
        pair(6)
        send(12, pa.at[6, p.c, upper], xf.at[1, upper], xm)
        give(7)
        pair(4)
        pair(7)

    def two():
        landed(8, zt)
        pa[3, p.c] = (pa[3, p.c].astype(F32) + zt[...].astype(F32)).astype(BF)
        send(13, pa.at[3, p.c, upper], hv.at[0], xp)
        send(14, pa.at[3, p.c, lower], hv.at[1], xm)

    def three():
        landed(9, xs.at[1])
        landed(10, xs.at[0])
        pa[4, p.c] = (pa[4, p.c].astype(F32) + xs[0].astype(F32) + xs[1].astype(F32)).astype(BF)
        send(15, pa.at[4, p.c], zf, zz)

    def four():
        landed(13, hv.at[0])
        pa[5, p.c, upper] = (pa[5, p.c, upper].astype(F32) + hv[0].astype(F32)).astype(BF)
        send(16, pa.at[5, p.c, upper], xf.at[0, upper], xp)
        landed(14, hv.at[1])
        pa[6, p.c, lower] = (pa[6, p.c, lower].astype(F32) + hv[1].astype(F32)).astype(BF)
        send(17, pa.at[6, p.c, lower], xf.at[1, lower], xm)

    def five():
        landed(11, xf.at[0, lower])
        landed(12, xf.at[1, upper])
        landed(15, zf)
        o_ref[...] = pa[7, p.c].astype(F32) + zf[...].astype(F32)

    def six():
        landed(16, xf.at[0, upper])
        landed(17, xf.at[1, lower])
        o_ref[...] = o_ref[...] + xf[0].astype(F32) + xf[1].astype(F32)

    return [one, more, two, three, four, five, six]


def value_kernel(rin_ref, g_ref, hid_ref, l_far, w_far, vt_far, lift_far, far_ref,
                 res_ref, gf_ref, rc_ref, ge_far, get_far, vg_far, *rest):
    scratch = rest[:7]
    (o_ref, f_ref, gate_ref, gkv, land, tile, l_ref, w_ref, vt_ref, lift_ref, ge_ref, get_ref, st_ref, acc,
     cs, cr, ss, rs, ts, ms) = rest[7:]
    p = Place()
    met = greet(near(p))
    c = Copies(cs, cr)
    moves = Moves(ms)
    R = o_ref.shape[0]
    T, U = l_ref.shape
    W = gf_ref.shape[2]
    C = tile.shape[2]
    fetch, have = column_tiles((far_ref,), tile, ts)
    l_in, w_in, vt_in, lift_in = (
        moves.start(a, b) for a, b in ((l_far, l_ref), (w_far, w_ref), (vt_far, vt_ref), (lift_far, lift_ref))
    )
    fetch(0, 0)
    sums = sum_plan(p, c, 0, l_ref, w_ref, o_ref, scratch)
    blk = blocks_of(land)
    plan = gather_plan(p, c, 18, gkv, blk)
    swap = Swap(p, lambda i: gf_ref.at[i], rc_ref, ss, rs)
    met()
    l_in.wait()
    w_in.wait()
    sums[0]()

    def unit(d, unused):
        pl.when(d < 7)(lambda: fetch(d + 1, 0))
        have(d, 0)
        cols = pl.ds(pl.multiple_of(d * C, C), C)
        part = lax.dot_general(rin_ref[:, cols], tile[d % 2], (NT, ((), ())), preferred_element_type=F32)

        @pl.when(d == 0)
        def _():
            f_ref[...] = part

        @pl.when(d > 0)
        def _():
            f_ref[...] += part

        return 0

    lax.fori_loop(0, 8, unit, 0)
    for s in range(16):
        at = ((s % 2) * 8 + s // 2) * W
        cols = slice(s * W, (s + 1) * W)
        gate = sigmoid(f_ref[:, at : at + W])
        gate_ref[:, cols] = gate
        gkv[:, cols] = (g_ref[:, cols].astype(F32) * gate).astype(BF)
    plan[0]()
    sums[1]()
    sums[2]()
    sums[3]()
    blk(p.s)[...] = gkv[...]
    acc[...] = jnp.zeros_like(acc)
    for r in range(0, T, 256):
        st_ref[:, r : r + 256] = l_ref[r : r + 256, :].T
    vt_in.wait()
    lift_in.wait()

    saves = []

    def work(k):
        rows = pl.ds(pl.multiple_of(k * 2 * R, 16), 2 * R)
        cols = pl.ds(pl.multiple_of(k * 2 * R, 128), 2 * R)
        gs = jnp.dot(land[k], vt_ref[...], preferred_element_type=F32)
        ge = gs * 2.0 * lift_ref[rows, :]
        ge_ref[rows, :] = ge.astype(BF)
        get_ref[:, cols] = ge.T.astype(BF)
        acc[...] += jnp.dot(st_ref[:, cols], land[k], preferred_element_type=F32)
        saves.append(moves.start(ge_ref.at[rows], ge_far.at[rows]))
        saves.append(moves.start(get_ref.at[:, cols], get_far.at[:, cols]))

    ready = plan[1]() + plan[2]()
    work(ready.pop(0))
    ready += plan[3]()
    work(ready.pop(0))
    ready += plan[5]()
    work(ready.pop(0))
    sums[4]()
    work(ready.pop(0))
    ready += plan[4]() + plan[6]()
    sums[5]()
    sums[6]()
    kv, gate = o_ref[...], gate_ref[...]
    gf = g_ref[...].astype(F32) * kv * (gate * (1.0 - gate))
    for s in range(16):
        gf_ref[s] = gf[:, s * W : (s + 1) * W].astype(BF)
    swap.all(swap.give)
    res_ref[...] = (hid_ref[...] + (gate * kv).astype(BF).astype(F32)).astype(BF)
    for n in range(7, 10):
        ready += plan[n]()
        work(ready.pop(0))
    for k in ready:
        work(k)
    for d in range(8):
        rows = slice((d % 4) * U, (d % 4 + 1) * U)
        tile[d // 4, rows, :] = acc[:, d * C : (d + 1) * C].astype(BF)
        saves.append(moves.start(tile.at[d // 4, pl.ds((d % 4) * U, U)], vg_far.at[d]))
    swap.all(swap.take)
    for cp in saves:
        cp.wait()
    swap.all(swap.sent)
    c.finish()


def value_side(rin, g, hidden, l, w, vt, lift, far, cid):
    R, C = hidden.shape
    T, U = l.shape
    W = C // 16
    return pl.pallas_call(
        value_kernel,
        out_shape=(
            jax.ShapeDtypeStruct((R, C), BF),
            jax.ShapeDtypeStruct((16, R, W), BF),
            jax.ShapeDtypeStruct((16, R, W), BF),
            jax.ShapeDtypeStruct((T, U), BF),
            jax.ShapeDtypeStruct((U, T), BF),
            jax.ShapeDtypeStruct((8, U, C // 8), BF),
        ),
        in_specs=[WHOLE] * 3 + [FAR] * 5,
        out_specs=(WHOLE,) * 3 + (FAR,) * 3,
        scratch_shapes=sum_scratch(R, C)
        + [VMEM((R, C), F32), VMEM((R, C), F32), VMEM((R, C), F32), VMEM((R, C), BF), VMEM((8, 2 * R, C), BF), VMEM((2, T, C // 8), BF)]
        + [VMEM((T, U), BF), VMEM((U, C), BF), VMEM((C, U), BF), VMEM((T, U), F32)]
        + [VMEM((T, U), BF), VMEM((U, T), BF), VMEM((U, T), BF), VMEM((U, C), F32)]
        + [DMA((36,)), DMA((36,)), DMA((16,)), DMA((16,)), DMA((2,)), DMA((28,))],
        compiler_params=params(cid, 62),
        name="value_side",
    )(rin, g, hidden, l, w, vt, lift, far)


def dp_scratch(J, C):
    return [VMEM((2, 2, J // 2, C), BF), VMEM((2, 2, J // 2, C), BF), VMEM((2, 2, J, C), BF), VMEM((2, J, C), BF)]


def dp_plan(p, nd, c, base, g_ref, o_ref, scratch):
    hv, stage, xf, zb = scratch
    J = g_ref.shape[1]
    ny = nd // 2
    y, zl = p.dp // 2, p.dp % 2
    yp, ym, yo = (y + 1) % ny, (y + ny - 1) % ny, (y + 2) % ny
    to_p, to_m, to_z = (2 * yp + zl, p.s), (2 * ym + zl, p.s), (2 * y + 1 - zl, p.s)

    def piece(base, first, rows):
        H = rows // 2
        every, up, lo = pl.ds(first, rows), pl.ds(first, H), pl.ds(first + H, H)
        half = pl.ds(first // 2, H)

        def pay(at, part):
            return g_ref.at[pl.ds(2 * at, 2), part]

        c.add(base, pay(yo, up), hv.at[0, :, half], to_p)
        c.add(base + 1, pay(yo, lo), hv.at[1, :, half], to_m)
        c.add(base + 2, pay(yp, lo), xf.at[0, :, lo], to_p)
        c.add(base + 3, pay(ym, up), xf.at[1, :, up], to_m)
        c.add(base + 4, stage.at[0, :, half], xf.at[0, :, up], to_p)
        c.add(base + 5, stage.at[1, :, half], xf.at[1, :, lo], to_m)
        c.add(base + 6, zb.at[0, every], zb.at[1, every], to_z)

        def one():
            c.start(base, base + 1, base + 2, base + 3)

        def two():
            c.landed(base, hv.at[0, :, half])
            stage[0, :, half] = (g_ref[pl.ds(2 * yp, 2), up].astype(F32) + hv[0, :, half].astype(F32)).astype(BF)
            c.start(base + 4)
            c.landed(base + 1, hv.at[1, :, half])
            stage[1, :, half] = (g_ref[pl.ds(2 * ym, 2), lo].astype(F32) + hv[1, :, half].astype(F32)).astype(BF)
            c.start(base + 5)

        def total(which):
            return g_ref[2 * y + which, every].astype(F32) + xf[0, which, every].astype(F32) + xf[1, which, every].astype(F32)

        def three():
            c.landed(base + 2, xf.at[0, :, lo])
            c.landed(base + 3, xf.at[1, :, up])
            c.landed(base + 4, xf.at[0, :, up])
            c.landed(base + 5, xf.at[1, :, lo])
            zb[0, every] = total(1 - zl).astype(BF)
            c.start(base + 6)
            o_ref[0, every] = total(zl)

        def four():
            c.landed(base + 6, zb.at[1, every])
            o_ref[0, every] += zb[1, every].astype(F32)

        return one, two, three, four

    first, second = piece(base, 0, J // 2), piece(base + 7, J // 2, J // 2)

    def both(n):
        def run():
            first[n]()
            second[n]()

        return run

    return [both(0), both(1), first[2], second[2], both(3)]


def no_sums(g_ref, o_ref):
    def copy():
        o_ref[...] = g_ref[...].astype(F32)

    return [lambda: None] * 4 + [copy]


def key_back_kernel(rc_ref, gf_ref, par_ref, g_ref, l_far, w_far, lt_far, col_far, hid_far, sh_far, vg_far,
                    in_hbm, n2_hbm, far_ref, out_far, gh_ref, ghb_ref, rows_ref, gg_far, gz_ref, *rest):
    scratch = rest[:7]
    (o_ref, rt, gfp, ga_ref, gzp, halo, tile, strip, l_ref, w_ref, lt_ref, col_ref, hid_ref, sh_ref, gg_ref,
     cs, cr, ss, rs, ts, os, ms) = rest[7:]
    p = Place()
    met = greet(near(p) + [p.dev((p.s + 1) % 16), p.dev((p.s + 15) % 16)])
    c = Copies(cs, cr)
    moves = Moves(ms)
    T, U = l_ref.shape
    R, width = o_ref.shape
    W = rc_ref.shape[2]
    C = tile.shape[2]
    l_in, w_in, lt_in, col_in, hid_in, sh_in, vg_in = (
        moves.start(a, b)
        for a, b in (
            (l_far, l_ref), (w_far, w_ref), (lt_far, lt_ref), (col_far, col_ref), (hid_far, hid_ref), (sh_far, sh_ref),
            (vg_far, gg_ref.at[:, pl.ds(0, U)]),
        )
    )
    fetch, have = column_tiles((in_hbm, n2_hbm, far_ref), tile, ts)
    fetch(0, 0)

    def strip_copy(n):
        return pltpu.make_async_copy(out_far.at[:, pl.ds(pl.multiple_of(n * 2 * W, 16), 2 * W)], strip.at[n % 2], os.at[n % 2])

    c.add(18, halo.at[0], halo.at[1], p.dev((p.s + 15) % 16))
    sums = sum_plan(p, c, 0, l_ref, w_ref, o_ref, scratch)
    swap = Swap(p, lambda i: gzp.at[i], gz_ref, ss, rs)
    met()
    nu_k, nu_r = par_ref[12:13, :], par_ref[13:14, :]

    def turn():
        last = lax.broadcasted_iota(jnp.int32, (R, 1), 0) == R - 1
        for b in range(16):
            part = rc_ref[b].astype(F32)
            after = rc_ref[b + 1, 0:16, :].astype(F32)[0:1] if b < 15 else jnp.zeros((1, W), F32)
            col = col_ref[b * R : (b + 1) * R, :]
            moved = jnp.where(last, after, pltpu.roll(part, R - 1, 0)) * equal(col[:, 0:1], col[:, 2:3])
            rt[0:W, b * R : (b + 1) * R] = part.T.astype(BF)
            rt[W:, b * R : (b + 1) * R] = moved.T.astype(BF)
        for s in range(16):
            at = ((s % 2) * 8 + s // 2) * W
            gfp[:, at : at + W] = gf_ref[s]

    def units(kind, lo, hi):
        def unit(d, unused):
            u = 8 * kind + d
            if hi < 8:
                fetch(u + 1, kind)
            else:
                pl.when(d < 7)(lambda: fetch(u + 1, kind))
                if kind < 2:
                    pl.when(d == 7)(lambda: fetch(u + 1, kind + 1))
            have(u, kind)
            rhs = tile[d % 2]
            cols = pl.ds(pl.multiple_of(d * C, C), C)
            if kind == 0:
                gg_ref[d, U : 2 * U, :] = jnp.dot(lt_ref[...], rhs, preferred_element_type=F32).astype(BF)
            elif kind == 1:
                out = jnp.dot(rt[...], rhs, preferred_element_type=F32)
                gg_ref[d, 2 * U :, :] = (out[:W] + par_ref[13:14, cols] * (out[W:] - out[:W])).astype(BF)
            else:
                ga_ref[:, cols] = jnp.dot(gfp[...], rhs, preferred_element_type=F32)
            return 0

        lax.fori_loop(lo, hi, unit, 0)

    l_in.wait()
    w_in.wait()
    sums[0]()
    sums[1]()
    lt_in.wait()
    units(0, 0, 4)
    sums[2]()
    sums[3]()
    units(0, 4, 8)
    col_in.wait()
    turn()
    units(1, 0, 4)
    sums[4]()
    units(1, 4, 8)
    vg_in.wait()
    saves = [moves.start(gg_ref, gg_far)]
    units(2, 0, 8)
    sums[5]()
    strip_copy(0).start()
    hid_in.wait()
    sh_in.wait()
    unused, scale, normed = norm_parts(hid_ref[...])
    sums[6]()
    ga_k, ga_r, shift = o_ref[...], ga_ref[...], sh_ref[...]
    here = pl.ds(pl.multiple_of(p.s * R, 16), R)
    col = col_ref[here, :]
    moved = (ga_k * nu_k + ga_r * nu_r) * equal(col[:, 0:1], col[:, 1:2])
    halo[0] = moved[0:8]
    c.start(18)
    held = ga_k - ga_k * nu_k + (ga_r - ga_r * nu_r)
    rows_ref[...] = jnp.zeros_like(rows_ref)
    rows_ref[2:3, :] = jnp.sum(ga_k * shift, axis=0, keepdims=True)
    rows_ref[3:4, :] = jnp.sum(ga_r * shift, axis=0, keepdims=True)
    c.landed(18, halo.at[1])
    last = lax.broadcasted_iota(jnp.int32, (R, 1), 0) == R - 1
    grad = held + jnp.where(last, halo[1, 0:1, :], pltpu.roll(moved, R - 1, 0))
    gh = g_ref[...].astype(F32) + norm_back(normed, scale, grad * par_ref[10:11, :])
    gh_ref[...] = gh
    ghb_ref[...] = gh.astype(BF)

    def back_out(n, unused):
        pl.when(n < 7)(lambda: strip_copy(n + 1).start())
        strip_copy(n).wait()
        part = lax.dot_general(ghb_ref[:, 0:C], strip[n % 2, 0], (NT, ((), ())), preferred_element_type=F32)
        for d in range(1, 8):
            part = part + lax.dot_general(
                ghb_ref[:, d * C : (d + 1) * C], strip[n % 2, d], (NT, ((), ())), preferred_element_type=F32
            )
        for k in range(2):
            to = 2 * ((2 * n + k) % 8) + (2 * n + k) // 8
            gzp[to] = part[:, k * W : (k + 1) * W].astype(BF)
            swap.give(to)
        return 0

    lax.fori_loop(0, 8, back_out, 0)
    rows_ref[0:1, :] = jnp.sum(grad * normed, axis=0, keepdims=True)
    rows_ref[1:2, :] = jnp.sum(grad, axis=0, keepdims=True)
    for cp in saves:
        cp.wait()
    swap.all(swap.take)
    swap.all(swap.sent)
    c.finish()


def key_back(rc, gf, par, g, l, w, lt, cols, hidden, sh, vg, key_in, n2_all, far, out_far, cid):
    R, C = hidden.shape
    T, U, W = 16 * R, l.shape[1], rc.shape[2]
    return pl.pallas_call(
        key_back_kernel,
        out_shape=(
            jax.ShapeDtypeStruct((R, C), F32),
            jax.ShapeDtypeStruct((R, C), BF),
            jax.ShapeDtypeStruct((8, C), F32),
            jax.ShapeDtypeStruct((8, 2 * U + W, C // 8), BF),
            jax.ShapeDtypeStruct((16, R, W), BF),
        ),
        in_specs=[WHOLE] * 4 + [FAR] * 11,
        out_specs=(WHOLE,) * 3 + (FAR, WHOLE),
        scratch_shapes=sum_scratch(R, C)
        + [VMEM((R, C), F32), VMEM((2 * W, T), BF), VMEM((R, C), BF), VMEM((R, C), F32), VMEM((16, R, W), BF), VMEM((2, 8, C), F32)]
        + [VMEM((2, T, C // 8), BF), VMEM((2, 8, 2 * W, C // 8), BF), VMEM((T, U), BF), VMEM((U, C), BF), VMEM((U, T), BF)]
        + [VMEM(cols.shape, F32), VMEM((R, C), F32), VMEM((R, C), F32), VMEM((8, 2 * U + W, C // 8), BF)]
        + [DMA((19,)), DMA((19,)), DMA((16,)), DMA((16,)), DMA((2,)), DMA((2,)), DMA((8,))],
        compiler_params=params(cid, 60),
        name="key_back",
    )(rc, gf, par, g, l, w, lt, cols, hidden, sh, vg, key_in, n2_all, far, out_far)


def time_back_kernel(nd, gh_ref, gz_ref, par_ref, row_ref, bound_ref, early_far, x_far, o_far, s_far, col_far, zt_far, mixt_far, n1_hbm,
                     g_far, gg_far, sums_ref, mug_ref, dp_ref,
                     tab, grad_state, acc, carry, land, turned, tile, vec, early_ref, x_ref, o_ref, s_ref, col_ref, zt_ref, mixt_ref,
                     g_ref, gg_ref, d0, d1, d2, d3, cs, cr, ts, ms):
    p = Place()
    met = greet(near(p) + beside(p, nd))
    c = Copies(cs, cr)
    moves = Moves(ms)
    W = vec.shape[1]
    chunks, L = row_ref.shape[0], row_ref.shape[2]
    C = tile.shape[2]
    early_in, x_in, o_in, s_in, col_in, zt_in, mixt_in = (
        moves.start(a, b)
        for a, b in (
            (early_far, early_ref), (x_far, x_ref), (o_far, o_ref), (s_far, s_ref), (col_far, col_ref), (zt_far, zt_ref),
            (mixt_far, mixt_ref),
        )
    )
    fetch, have = column_tiles((n1_hbm,), tile, ts)
    fetch(0, 0)
    blk = rows_of(land)
    plan = gather_plan(p, c, 0, gh_ref, blk)
    sums = dp_plan(p, nd, c, 18, early_ref, dp_ref, (d0, d1, d2, d3)) if nd > 1 else no_sums(early_ref, dp_ref)
    own_vectors(p, par_ref, vec)
    met()
    plan[0]()
    early_in.wait()
    sums[0]()
    blk(p.s)[...] = gh_ref[...]
    when = {6: [plan[1], plan[2]], 8: [sums[1]], 11: [plan[3], plan[4]], 14: [plan[5], plan[6], plan[7]]}
    for cp in (x_in, o_in, s_in, col_in):
        cp.wait()
    chunk = back_chunk(x_ref, o_ref, s_ref, gz_ref, col_ref, row_ref, bound_ref, vec, g_ref, sums_ref, tab, grad_state, acc, carry, turned)

    def step(n, unused):
        chunk(n)
        for at, parts in when.items():
            @pl.when(n == at)
            def _():
                for part in parts:
                    part()
        return 0

    lax.fori_loop(0, chunks, step, 0)
    saves = [moves.start(g_ref, g_far)]
    back_finish(vec, sums_ref, acc, L)
    mug_ref[...] = jnp.zeros_like(mug_ref)
    mixt_in.wait()

    def mix(d, unused):
        pl.when(d < 7)(lambda: fetch(d + 1, 0))
        have(d, 0)
        rhs = tile[d % 2]
        cols = pl.ds(pl.multiple_of(d * C, C), C)
        a = jnp.dot(turned[: 4 * W, :], rhs, preferred_element_type=F32)
        b = jnp.dot(turned[4 * W :, :], rhs, preferred_element_type=F32)
        for q in range(4):
            rows = slice(q * W, (q + 1) * W)
            diff = b[rows] - a[rows]
            gg_ref[d, rows, :] = (a[rows] + par_ref[2 + q : 3 + q, cols] * diff).astype(BF)
            mug_ref[q : q + 1, cols] = jnp.sum(mixt_ref[rows, cols].astype(F32) * diff, axis=0, keepdims=True)
        return 0

    lax.fori_loop(0, 4, mix, 0)
    plan[8]()
    sums[2]()
    lax.fori_loop(4, 8, mix, 0)
    sums[3]()
    zt_in.wait()
    plan[9]()

    def out(d, unused):
        cols = pl.ds(pl.multiple_of(d * C, C), C)
        gg_ref[d, 4 * W :, :] = jnp.dot(zt_ref[...], land[:, cols], preferred_element_type=F32).astype(BF)
        return 0

    lax.fori_loop(0, 8, out, 0)
    saves.append(moves.start(gg_ref, gg_far))
    sums[4]()
    for cp in saves:
        cp.wait()
    c.finish()


def time_back(nd, gh, gz, par, rows, bounds, early, x, o, states, cols, zt, mixt, n1_all, cid):
    T, W = o.shape
    L = rows.shape[2]
    R, C = gh.shape
    J = early.shape[1]
    return pl.pallas_call(
        functools.partial(time_back_kernel, nd),
        out_shape=(
            jax.ShapeDtypeStruct((T, 8 * W), BF),
            jax.ShapeDtypeStruct((8, 5 * W, C // 8), BF),
            jax.ShapeDtypeStruct((8, W), F32),
            jax.ShapeDtypeStruct((4, C), F32),
            jax.ShapeDtypeStruct((8 // nd, J, C // 8), F32),
        ),
        in_specs=[WHOLE] * 4 + [pl.BlockSpec(memory_space=pltpu.SMEM)] + [FAR] * 8,
        out_specs=(FAR,) * 2 + (WHOLE,) * 3,
        scratch_shapes=[
            VMEM((4, L, W), F32), VMEM((W, W), F32), VMEM((W, W), F32), VMEM((8, 4 * W), F32),
            VMEM((T, C), BF), VMEM((8 * W, T), BF), VMEM((2, T, C // 8), BF), VMEM((8 + W, W), F32),
            VMEM((8, J, C // 8), BF), VMEM(x.shape, F32), VMEM((T, W), F32), VMEM(states.shape, F32), VMEM(cols.shape, F32),
            VMEM((W, T), BF), VMEM(mixt.shape, BF), VMEM((T, 8 * W), BF), VMEM((8, 5 * W, C // 8), BF),
        ]
        + dp_scratch(J, C // 8)
        + [DMA((32,)), DMA((32,)), DMA((2,)), DMA((9,))],
        compiler_params=params(cid, 60),
        name="time_back",
    )(gh, gz, par, rows, bounds, early, x, o, states, cols, zt, mixt, n1_all)


def last_kernel(nd, x_ref, par_ref, mug_ref, head_ref, norm_ref, gg_far, l_far, w_far, gh_far, ig_ref, dp_ref, v_ref, *rest):
    scratch = rest[:7]
    o_ref, d0, d1, d2, d3, tv, b1, t1, b2, gg_ref, l_ref, w_ref, gh_ref, cs, cr, ms = rest[7:]
    p = Place()
    met = greet(near(p) + beside(p, nd))
    c = Copies(cs, cr)
    moves = Moves(ms)
    gg_in, w_in, l_in, gh_in = (
        moves.start(a, b) for a, b in ((gg_far, gg_ref), (w_far, w_ref), (l_far, l_ref), (gh_far, gh_ref))
    )
    sums = dp_plan(p, nd, c, 18, gg_ref, dp_ref, (d0, d1, d2, d3)) if nd > 1 else no_sums(gg_ref, dp_ref)
    steps = sum_plan(p, c, 0, l_ref, w_ref, o_ref, scratch)
    W = head_ref.shape[1]
    tv[...] = jnp.zeros_like(tv)
    tv[2:6, :] = mug_ref[...]
    tv[6:10, pl.ds(pl.multiple_of(p.s * W, 128), W)] = head_ref[0:4, :]
    tv[10:14, :] = norm_ref[0:4, :]
    met()
    gg_in.wait()
    sums[0]()
    l_in.wait()
    w_in.wait()
    steps[0]()
    steps[1]()
    sums[1]()
    steps[2]()
    steps[3]()
    steps[4]()
    sums[2]()
    sums[3]()
    unused, scale, normed = norm_parts(x_ref[...].astype(F32))
    gh_in.wait()
    steps[5]()
    steps[6]()
    gn = o_ref[...]
    tv[0:1, :] = jnp.sum(gn * normed, axis=0, keepdims=True)
    tv[1:2, :] = jnp.sum(gn, axis=0, keepdims=True)
    sums[4]()
    C = b1.shape[2]
    for k in range(1, nd):
        to = (p.dp + k) % nd
        c.add(31 + k, tv.at[:, pl.ds(pl.multiple_of(to * C, 128), C)], b1.at[k - 1], (to, p.s))
        c.start(31 + k)
    ig_ref[...] = gh_ref[...] + norm_back(normed, scale, gn * par_ref[0:1, :])
    total = tv[:, pl.ds(pl.multiple_of(p.dp * C, 128), C)]
    for k in range(1, nd):
        c.landed(31 + k, b1.at[k - 1])
        total = total + b1[k - 1]
    t1[...] = total
    for k in range(1, 16):
        c.add(38 + k, t1, b2.at[k - 1], p.dev((p.s + k) % 16))
        c.start(38 + k)
    for k in range(1, 16):
        c.landed(38 + k, b2.at[k - 1])
        total = total + b2[k - 1]
    v_ref[...] = total
    c.finish()


def last_sums(nd, x, par, mug, head, norm, gg, l, w, gh, cid):
    R, C = x.shape
    J = gg.shape[1]
    piece = (16, C // nd)
    return pl.pallas_call(
        functools.partial(last_kernel, nd),
        out_shape=(jax.ShapeDtypeStruct((R, C), F32), jax.ShapeDtypeStruct((8 // nd, J, C // 8), F32), jax.ShapeDtypeStruct(piece, F32)),
        in_specs=[WHOLE] * 5 + [FAR] * 4,
        out_specs=(WHOLE,) * 3,
        scratch_shapes=sum_scratch(R, C)
        + [VMEM((R, C), F32)]
        + dp_scratch(J, C // 8)
        + [VMEM((16, C), F32), VMEM((max(nd - 1, 1),) + piece, F32), VMEM(piece, F32), VMEM((15,) + piece, F32)]
        + [VMEM(gg.shape, BF), VMEM(l.shape, BF), VMEM(w.shape, BF), VMEM((R, C), F32)]
        + [DMA((54,)), DMA((54,)), DMA((4,))],
        compiler_params=params(cid, 60),
        name="last_sums",
    )(x, par, mug, head, norm, gg, l, w, gh)


def body(nd, inputs, cotangent, mix_weights, out_weight, key_weight, value_weight, recept_weight, vectors, segment_ids):
    tokens, width = inputs.shape
    group = segment_ids.shape[0]
    cols = mix_weights.shape[2]
    units = key_weight.shape[1]
    s = lax.axis_index("sp")
    ring = group // tokens
    chunks = group // CHUNK

    edge = jnp.full((1,), -1.0, F32)
    seg = jnp.concatenate([edge, segment_ids.astype(F32), edge])
    tok_cols = jnp.stack([seg[1:-1], seg[:-2], seg[2:]], axis=1)
    tok_rows = seg[1:-1].reshape(chunks, 1, CHUNK)
    ends = seg[: group + 1 : CHUNK]
    bounds = jnp.stack([ends, jnp.concatenate([(ends[1:] == ends[:-1]).astype(F32), edge])])

    n1_all, projected, z_t, mixed_time, states, hidden, n2, recept_part, out_far = time_forward(
        nd, inputs, vectors, tok_rows, bounds, mix_weights, out_weight, recept_weight, tok_cols, 0
    )
    n2_all, key_in, lifted, squared, recept_in, shift, value_t, mixt, folded, recept_far = key_side(
        nd, n2, recept_part, vectors, key_weight.T, tok_cols, value_weight, mix_weights, 1
    )
    result, grad_recept, recept_cols, grad_key, grad_key_t, value_grad = value_side(
        recept_in, cotangent, hidden, squared, value_weight, value_t, lifted, recept_far, 2
    )
    grad_hidden, grad_hidden_b, norm_rows, early, gz = key_back(
        recept_cols, grad_recept, vectors, cotangent, grad_key, key_weight.T, grad_key_t, tok_cols, hidden, shift, value_grad,
        key_in.reshape(group, width), n2_all, recept_far, out_far, 3,
    )
    grads_two, late, head_rows, mu_rows, early_sum = time_back(
        nd, grad_hidden_b, gz, vectors, tok_rows, bounds, early, projected, mixed_time, states, tok_cols, z_t, mixt, n1_all, 4
    )
    input_grad, late_sum, vector_sum = last_sums(
        nd, inputs, vectors, mu_rows, head_rows, norm_rows, late, grads_two, folded, grad_hidden, 5
    )
    piece = width // (nd * ring)
    vectors_grad = lax.dynamic_slice_in_dim(vector_sum[:14], s * piece, piece, 1)

    def columns(part):
        return part.transpose(1, 0, 2).reshape(part.shape[1], width // nd)

    early_sum, late_sum = columns(early_sum), columns(late_sum)
    return (
        result,
        input_grad,
        late_sum[: 4 * cols].reshape(4, cols, width // nd).transpose(0, 2, 1),
        late_sum[4 * cols :],
        early_sum[units : 2 * units].T,
        early_sum[:units],
        early_sum[2 * units :].T,
        vectors_grad,
    )


def solution(mesh):
    placed = (
        P(("dp", "sp"), None),
        P(("dp", "sp"), None),
        P(None, None, "sp"),
        P("sp", None),
        P(None, "sp"),
        P("sp", None),
        P(None, "sp"),
        P(),
        P("dp"),
    )
    return jax.shard_map(
        functools.partial(body, mesh.shape["dp"]),
        mesh=mesh,
        in_specs=placed,
        out_specs=(
            P(("dp", "sp"), None),
            P(("dp", "sp"), None),
            P(None, "dp", "sp"),
            P("sp", "dp"),
            P("dp", "sp"),
            P("sp", "dp"),
            P("dp", "sp"),
            P(None, ("dp", "sp")),
        ),
        check_vma=False,
    )
```

```python
import functools

import jax
import jax.numpy as jnp
from jax import lax
from jax.experimental import pallas as pl
from jax.experimental.pallas import tpu as pltpu
from jax.sharding import PartitionSpec as P

MESH = pl.DeviceIdType.MESH
VMEM = pltpu.VMEM
DMA = pltpu.SemaphoreType.DMA
BF = jnp.bfloat16
F32 = jnp.float32

ATTENTION_WIDTH = 64
CHUNK = 128
WHOLE = pl.BlockSpec(memory_space=VMEM)
FAR = pl.BlockSpec(memory_space=pl.ANY)


class Place:
    def __init__(self):
        self.dp = lax.axis_index("dp")
        s = lax.axis_index("sp")
        self.s = s
        self.x, self.z, self.c = s // 4, (s // 2) % 2, s % 2

    def at(self, dx=0, dz=0, dc=0):
        return ((self.x + dx) % 4) * 4 + ((self.z + dz) % 2) * 2 + (self.c + dc) % 2

    def dev(self, s):
        return (self.dp, s)


class Across:
    def __init__(self, p, nd):
        self.p, self.ny = p, nd // 2
        self.x, self.z, self.c = p.dp // 2, p.dp % 2, p.c
        self.s = p.dp * 2 + p.c

    def at(self, dx=0, dz=0, dc=0):
        return ((self.x + dx) % self.ny) * 4 + ((self.z + dz) % 2) * 2 + (self.c + dc) % 2

    def dev(self, i):
        return (i // 2, self.p.s - self.p.c + i % 2)


class Copies:
    def __init__(self, ss, rs):
        self.ss, self.rs, self.items = ss, rs, {}

    def add(self, k, src, dst, to):
        self.items[k] = (src, dst, to)

    def make(self, k, src, dst, to):
        return pltpu.make_async_remote_copy(
            src_ref=src, dst_ref=dst, send_sem=self.ss.at[k], recv_sem=self.rs.at[k], device_id=to, device_id_type=MESH
        )

    def start(self, *ks):
        for k in ks:
            self.make(k, *self.items[k]).start()

    def landed(self, k, ref):
        self.make(k, ref, ref, self.items[k][2]).wait_recv()

    def finish(self):
        for k in self.items:
            self.make(k, *self.items[k]).wait_send()


def greet(devices):
    barrier = pltpu.get_barrier_semaphore()
    for device in devices:
        pl.semaphore_signal(barrier, inc=1, device_id=device, device_id_type=MESH)
    return lambda: pl.semaphore_wait(barrier, len(devices))


def near(p):
    return [p.dev(p.at(dc=1)), p.dev(p.at(dx=1)), p.dev(p.at(dx=-1)), p.dev(p.at(dz=1))]


def beside(p, nd):
    y, zl, ny = p.dp // 2, p.dp % 2, nd // 2
    if nd == 1:
        return []
    return [(2 * ((y + 1) % ny) + zl, p.s), (2 * ((y + ny - 1) % ny) + zl, p.s), (2 * y + 1 - zl, p.s)]


def chip_mates(p):
    return [p.dev(p.at(dx, dz)) for dz in range(2) for dx in range(4)][1:]


def ring_mates(p):
    return [p.dev((p.s + k) % 16) for k in range(1, 16)]


def dp_mates(p, nd):
    return [((p.dp + k) % nd, p.s) for k in range(1, nd)]


def params(cid, mib):
    return pltpu.CompilerParams(collective_id=cid, has_side_effects=True, vmem_limit_bytes=mib * 2**20)


class Swap:
    def __init__(self, p, src, dst, ss, rs):
        self.p, self.src, self.dst, self.ss, self.rs = p, src, dst, ss, rs

    def make(self, src, dst, at, to):
        return pltpu.make_async_remote_copy(
            src_ref=src, dst_ref=dst, send_sem=self.ss.at[to], recv_sem=self.rs.at[at], device_id=self.p.dev(to), device_id_type=MESH
        )

    def give(self, i):
        @pl.when(i != self.p.s)
        def _():
            self.make(self.src(i), self.dst.at[self.p.s], self.p.s, i).start()

        @pl.when(i == self.p.s)
        def _():
            self.dst[self.p.s] = self.src(i)[...]

    def take(self, i):
        @pl.when(i != self.p.s)
        def _():
            self.make(self.dst.at[i], self.dst.at[i], i, i).wait_recv()

    def sent(self, i):
        @pl.when(i != self.p.s)
        def _():
            self.make(self.src(i), self.dst.at[self.p.s], self.p.s, i).wait_send()

    def all(self, act):
        def step(i, unused):
            act(i)
            return 0

        lax.fori_loop(0, 16, step, 0)


class Moves:
    def __init__(self, sem):
        self.sem, self.n = sem, 0

    def start(self, src, dst):
        cp = pltpu.make_async_copy(src, dst, self.sem.at[self.n])
        self.n += 1
        cp.start()
        return cp


def equal(a, b):
    return jnp.where(a == b, 1.0, 0.0)


def blocks_of(land):
    R = land.shape[1] // 2

    def blk(i, half=None):
        rows = R if half is None else R // 2
        return land.at[i // 2, pl.ds(pl.multiple_of((i % 2) * R + (half or 0) * rows, 16), rows)]

    return blk


def rows_of(land):
    R = land.shape[0] // 16

    def blk(i, half=None):
        rows = R if half is None else R // 2
        return land.at[pl.ds(pl.multiple_of(i * R + (half or 0) * rows, 16), rows)]

    return blk


def matrix_blocks(land):
    K = land.shape[1] // 2

    def blk(i, half=None):
        rows = K if half is None else K // 2
        return land.at[i // 2, pl.ds(pl.multiple_of((i % 2) * K + (half or 0) * rows, 16), rows)]

    return blk


def gather_plan(p, c, base, a_ref, blk, around=False):
    core, xp, xm, zz = p.at(dc=1), p.at(dx=1), p.at(dx=-1), p.at(dz=1)
    d2, zxm, zxp, zd2 = p.at(dx=2), p.at(dx=-1, dz=1), p.at(dx=1, dz=1), p.at(dx=2, dz=1)
    up, lo = 0, 1

    def relay(k, ref, to):
        c.add(base + k, ref, ref, p.dev(to))

    for k, to in enumerate((xp, xm, zz, core)):
        c.add(base + k, a_ref, blk(p.s), p.dev(to))
    relay(4, blk(xm, up), xp)
    relay(5, blk(xp, lo), xm)
    relay(6, blk(xm), core)
    relay(7, blk(xp), core)
    relay(8, blk(zz), xp)
    relay(9, blk(zz), xm)
    relay(10, blk(zz), core)
    if around:
        relay(11, blk(zxm, up), xp)
        relay(12, blk(zxp, lo), xm)
    else:
        relay(11, blk(d2, up), zz)
        relay(12, blk(d2, lo), zz)
    relay(13, blk(d2), core)
    relay(14, blk(zxm), core)
    relay(15, blk(zxp), core)
    relay(16, blk(zd2, up), core)
    relay(17, blk(zd2, lo), core)

    def start(*ks):
        c.start(*(base + k for k in ks))

    def landed(k, ref):
        c.landed(base + k, ref)

    def other(**k):
        return p.at(dc=1, **k)

    def one():
        start(0, 1, 2, 3)
        return []

    def own():
        landed(3, blk(core))
        return [core // 2]

    def two():
        landed(0, blk(xm))
        start(4)
        landed(1, blk(xp))
        start(5, 6, 7)
        landed(2, blk(zz))
        start(8, 9, 10)
        return []

    def third():
        landed(6, blk(other(dx=-1)))
        return [xm // 2]

    def three():
        landed(4, blk(d2, up))
        if not around:
            start(11)
        landed(5, blk(d2, lo))
        if not around:
            start(12)
        start(13)
        return []

    def third_more():
        landed(7, blk(other(dx=1)))
        landed(10, blk(other(dz=1)))
        return [xp // 2, zz // 2]

    def fourth():
        landed(13, blk(other(dx=2)))
        return [d2 // 2]

    def four():
        landed(8, blk(zxm))
        if around:
            start(11)
        landed(9, blk(zxp))
        if around:
            start(12)
        start(14, 15)
        return []

    def five():
        landed(11, blk(zd2, up))
        start(16)
        landed(12, blk(zd2, lo))
        start(17)
        landed(14, blk(other(dx=-1, dz=1)))
        landed(15, blk(other(dx=1, dz=1)))
        return [zxm // 2, zxp // 2]

    def six():
        landed(16, blk(other(dx=2, dz=1), up))
        landed(17, blk(other(dx=2, dz=1), lo))
        return [zd2 // 2]

    return [one, own, two, third, three, third_more, fourth, four, five, six]


def run_gather(plan, work, hooks):
    ready = []
    for n, step in enumerate(plan):
        ready += step()
        for hook in hooks.get(n, ()):
            hook()
        if ready:
            work(ready.pop(0))
    for chip in ready:
        work(chip)


def chip_plan(p, c, base, w_ref, part):
    R, C = w_ref.shape[0], part.shape[1]
    cols = pl.ds(pl.multiple_of(p.dp * C, C), C)
    mates = [(dx, dz) for dz in range(2) for dx in range(4)][1:]

    def rows(s):
        return pl.ds(pl.multiple_of((s // 2) * R, 16), R)

    for k, (dx, dz) in enumerate(mates):
        c.add(base + k, w_ref.at[:, cols], part.at[rows(p.s)], p.dev(p.at(dx, dz)))

    def begin():
        part[rows(p.s), :] = w_ref[:, cols]
        c.start(*range(base, base + 7))

    def end():
        for k, (dx, dz) in enumerate(mates):
            c.landed(base + k, part.at[rows(p.at(-dx, dz))])

    return begin, end


def across_plan(p, nd, c, base, part, land):
    q = Across(p, nd)
    K = part.shape[0]
    plan = gather_plan(q, c, base, part, matrix_blocks(land), around=True)

    def go(*ns):
        def run():
            for n in ns:
                plan[n]()

        return run

    return go, land.at[p.dp, pl.ds(pl.multiple_of(p.c * K, 16), K)]


def save_blocks(land, all_ref, sem):
    R = land.shape[1]

    def copy(k):
        return pltpu.make_async_copy(land.at[k], all_ref.at[pl.ds(pl.multiple_of(k * R, 16), R)], sem.at[k])

    def wait():
        for k in range(8):
            copy(k).wait()

    return lambda k: copy(k).start(), wait


def heads_of_blocks(land, col):
    R = land.shape[1] // 2

    def row(b, at):
        at += (b % 2) * R
        return land[b // 2, at // 16 * 16 : at // 16 * 16 + 16, :].astype(F32)[at % 16 : at % 16 + 1]

    first = jnp.concatenate([row(b, 0) for b in range(16)], axis=0)
    before = jnp.concatenate([jnp.zeros_like(first[0:1])] + [row(b, R - 1) for b in range(15)], axis=0)
    heads = jnp.concatenate([col[b * R : b * R + 1, :] for b in range(16)], axis=0)
    return first, before * equal(heads[:, 0:1], heads[:, 1:2]) - first


def shifted(n, col):
    same = equal(col[:, 0:1], col[:, 1:2])
    rows = lax.broadcasted_iota(jnp.int32, n.shape, 0)
    before = jnp.where(rows == 0, 0.0, pltpu.roll(n, 1, 0))
    return before * same - n


def norm_parts(a):
    width = a.shape[1]
    center = a - jnp.sum(a, axis=1, keepdims=True) * (1.0 / width)
    scale = lax.rsqrt(jnp.sum(center * center, axis=1, keepdims=True) * (1.0 / width) + 1e-05)
    return center, scale, center * scale


def norm_back(normed, scale, grad):
    width = grad.shape[1]
    inner = grad - jnp.sum(grad, axis=1, keepdims=True) * (1.0 / width)
    return scale * (inner - normed * (jnp.sum(grad * normed, axis=1, keepdims=True) * (1.0 / width)))


def sigmoid(a):
    return 1.0 / (1.0 + jnp.exp(-a))


CHUNK = 128


def halves(a):
    high = a.astype(BF)
    return high, (a - high.astype(F32)).astype(BF)


def dot3(a, b, dims):
    def one(x, y):
        return lax.dot_general(x, y, (dims, ((), ())), preferred_element_type=F32)

    return one(a[0], b[0]) + (one(a[0], b[1]) + one(a[1], b[0]))


NN, NT, TN = ((1,), (0,)), ((1,), (1,)), ((0,), (0,))


def head_sums(a, ones):
    high, rest = a.astype(BF), a - a.astype(BF).astype(F32)
    mid = rest.astype(BF)
    low = (rest - mid.astype(F32)).astype(BF)

    def one(x):
        return lax.dot_general(x, ones, (NN, ((), ())), preferred_element_type=F32)

    return one(high) + (one(mid) + one(low))


def iota(shape, dim):
    return lax.broadcasted_iota(jnp.int32, shape, dim)


def head_ones(width, dtype):
    return (iota((width, width), 0) // ATTENTION_WIDTH == iota((width, width), 1) // ATTENTION_WIDTH).astype(dtype)


def by_head(pair):
    lane = iota(pair[0].shape, 1) // ATTENTION_WIDTH
    heads = pair[0].shape[1] // ATTENTION_WIDTH
    zero = jnp.zeros_like(pair[0])
    return tuple(jnp.concatenate([jnp.where(lane == h, a, zero) for h in range(heads)], axis=0) for a in pair)


def pick_heads(a, rows):
    lane = iota((rows, a.shape[1]), 1) // ATTENTION_WIDTH
    out = a[:rows]
    for h in range(1, a.shape[1] // ATTENTION_WIDTH):
        out = jnp.where(lane == h, a[h * rows : (h + 1) * rows], out)
    return out


def powers(lam, tab):
    L = tab.shape[1]
    at = iota((L, 1), 0).astype(F32)
    mid = L // 2
    tab[0] = jnp.exp(lam * (at - mid))
    tab[1] = jnp.exp(-lam * (at + (1.0 - mid)))
    tab[2] = jnp.exp(lam * at)
    tab[3] = jnp.exp(lam * (L - 1.0 - at))


def own_vectors(p, par_ref, vec):
    W = vec.shape[1]
    own = par_ref[6:10, pl.ds(pl.multiple_of(p.s * W, 128), W)]
    lam = -jnp.exp(own[0:1])
    vec[0:1, :] = lam
    vec[1:4, :] = own[1:4]
    vec[8:, :] = jnp.broadcast_to(jnp.exp(lam * CHUNK), (W, W)).T


def chunk_mask(col, row):
    L = col.shape[0]
    return (iota((L, L), 1) < iota((L, L), 0)) & (col == row)


def forward_chunk(x_ref, col_ref, row_ref, bound_ref, vec_ref, z_ref, zt_ref, o_ref, s_ref, tab, state):
    chunks, L = row_ref.shape[0], row_ref.shape[2]
    W = vec_ref.shape[1]
    heads = W // ATTENTION_WIDTH
    lam, bonus, gain, bias = (vec_ref[q : q + 1, :] for q in range(4))
    powers(lam, tab)
    ones = head_ones(W, BF)
    diag = head_ones(W, F32)
    decay = vec_ref[8 : 8 + W, :]
    state[...] = jnp.zeros_like(state)

    def step(i):
        rows = pl.ds(pl.multiple_of(i * L, L), L)
        r, k, v, p = (x_ref[rows, q * W : (q + 1) * W] for q in range(4))
        col = col_ref[rows, :]
        seg = col[:, 0:1]
        kept, tail = equal(seg, bound_ref[0, i]), equal(seg, bound_ref[0, i + 1])
        mask = chunk_mask(seg, row_ref[i])
        mask = jnp.concatenate([mask] * heads, axis=1)
        rs, ks = halves(r * tab[0]), halves(k * tab[1])
        scores = jnp.where(mask, dot3(rs, by_head(ks), NT), 0.0)
        vh = halves(v)
        out = dot3(halves(scores), by_head(vh), NN) + head_sums(r * k * bonus, ones) * v
        memory = state[...]
        s_ref[i] = memory
        out = out + kept * dot3(halves(r * tab[2]), halves(memory), NN)
        state[...] = bound_ref[1, i] * decay * memory + diag * dot3(halves(k * tab[3] * tail), vh, TN)
        o_ref[rows, :] = out
        center = out - head_sums(out, ones) * (1.0 / ATTENTION_WIDTH)
        spread = head_sums(center * center, ones) * (1.0 / ATTENTION_WIDTH)
        normed = center * lax.rsqrt(spread + 0.00064) * gain + bias
        z = (normed * (p * sigmoid(p))).astype(BF).astype(F32)
        z_ref[rows, :] = z.astype(BF)
        zt_ref[:, rows] = z.T.astype(BF)

    return step


def back_chunk(x_ref, o_ref, s_ref, gz_ref, col_ref, row_ref, bound_ref, vec_ref, g_ref, sums_ref, tab, grad_state, acc, carry, turned):
    chunks, L = row_ref.shape[0], row_ref.shape[2]
    W = vec_ref.shape[1]
    heads = W // ATTENTION_WIDTH
    lam, bonus, gain, bias = (vec_ref[q : q + 1, :] for q in range(4))
    powers(lam, tab)
    ones = head_ones(W, BF)
    diag = head_ones(W, F32)
    decay = vec_ref[8 : 8 + W, :]
    at = iota((L, 1), 0).astype(F32)
    mid = float(L // 2)
    grad_state[...] = jnp.zeros_like(grad_state)
    acc[...] = jnp.zeros_like(acc)
    carry[...] = jnp.zeros_like(carry)
    sums_ref[...] = jnp.zeros_like(sums_ref)

    def add(q, term):
        sums_ref[q : q + 1, :] += jnp.sum(term, axis=0, keepdims=True)

    def step(n):
        i = chunks - 1 - n
        rows = pl.ds(pl.multiple_of(i * L, L), L)
        r, k, v, p = (x_ref[rows, q * W : (q + 1) * W] for q in range(4))
        col = col_ref[rows, :]
        seg = col[:, 0:1]
        kept, tail = equal(seg, bound_ref[0, i]), equal(seg, bound_ref[0, i + 1])
        same_next = equal(seg, col[:, 2:3])
        o = o_ref[rows, :]
        gz = gz_ref[i].astype(F32)
        center = o - head_sums(o, ones) * (1.0 / ATTENTION_WIDTH)
        spread = head_sums(center * center, ones) * (1.0 / ATTENTION_WIDTH)
        scale = lax.rsqrt(spread + 0.00064)
        normed = center * scale
        gate = sigmoid(p)
        silu = p * gate
        gy = gz * silu
        gp = gz * (normed * gain + bias) * (gate * (1.0 + p * (1.0 - gate)))
        add(2, gy * normed)
        add(3, gy)
        gn = gy * gain
        go = scale * (
            gn
            - head_sums(gn, ones) * (1.0 / ATTENTION_WIDTH)
            - normed * (head_sums(gn * normed, ones) * (1.0 / ATTENTION_WIDTH))
        )
        mask = chunk_mask(seg, row_ref[i])
        mask = jnp.concatenate([mask] * heads, axis=1)
        rs_f, ks_f = r * tab[0], k * tab[1]
        r0_f, ke_f = r * tab[2] * kept, k * tab[3] * tail
        rs, ks, vh, goh = halves(rs_f), halves(ks_f), halves(v), halves(go)
        ks_by, v_by = by_head(ks), by_head(vh)
        scores = halves(jnp.where(mask, dot3(rs, ks_by, NT), 0.0))
        grad_scores = halves(jnp.where(mask, dot3(goh, v_by, NT), 0.0))
        memory = s_ref[i]
        gs = grad_state[...]
        mh, gsh = halves(memory), halves(gs)
        reward = head_sums(r * k * bonus, ones)
        grad_reward = head_sums(go * v, ones)
        g_rs = dot3(grad_scores, ks_by, NN)
        g_r0 = dot3(goh, mh, NT)
        g_ks = pick_heads(dot3(grad_scores, rs, TN), L)
        g_ke = dot3(vh, gsh, NT)
        gv = pick_heads(dot3(scores, goh, TN), L) + reward * go + dot3(halves(ke_f), gsh, NN)
        keep = bound_ref[1, i]
        acc[...] += keep * memory * gs
        grad_state[...] = keep * decay * gs + diag * dot3(halves(r0_f), goh, TN)
        gr = g_rs * tab[0] + g_r0 * (tab[2] * kept) + grad_reward * bonus * k
        gk = g_ks * tab[1] + g_ke * (tab[3] * tail) + grad_reward * bonus * r
        add(1, grad_reward * r * k)
        add(0, (at - mid) * (g_rs * rs_f) - (at + (1.0 - mid)) * (g_ks * ks_f) + at * (g_r0 * r0_f) + (L - 1.0 - at) * (g_ke * ke_f))
        grads = jnp.concatenate([gr, gk, gv, gp], axis=1).astype(BF).astype(F32)
        last = iota((L, 1), 0) == L - 1
        after = jnp.where(last, carry[0:1, :], pltpu.roll(grads, L - 1, 0)) * same_next
        carry[0:1, :] = grads[0:1, :]
        g_ref[rows, : 4 * W] = grads.astype(BF)
        g_ref[rows, 4 * W :] = after.astype(BF)
        turned[0 : 4 * W, rows] = grads.T.astype(BF)
        turned[4 * W :, rows] = after.T.astype(BF)

    return step


def back_finish(vec_ref, sums_ref, acc, L):
    W = vec_ref.shape[1]
    whole = dot3(halves(jnp.ones((8, W), F32)), halves(acc[...] * vec_ref[8 : 8 + W, :]), NT)
    sums_ref[0:1, :] = (sums_ref[0:1, :] + L * whole[0:1, :]) * vec_ref[0:1, :]


def time_forward_kernel(nd, x_ref, par_ref, row_ref, bound_ref, w_far, ow_far, rw_far, col_far,
                        all_ref, proj_far, zt_far, o_far, s_far, hid_ref, n2_ref, rp_ref, far_ref,
                        n1, land, op, lw, tab, state, zin, w_ref, ow_ref, rw_ref, rt_ref, col_ref, proj_ref, z_ref, zt_ref,
                        o_ref, s_ref, vec, cs, cr, ss, rs, ls, ms):
    p = Place()
    met = greet(chip_mates(p) + [p.dev(p.at(dc=1))] + beside(p, nd))
    c = Copies(cs, cr)
    moves = Moves(ms)
    ow_in, w_in, col_in, rw_in = (
        moves.start(a, b) for a, b in ((ow_far, ow_ref), (w_far, w_ref), (col_far, col_ref), (rw_far, rw_ref))
    )
    R = x_ref.shape[0]
    Q, W = w_ref.shape[0], w_ref.shape[2]
    C = lw.shape[2]
    begin, end = chip_plan(p, c, 18, ow_ref, op)
    go, own_part = across_plan(p, nd, c, 25, op, lw)
    recept_begin, recept_end = chip_plan(p, c, 43, rt_ref, rp_ref)
    blk = blocks_of(land)
    plan = gather_plan(p, c, 0, n1, blk, around=True)
    start, wait = save_blocks(land, all_ref, ls)
    n1[...] = (norm_parts(x_ref[...].astype(F32))[2] * par_ref[0:1, :] + par_ref[1:2, :]).astype(BF)
    met()

    def ready():
        begin()
        blk(p.s)[...] = n1[...]
        own_vectors(p, par_ref, vec)
        w_in.wait()
        col_in.wait()

    def turn():
        rw_in.wait()
        for k in range(0, rw_ref.shape[0], 256):
            rt_ref[:, k : k + 256] = rw_ref[k : k + 256, :].T

    def across():
        own_part[...] = op[...]
        go(0)()

    def work(k):
        start(k)
        rows = pl.ds(pl.multiple_of(k * 2 * R, 16), 2 * R)
        n = land[k].astype(F32)
        shift = shifted(n, col_ref[rows, :])
        for q in range(Q):
            m = (n + shift * par_ref[2 + q : 3 + q, :]).astype(BF)
            proj_ref[rows, q * W : (q + 1) * W] = jnp.dot(m, w_ref[q], preferred_element_type=F32)

    ow_in.wait()
    run_gather(plan, work, {0: [ready], 1: [turn], 3: [end, across], 7: [go(1, 2)]})
    recept_begin()
    first, shift = heads_of_blocks(land, col_ref)
    for q in range(Q):
        m = (first + shift * par_ref[2 + q : 3 + q, :]).astype(BF)
        out = jnp.dot(m, w_ref[q], preferred_element_type=F32)
        for b in range(0, 16, 2):
            proj_ref[b * R : b * R + 1, q * W : (q + 1) * W] = out[b : b + 1]
    saves = [moves.start(proj_ref, proj_far)]

    chunk = forward_chunk(proj_ref, col_ref, row_ref, bound_ref, vec, z_ref, zt_ref, o_ref, s_ref, tab, state)
    swap = Swap(p, lambda i: z_ref.at[pl.ds(pl.multiple_of(i * R, 16), R)], zin, ss, rs)
    when = {0: go(3, 4), 2: go(5, 6, 7)}

    def step(n, unused):
        chunk(2 * n)
        chunk(2 * n + 1)
        swap.give(2 * n)
        swap.give(2 * n + 1)
        for at, act in when.items():
            pl.when(n == at)(act)
        return 0

    lax.fori_loop(0, row_ref.shape[0] // 2, step, 0)
    saves += [moves.start(a, b) for a, b in ((zt_ref, zt_far), (o_ref, o_far), (s_ref, s_far))]
    go(8, 9)()
    saves.append(moves.start(lw, far_ref))
    swap.all(swap.take)
    z_here = jnp.concatenate([zin[2 * k + core] for core in range(2) for k in range(8)], axis=1)
    for d in range(8):
        cols = slice(d * C, (d + 1) * C)
        hid_ref[:, cols] = x_ref[:, cols].astype(F32) + jnp.dot(z_here, lw[d], preferred_element_type=F32)
    n2_ref[...] = (norm_parts(hid_ref[...])[2] * par_ref[10:11, :] + par_ref[11:12, :]).astype(BF)
    recept_end()
    wait()
    for cp in saves:
        cp.wait()
    swap.all(swap.sent)
    c.finish()


def time_forward(nd, x, par, rows, bounds, w, ow, rw, cols, cid):
    R, C = x.shape
    T, W = 16 * R, w.shape[2]
    chunks, L = rows.shape[0], rows.shape[2]
    return pl.pallas_call(
        functools.partial(time_forward_kernel, nd),
        out_shape=(
            jax.ShapeDtypeStruct((T, C), BF),
            jax.ShapeDtypeStruct((T, 4 * W), F32),
            jax.ShapeDtypeStruct((W, T), BF),
            jax.ShapeDtypeStruct((T, W), F32),
            jax.ShapeDtypeStruct((chunks, W, W), F32),
            jax.ShapeDtypeStruct((R, C), F32),
            jax.ShapeDtypeStruct((R, C), BF),
            jax.ShapeDtypeStruct((8 * R, C // nd), BF),
            jax.ShapeDtypeStruct((8, 16 * R, C // 8), BF),
        ),
        in_specs=[WHOLE] * 3 + [pl.BlockSpec(memory_space=pltpu.SMEM)] + [FAR] * 4,
        out_specs=(FAR,) * 5 + (WHOLE,) * 3 + (FAR,),
        scratch_shapes=[
            VMEM((R, C), BF), VMEM((8, 2 * R, C), BF), VMEM((8 * R, C // nd), BF), VMEM((8, 16 * R, C // 8), BF), VMEM((4, L, W), F32),
            VMEM((W, W), F32), VMEM((16, R, W), BF), VMEM(w.shape, BF), VMEM((R, C), BF), VMEM((C, W), BF), VMEM((W, C), BF),
            VMEM(cols.shape, F32), VMEM((T, 4 * W), F32), VMEM((T, W), BF), VMEM((W, T), BF), VMEM((T, W), F32),
            VMEM((chunks, W, W), F32), VMEM((8 + W, W), F32),
            DMA((50,)), DMA((50,)), DMA((16,)), DMA((16,)), DMA((16,)), DMA((9,)),
        ],
        compiler_params=params(cid, 56),
        name="time_forward",
    )(x, par, rows, bounds, w, ow, rw, cols)


def key_kernel(nd, a_ref, rp_ref, par_ref, k_far, col_far, vw_far, mw_far,
               all_ref, in_ref, lift_far, sq_far, rin_ref, sh_ref, vt_far, mt_far, fold_far, far_ref,
               land, mixed, k_ref, w_ref, col_ref, vw_ref, mw_ref, lift_ref, sq_ref, vt_ref, mt_ref, fold_ref,
               cs, cr, ls, ms, ks):
    p = Place()
    met = greet(near(p) + beside(p, nd))
    c = Copies(cs, cr)
    moves = Moves(ms)
    col_in, k_in, mw_in, vw_in = (
        moves.start(a, b) for a, b in ((col_far, col_ref), (k_far, k_ref), (mw_far, mw_ref), (vw_far, vw_ref))
    )
    R = a_ref.shape[0]
    go, own_part = across_plan(p, nd, c, 18, rp_ref, far_ref)
    saves = [moves.start(rp_ref, own_part)]
    blk = blocks_of(land)
    plan = gather_plan(p, c, 0, a_ref, blk)
    start, wait = save_blocks(land, all_ref, ls)
    met()
    nu_k, nu_r = par_ref[12:13, :], par_ref[13:14, :]
    Q, W = mw_ref.shape[0], mw_ref.shape[2]

    def ready():
        go(0)()
        blk(p.s)[...] = a_ref[...]
        k_in.wait()
        for k in range(0, w_ref.shape[0], 256):
            w_ref[k : k + 256, :] = k_ref[:, k : k + 256].T
        col_in.wait()

    def turn():
        vw_in.wait()
        for k in range(0, w_ref.shape[0], 256):
            vt_ref[k : k + 256, :] = vw_ref[:, k : k + 256].T
        saves.append(moves.start(vt_ref, vt_far))

    def fold(*qs):
        def run():
            if qs[0] == 0:
                mw_in.wait()
            for q in qs:
                for k in range(0, mw_ref.shape[1], 256):
                    cols, rows = slice(k, k + 256), slice(q * W, (q + 1) * W)
                    turned = mw_ref[q, cols, :].T
                    mt_ref[rows, cols] = turned
                    part = turned.astype(F32)
                    mu = par_ref[2 + q : 3 + q, cols]
                    fold_ref[rows, cols] = ((1.0 - mu) * part).astype(BF)
                    fold_ref[(Q + q) * W : (Q + q + 1) * W, cols] = (mu * part).astype(BF)
            if qs[-1] == Q - 1:
                saves.append(moves.start(mt_ref, mt_far))
                saves.append(moves.start(fold_ref, fold_far))

        return run

    def tail_copy(k):
        rows = pl.ds(16, 2 * R - 16)
        return pltpu.make_async_copy(mixed.at[k, rows], in_ref.at[k, rows], ks.at[k])

    def work(k):
        start(k)
        n = land[k].astype(F32)
        rows = pl.ds(pl.multiple_of(k * 2 * R, 16), 2 * R)
        m = (n + shifted(n, col_ref[rows, :]) * nu_k).astype(BF)
        mixed[k] = m
        e = jnp.maximum(jnp.dot(m, w_ref[...], preferred_element_type=F32), 0.0)
        lift_ref[rows, :] = e
        sq_ref[rows, :] = (e * e).astype(BF)
        tail_copy(k).start()

    run_gather(plan, work, {0: [ready], 1: [turn], 3: [go(1, 2)], 4: [fold(0, 1)], 5: [go(3, 4)], 6: [fold(2, 3)], 7: [go(5, 6, 7)]})
    first, shift = heads_of_blocks(land, col_ref)
    head = first + shift * nu_k
    e = jnp.maximum(jnp.dot(head.astype(BF), w_ref[...], preferred_element_type=F32), 0.0)
    sq = e * e
    top = lax.broadcasted_iota(jnp.int32, (16, 1), 0) == 0
    for b in range(0, 16, 2):
        rows = slice(b * R, b * R + 16)
        mixed[b // 2, 0:16, :] = jnp.where(top, head[b : b + 1], mixed[b // 2, 0:16, :].astype(F32)).astype(BF)
        lift_ref[b * R : b * R + 1, :] = e[b : b + 1]
        sq_ref[rows, :] = jnp.where(top, sq[b : b + 1], sq_ref[rows, :].astype(F32)).astype(BF)
    saves.append(moves.start(lift_ref, lift_far))
    saves.append(moves.start(sq_ref, sq_far))
    saves.append(moves.start(mixed.at[:, pl.ds(0, 16)], in_ref.at[:, pl.ds(0, 16)]))
    n = a_ref[...].astype(F32)
    mine = lax.broadcasted_iota(jnp.int32, (16, 1), 0) == p.s
    own_first = jnp.sum(jnp.where(mine, shift, 0.0), axis=0, keepdims=True)
    here = pl.ds(pl.multiple_of(p.s * R, 16), R)
    topmost = lax.broadcasted_iota(jnp.int32, (R, 1), 0) == 0
    moved = jnp.where(topmost, own_first, shifted(n, col_ref[here, :]))
    sh_ref[...] = moved
    rin_ref[...] = (n + moved * nu_r).astype(BF)
    go(8, 9)()
    for k in range(8):
        tail_copy(k).wait()
    wait()
    for cp in saves:
        cp.wait()
    c.finish()


def key_side(nd, a, part, par, kt, cols, vw, mw, cid):
    R, C = a.shape
    T, units = 16 * R, kt.shape[0]
    Q, W = mw.shape[0], mw.shape[2]
    return pl.pallas_call(
        functools.partial(key_kernel, nd),
        out_shape=(
            jax.ShapeDtypeStruct((T, C), BF),
            jax.ShapeDtypeStruct((8, 2 * R, C), BF),
            jax.ShapeDtypeStruct((T, units), F32),
            jax.ShapeDtypeStruct((T, units), BF),
            jax.ShapeDtypeStruct((R, C), BF),
            jax.ShapeDtypeStruct((R, C), F32),
            jax.ShapeDtypeStruct((C, units), BF),
            jax.ShapeDtypeStruct((Q * W, C), BF),
            jax.ShapeDtypeStruct((2 * Q * W, C), BF),
            jax.ShapeDtypeStruct((8, T, C // 8), BF),
        ),
        in_specs=[WHOLE] * 3 + [FAR] * 4,
        out_specs=(FAR,) * 4 + (WHOLE,) * 2 + (FAR,) * 4,
        scratch_shapes=[
            VMEM((8, 2 * R, C), BF), VMEM((8, 2 * R, C), BF), VMEM((units, C), BF), VMEM((C, units), BF), VMEM(cols.shape, F32),
            VMEM((units, C), BF), VMEM(mw.shape, BF), VMEM((T, units), F32), VMEM((T, units), BF), VMEM((C, units), BF),
            VMEM((Q * W, C), BF), VMEM((2 * Q * W, C), BF),
            DMA((36,)), DMA((36,)), DMA((16,)), DMA((12,)), DMA((16,)),
        ],
        compiler_params=params(cid, 60),
        name="key_side",
    )(a, part, par, kt, cols, vw, mw)


def column_tiles(refs, tile, sem):
    C = tile.shape[2]

    def copy(u, ref):
        if len(ref.shape) == 3:
            return pltpu.make_async_copy(ref.at[u % 8], tile.at[u % 2], sem.at[u % 2])
        return pltpu.make_async_copy(ref.at[:, pl.ds(pl.multiple_of((u % 8) * C, C), C)], tile.at[u % 2], sem.at[u % 2])

    def start(u, kind):
        copy(u, refs[kind]).start()

    def wait(u, kind):
        copy(u, refs[kind]).wait()

    return start, wait


def sum_scratch(R, C):
    return [
        VMEM((8, 2, R, C), BF), VMEM((8, R, C), BF), VMEM((R, C), BF), VMEM((2, R, C), BF), VMEM((R, C), BF),
        VMEM((2, R // 2, C), BF), VMEM((2, R, C), BF),
    ]


def sum_plan(p, c, base, l_ref, w_ref, o_ref, scratch):
    pa, cb, zt, xs, zf, hv, xf = scratch
    R = o_ref.shape[0]
    H = R // 2
    core, xp, xm, zz = (p.dev(i) for i in (p.at(dc=1), p.at(dx=1), p.at(dx=-1), p.at(dz=1)))
    upper, lower = pl.ds(0, H), pl.ds(H, H)
    order = [(2, 1), (-1, 1), (1, 1), (2, 0), (0, 1), (1, 0), (-1, 0), (0, 0)]

    def send(k, src, dst, to):
        c.add(base + k, src, dst, to)
        c.start(base + k)

    def landed(k, ref):
        c.landed(base + k, ref)

    def give(i):
        k = p.at(*order[i]) // 2
        rows = l_ref[pl.ds(pl.multiple_of(k * 2 * R, 16), 2 * R), :]
        pa[i] = jnp.dot(rows, w_ref[...], preferred_element_type=F32).astype(BF).reshape(2, R, -1)
        send(i, pa.at[i, 1 - p.c], cb.at[i], core)

    def pair(i):
        landed(i, cb.at[i])
        pa[i, p.c] = (pa[i, p.c].astype(F32) + cb[i].astype(F32)).astype(BF)

    def one():
        give(0)
        give(1)
        pair(0)
        send(8, pa.at[0, p.c], zt, zz)
        give(2)
        pair(1)
        send(9, pa.at[1, p.c], xs.at[1], xm)
        pair(2)
        send(10, pa.at[2, p.c], xs.at[0], xp)

    def more():
        give(3)
        give(5)
        pair(3)
        give(6)
        pair(5)
        send(11, pa.at[5, p.c, lower], xf.at[0, lower], xp)
        give(4)
        pair(6)
        send(12, pa.at[6, p.c, upper], xf.at[1, upper], xm)
        give(7)
        pair(4)
        pair(7)

    def two():
        landed(8, zt)
        pa[3, p.c] = (pa[3, p.c].astype(F32) + zt[...].astype(F32)).astype(BF)
        send(13, pa.at[3, p.c, upper], hv.at[0], xp)
        send(14, pa.at[3, p.c, lower], hv.at[1], xm)

    def three():
        landed(9, xs.at[1])
        landed(10, xs.at[0])
        pa[4, p.c] = (pa[4, p.c].astype(F32) + xs[0].astype(F32) + xs[1].astype(F32)).astype(BF)
        send(15, pa.at[4, p.c], zf, zz)

    def four():
        landed(13, hv.at[0])
        pa[5, p.c, upper] = (pa[5, p.c, upper].astype(F32) + hv[0].astype(F32)).astype(BF)
        send(16, pa.at[5, p.c, upper], xf.at[0, upper], xp)
        landed(14, hv.at[1])
        pa[6, p.c, lower] = (pa[6, p.c, lower].astype(F32) + hv[1].astype(F32)).astype(BF)
        send(17, pa.at[6, p.c, lower], xf.at[1, lower], xm)

    def five():
        landed(11, xf.at[0, lower])
        landed(12, xf.at[1, upper])
        landed(15, zf)
        o_ref[...] = pa[7, p.c].astype(F32) + zf[...].astype(F32)

    def six():
        landed(16, xf.at[0, upper])
        landed(17, xf.at[1, lower])
        o_ref[...] = o_ref[...] + xf[0].astype(F32) + xf[1].astype(F32)

    return [one, more, two, three, four, five, six]


def value_kernel(rin_ref, g_ref, hid_ref, l_far, w_far, vt_far, lift_far, far_ref,
                 res_ref, gf_ref, rc_ref, ge_far, get_far, vg_far, *rest):
    scratch = rest[:7]
    (o_ref, f_ref, gate_ref, gkv, land, tile, l_ref, w_ref, vt_ref, lift_ref, ge_ref, get_ref, st_ref, acc,
     cs, cr, ss, rs, ts, ms) = rest[7:]
    p = Place()
    met = greet(near(p))
    c = Copies(cs, cr)
    moves = Moves(ms)
    R = o_ref.shape[0]
    T, U = l_ref.shape
    W = gf_ref.shape[2]
    C = tile.shape[2]
    fetch, have = column_tiles((far_ref,), tile, ts)
    l_in, w_in, vt_in, lift_in = (
        moves.start(a, b) for a, b in ((l_far, l_ref), (w_far, w_ref), (vt_far, vt_ref), (lift_far, lift_ref))
    )
    fetch(0, 0)
    sums = sum_plan(p, c, 0, l_ref, w_ref, o_ref, scratch)
    blk = blocks_of(land)
    plan = gather_plan(p, c, 18, gkv, blk)
    swap = Swap(p, lambda i: gf_ref.at[i], rc_ref, ss, rs)
    met()
    l_in.wait()
    w_in.wait()
    sums[0]()

    def unit(d, unused):
        pl.when(d < 7)(lambda: fetch(d + 1, 0))
        have(d, 0)
        cols = pl.ds(pl.multiple_of(d * C, C), C)
        part = lax.dot_general(rin_ref[:, cols], tile[d % 2], (NT, ((), ())), preferred_element_type=F32)

        @pl.when(d == 0)
        def _():
            f_ref[...] = part

        @pl.when(d > 0)
        def _():
            f_ref[...] += part

        return 0

    lax.fori_loop(0, 8, unit, 0)
    for s in range(16):
        at = ((s % 2) * 8 + s // 2) * W
        cols = slice(s * W, (s + 1) * W)
        gate = sigmoid(f_ref[:, at : at + W])
        gate_ref[:, cols] = gate
        gkv[:, cols] = (g_ref[:, cols].astype(F32) * gate).astype(BF)
    plan[0]()
    sums[1]()
    sums[2]()
    sums[3]()
    blk(p.s)[...] = gkv[...]
    acc[...] = jnp.zeros_like(acc)
    for r in range(0, T, 256):
        st_ref[:, r : r + 256] = l_ref[r : r + 256, :].T
    vt_in.wait()
    lift_in.wait()

    saves = []

    def work(k):
        rows = pl.ds(pl.multiple_of(k * 2 * R, 16), 2 * R)
        cols = pl.ds(pl.multiple_of(k * 2 * R, 128), 2 * R)
        gs = jnp.dot(land[k], vt_ref[...], preferred_element_type=F32)
        ge = gs * 2.0 * lift_ref[rows, :]
        ge_ref[rows, :] = ge.astype(BF)
        get_ref[:, cols] = ge.T.astype(BF)
        acc[...] += jnp.dot(st_ref[:, cols], land[k], preferred_element_type=F32)
        saves.append(moves.start(ge_ref.at[rows], ge_far.at[rows]))
        saves.append(moves.start(get_ref.at[:, cols], get_far.at[:, cols]))

    ready = plan[1]() + plan[2]()
    work(ready.pop(0))
    ready += plan[3]()
    work(ready.pop(0))
    ready += plan[5]()
    work(ready.pop(0))
    sums[4]()
    work(ready.pop(0))
    ready += plan[4]() + plan[6]()
    sums[5]()
    sums[6]()
    kv, gate = o_ref[...], gate_ref[...]
    gf = g_ref[...].astype(F32) * kv * (gate * (1.0 - gate))
    for s in range(16):
        gf_ref[s] = gf[:, s * W : (s + 1) * W].astype(BF)
    swap.all(swap.give)
    res_ref[...] = (hid_ref[...] + (gate * kv).astype(BF).astype(F32)).astype(BF)
    for n in range(7, 10):
        ready += plan[n]()
        work(ready.pop(0))
    for k in ready:
        work(k)
    for d in range(8):
        rows = slice((d % 4) * U, (d % 4 + 1) * U)
        tile[d // 4, rows, :] = acc[:, d * C : (d + 1) * C].astype(BF)
        saves.append(moves.start(tile.at[d // 4, pl.ds((d % 4) * U, U)], vg_far.at[d]))
    swap.all(swap.take)
    for cp in saves:
        cp.wait()
    swap.all(swap.sent)
    c.finish()


def value_side(rin, g, hidden, l, w, vt, lift, far, cid):
    R, C = hidden.shape
    T, U = l.shape
    W = C // 16
    return pl.pallas_call(
        value_kernel,
        out_shape=(
            jax.ShapeDtypeStruct((R, C), BF),
            jax.ShapeDtypeStruct((16, R, W), BF),
            jax.ShapeDtypeStruct((16, R, W), BF),
            jax.ShapeDtypeStruct((T, U), BF),
            jax.ShapeDtypeStruct((U, T), BF),
            jax.ShapeDtypeStruct((8, U, C // 8), BF),
        ),
        in_specs=[WHOLE] * 3 + [FAR] * 5,
        out_specs=(WHOLE,) * 3 + (FAR,) * 3,
        scratch_shapes=sum_scratch(R, C)
        + [VMEM((R, C), F32), VMEM((R, C), F32), VMEM((R, C), F32), VMEM((R, C), BF), VMEM((8, 2 * R, C), BF), VMEM((2, T, C // 8), BF)]
        + [VMEM((T, U), BF), VMEM((U, C), BF), VMEM((C, U), BF), VMEM((T, U), F32)]
        + [VMEM((T, U), BF), VMEM((U, T), BF), VMEM((U, T), BF), VMEM((U, C), F32)]
        + [DMA((36,)), DMA((36,)), DMA((16,)), DMA((16,)), DMA((2,)), DMA((28,))],
        compiler_params=params(cid, 62),
        name="value_side",
    )(rin, g, hidden, l, w, vt, lift, far)


def dp_scratch(J, C):
    return [VMEM((2, 2, J // 2, C), BF), VMEM((2, 2, J // 2, C), BF), VMEM((2, 2, J, C), BF), VMEM((2, J, C), BF)]


def dp_plan(p, nd, c, base, g_ref, o_ref, scratch):
    hv, stage, xf, zb = scratch
    J = g_ref.shape[1]
    ny = nd // 2
    y, zl = p.dp // 2, p.dp % 2
    yp, ym, yo = (y + 1) % ny, (y + ny - 1) % ny, (y + 2) % ny
    to_p, to_m, to_z = (2 * yp + zl, p.s), (2 * ym + zl, p.s), (2 * y + 1 - zl, p.s)

    def piece(base, first, rows):
        H = rows // 2
        every, up, lo = pl.ds(first, rows), pl.ds(first, H), pl.ds(first + H, H)
        half = pl.ds(first // 2, H)

        def pay(at, part):
            return g_ref.at[pl.ds(2 * at, 2), part]

        c.add(base, pay(yo, up), hv.at[0, :, half], to_p)
        c.add(base + 1, pay(yo, lo), hv.at[1, :, half], to_m)
        c.add(base + 2, pay(yp, lo), xf.at[0, :, lo], to_p)
        c.add(base + 3, pay(ym, up), xf.at[1, :, up], to_m)
        c.add(base + 4, stage.at[0, :, half], xf.at[0, :, up], to_p)
        c.add(base + 5, stage.at[1, :, half], xf.at[1, :, lo], to_m)
        c.add(base + 6, zb.at[0, every], zb.at[1, every], to_z)

        def one():
            c.start(base, base + 1, base + 2, base + 3)

        def two():
            c.landed(base, hv.at[0, :, half])
            stage[0, :, half] = (g_ref[pl.ds(2 * yp, 2), up].astype(F32) + hv[0, :, half].astype(F32)).astype(BF)
            c.start(base + 4)
            c.landed(base + 1, hv.at[1, :, half])
            stage[1, :, half] = (g_ref[pl.ds(2 * ym, 2), lo].astype(F32) + hv[1, :, half].astype(F32)).astype(BF)
            c.start(base + 5)

        def total(which):
            return g_ref[2 * y + which, every].astype(F32) + xf[0, which, every].astype(F32) + xf[1, which, every].astype(F32)

        def three():
            c.landed(base + 2, xf.at[0, :, lo])
            c.landed(base + 3, xf.at[1, :, up])
            c.landed(base + 4, xf.at[0, :, up])
            c.landed(base + 5, xf.at[1, :, lo])
            zb[0, every] = total(1 - zl).astype(BF)
            c.start(base + 6)
            o_ref[0, every] = total(zl)

        def four():
            c.landed(base + 6, zb.at[1, every])
            o_ref[0, every] += zb[1, every].astype(F32)

        return one, two, three, four

    first, second = piece(base, 0, J // 2), piece(base + 7, J // 2, J // 2)

    def both(n):
        def run():
            first[n]()
            second[n]()

        return run

    return [both(0), both(1), first[2], second[2], both(3)]


def no_sums(g_ref, o_ref):
    def copy():
        o_ref[...] = g_ref[...].astype(F32)

    return [lambda: None] * 4 + [copy]


def key_back_kernel(rc_ref, gf_ref, par_ref, g_ref, l_far, w_far, lt_far, col_far, hid_far, sh_far, vg_far,
                    in_hbm, n2_hbm, far_ref, out_far, gh_ref, ghb_ref, rows_ref, gg_far, gz_ref, *rest):
    scratch = rest[:7]
    (o_ref, rt, gfp, ga_ref, gzp, halo, tile, strip, l_ref, w_ref, lt_ref, col_ref, hid_ref, sh_ref, gg_ref,
     cs, cr, ss, rs, ts, os, ms) = rest[7:]
    p = Place()
    met = greet(near(p) + [p.dev((p.s + 1) % 16), p.dev((p.s + 15) % 16)])
    c = Copies(cs, cr)
    moves = Moves(ms)
    T, U = l_ref.shape
    R, width = o_ref.shape
    W = rc_ref.shape[2]
    C = tile.shape[2]
    l_in, w_in, lt_in, col_in, hid_in, sh_in, vg_in = (
        moves.start(a, b)
        for a, b in (
            (l_far, l_ref), (w_far, w_ref), (lt_far, lt_ref), (col_far, col_ref), (hid_far, hid_ref), (sh_far, sh_ref),
            (vg_far, gg_ref.at[:, pl.ds(0, U)]),
        )
    )
    fetch, have = column_tiles((in_hbm, n2_hbm, far_ref), tile, ts)
    fetch(0, 0)

    def strip_copy(n):
        return pltpu.make_async_copy(out_far.at[:, pl.ds(pl.multiple_of(n * 2 * W, 16), 2 * W)], strip.at[n % 2], os.at[n % 2])

    c.add(18, halo.at[0], halo.at[1], p.dev((p.s + 15) % 16))
    sums = sum_plan(p, c, 0, l_ref, w_ref, o_ref, scratch)
    swap = Swap(p, lambda i: gzp.at[i], gz_ref, ss, rs)
    met()
    nu_k, nu_r = par_ref[12:13, :], par_ref[13:14, :]

    def turn():
        last = lax.broadcasted_iota(jnp.int32, (R, 1), 0) == R - 1
        for b in range(16):
            part = rc_ref[b].astype(F32)
            after = rc_ref[b + 1, 0:16, :].astype(F32)[0:1] if b < 15 else jnp.zeros((1, W), F32)
            col = col_ref[b * R : (b + 1) * R, :]
            moved = jnp.where(last, after, pltpu.roll(part, R - 1, 0)) * equal(col[:, 0:1], col[:, 2:3])
            rt[0:W, b * R : (b + 1) * R] = part.T.astype(BF)
            rt[W:, b * R : (b + 1) * R] = moved.T.astype(BF)
        for s in range(16):
            at = ((s % 2) * 8 + s // 2) * W
            gfp[:, at : at + W] = gf_ref[s]

    def units(kind, lo, hi):
        def unit(d, unused):
            u = 8 * kind + d
            if hi < 8:
                fetch(u + 1, kind)
            else:
                pl.when(d < 7)(lambda: fetch(u + 1, kind))
                if kind < 2:
                    pl.when(d == 7)(lambda: fetch(u + 1, kind + 1))
            have(u, kind)
            rhs = tile[d % 2]
            cols = pl.ds(pl.multiple_of(d * C, C), C)
            if kind == 0:
                gg_ref[d, U : 2 * U, :] = jnp.dot(lt_ref[...], rhs, preferred_element_type=F32).astype(BF)
            elif kind == 1:
                out = jnp.dot(rt[...], rhs, preferred_element_type=F32)
                gg_ref[d, 2 * U :, :] = (out[:W] + par_ref[13:14, cols] * (out[W:] - out[:W])).astype(BF)
            else:
                ga_ref[:, cols] = jnp.dot(gfp[...], rhs, preferred_element_type=F32)
            return 0

        lax.fori_loop(lo, hi, unit, 0)

    l_in.wait()
    w_in.wait()
    sums[0]()
    sums[1]()
    lt_in.wait()
    units(0, 0, 4)
    sums[2]()
    sums[3]()
    units(0, 4, 8)
    col_in.wait()
    turn()
    units(1, 0, 4)
    sums[4]()
    units(1, 4, 8)
    vg_in.wait()
    saves = [moves.start(gg_ref, gg_far)]
    units(2, 0, 8)
    sums[5]()
    strip_copy(0).start()
    hid_in.wait()
    sh_in.wait()
    unused, scale, normed = norm_parts(hid_ref[...])
    sums[6]()
    ga_k, ga_r, shift = o_ref[...], ga_ref[...], sh_ref[...]
    here = pl.ds(pl.multiple_of(p.s * R, 16), R)
    col = col_ref[here, :]
    moved = (ga_k * nu_k + ga_r * nu_r) * equal(col[:, 0:1], col[:, 1:2])
    halo[0] = moved[0:8]
    c.start(18)
    held = ga_k - ga_k * nu_k + (ga_r - ga_r * nu_r)
    rows_ref[...] = jnp.zeros_like(rows_ref)
    rows_ref[2:3, :] = jnp.sum(ga_k * shift, axis=0, keepdims=True)
    rows_ref[3:4, :] = jnp.sum(ga_r * shift, axis=0, keepdims=True)
    c.landed(18, halo.at[1])
    last = lax.broadcasted_iota(jnp.int32, (R, 1), 0) == R - 1
    grad = held + jnp.where(last, halo[1, 0:1, :], pltpu.roll(moved, R - 1, 0))
    gh = g_ref[...].astype(F32) + norm_back(normed, scale, grad * par_ref[10:11, :])
    gh_ref[...] = gh
    ghb_ref[...] = gh.astype(BF)

    def back_out(n, unused):
        pl.when(n < 7)(lambda: strip_copy(n + 1).start())
        strip_copy(n).wait()
        part = lax.dot_general(ghb_ref[:, 0:C], strip[n % 2, 0], (NT, ((), ())), preferred_element_type=F32)
        for d in range(1, 8):
            part = part + lax.dot_general(
                ghb_ref[:, d * C : (d + 1) * C], strip[n % 2, d], (NT, ((), ())), preferred_element_type=F32
            )
        for k in range(2):
            to = 2 * ((2 * n + k) % 8) + (2 * n + k) // 8
            gzp[to] = part[:, k * W : (k + 1) * W].astype(BF)
            swap.give(to)
        return 0

    lax.fori_loop(0, 8, back_out, 0)
    rows_ref[0:1, :] = jnp.sum(grad * normed, axis=0, keepdims=True)
    rows_ref[1:2, :] = jnp.sum(grad, axis=0, keepdims=True)
    for cp in saves:
        cp.wait()
    swap.all(swap.take)
    swap.all(swap.sent)
    c.finish()


def key_back(rc, gf, par, g, l, w, lt, cols, hidden, sh, vg, key_in, n2_all, far, out_far, cid):
    R, C = hidden.shape
    T, U, W = 16 * R, l.shape[1], rc.shape[2]
    return pl.pallas_call(
        key_back_kernel,
        out_shape=(
            jax.ShapeDtypeStruct((R, C), F32),
            jax.ShapeDtypeStruct((R, C), BF),
            jax.ShapeDtypeStruct((8, C), F32),
            jax.ShapeDtypeStruct((8, 2 * U + W, C // 8), BF),
            jax.ShapeDtypeStruct((16, R, W), BF),
        ),
        in_specs=[WHOLE] * 4 + [FAR] * 11,
        out_specs=(WHOLE,) * 3 + (FAR, WHOLE),
        scratch_shapes=sum_scratch(R, C)
        + [VMEM((R, C), F32), VMEM((2 * W, T), BF), VMEM((R, C), BF), VMEM((R, C), F32), VMEM((16, R, W), BF), VMEM((2, 8, C), F32)]
        + [VMEM((2, T, C // 8), BF), VMEM((2, 8, 2 * W, C // 8), BF), VMEM((T, U), BF), VMEM((U, C), BF), VMEM((U, T), BF)]
        + [VMEM(cols.shape, F32), VMEM((R, C), F32), VMEM((R, C), F32), VMEM((8, 2 * U + W, C // 8), BF)]
        + [DMA((19,)), DMA((19,)), DMA((16,)), DMA((16,)), DMA((2,)), DMA((2,)), DMA((8,))],
        compiler_params=params(cid, 60),
        name="key_back",
    )(rc, gf, par, g, l, w, lt, cols, hidden, sh, vg, key_in, n2_all, far, out_far)


def time_back_kernel(nd, gh_ref, gz_ref, par_ref, row_ref, bound_ref, early_far, x_far, o_far, s_far, col_far, zt_far, mixt_far, n1_hbm,
                     g_far, gg_far, sums_ref, mug_ref, dp_ref,
                     tab, grad_state, acc, carry, land, turned, tile, vec, early_ref, x_ref, o_ref, s_ref, col_ref, zt_ref, mixt_ref,
                     g_ref, gg_ref, d0, d1, d2, d3, cs, cr, ts, ms):
    p = Place()
    met = greet(near(p) + beside(p, nd))
    c = Copies(cs, cr)
    moves = Moves(ms)
    W = vec.shape[1]
    chunks, L = row_ref.shape[0], row_ref.shape[2]
    C = tile.shape[2]
    early_in, x_in, o_in, s_in, col_in, zt_in, mixt_in = (
        moves.start(a, b)
        for a, b in (
            (early_far, early_ref), (x_far, x_ref), (o_far, o_ref), (s_far, s_ref), (col_far, col_ref), (zt_far, zt_ref),
            (mixt_far, mixt_ref),
        )
    )
    fetch, have = column_tiles((n1_hbm,), tile, ts)
    fetch(0, 0)
    blk = rows_of(land)
    plan = gather_plan(p, c, 0, gh_ref, blk)
    sums = dp_plan(p, nd, c, 18, early_ref, dp_ref, (d0, d1, d2, d3)) if nd > 1 else no_sums(early_ref, dp_ref)
    own_vectors(p, par_ref, vec)
    met()
    plan[0]()
    early_in.wait()
    sums[0]()
    blk(p.s)[...] = gh_ref[...]
    when = {6: [plan[1], plan[2]], 8: [sums[1]], 11: [plan[3], plan[4]], 14: [plan[5], plan[6], plan[7]]}
    for cp in (x_in, o_in, s_in, col_in):
        cp.wait()
    chunk = back_chunk(x_ref, o_ref, s_ref, gz_ref, col_ref, row_ref, bound_ref, vec, g_ref, sums_ref, tab, grad_state, acc, carry, turned)

    def step(n, unused):
        chunk(n)
        for at, parts in when.items():
            @pl.when(n == at)
            def _():
                for part in parts:
                    part()
        return 0

    lax.fori_loop(0, chunks, step, 0)
    saves = [moves.start(g_ref, g_far)]
    back_finish(vec, sums_ref, acc, L)
    mug_ref[...] = jnp.zeros_like(mug_ref)
    mixt_in.wait()

    def mix(d, unused):
        pl.when(d < 7)(lambda: fetch(d + 1, 0))
        have(d, 0)
        rhs = tile[d % 2]
        cols = pl.ds(pl.multiple_of(d * C, C), C)
        a = jnp.dot(turned[: 4 * W, :], rhs, preferred_element_type=F32)
        b = jnp.dot(turned[4 * W :, :], rhs, preferred_element_type=F32)
        for q in range(4):
            rows = slice(q * W, (q + 1) * W)
            diff = b[rows] - a[rows]
            gg_ref[d, rows, :] = (a[rows] + par_ref[2 + q : 3 + q, cols] * diff).astype(BF)
            mug_ref[q : q + 1, cols] = jnp.sum(mixt_ref[rows, cols].astype(F32) * diff, axis=0, keepdims=True)
        return 0

    lax.fori_loop(0, 4, mix, 0)
    plan[8]()
    sums[2]()
    lax.fori_loop(4, 8, mix, 0)
    sums[3]()
    zt_in.wait()
    plan[9]()

    def out(d, unused):
        cols = pl.ds(pl.multiple_of(d * C, C), C)
        gg_ref[d, 4 * W :, :] = jnp.dot(zt_ref[...], land[:, cols], preferred_element_type=F32).astype(BF)
        return 0

    lax.fori_loop(0, 8, out, 0)
    saves.append(moves.start(gg_ref, gg_far))
    sums[4]()
    for cp in saves:
        cp.wait()
    c.finish()


def time_back(nd, gh, gz, par, rows, bounds, early, x, o, states, cols, zt, mixt, n1_all, cid):
    T, W = o.shape
    L = rows.shape[2]
    R, C = gh.shape
    J = early.shape[1]
    return pl.pallas_call(
        functools.partial(time_back_kernel, nd),
        out_shape=(
            jax.ShapeDtypeStruct((T, 8 * W), BF),
            jax.ShapeDtypeStruct((8, 5 * W, C // 8), BF),
            jax.ShapeDtypeStruct((8, W), F32),
            jax.ShapeDtypeStruct((4, C), F32),
            jax.ShapeDtypeStruct((8 // nd, J, C // 8), F32),
        ),
        in_specs=[WHOLE] * 4 + [pl.BlockSpec(memory_space=pltpu.SMEM)] + [FAR] * 8,
        out_specs=(FAR,) * 2 + (WHOLE,) * 3,
        scratch_shapes=[
            VMEM((4, L, W), F32), VMEM((W, W), F32), VMEM((W, W), F32), VMEM((8, 4 * W), F32),
            VMEM((T, C), BF), VMEM((8 * W, T), BF), VMEM((2, T, C // 8), BF), VMEM((8 + W, W), F32),
            VMEM((8, J, C // 8), BF), VMEM(x.shape, F32), VMEM((T, W), F32), VMEM(states.shape, F32), VMEM(cols.shape, F32),
            VMEM((W, T), BF), VMEM(mixt.shape, BF), VMEM((T, 8 * W), BF), VMEM((8, 5 * W, C // 8), BF),
        ]
        + dp_scratch(J, C // 8)
        + [DMA((32,)), DMA((32,)), DMA((2,)), DMA((9,))],
        compiler_params=params(cid, 60),
        name="time_back",
    )(gh, gz, par, rows, bounds, early, x, o, states, cols, zt, mixt, n1_all)


def last_kernel(nd, x_ref, par_ref, mug_ref, head_ref, norm_ref, gg_far, l_far, w_far, gh_far, ig_ref, dp_ref, v_ref, *rest):
    scratch = rest[:7]
    o_ref, d0, d1, d2, d3, tv, b1, t1, b2, gg_ref, l_ref, w_ref, gh_ref, cs, cr, ms = rest[7:]
    p = Place()
    met = greet(near(p) + beside(p, nd))
    c = Copies(cs, cr)
    moves = Moves(ms)
    gg_in, w_in, l_in, gh_in = (
        moves.start(a, b) for a, b in ((gg_far, gg_ref), (w_far, w_ref), (l_far, l_ref), (gh_far, gh_ref))
    )
    sums = dp_plan(p, nd, c, 18, gg_ref, dp_ref, (d0, d1, d2, d3)) if nd > 1 else no_sums(gg_ref, dp_ref)
    steps = sum_plan(p, c, 0, l_ref, w_ref, o_ref, scratch)
    W = head_ref.shape[1]
    tv[...] = jnp.zeros_like(tv)
    tv[2:6, :] = mug_ref[...]
    tv[6:10, pl.ds(pl.multiple_of(p.s * W, 128), W)] = head_ref[0:4, :]
    tv[10:14, :] = norm_ref[0:4, :]
    met()
    gg_in.wait()
    sums[0]()
    l_in.wait()
    w_in.wait()
    steps[0]()
    steps[1]()
    sums[1]()
    steps[2]()
    steps[3]()
    steps[4]()
    sums[2]()
    sums[3]()
    unused, scale, normed = norm_parts(x_ref[...].astype(F32))
    gh_in.wait()
    steps[5]()
    steps[6]()
    gn = o_ref[...]
    tv[0:1, :] = jnp.sum(gn * normed, axis=0, keepdims=True)
    tv[1:2, :] = jnp.sum(gn, axis=0, keepdims=True)
    sums[4]()
    C = b1.shape[2]
    for k in range(1, nd):
        to = (p.dp + k) % nd
        c.add(31 + k, tv.at[:, pl.ds(pl.multiple_of(to * C, 128), C)], b1.at[k - 1], (to, p.s))
        c.start(31 + k)
    ig_ref[...] = gh_ref[...] + norm_back(normed, scale, gn * par_ref[0:1, :])
    total = tv[:, pl.ds(pl.multiple_of(p.dp * C, 128), C)]
    for k in range(1, nd):
        c.landed(31 + k, b1.at[k - 1])
        total = total + b1[k - 1]
    t1[...] = total
    for k in range(1, 16):
        c.add(38 + k, t1, b2.at[k - 1], p.dev((p.s + k) % 16))
        c.start(38 + k)
    for k in range(1, 16):
        c.landed(38 + k, b2.at[k - 1])
        total = total + b2[k - 1]
    v_ref[...] = total
    c.finish()


def last_sums(nd, x, par, mug, head, norm, gg, l, w, gh, cid):
    R, C = x.shape
    J = gg.shape[1]
    piece = (16, C // nd)
    return pl.pallas_call(
        functools.partial(last_kernel, nd),
        out_shape=(jax.ShapeDtypeStruct((R, C), F32), jax.ShapeDtypeStruct((8 // nd, J, C // 8), F32), jax.ShapeDtypeStruct(piece, F32)),
        in_specs=[WHOLE] * 5 + [FAR] * 4,
        out_specs=(WHOLE,) * 3,
        scratch_shapes=sum_scratch(R, C)
        + [VMEM((R, C), F32)]
        + dp_scratch(J, C // 8)
        + [VMEM((16, C), F32), VMEM((max(nd - 1, 1),) + piece, F32), VMEM(piece, F32), VMEM((15,) + piece, F32)]
        + [VMEM(gg.shape, BF), VMEM(l.shape, BF), VMEM(w.shape, BF), VMEM((R, C), F32)]
        + [DMA((54,)), DMA((54,)), DMA((4,))],
        compiler_params=params(cid, 60),
        name="last_sums",
    )(x, par, mug, head, norm, gg, l, w, gh)


def body(nd, inputs, cotangent, mix_weights, out_weight, key_weight, value_weight, recept_weight, vectors, segment_ids):
    tokens, width = inputs.shape
    group = segment_ids.shape[0]
    cols = mix_weights.shape[2]
    units = key_weight.shape[1]
    s = lax.axis_index("sp")
    ring = group // tokens
    chunks = group // CHUNK

    edge = jnp.full((1,), -1.0, F32)
    seg = jnp.concatenate([edge, segment_ids.astype(F32), edge])
    tok_cols = jnp.stack([seg[1:-1], seg[:-2], seg[2:]], axis=1)
    tok_rows = seg[1:-1].reshape(chunks, 1, CHUNK)
    ends = seg[: group + 1 : CHUNK]
    bounds = jnp.stack([ends, jnp.concatenate([(ends[1:] == ends[:-1]).astype(F32), edge])])

    n1_all, projected, z_t, mixed_time, states, hidden, n2, recept_part, out_far = time_forward(
        nd, inputs, vectors, tok_rows, bounds, mix_weights, out_weight, recept_weight, tok_cols, 0
    )
    n2_all, key_in, lifted, squared, recept_in, shift, value_t, mixt, folded, recept_far = key_side(
        nd, n2, recept_part, vectors, key_weight.T, tok_cols, value_weight, mix_weights, 1
    )
    result, grad_recept, recept_cols, grad_key, grad_key_t, value_grad = value_side(
        recept_in, cotangent, hidden, squared, value_weight, value_t, lifted, recept_far, 2
    )
    grad_hidden, grad_hidden_b, norm_rows, early, gz = key_back(
        recept_cols, grad_recept, vectors, cotangent, grad_key, key_weight.T, grad_key_t, tok_cols, hidden, shift, value_grad,
        key_in.reshape(group, width), n2_all, recept_far, out_far, 3,
    )
    grads_two, late, head_rows, mu_rows, early_sum = time_back(
        nd, grad_hidden_b, gz, vectors, tok_rows, bounds, early, projected, mixed_time, states, tok_cols, z_t, mixt, n1_all, 4
    )
    input_grad, late_sum, vector_sum = last_sums(
        nd, inputs, vectors, mu_rows, head_rows, norm_rows, late, grads_two, folded, grad_hidden, 5
    )
    piece = width // (nd * ring)
    vectors_grad = lax.dynamic_slice_in_dim(vector_sum[:14], s * piece, piece, 1)

    def columns(part):
        return part.transpose(1, 0, 2).reshape(part.shape[1], width // nd)

    early_sum, late_sum = columns(early_sum), columns(late_sum)
    return (
        result,
        input_grad,
        late_sum[: 4 * cols].reshape(4, cols, width // nd).transpose(0, 2, 1),
        late_sum[4 * cols :],
        early_sum[units : 2 * units].T,
        early_sum[:units],
        early_sum[2 * units :].T,
        vectors_grad,
    )


def solution(mesh):
    placed = (
        P(("dp", "sp"), None),
        P(("dp", "sp"), None),
        P(None, None, "sp"),
        P("sp", None),
        P(None, "sp"),
        P("sp", None),
        P(None, "sp"),
        P(),
        P("dp"),
    )
    return jax.shard_map(
        functools.partial(body, mesh.shape["dp"]),
        mesh=mesh,
        in_specs=placed,
        out_specs=(
            P(("dp", "sp"), None),
            P(("dp", "sp"), None),
            P(None, "dp", "sp"),
            P("sp", "dp"),
            P("dp", "sp"),
            P("sp", "dp"),
            P("dp", "sp"),
            P(None, ("dp", "sp")),
        ),
        check_vma=False,
    )
```

```python
import functools

import jax
import jax.numpy as jnp
from jax import lax
from jax.experimental import pallas as pl
from jax.experimental.pallas import tpu as pltpu
from jax.sharding import PartitionSpec as P

MESH = pl.DeviceIdType.MESH
VMEM = pltpu.VMEM
DMA = pltpu.SemaphoreType.DMA
BF = jnp.bfloat16
F32 = jnp.float32

ATTENTION_WIDTH = 64
CHUNK = 128
WHOLE = pl.BlockSpec(memory_space=VMEM)
FAR = pl.BlockSpec(memory_space=pl.ANY)


class Place:
    def __init__(self):
        self.dp = lax.axis_index("dp")
        s = lax.axis_index("sp")
        self.s = s
        self.x, self.z, self.c = s // 4, (s // 2) % 2, s % 2

    def at(self, dx=0, dz=0, dc=0):
        return ((self.x + dx) % 4) * 4 + ((self.z + dz) % 2) * 2 + (self.c + dc) % 2

    def dev(self, s):
        return (self.dp, s)


class Across:
    def __init__(self, p, nd):
        self.p, self.ny = p, nd // 2
        self.x, self.z, self.c = p.dp // 2, p.dp % 2, p.c
        self.s = p.dp * 2 + p.c

    def at(self, dx=0, dz=0, dc=0):
        return ((self.x + dx) % self.ny) * 4 + ((self.z + dz) % 2) * 2 + (self.c + dc) % 2

    def dev(self, i):
        return (i // 2, self.p.s - self.p.c + i % 2)


class Copies:
    def __init__(self, ss, rs):
        self.ss, self.rs, self.items = ss, rs, {}

    def add(self, k, src, dst, to):
        self.items[k] = (src, dst, to)

    def make(self, k, src, dst, to):
        return pltpu.make_async_remote_copy(
            src_ref=src, dst_ref=dst, send_sem=self.ss.at[k], recv_sem=self.rs.at[k], device_id=to, device_id_type=MESH
        )

    def start(self, *ks):
        for k in ks:
            self.make(k, *self.items[k]).start()

    def landed(self, k, ref):
        self.make(k, ref, ref, self.items[k][2]).wait_recv()

    def finish(self):
        for k in self.items:
            self.make(k, *self.items[k]).wait_send()


def greet(devices):
    barrier = pltpu.get_barrier_semaphore()
    for device in devices:
        pl.semaphore_signal(barrier, inc=1, device_id=device, device_id_type=MESH)
    return lambda: pl.semaphore_wait(barrier, len(devices))


def near(p):
    return [p.dev(p.at(dc=1)), p.dev(p.at(dx=1)), p.dev(p.at(dx=-1)), p.dev(p.at(dz=1))]


def beside(p, nd):
    y, zl, ny = p.dp // 2, p.dp % 2, nd // 2
    if nd == 1:
        return []
    return [(2 * ((y + 1) % ny) + zl, p.s), (2 * ((y + ny - 1) % ny) + zl, p.s), (2 * y + 1 - zl, p.s)]


def chip_mates(p):
    return [p.dev(p.at(dx, dz)) for dz in range(2) for dx in range(4)][1:]


def ring_mates(p):
    return [p.dev((p.s + k) % 16) for k in range(1, 16)]


def dp_mates(p, nd):
    return [((p.dp + k) % nd, p.s) for k in range(1, nd)]


def params(cid, mib):
    return pltpu.CompilerParams(collective_id=cid, has_side_effects=True, vmem_limit_bytes=mib * 2**20)


class Swap:
    def __init__(self, p, src, dst, ss, rs):
        self.p, self.src, self.dst, self.ss, self.rs = p, src, dst, ss, rs

    def make(self, src, dst, at, to):
        return pltpu.make_async_remote_copy(
            src_ref=src, dst_ref=dst, send_sem=self.ss.at[to], recv_sem=self.rs.at[at], device_id=self.p.dev(to), device_id_type=MESH
        )

    def give(self, i):
        @pl.when(i != self.p.s)
        def _():
            self.make(self.src(i), self.dst.at[self.p.s], self.p.s, i).start()

        @pl.when(i == self.p.s)
        def _():
            self.dst[self.p.s] = self.src(i)[...]

    def take(self, i):
        @pl.when(i != self.p.s)
        def _():
            self.make(self.dst.at[i], self.dst.at[i], i, i).wait_recv()

    def sent(self, i):
        @pl.when(i != self.p.s)
        def _():
            self.make(self.src(i), self.dst.at[self.p.s], self.p.s, i).wait_send()

    def all(self, act):
        def step(i, unused):
            act(i)
            return 0

        lax.fori_loop(0, 16, step, 0)


class Moves:
    def __init__(self, sem):
        self.sem, self.n = sem, 0

    def start(self, src, dst):
        cp = pltpu.make_async_copy(src, dst, self.sem.at[self.n])
        self.n += 1
        cp.start()
        return cp


def equal(a, b):
    return jnp.where(a == b, 1.0, 0.0)


def blocks_of(land):
    R = land.shape[1] // 2

    def blk(i, half=None):
        rows = R if half is None else R // 2
        return land.at[i // 2, pl.ds(pl.multiple_of((i % 2) * R + (half or 0) * rows, 16), rows)]

    return blk


def rows_of(land):
    R = land.shape[0] // 16

    def blk(i, half=None):
        rows = R if half is None else R // 2
        return land.at[pl.ds(pl.multiple_of(i * R + (half or 0) * rows, 16), rows)]

    return blk


def matrix_blocks(land):
    K = land.shape[1] // 2

    def blk(i, half=None):
        rows = K if half is None else K // 2
        return land.at[i // 2, pl.ds(pl.multiple_of((i % 2) * K + (half or 0) * rows, 16), rows)]

    return blk


def gather_plan(p, c, base, a_ref, blk, around=False):
    core, xp, xm, zz = p.at(dc=1), p.at(dx=1), p.at(dx=-1), p.at(dz=1)
    d2, zxm, zxp, zd2 = p.at(dx=2), p.at(dx=-1, dz=1), p.at(dx=1, dz=1), p.at(dx=2, dz=1)
    up, lo = 0, 1

    def relay(k, ref, to):
        c.add(base + k, ref, ref, p.dev(to))

    for k, to in enumerate((xp, xm, zz, core)):
        c.add(base + k, a_ref, blk(p.s), p.dev(to))
    relay(4, blk(xm, up), xp)
    relay(5, blk(xp, lo), xm)
    relay(6, blk(xm), core)
    relay(7, blk(xp), core)
    relay(8, blk(zz), xp)
    relay(9, blk(zz), xm)
    relay(10, blk(zz), core)
    if around:
        relay(11, blk(zxm, up), xp)
        relay(12, blk(zxp, lo), xm)
    else:
        relay(11, blk(d2, up), zz)
        relay(12, blk(d2, lo), zz)
    relay(13, blk(d2), core)
    relay(14, blk(zxm), core)
    relay(15, blk(zxp), core)
    relay(16, blk(zd2, up), core)
    relay(17, blk(zd2, lo), core)

    def start(*ks):
        c.start(*(base + k for k in ks))

    def landed(k, ref):
        c.landed(base + k, ref)

    def other(**k):
        return p.at(dc=1, **k)

    def one():
        start(0, 1, 2, 3)
        return []

    def own():
        landed(3, blk(core))
        return [core // 2]

    def two():
        landed(0, blk(xm))
        start(4)
        landed(1, blk(xp))
        start(5, 6, 7)
        landed(2, blk(zz))
        start(8, 9, 10)
        return []

    def third():
        landed(6, blk(other(dx=-1)))
        return [xm // 2]

    def three():
        landed(4, blk(d2, up))
        if not around:
            start(11)
        landed(5, blk(d2, lo))
        if not around:
            start(12)
        start(13)
        return []

    def third_more():
        landed(7, blk(other(dx=1)))
        landed(10, blk(other(dz=1)))
        return [xp // 2, zz // 2]

    def fourth():
        landed(13, blk(other(dx=2)))
        return [d2 // 2]

    def four():
        landed(8, blk(zxm))
        if around:
            start(11)
        landed(9, blk(zxp))
        if around:
            start(12)
        start(14, 15)
        return []

    def five():
        landed(11, blk(zd2, up))
        start(16)
        landed(12, blk(zd2, lo))
        start(17)
        landed(14, blk(other(dx=-1, dz=1)))
        landed(15, blk(other(dx=1, dz=1)))
        return [zxm // 2, zxp // 2]

    def six():
        landed(16, blk(other(dx=2, dz=1), up))
        landed(17, blk(other(dx=2, dz=1), lo))
        return [zd2 // 2]

    return [one, own, two, third, three, third_more, fourth, four, five, six]


def run_gather(plan, work, hooks):
    ready = []
    for n, step in enumerate(plan):
        ready += step()
        for hook in hooks.get(n, ()):
            hook()
        if ready:
            work(ready.pop(0))
    for chip in ready:
        work(chip)


def chip_plan(p, c, base, w_ref, part):
    R, C = w_ref.shape[0], part.shape[1]
    cols = pl.ds(pl.multiple_of(p.dp * C, C), C)
    mates = [(dx, dz) for dz in range(2) for dx in range(4)][1:]

    def rows(s):
        return pl.ds(pl.multiple_of((s // 2) * R, 16), R)

    for k, (dx, dz) in enumerate(mates):
        c.add(base + k, w_ref.at[:, cols], part.at[rows(p.s)], p.dev(p.at(dx, dz)))

    def begin():
        part[rows(p.s), :] = w_ref[:, cols]
        c.start(*range(base, base + 7))

    def end():
        for k, (dx, dz) in enumerate(mates):
            c.landed(base + k, part.at[rows(p.at(-dx, dz))])

    return begin, end


def across_plan(p, nd, c, base, part, land):
    q = Across(p, nd)
    K = part.shape[0]
    plan = gather_plan(q, c, base, part, matrix_blocks(land), around=True)

    def go(*ns):
        def run():
            for n in ns:
                plan[n]()

        return run

    return go, land.at[p.dp, pl.ds(pl.multiple_of(p.c * K, 16), K)]


def save_blocks(land, all_ref, sem):
    R = land.shape[1]

    def copy(k):
        return pltpu.make_async_copy(land.at[k], all_ref.at[pl.ds(pl.multiple_of(k * R, 16), R)], sem.at[k])

    def wait():
        for k in range(8):
            copy(k).wait()

    return lambda k: copy(k).start(), wait


def heads_of_blocks(land, col):
    R = land.shape[1] // 2

    def row(b, at):
        at += (b % 2) * R
        return land[b // 2, at // 16 * 16 : at // 16 * 16 + 16, :].astype(F32)[at % 16 : at % 16 + 1]

    first = jnp.concatenate([row(b, 0) for b in range(16)], axis=0)
    before = jnp.concatenate([jnp.zeros_like(first[0:1])] + [row(b, R - 1) for b in range(15)], axis=0)
    heads = jnp.concatenate([col[b * R : b * R + 1, :] for b in range(16)], axis=0)
    return first, before * equal(heads[:, 0:1], heads[:, 1:2]) - first


def shifted(n, col):
    same = equal(col[:, 0:1], col[:, 1:2])
    rows = lax.broadcasted_iota(jnp.int32, n.shape, 0)
    before = jnp.where(rows == 0, 0.0, pltpu.roll(n, 1, 0))
    return before * same - n


def norm_parts(a):
    width = a.shape[1]
    center = a - jnp.sum(a, axis=1, keepdims=True) * (1.0 / width)
    scale = lax.rsqrt(jnp.sum(center * center, axis=1, keepdims=True) * (1.0 / width) + 1e-05)
    return center, scale, center * scale


def norm_back(normed, scale, grad):
    width = grad.shape[1]
    inner = grad - jnp.sum(grad, axis=1, keepdims=True) * (1.0 / width)
    return scale * (inner - normed * (jnp.sum(grad * normed, axis=1, keepdims=True) * (1.0 / width)))


def sigmoid(a):
    return 1.0 / (1.0 + jnp.exp(-a))


CHUNK = 128


def halves(a):
    high = a.astype(BF)
    return high, (a - high.astype(F32)).astype(BF)


def dot3(a, b, dims):
    def one(x, y):
        return lax.dot_general(x, y, (dims, ((), ())), preferred_element_type=F32)

    return one(a[0], b[0]) + (one(a[0], b[1]) + one(a[1], b[0]))


NN, NT, TN = ((1,), (0,)), ((1,), (1,)), ((0,), (0,))


def head_sums(a, ones):
    high, rest = a.astype(BF), a - a.astype(BF).astype(F32)
    mid = rest.astype(BF)
    low = (rest - mid.astype(F32)).astype(BF)

    def one(x):
        return lax.dot_general(x, ones, (NN, ((), ())), preferred_element_type=F32)

    return one(high) + (one(mid) + one(low))


def iota(shape, dim):
    return lax.broadcasted_iota(jnp.int32, shape, dim)


def head_ones(width, dtype):
    return (iota((width, width), 0) // ATTENTION_WIDTH == iota((width, width), 1) // ATTENTION_WIDTH).astype(dtype)


def by_head(pair):
    lane = iota(pair[0].shape, 1) // ATTENTION_WIDTH
    heads = pair[0].shape[1] // ATTENTION_WIDTH
    zero = jnp.zeros_like(pair[0])
    return tuple(jnp.concatenate([jnp.where(lane == h, a, zero) for h in range(heads)], axis=0) for a in pair)


def pick_heads(a, rows):
    lane = iota((rows, a.shape[1]), 1) // ATTENTION_WIDTH
    out = a[:rows]
    for h in range(1, a.shape[1] // ATTENTION_WIDTH):
        out = jnp.where(lane == h, a[h * rows : (h + 1) * rows], out)
    return out


def powers(lam, tab):
    L = tab.shape[1]
    at = iota((L, 1), 0).astype(F32)
    mid = L // 2
    tab[0] = jnp.exp(lam * (at - mid))
    tab[1] = jnp.exp(-lam * (at + (1.0 - mid)))
    tab[2] = jnp.exp(lam * at)
    tab[3] = jnp.exp(lam * (L - 1.0 - at))


def own_vectors(p, par_ref, vec):
    W = vec.shape[1]
    own = par_ref[6:10, pl.ds(pl.multiple_of(p.s * W, 128), W)]
    lam = -jnp.exp(own[0:1])
    vec[0:1, :] = lam
    vec[1:4, :] = own[1:4]
    vec[8:, :] = jnp.broadcast_to(jnp.exp(lam * CHUNK), (W, W)).T


def chunk_mask(col, row):
    L = col.shape[0]
    return (iota((L, L), 1) < iota((L, L), 0)) & (col == row)


def forward_chunk(x_ref, col_ref, row_ref, bound_ref, vec_ref, z_ref, zt_ref, o_ref, s_ref, tab, state):
    chunks, L = row_ref.shape[0], row_ref.shape[2]
    W = vec_ref.shape[1]
    heads = W // ATTENTION_WIDTH
    lam, bonus, gain, bias = (vec_ref[q : q + 1, :] for q in range(4))
    powers(lam, tab)
    ones = head_ones(W, BF)
    diag = head_ones(W, F32)
    decay = vec_ref[8 : 8 + W, :]
    state[...] = jnp.zeros_like(state)

    def step(i):
        rows = pl.ds(pl.multiple_of(i * L, L), L)
        r, k, v, p = (x_ref[rows, q * W : (q + 1) * W] for q in range(4))
        col = col_ref[rows, :]
        seg = col[:, 0:1]
        kept, tail = equal(seg, bound_ref[0, i]), equal(seg, bound_ref[0, i + 1])
        mask = chunk_mask(seg, row_ref[i])
        mask = jnp.concatenate([mask] * heads, axis=1)
        rs, ks = halves(r * tab[0]), halves(k * tab[1])
        scores = jnp.where(mask, dot3(rs, by_head(ks), NT), 0.0)
        vh = halves(v)
        out = dot3(halves(scores), by_head(vh), NN) + head_sums(r * k * bonus, ones) * v
        memory = state[...]
        s_ref[i] = memory
        out = out + kept * dot3(halves(r * tab[2]), halves(memory), NN)
        state[...] = bound_ref[1, i] * decay * memory + diag * dot3(halves(k * tab[3] * tail), vh, TN)
        o_ref[rows, :] = out
        center = out - head_sums(out, ones) * (1.0 / ATTENTION_WIDTH)
        spread = head_sums(center * center, ones) * (1.0 / ATTENTION_WIDTH)
        normed = center * lax.rsqrt(spread + 0.00064) * gain + bias
        z = (normed * (p * sigmoid(p))).astype(BF).astype(F32)
        z_ref[rows, :] = z.astype(BF)
        zt_ref[:, rows] = z.T.astype(BF)

    return step


def back_chunk(x_ref, o_ref, s_ref, gz_ref, col_ref, row_ref, bound_ref, vec_ref, g_ref, sums_ref, tab, grad_state, acc, carry, turned):
    chunks, L = row_ref.shape[0], row_ref.shape[2]
    W = vec_ref.shape[1]
    heads = W // ATTENTION_WIDTH
    lam, bonus, gain, bias = (vec_ref[q : q + 1, :] for q in range(4))
    powers(lam, tab)
    ones = head_ones(W, BF)
    diag = head_ones(W, F32)
    decay = vec_ref[8 : 8 + W, :]
    at = iota((L, 1), 0).astype(F32)
    mid = float(L // 2)
    grad_state[...] = jnp.zeros_like(grad_state)
    acc[...] = jnp.zeros_like(acc)
    carry[...] = jnp.zeros_like(carry)
    sums_ref[...] = jnp.zeros_like(sums_ref)

    def add(q, term):
        sums_ref[q : q + 1, :] += jnp.sum(term, axis=0, keepdims=True)

    def step(n):
        i = chunks - 1 - n
        rows = pl.ds(pl.multiple_of(i * L, L), L)
        r, k, v, p = (x_ref[rows, q * W : (q + 1) * W] for q in range(4))
        col = col_ref[rows, :]
        seg = col[:, 0:1]
        kept, tail = equal(seg, bound_ref[0, i]), equal(seg, bound_ref[0, i + 1])
        same_next = equal(seg, col[:, 2:3])
        o = o_ref[rows, :]
        gz = gz_ref[i].astype(F32)
        center = o - head_sums(o, ones) * (1.0 / ATTENTION_WIDTH)
        spread = head_sums(center * center, ones) * (1.0 / ATTENTION_WIDTH)
        scale = lax.rsqrt(spread + 0.00064)
        normed = center * scale
        gate = sigmoid(p)
        silu = p * gate
        gy = gz * silu
        gp = gz * (normed * gain + bias) * (gate * (1.0 + p * (1.0 - gate)))
        add(2, gy * normed)
        add(3, gy)
        gn = gy * gain
        go = scale * (
            gn
            - head_sums(gn, ones) * (1.0 / ATTENTION_WIDTH)
            - normed * (head_sums(gn * normed, ones) * (1.0 / ATTENTION_WIDTH))
        )
        mask = chunk_mask(seg, row_ref[i])
        mask = jnp.concatenate([mask] * heads, axis=1)
        rs_f, ks_f = r * tab[0], k * tab[1]
        r0_f, ke_f = r * tab[2] * kept, k * tab[3] * tail
        rs, ks, vh, goh = halves(rs_f), halves(ks_f), halves(v), halves(go)
        ks_by, v_by = by_head(ks), by_head(vh)
        scores = halves(jnp.where(mask, dot3(rs, ks_by, NT), 0.0))
        grad_scores = halves(jnp.where(mask, dot3(goh, v_by, NT), 0.0))
        memory = s_ref[i]
        gs = grad_state[...]
        mh, gsh = halves(memory), halves(gs)
        reward = head_sums(r * k * bonus, ones)
        grad_reward = head_sums(go * v, ones)
        g_rs = dot3(grad_scores, ks_by, NN)
        g_r0 = dot3(goh, mh, NT)
        g_ks = pick_heads(dot3(grad_scores, rs, TN), L)
        g_ke = dot3(vh, gsh, NT)
        gv = pick_heads(dot3(scores, goh, TN), L) + reward * go + dot3(halves(ke_f), gsh, NN)
        keep = bound_ref[1, i]
        acc[...] += keep * memory * gs
        grad_state[...] = keep * decay * gs + diag * dot3(halves(r0_f), goh, TN)
        gr = g_rs * tab[0] + g_r0 * (tab[2] * kept) + grad_reward * bonus * k
        gk = g_ks * tab[1] + g_ke * (tab[3] * tail) + grad_reward * bonus * r
        add(1, grad_reward * r * k)
        add(0, (at - mid) * (g_rs * rs_f) - (at + (1.0 - mid)) * (g_ks * ks_f) + at * (g_r0 * r0_f) + (L - 1.0 - at) * (g_ke * ke_f))
        grads = jnp.concatenate([gr, gk, gv, gp], axis=1).astype(BF).astype(F32)
        last = iota((L, 1), 0) == L - 1
        after = jnp.where(last, carry[0:1, :], pltpu.roll(grads, L - 1, 0)) * same_next
        carry[0:1, :] = grads[0:1, :]
        g_ref[rows, : 4 * W] = grads.astype(BF)
        g_ref[rows, 4 * W :] = after.astype(BF)
        turned[0 : 4 * W, rows] = grads.T.astype(BF)
        turned[4 * W :, rows] = after.T.astype(BF)

    return step


def back_finish(vec_ref, sums_ref, acc, L):
    W = vec_ref.shape[1]
    whole = dot3(halves(jnp.ones((8, W), F32)), halves(acc[...] * vec_ref[8 : 8 + W, :]), NT)
    sums_ref[0:1, :] = (sums_ref[0:1, :] + L * whole[0:1, :]) * vec_ref[0:1, :]


def time_forward_kernel(nd, x_ref, par_ref, row_ref, bound_ref, w_far, ow_far, rw_far, col_far,
                        all_ref, proj_far, zt_far, o_far, s_far, hid_ref, n2_ref, rp_ref, far_ref,
                        n1, land, op, lw, tab, state, zin, w_ref, ow_ref, rw_ref, rt_ref, col_ref, proj_ref, z_ref, zt_ref,
                        o_ref, s_ref, vec, cs, cr, ss, rs, ls, ms):
    p = Place()
    met = greet(chip_mates(p) + [p.dev(p.at(dc=1))] + beside(p, nd))
    c = Copies(cs, cr)
    moves = Moves(ms)
    ow_in, w_in, col_in, rw_in = (
        moves.start(a, b) for a, b in ((ow_far, ow_ref), (w_far, w_ref), (col_far, col_ref), (rw_far, rw_ref))
    )
    R = x_ref.shape[0]
    Q, W = w_ref.shape[0], w_ref.shape[2]
    C = lw.shape[2]
    begin, end = chip_plan(p, c, 18, ow_ref, op)
    go, own_part = across_plan(p, nd, c, 25, op, lw)
    recept_begin, recept_end = chip_plan(p, c, 43, rt_ref, rp_ref)
    blk = blocks_of(land)
    plan = gather_plan(p, c, 0, n1, blk, around=True)
    start, wait = save_blocks(land, all_ref, ls)
    n1[...] = (norm_parts(x_ref[...].astype(F32))[2] * par_ref[0:1, :] + par_ref[1:2, :]).astype(BF)
    met()

    def ready():
        begin()
        blk(p.s)[...] = n1[...]
        own_vectors(p, par_ref, vec)
        w_in.wait()
        col_in.wait()

    def turn():
        rw_in.wait()
        for k in range(0, rw_ref.shape[0], 256):
            rt_ref[:, k : k + 256] = rw_ref[k : k + 256, :].T

    def across():
        own_part[...] = op[...]
        go(0)()

    def work(k):
        start(k)
        rows = pl.ds(pl.multiple_of(k * 2 * R, 16), 2 * R)
        n = land[k].astype(F32)
        shift = shifted(n, col_ref[rows, :])
        for q in range(Q):
            m = (n + shift * par_ref[2 + q : 3 + q, :]).astype(BF)
            proj_ref[rows, q * W : (q + 1) * W] = jnp.dot(m, w_ref[q], preferred_element_type=F32)

    ow_in.wait()
    run_gather(plan, work, {0: [ready], 1: [turn], 3: [end, across], 7: [go(1, 2)]})
    recept_begin()
    first, shift = heads_of_blocks(land, col_ref)
    for q in range(Q):
        m = (first + shift * par_ref[2 + q : 3 + q, :]).astype(BF)
        out = jnp.dot(m, w_ref[q], preferred_element_type=F32)
        for b in range(0, 16, 2):
            proj_ref[b * R : b * R + 1, q * W : (q + 1) * W] = out[b : b + 1]
    saves = [moves.start(proj_ref, proj_far)]

    chunk = forward_chunk(proj_ref, col_ref, row_ref, bound_ref, vec, z_ref, zt_ref, o_ref, s_ref, tab, state)
    swap = Swap(p, lambda i: z_ref.at[pl.ds(pl.multiple_of(i * R, 16), R)], zin, ss, rs)
    when = {0: go(3, 4), 2: go(5, 6, 7)}

    def step(n, unused):
        chunk(2 * n)
        chunk(2 * n + 1)
        swap.give(2 * n)
        swap.give(2 * n + 1)
        for at, act in when.items():
            pl.when(n == at)(act)
        return 0

    lax.fori_loop(0, row_ref.shape[0] // 2, step, 0)
    saves += [moves.start(a, b) for a, b in ((zt_ref, zt_far), (o_ref, o_far), (s_ref, s_far))]
    go(8, 9)()
    saves.append(moves.start(lw, far_ref))
    swap.all(swap.take)
    z_here = jnp.concatenate([zin[2 * k + core] for core in range(2) for k in range(8)], axis=1)
    for d in range(8):
        cols = slice(d * C, (d + 1) * C)
        hid_ref[:, cols] = x_ref[:, cols].astype(F32) + jnp.dot(z_here, lw[d], preferred_element_type=F32)
    n2_ref[...] = (norm_parts(hid_ref[...])[2] * par_ref[10:11, :] + par_ref[11:12, :]).astype(BF)
    recept_end()
    wait()
    for cp in saves:
        cp.wait()
    swap.all(swap.sent)
    c.finish()


def time_forward(nd, x, par, rows, bounds, w, ow, rw, cols, cid):
    R, C = x.shape
    T, W = 16 * R, w.shape[2]
    chunks, L = rows.shape[0], rows.shape[2]
    return pl.pallas_call(
        functools.partial(time_forward_kernel, nd),
        out_shape=(
            jax.ShapeDtypeStruct((T, C), BF),
            jax.ShapeDtypeStruct((T, 4 * W), F32),
            jax.ShapeDtypeStruct((W, T), BF),
            jax.ShapeDtypeStruct((T, W), F32),
            jax.ShapeDtypeStruct((chunks, W, W), F32),
            jax.ShapeDtypeStruct((R, C), F32),
            jax.ShapeDtypeStruct((R, C), BF),
            jax.ShapeDtypeStruct((8 * R, C // nd), BF),
            jax.ShapeDtypeStruct((8, 16 * R, C // 8), BF),
        ),
        in_specs=[WHOLE] * 3 + [pl.BlockSpec(memory_space=pltpu.SMEM)] + [FAR] * 4,
        out_specs=(FAR,) * 5 + (WHOLE,) * 3 + (FAR,),
        scratch_shapes=[
            VMEM((R, C), BF), VMEM((8, 2 * R, C), BF), VMEM((8 * R, C // nd), BF), VMEM((8, 16 * R, C // 8), BF), VMEM((4, L, W), F32),
            VMEM((W, W), F32), VMEM((16, R, W), BF), VMEM(w.shape, BF), VMEM((R, C), BF), VMEM((C, W), BF), VMEM((W, C), BF),
            VMEM(cols.shape, F32), VMEM((T, 4 * W), F32), VMEM((T, W), BF), VMEM((W, T), BF), VMEM((T, W), F32),
            VMEM((chunks, W, W), F32), VMEM((8 + W, W), F32),
            DMA((50,)), DMA((50,)), DMA((16,)), DMA((16,)), DMA((16,)), DMA((9,)),
        ],
        compiler_params=params(cid, 56),
        name="time_forward",
    )(x, par, rows, bounds, w, ow, rw, cols)


def key_kernel(nd, a_ref, rp_ref, par_ref, k_far, col_far, vw_far, mw_far,
               all_ref, in_ref, lift_far, sq_far, rin_ref, sh_ref, vt_far, mt_far, fold_far, far_ref,
               land, mixed, k_ref, w_ref, col_ref, vw_ref, mw_ref, lift_ref, sq_ref, vt_ref, mt_ref, fold_ref,
               cs, cr, ls, ms, ks):
    p = Place()
    met = greet(near(p) + beside(p, nd))
    c = Copies(cs, cr)
    moves = Moves(ms)
    col_in, k_in, mw_in, vw_in = (
        moves.start(a, b) for a, b in ((col_far, col_ref), (k_far, k_ref), (mw_far, mw_ref), (vw_far, vw_ref))
    )
    R = a_ref.shape[0]
    go, own_part = across_plan(p, nd, c, 18, rp_ref, far_ref)
    saves = [moves.start(rp_ref, own_part)]
    blk = blocks_of(land)
    plan = gather_plan(p, c, 0, a_ref, blk)
    start, wait = save_blocks(land, all_ref, ls)
    met()
    nu_k, nu_r = par_ref[12:13, :], par_ref[13:14, :]
    Q, W = mw_ref.shape[0], mw_ref.shape[2]

    def ready():
        go(0)()
        blk(p.s)[...] = a_ref[...]
        k_in.wait()
        for k in range(0, w_ref.shape[0], 256):
            w_ref[k : k + 256, :] = k_ref[:, k : k + 256].T
        col_in.wait()

    def turn():
        vw_in.wait()
        for k in range(0, w_ref.shape[0], 256):
            vt_ref[k : k + 256, :] = vw_ref[:, k : k + 256].T
        saves.append(moves.start(vt_ref, vt_far))

    def fold(*qs):
        def run():
            if qs[0] == 0:
                mw_in.wait()
            for q in qs:
                for k in range(0, mw_ref.shape[1], 256):
                    cols, rows = slice(k, k + 256), slice(q * W, (q + 1) * W)
                    turned = mw_ref[q, cols, :].T
                    mt_ref[rows, cols] = turned
                    part = turned.astype(F32)
                    mu = par_ref[2 + q : 3 + q, cols]
                    fold_ref[rows, cols] = ((1.0 - mu) * part).astype(BF)
                    fold_ref[(Q + q) * W : (Q + q + 1) * W, cols] = (mu * part).astype(BF)
            if qs[-1] == Q - 1:
                saves.append(moves.start(mt_ref, mt_far))
                saves.append(moves.start(fold_ref, fold_far))

        return run

    def tail_copy(k):
        rows = pl.ds(16, 2 * R - 16)
        return pltpu.make_async_copy(mixed.at[k, rows], in_ref.at[k, rows], ks.at[k])

    def work(k):
        start(k)
        n = land[k].astype(F32)
        rows = pl.ds(pl.multiple_of(k * 2 * R, 16), 2 * R)
        m = (n + shifted(n, col_ref[rows, :]) * nu_k).astype(BF)
        mixed[k] = m
        e = jnp.maximum(jnp.dot(m, w_ref[...], preferred_element_type=F32), 0.0)
        lift_ref[rows, :] = e
        sq_ref[rows, :] = (e * e).astype(BF)
        tail_copy(k).start()

    run_gather(plan, work, {0: [ready], 1: [turn], 3: [go(1, 2)], 4: [fold(0, 1)], 5: [go(3, 4)], 6: [fold(2, 3)], 7: [go(5, 6, 7)]})
    first, shift = heads_of_blocks(land, col_ref)
    head = first + shift * nu_k
    e = jnp.maximum(jnp.dot(head.astype(BF), w_ref[...], preferred_element_type=F32), 0.0)
    sq = e * e
    top = lax.broadcasted_iota(jnp.int32, (16, 1), 0) == 0
    for b in range(0, 16, 2):
        rows = slice(b * R, b * R + 16)
        mixed[b // 2, 0:16, :] = jnp.where(top, head[b : b + 1], mixed[b // 2, 0:16, :].astype(F32)).astype(BF)
        lift_ref[b * R : b * R + 1, :] = e[b : b + 1]
        sq_ref[rows, :] = jnp.where(top, sq[b : b + 1], sq_ref[rows, :].astype(F32)).astype(BF)
    saves.append(moves.start(lift_ref, lift_far))
    saves.append(moves.start(sq_ref, sq_far))
    saves.append(moves.start(mixed.at[:, pl.ds(0, 16)], in_ref.at[:, pl.ds(0, 16)]))
    n = a_ref[...].astype(F32)
    mine = lax.broadcasted_iota(jnp.int32, (16, 1), 0) == p.s
    own_first = jnp.sum(jnp.where(mine, shift, 0.0), axis=0, keepdims=True)
    here = pl.ds(pl.multiple_of(p.s * R, 16), R)
    topmost = lax.broadcasted_iota(jnp.int32, (R, 1), 0) == 0
    moved = jnp.where(topmost, own_first, shifted(n, col_ref[here, :]))
    sh_ref[...] = moved
    rin_ref[...] = (n + moved * nu_r).astype(BF)
    go(8, 9)()
    for k in range(8):
        tail_copy(k).wait()
    wait()
    for cp in saves:
        cp.wait()
    c.finish()


def key_side(nd, a, part, par, kt, cols, vw, mw, cid):
    R, C = a.shape
    T, units = 16 * R, kt.shape[0]
    Q, W = mw.shape[0], mw.shape[2]
    return pl.pallas_call(
        functools.partial(key_kernel, nd),
        out_shape=(
            jax.ShapeDtypeStruct((T, C), BF),
            jax.ShapeDtypeStruct((8, 2 * R, C), BF),
            jax.ShapeDtypeStruct((T, units), F32),
            jax.ShapeDtypeStruct((T, units), BF),
            jax.ShapeDtypeStruct((R, C), BF),
            jax.ShapeDtypeStruct((R, C), F32),
            jax.ShapeDtypeStruct((C, units), BF),
            jax.ShapeDtypeStruct((Q * W, C), BF),
            jax.ShapeDtypeStruct((2 * Q * W, C), BF),
            jax.ShapeDtypeStruct((8, T, C // 8), BF),
        ),
        in_specs=[WHOLE] * 3 + [FAR] * 4,
        out_specs=(FAR,) * 4 + (WHOLE,) * 2 + (FAR,) * 4,
        scratch_shapes=[
            VMEM((8, 2 * R, C), BF), VMEM((8, 2 * R, C), BF), VMEM((units, C), BF), VMEM((C, units), BF), VMEM(cols.shape, F32),
            VMEM((units, C), BF), VMEM(mw.shape, BF), VMEM((T, units), F32), VMEM((T, units), BF), VMEM((C, units), BF),
            VMEM((Q * W, C), BF), VMEM((2 * Q * W, C), BF),
            DMA((36,)), DMA((36,)), DMA((16,)), DMA((12,)), DMA((16,)),
        ],
        compiler_params=params(cid, 60),
        name="key_side",
    )(a, part, par, kt, cols, vw, mw)


def column_tiles(refs, tile, sem):
    C = tile.shape[2]

    def copy(u, ref):
        if len(ref.shape) == 3:
            return pltpu.make_async_copy(ref.at[u % 8], tile.at[u % 2], sem.at[u % 2])
        return pltpu.make_async_copy(ref.at[:, pl.ds(pl.multiple_of((u % 8) * C, C), C)], tile.at[u % 2], sem.at[u % 2])

    def start(u, kind):
        copy(u, refs[kind]).start()

    def wait(u, kind):
        copy(u, refs[kind]).wait()

    return start, wait


def sum_scratch(R, C):
    return [
        VMEM((8, 2, R, C), BF), VMEM((8, R, C), BF), VMEM((R, C), BF), VMEM((2, R, C), BF), VMEM((R, C), BF),
        VMEM((2, R // 2, C), BF), VMEM((2, R, C), BF),
    ]


def sum_plan(p, c, base, l_ref, w_ref, o_ref, scratch):
    pa, cb, zt, xs, zf, hv, xf = scratch
    R = o_ref.shape[0]
    H = R // 2
    core, xp, xm, zz = (p.dev(i) for i in (p.at(dc=1), p.at(dx=1), p.at(dx=-1), p.at(dz=1)))
    upper, lower = pl.ds(0, H), pl.ds(H, H)
    order = [(2, 1), (-1, 1), (1, 1), (2, 0), (0, 1), (1, 0), (-1, 0), (0, 0)]

    def send(k, src, dst, to):
        c.add(base + k, src, dst, to)
        c.start(base + k)

    def landed(k, ref):
        c.landed(base + k, ref)

    def give(i):
        k = p.at(*order[i]) // 2
        rows = l_ref[pl.ds(pl.multiple_of(k * 2 * R, 16), 2 * R), :]
        pa[i] = jnp.dot(rows, w_ref[...], preferred_element_type=F32).astype(BF).reshape(2, R, -1)
        send(i, pa.at[i, 1 - p.c], cb.at[i], core)

    def pair(i):
        landed(i, cb.at[i])
        pa[i, p.c] = (pa[i, p.c].astype(F32) + cb[i].astype(F32)).astype(BF)

    def one():
        give(0)
        give(1)
        pair(0)
        send(8, pa.at[0, p.c], zt, zz)
        give(2)
        pair(1)
        send(9, pa.at[1, p.c], xs.at[1], xm)
        pair(2)
        send(10, pa.at[2, p.c], xs.at[0], xp)

    def more():
        give(3)
        give(5)
        pair(3)
        give(6)
        pair(5)
        send(11, pa.at[5, p.c, lower], xf.at[0, lower], xp)
        give(4)
        pair(6)
        send(12, pa.at[6, p.c, upper], xf.at[1, upper], xm)
        give(7)
        pair(4)
        pair(7)

    def two():
        landed(8, zt)
        pa[3, p.c] = (pa[3, p.c].astype(F32) + zt[...].astype(F32)).astype(BF)
        send(13, pa.at[3, p.c, upper], hv.at[0], xp)
        send(14, pa.at[3, p.c, lower], hv.at[1], xm)

    def three():
        landed(9, xs.at[1])
        landed(10, xs.at[0])
        pa[4, p.c] = (pa[4, p.c].astype(F32) + xs[0].astype(F32) + xs[1].astype(F32)).astype(BF)
        send(15, pa.at[4, p.c], zf, zz)

    def four():
        landed(13, hv.at[0])
        pa[5, p.c, upper] = (pa[5, p.c, upper].astype(F32) + hv[0].astype(F32)).astype(BF)
        send(16, pa.at[5, p.c, upper], xf.at[0, upper], xp)
        landed(14, hv.at[1])
        pa[6, p.c, lower] = (pa[6, p.c, lower].astype(F32) + hv[1].astype(F32)).astype(BF)
        send(17, pa.at[6, p.c, lower], xf.at[1, lower], xm)

    def five():
        landed(11, xf.at[0, lower])
        landed(12, xf.at[1, upper])
        landed(15, zf)
        o_ref[...] = pa[7, p.c].astype(F32) + zf[...].astype(F32)

    def six():
        landed(16, xf.at[0, upper])
        landed(17, xf.at[1, lower])
        o_ref[...] = o_ref[...] + xf[0].astype(F32) + xf[1].astype(F32)

    return [one, more, two, three, four, five, six]


def value_kernel(rin_ref, g_ref, hid_ref, l_far, w_far, vt_far, lift_far, far_ref,
                 res_ref, gf_ref, rc_ref, ge_far, get_far, vg_far, *rest):
    scratch = rest[:7]
    (o_ref, f_ref, gate_ref, gkv, land, tile, l_ref, w_ref, vt_ref, lift_ref, ge_ref, get_ref, st_ref, acc,
     cs, cr, ss, rs, ts, ms) = rest[7:]
    p = Place()
    met = greet(near(p))
    c = Copies(cs, cr)
    moves = Moves(ms)
    R = o_ref.shape[0]
    T, U = l_ref.shape
    W = gf_ref.shape[2]
    C = tile.shape[2]
    fetch, have = column_tiles((far_ref,), tile, ts)
    l_in, w_in, vt_in, lift_in = (
        moves.start(a, b) for a, b in ((l_far, l_ref), (w_far, w_ref), (vt_far, vt_ref), (lift_far, lift_ref))
    )
    fetch(0, 0)
    sums = sum_plan(p, c, 0, l_ref, w_ref, o_ref, scratch)
    blk = blocks_of(land)
    plan = gather_plan(p, c, 18, gkv, blk)
    swap = Swap(p, lambda i: gf_ref.at[i], rc_ref, ss, rs)
    met()
    l_in.wait()
    w_in.wait()
    sums[0]()

    def unit(d, unused):
        pl.when(d < 7)(lambda: fetch(d + 1, 0))
        have(d, 0)
        cols = pl.ds(pl.multiple_of(d * C, C), C)
        part = lax.dot_general(rin_ref[:, cols], tile[d % 2], (NT, ((), ())), preferred_element_type=F32)

        @pl.when(d == 0)
        def _():
            f_ref[...] = part

        @pl.when(d > 0)
        def _():
            f_ref[...] += part

        return 0

    lax.fori_loop(0, 8, unit, 0)
    for s in range(16):
        at = ((s % 2) * 8 + s // 2) * W
        cols = slice(s * W, (s + 1) * W)
        gate = sigmoid(f_ref[:, at : at + W])
        gate_ref[:, cols] = gate
        gkv[:, cols] = (g_ref[:, cols].astype(F32) * gate).astype(BF)
    plan[0]()
    sums[1]()
    sums[2]()
    sums[3]()
    blk(p.s)[...] = gkv[...]
    acc[...] = jnp.zeros_like(acc)
    for r in range(0, T, 256):
        st_ref[:, r : r + 256] = l_ref[r : r + 256, :].T
    vt_in.wait()
    lift_in.wait()

    saves = []

    def work(k):
        rows = pl.ds(pl.multiple_of(k * 2 * R, 16), 2 * R)
        cols = pl.ds(pl.multiple_of(k * 2 * R, 128), 2 * R)
        gs = jnp.dot(land[k], vt_ref[...], preferred_element_type=F32)
        ge = gs * 2.0 * lift_ref[rows, :]
        ge_ref[rows, :] = ge.astype(BF)
        get_ref[:, cols] = ge.T.astype(BF)
        acc[...] += jnp.dot(st_ref[:, cols], land[k], preferred_element_type=F32)
        saves.append(moves.start(ge_ref.at[rows], ge_far.at[rows]))
        saves.append(moves.start(get_ref.at[:, cols], get_far.at[:, cols]))

    ready = plan[1]() + plan[2]()
    work(ready.pop(0))
    ready += plan[3]()
    work(ready.pop(0))
    ready += plan[5]()
    work(ready.pop(0))
    sums[4]()
    work(ready.pop(0))
    ready += plan[4]() + plan[6]()
    sums[5]()
    sums[6]()
    kv, gate = o_ref[...], gate_ref[...]
    gf = g_ref[...].astype(F32) * kv * (gate * (1.0 - gate))
    for s in range(16):
        gf_ref[s] = gf[:, s * W : (s + 1) * W].astype(BF)
    swap.all(swap.give)
    res_ref[...] = (hid_ref[...] + (gate * kv).astype(BF).astype(F32)).astype(BF)
    for n in range(7, 10):
        ready += plan[n]()
        work(ready.pop(0))
    for k in ready:
        work(k)
    for d in range(8):
        rows = slice((d % 4) * U, (d % 4 + 1) * U)
        tile[d // 4, rows, :] = acc[:, d * C : (d + 1) * C].astype(BF)
        saves.append(moves.start(tile.at[d // 4, pl.ds((d % 4) * U, U)], vg_far.at[d]))
    swap.all(swap.take)
    for cp in saves:
        cp.wait()
    swap.all(swap.sent)
    c.finish()


def value_side(rin, g, hidden, l, w, vt, lift, far, cid):
    R, C = hidden.shape
    T, U = l.shape
    W = C // 16
    return pl.pallas_call(
        value_kernel,
        out_shape=(
            jax.ShapeDtypeStruct((R, C), BF),
            jax.ShapeDtypeStruct((16, R, W), BF),
            jax.ShapeDtypeStruct((16, R, W), BF),
            jax.ShapeDtypeStruct((T, U), BF),
            jax.ShapeDtypeStruct((U, T), BF),
            jax.ShapeDtypeStruct((8, U, C // 8), BF),
        ),
        in_specs=[WHOLE] * 3 + [FAR] * 5,
        out_specs=(WHOLE,) * 3 + (FAR,) * 3,
        scratch_shapes=sum_scratch(R, C)
        + [VMEM((R, C), F32), VMEM((R, C), F32), VMEM((R, C), F32), VMEM((R, C), BF), VMEM((8, 2 * R, C), BF), VMEM((2, T, C // 8), BF)]
        + [VMEM((T, U), BF), VMEM((U, C), BF), VMEM((C, U), BF), VMEM((T, U), F32)]
        + [VMEM((T, U), BF), VMEM((U, T), BF), VMEM((U, T), BF), VMEM((U, C), F32)]
        + [DMA((36,)), DMA((36,)), DMA((16,)), DMA((16,)), DMA((2,)), DMA((28,))],
        compiler_params=params(cid, 62),
        name="value_side",
    )(rin, g, hidden, l, w, vt, lift, far)


def dp_scratch(J, C):
    return [VMEM((2, 2, J // 2, C), BF), VMEM((2, 2, J // 2, C), BF), VMEM((2, 2, J, C), BF), VMEM((2, J, C), BF)]


def dp_plan(p, nd, c, base, g_ref, o_ref, scratch):
    hv, stage, xf, zb = scratch
    J = g_ref.shape[1]
    ny = nd // 2
    y, zl = p.dp // 2, p.dp % 2
    yp, ym, yo = (y + 1) % ny, (y + ny - 1) % ny, (y + 2) % ny
    to_p, to_m, to_z = (2 * yp + zl, p.s), (2 * ym + zl, p.s), (2 * y + 1 - zl, p.s)

    def piece(base, first, rows):
        H = rows // 2
        every, up, lo = pl.ds(first, rows), pl.ds(first, H), pl.ds(first + H, H)
        half = pl.ds(first // 2, H)

        def pay(at, part):
            return g_ref.at[pl.ds(2 * at, 2), part]

        c.add(base, pay(yo, up), hv.at[0, :, half], to_p)
        c.add(base + 1, pay(yo, lo), hv.at[1, :, half], to_m)
        c.add(base + 2, pay(yp, lo), xf.at[0, :, lo], to_p)
        c.add(base + 3, pay(ym, up), xf.at[1, :, up], to_m)
        c.add(base + 4, stage.at[0, :, half], xf.at[0, :, up], to_p)
        c.add(base + 5, stage.at[1, :, half], xf.at[1, :, lo], to_m)
        c.add(base + 6, zb.at[0, every], zb.at[1, every], to_z)

        def one():
            c.start(base, base + 1, base + 2, base + 3)

        def two():
            c.landed(base, hv.at[0, :, half])
            stage[0, :, half] = (g_ref[pl.ds(2 * yp, 2), up].astype(F32) + hv[0, :, half].astype(F32)).astype(BF)
            c.start(base + 4)
            c.landed(base + 1, hv.at[1, :, half])
            stage[1, :, half] = (g_ref[pl.ds(2 * ym, 2), lo].astype(F32) + hv[1, :, half].astype(F32)).astype(BF)
            c.start(base + 5)

        def total(which):
            return g_ref[2 * y + which, every].astype(F32) + xf[0, which, every].astype(F32) + xf[1, which, every].astype(F32)

        def three():
            c.landed(base + 2, xf.at[0, :, lo])
            c.landed(base + 3, xf.at[1, :, up])
            c.landed(base + 4, xf.at[0, :, up])
            c.landed(base + 5, xf.at[1, :, lo])
            zb[0, every] = total(1 - zl).astype(BF)
            c.start(base + 6)
            o_ref[0, every] = total(zl)

        def four():
            c.landed(base + 6, zb.at[1, every])
            o_ref[0, every] += zb[1, every].astype(F32)

        return one, two, three, four

    first, second = piece(base, 0, J // 2), piece(base + 7, J // 2, J // 2)

    def both(n):
        def run():
            first[n]()
            second[n]()

        return run

    return [both(0), both(1), first[2], second[2], both(3)]


def no_sums(g_ref, o_ref):
    def copy():
        o_ref[...] = g_ref[...].astype(F32)

    return [lambda: None] * 4 + [copy]


def key_back_kernel(rc_ref, gf_ref, par_ref, g_ref, l_far, w_far, lt_far, col_far, hid_far, sh_far, vg_far,
                    in_hbm, n2_hbm, far_ref, out_far, gh_ref, ghb_ref, rows_ref, gg_far, gz_ref, *rest):
    scratch = rest[:7]
    (o_ref, rt, gfp, ga_ref, gzp, halo, tile, strip, l_ref, w_ref, lt_ref, col_ref, hid_ref, sh_ref, gg_ref,
     cs, cr, ss, rs, ts, os, ms) = rest[7:]
    p = Place()
    met = greet(near(p) + [p.dev((p.s + 1) % 16), p.dev((p.s + 15) % 16)])
    c = Copies(cs, cr)
    moves = Moves(ms)
    T, U = l_ref.shape
    R, width = o_ref.shape
    W = rc_ref.shape[2]
    C = tile.shape[2]
    l_in, w_in, lt_in, col_in, hid_in, sh_in, vg_in = (
        moves.start(a, b)
        for a, b in (
            (l_far, l_ref), (w_far, w_ref), (lt_far, lt_ref), (col_far, col_ref), (hid_far, hid_ref), (sh_far, sh_ref),
            (vg_far, gg_ref.at[:, pl.ds(0, U)]),
        )
    )
    fetch, have = column_tiles((in_hbm, n2_hbm, far_ref), tile, ts)
    fetch(0, 0)

    def strip_copy(n):
        return pltpu.make_async_copy(out_far.at[:, pl.ds(pl.multiple_of(n * 2 * W, 16), 2 * W)], strip.at[n % 2], os.at[n % 2])

    c.add(18, halo.at[0], halo.at[1], p.dev((p.s + 15) % 16))
    sums = sum_plan(p, c, 0, l_ref, w_ref, o_ref, scratch)
    swap = Swap(p, lambda i: gzp.at[i], gz_ref, ss, rs)
    met()
    nu_k, nu_r = par_ref[12:13, :], par_ref[13:14, :]

    def turn():
        last = lax.broadcasted_iota(jnp.int32, (R, 1), 0) == R - 1
        for b in range(16):
            part = rc_ref[b].astype(F32)
            after = rc_ref[b + 1, 0:16, :].astype(F32)[0:1] if b < 15 else jnp.zeros((1, W), F32)
            col = col_ref[b * R : (b + 1) * R, :]
            moved = jnp.where(last, after, pltpu.roll(part, R - 1, 0)) * equal(col[:, 0:1], col[:, 2:3])
            rt[0:W, b * R : (b + 1) * R] = part.T.astype(BF)
            rt[W:, b * R : (b + 1) * R] = moved.T.astype(BF)
        for s in range(16):
            at = ((s % 2) * 8 + s // 2) * W
            gfp[:, at : at + W] = gf_ref[s]

    def units(kind, lo, hi):
        def unit(d, unused):
            u = 8 * kind + d
            if hi < 8:
                fetch(u + 1, kind)
            else:
                pl.when(d < 7)(lambda: fetch(u + 1, kind))
                if kind < 2:
                    pl.when(d == 7)(lambda: fetch(u + 1, kind + 1))
            have(u, kind)
            rhs = tile[d % 2]
            cols = pl.ds(pl.multiple_of(d * C, C), C)
            if kind == 0:
                gg_ref[d, U : 2 * U, :] = jnp.dot(lt_ref[...], rhs, preferred_element_type=F32).astype(BF)
            elif kind == 1:
                out = jnp.dot(rt[...], rhs, preferred_element_type=F32)
                gg_ref[d, 2 * U :, :] = (out[:W] + par_ref[13:14, cols] * (out[W:] - out[:W])).astype(BF)
            else:
                ga_ref[:, cols] = jnp.dot(gfp[...], rhs, preferred_element_type=F32)
            return 0

        lax.fori_loop(lo, hi, unit, 0)

    l_in.wait()
    w_in.wait()
    sums[0]()
    sums[1]()
    lt_in.wait()
    units(0, 0, 4)
    sums[2]()
    sums[3]()
    units(0, 4, 8)
    col_in.wait()
    turn()
    units(1, 0, 4)
    sums[4]()
    units(1, 4, 8)
    vg_in.wait()
    saves = [moves.start(gg_ref, gg_far)]
    units(2, 0, 8)
    sums[5]()
    strip_copy(0).start()
    hid_in.wait()
    sh_in.wait()
    unused, scale, normed = norm_parts(hid_ref[...])
    sums[6]()
    ga_k, ga_r, shift = o_ref[...], ga_ref[...], sh_ref[...]
    here = pl.ds(pl.multiple_of(p.s * R, 16), R)
    col = col_ref[here, :]
    moved = (ga_k * nu_k + ga_r * nu_r) * equal(col[:, 0:1], col[:, 1:2])
    halo[0] = moved[0:8]
    c.start(18)
    held = ga_k - ga_k * nu_k + (ga_r - ga_r * nu_r)
    rows_ref[...] = jnp.zeros_like(rows_ref)
    rows_ref[2:3, :] = jnp.sum(ga_k * shift, axis=0, keepdims=True)
    rows_ref[3:4, :] = jnp.sum(ga_r * shift, axis=0, keepdims=True)
    c.landed(18, halo.at[1])
    last = lax.broadcasted_iota(jnp.int32, (R, 1), 0) == R - 1
    grad = held + jnp.where(last, halo[1, 0:1, :], pltpu.roll(moved, R - 1, 0))
    gh = g_ref[...].astype(F32) + norm_back(normed, scale, grad * par_ref[10:11, :])
    gh_ref[...] = gh
    ghb_ref[...] = gh.astype(BF)

    def back_out(n, unused):
        pl.when(n < 7)(lambda: strip_copy(n + 1).start())
        strip_copy(n).wait()
        part = lax.dot_general(ghb_ref[:, 0:C], strip[n % 2, 0], (NT, ((), ())), preferred_element_type=F32)
        for d in range(1, 8):
            part = part + lax.dot_general(
                ghb_ref[:, d * C : (d + 1) * C], strip[n % 2, d], (NT, ((), ())), preferred_element_type=F32
            )
        for k in range(2):
            to = 2 * ((2 * n + k) % 8) + (2 * n + k) // 8
            gzp[to] = part[:, k * W : (k + 1) * W].astype(BF)
            swap.give(to)
        return 0

    lax.fori_loop(0, 8, back_out, 0)
    rows_ref[0:1, :] = jnp.sum(grad * normed, axis=0, keepdims=True)
    rows_ref[1:2, :] = jnp.sum(grad, axis=0, keepdims=True)
    for cp in saves:
        cp.wait()
    swap.all(swap.take)
    swap.all(swap.sent)
    c.finish()


def key_back(rc, gf, par, g, l, w, lt, cols, hidden, sh, vg, key_in, n2_all, far, out_far, cid):
    R, C = hidden.shape
    T, U, W = 16 * R, l.shape[1], rc.shape[2]
    return pl.pallas_call(
        key_back_kernel,
        out_shape=(
            jax.ShapeDtypeStruct((R, C), F32),
            jax.ShapeDtypeStruct((R, C), BF),
            jax.ShapeDtypeStruct((8, C), F32),
            jax.ShapeDtypeStruct((8, 2 * U + W, C // 8), BF),
            jax.ShapeDtypeStruct((16, R, W), BF),
        ),
        in_specs=[WHOLE] * 4 + [FAR] * 11,
        out_specs=(WHOLE,) * 3 + (FAR, WHOLE),
        scratch_shapes=sum_scratch(R, C)
        + [VMEM((R, C), F32), VMEM((2 * W, T), BF), VMEM((R, C), BF), VMEM((R, C), F32), VMEM((16, R, W), BF), VMEM((2, 8, C), F32)]
        + [VMEM((2, T, C // 8), BF), VMEM((2, 8, 2 * W, C // 8), BF), VMEM((T, U), BF), VMEM((U, C), BF), VMEM((U, T), BF)]
        + [VMEM(cols.shape, F32), VMEM((R, C), F32), VMEM((R, C), F32), VMEM((8, 2 * U + W, C // 8), BF)]
        + [DMA((19,)), DMA((19,)), DMA((16,)), DMA((16,)), DMA((2,)), DMA((2,)), DMA((8,))],
        compiler_params=params(cid, 60),
        name="key_back",
    )(rc, gf, par, g, l, w, lt, cols, hidden, sh, vg, key_in, n2_all, far, out_far)


def time_back_kernel(nd, gh_ref, gz_ref, par_ref, row_ref, bound_ref, early_far, x_far, o_far, s_far, col_far, zt_far, mixt_far, n1_hbm,
                     g_far, gg_far, sums_ref, mug_ref, dp_ref,
                     tab, grad_state, acc, carry, land, turned, tile, vec, early_ref, x_ref, o_ref, s_ref, col_ref, zt_ref, mixt_ref,
                     g_ref, gg_ref, d0, d1, d2, d3, cs, cr, ts, ms):
    p = Place()
    met = greet(near(p) + beside(p, nd))
    c = Copies(cs, cr)
    moves = Moves(ms)
    W = vec.shape[1]
    chunks, L = row_ref.shape[0], row_ref.shape[2]
    C = tile.shape[2]
    early_in, x_in, o_in, s_in, col_in, zt_in, mixt_in = (
        moves.start(a, b)
        for a, b in (
            (early_far, early_ref), (x_far, x_ref), (o_far, o_ref), (s_far, s_ref), (col_far, col_ref), (zt_far, zt_ref),
            (mixt_far, mixt_ref),
        )
    )
    fetch, have = column_tiles((n1_hbm,), tile, ts)
    fetch(0, 0)
    blk = rows_of(land)
    plan = gather_plan(p, c, 0, gh_ref, blk)
    sums = dp_plan(p, nd, c, 18, early_ref, dp_ref, (d0, d1, d2, d3)) if nd > 1 else no_sums(early_ref, dp_ref)
    own_vectors(p, par_ref, vec)
    met()
    plan[0]()
    early_in.wait()
    sums[0]()
    blk(p.s)[...] = gh_ref[...]
    when = {6: [plan[1], plan[2]], 11: [plan[3], plan[4], sums[1]], 14: [plan[5], plan[6], plan[7]]}
    for cp in (x_in, o_in, s_in, col_in):
        cp.wait()
    chunk = back_chunk(x_ref, o_ref, s_ref, gz_ref, col_ref, row_ref, bound_ref, vec, g_ref, sums_ref, tab, grad_state, acc, carry, turned)

    def step(n, unused):
        chunk(n)
        for at, parts in when.items():
            @pl.when(n == at)
            def _():
                for part in parts:
                    part()
        return 0

    lax.fori_loop(0, chunks, step, 0)
    saves = [moves.start(g_ref, g_far)]
    back_finish(vec, sums_ref, acc, L)
    mug_ref[...] = jnp.zeros_like(mug_ref)
    mixt_in.wait()

    def mix(d, unused):
        pl.when(d < 7)(lambda: fetch(d + 1, 0))
        have(d, 0)
        rhs = tile[d % 2]
        cols = pl.ds(pl.multiple_of(d * C, C), C)
        a = jnp.dot(turned[: 4 * W, :], rhs, preferred_element_type=F32)
        b = jnp.dot(turned[4 * W :, :], rhs, preferred_element_type=F32)
        for q in range(4):
            rows = slice(q * W, (q + 1) * W)
            diff = b[rows] - a[rows]
            gg_ref[d, rows, :] = (a[rows] + par_ref[2 + q : 3 + q, cols] * diff).astype(BF)
            mug_ref[q : q + 1, cols] = jnp.sum(mixt_ref[rows, cols].astype(F32) * diff, axis=0, keepdims=True)
        return 0

    lax.fori_loop(0, 4, mix, 0)
    plan[8]()
    sums[2]()
    lax.fori_loop(4, 8, mix, 0)
    sums[3]()
    zt_in.wait()
    plan[9]()

    def out(d, unused):
        cols = pl.ds(pl.multiple_of(d * C, C), C)
        gg_ref[d, 4 * W :, :] = jnp.dot(zt_ref[...], land[:, cols], preferred_element_type=F32).astype(BF)
        return 0

    lax.fori_loop(0, 8, out, 0)
    saves.append(moves.start(gg_ref, gg_far))
    sums[4]()
    for cp in saves:
        cp.wait()
    c.finish()


def time_back(nd, gh, gz, par, rows, bounds, early, x, o, states, cols, zt, mixt, n1_all, cid):
    T, W = o.shape
    L = rows.shape[2]
    R, C = gh.shape
    J = early.shape[1]
    return pl.pallas_call(
        functools.partial(time_back_kernel, nd),
        out_shape=(
            jax.ShapeDtypeStruct((T, 8 * W), BF),
            jax.ShapeDtypeStruct((8, 5 * W, C // 8), BF),
            jax.ShapeDtypeStruct((8, W), F32),
            jax.ShapeDtypeStruct((4, C), F32),
            jax.ShapeDtypeStruct((8 // nd, J, C // 8), F32),
        ),
        in_specs=[WHOLE] * 4 + [pl.BlockSpec(memory_space=pltpu.SMEM)] + [FAR] * 8,
        out_specs=(FAR,) * 2 + (WHOLE,) * 3,
        scratch_shapes=[
            VMEM((4, L, W), F32), VMEM((W, W), F32), VMEM((W, W), F32), VMEM((8, 4 * W), F32),
            VMEM((T, C), BF), VMEM((8 * W, T), BF), VMEM((2, T, C // 8), BF), VMEM((8 + W, W), F32),
            VMEM((8, J, C // 8), BF), VMEM(x.shape, F32), VMEM((T, W), F32), VMEM(states.shape, F32), VMEM(cols.shape, F32),
            VMEM((W, T), BF), VMEM(mixt.shape, BF), VMEM((T, 8 * W), BF), VMEM((8, 5 * W, C // 8), BF),
        ]
        + dp_scratch(J, C // 8)
        + [DMA((32,)), DMA((32,)), DMA((2,)), DMA((9,))],
        compiler_params=params(cid, 60),
        name="time_back",
    )(gh, gz, par, rows, bounds, early, x, o, states, cols, zt, mixt, n1_all)


def last_kernel(nd, x_ref, par_ref, mug_ref, head_ref, norm_ref, gg_far, l_far, w_far, gh_far, ig_ref, dp_ref, v_ref, *rest):
    scratch = rest[:7]
    o_ref, d0, d1, d2, d3, tv, b1, t1, b2, gg_ref, l_ref, w_ref, gh_ref, cs, cr, ms = rest[7:]
    p = Place()
    met = greet(near(p) + beside(p, nd))
    c = Copies(cs, cr)
    moves = Moves(ms)
    gg_in, w_in, l_in, gh_in = (
        moves.start(a, b) for a, b in ((gg_far, gg_ref), (w_far, w_ref), (l_far, l_ref), (gh_far, gh_ref))
    )
    sums = dp_plan(p, nd, c, 18, gg_ref, dp_ref, (d0, d1, d2, d3)) if nd > 1 else no_sums(gg_ref, dp_ref)
    steps = sum_plan(p, c, 0, l_ref, w_ref, o_ref, scratch)
    W = head_ref.shape[1]
    tv[...] = jnp.zeros_like(tv)
    tv[2:6, :] = mug_ref[...]
    tv[6:10, pl.ds(pl.multiple_of(p.s * W, 128), W)] = head_ref[0:4, :]
    tv[10:14, :] = norm_ref[0:4, :]
    met()
    gg_in.wait()
    sums[0]()
    l_in.wait()
    w_in.wait()
    steps[0]()
    steps[1]()
    sums[1]()
    steps[2]()
    steps[3]()
    steps[4]()
    sums[2]()
    sums[3]()
    unused, scale, normed = norm_parts(x_ref[...].astype(F32))
    gh_in.wait()
    steps[5]()
    steps[6]()
    gn = o_ref[...]
    tv[0:1, :] = jnp.sum(gn * normed, axis=0, keepdims=True)
    tv[1:2, :] = jnp.sum(gn, axis=0, keepdims=True)
    sums[4]()
    C = b1.shape[2]
    for k in range(1, nd):
        to = (p.dp + k) % nd
        c.add(31 + k, tv.at[:, pl.ds(pl.multiple_of(to * C, 128), C)], b1.at[k - 1], (to, p.s))
        c.start(31 + k)
    ig_ref[...] = gh_ref[...] + norm_back(normed, scale, gn * par_ref[0:1, :])
    total = tv[:, pl.ds(pl.multiple_of(p.dp * C, 128), C)]
    for k in range(1, nd):
        c.landed(31 + k, b1.at[k - 1])
        total = total + b1[k - 1]
    t1[...] = total
    for k in range(1, 16):
        c.add(38 + k, t1, b2.at[k - 1], p.dev((p.s + k) % 16))
        c.start(38 + k)
    for k in range(1, 16):
        c.landed(38 + k, b2.at[k - 1])
        total = total + b2[k - 1]
    v_ref[...] = total
    c.finish()


def last_sums(nd, x, par, mug, head, norm, gg, l, w, gh, cid):
    R, C = x.shape
    J = gg.shape[1]
    piece = (16, C // nd)
    return pl.pallas_call(
        functools.partial(last_kernel, nd),
        out_shape=(jax.ShapeDtypeStruct((R, C), F32), jax.ShapeDtypeStruct((8 // nd, J, C // 8), F32), jax.ShapeDtypeStruct(piece, F32)),
        in_specs=[WHOLE] * 5 + [FAR] * 4,
        out_specs=(WHOLE,) * 3,
        scratch_shapes=sum_scratch(R, C)
        + [VMEM((R, C), F32)]
        + dp_scratch(J, C // 8)
        + [VMEM((16, C), F32), VMEM((max(nd - 1, 1),) + piece, F32), VMEM(piece, F32), VMEM((15,) + piece, F32)]
        + [VMEM(gg.shape, BF), VMEM(l.shape, BF), VMEM(w.shape, BF), VMEM((R, C), F32)]
        + [DMA((54,)), DMA((54,)), DMA((4,))],
        compiler_params=params(cid, 60),
        name="last_sums",
    )(x, par, mug, head, norm, gg, l, w, gh)


def body(nd, inputs, cotangent, mix_weights, out_weight, key_weight, value_weight, recept_weight, vectors, segment_ids):
    tokens, width = inputs.shape
    group = segment_ids.shape[0]
    cols = mix_weights.shape[2]
    units = key_weight.shape[1]
    s = lax.axis_index("sp")
    ring = group // tokens
    chunks = group // CHUNK

    edge = jnp.full((1,), -1.0, F32)
    seg = jnp.concatenate([edge, segment_ids.astype(F32), edge])
    tok_cols = jnp.stack([seg[1:-1], seg[:-2], seg[2:]], axis=1)
    tok_rows = seg[1:-1].reshape(chunks, 1, CHUNK)
    ends = seg[: group + 1 : CHUNK]
    bounds = jnp.stack([ends, jnp.concatenate([(ends[1:] == ends[:-1]).astype(F32), edge])])

    n1_all, projected, z_t, mixed_time, states, hidden, n2, recept_part, out_far = time_forward(
        nd, inputs, vectors, tok_rows, bounds, mix_weights, out_weight, recept_weight, tok_cols, 0
    )
    n2_all, key_in, lifted, squared, recept_in, shift, value_t, mixt, folded, recept_far = key_side(
        nd, n2, recept_part, vectors, key_weight.T, tok_cols, value_weight, mix_weights, 1
    )
    result, grad_recept, recept_cols, grad_key, grad_key_t, value_grad = value_side(
        recept_in, cotangent, hidden, squared, value_weight, value_t, lifted, recept_far, 2
    )
    grad_hidden, grad_hidden_b, norm_rows, early, gz = key_back(
        recept_cols, grad_recept, vectors, cotangent, grad_key, key_weight.T, grad_key_t, tok_cols, hidden, shift, value_grad,
        key_in.reshape(group, width), n2_all, recept_far, out_far, 3,
    )
    grads_two, late, head_rows, mu_rows, early_sum = time_back(
        nd, grad_hidden_b, gz, vectors, tok_rows, bounds, early, projected, mixed_time, states, tok_cols, z_t, mixt, n1_all, 4
    )
    input_grad, late_sum, vector_sum = last_sums(
        nd, inputs, vectors, mu_rows, head_rows, norm_rows, late, grads_two, folded, grad_hidden, 5
    )
    piece = width // (nd * ring)
    vectors_grad = lax.dynamic_slice_in_dim(vector_sum[:14], s * piece, piece, 1)

    def columns(part):
        return part.transpose(1, 0, 2).reshape(part.shape[1], width // nd)

    early_sum, late_sum = columns(early_sum), columns(late_sum)
    return (
        result,
        input_grad,
        late_sum[: 4 * cols].reshape(4, cols, width // nd).transpose(0, 2, 1),
        late_sum[4 * cols :],
        early_sum[units : 2 * units].T,
        early_sum[:units],
        early_sum[2 * units :].T,
        vectors_grad,
    )


def solution(mesh):
    placed = (
        P(("dp", "sp"), None),
        P(("dp", "sp"), None),
        P(None, None, "sp"),
        P("sp", None),
        P(None, "sp"),
        P("sp", None),
        P(None, "sp"),
        P(),
        P("dp"),
    )
    return jax.shard_map(
        functools.partial(body, mesh.shape["dp"]),
        mesh=mesh,
        in_specs=placed,
        out_specs=(
            P(("dp", "sp"), None),
            P(("dp", "sp"), None),
            P(None, "dp", "sp"),
            P("sp", "dp"),
            P("dp", "sp"),
            P("sp", "dp"),
            P("dp", "sp"),
            P(None, ("dp", "sp")),
        ),
        check_vma=False,
    )
```
